32 devices in a mesh: img: 8 (over z, core), seq: 4 (over y, x).
Axes of the slice: x: 2, y: 2, z: 4, core: 2. Of those that a mesh axis runs over, the one named last changes fastest.
Arguments:
- images: bfloat16 [32, 28, 224, 256], P('img', 'seq'), may hold values from -6 to 6
- cotangent: bfloat16 [32, 28, 224, 256], P('img', 'seq'), may hold values from -6 to 6
- valid_mask: int32 [32, 224], P('img'), may hold values from 0 to 1, as said below
- qkv_weight: float32 [256, 768], P('seq'), may hold values from -0.375 to 0.375
- out_weight: float32 [256, 256], P('seq'), may hold values from -3.5 to 3.5
- expand_weight: float32 [256, 1024], P('seq'), may hold values from -0.375 to 0.375
- shrink_weight: float32 [1024, 256], P('seq'), may hold values from -0.1875 to 0.1875
- small_params: float32 [16, 256], P(None, 'seq')
- expand_bias: float32 [1024], P('seq'), may hold values from -0.8 to 0.8
- first_qkv: float32 [256, 768], P('seq'), may hold values from -0.00067439064 to 0.00067439064
- first_out: float32 [256, 256], P('seq'), may hold values from -0.00067439064 to 0.00067439064
- first_expand: float32 [256, 1024], P('seq'), may hold values from -0.00067439064 to 0.00067439064
- first_shrink: float32 [1024, 256], P('seq'), may hold values from -0.00067439064 to 0.00067439064
- first_small: float32 [16, 256], P(None, 'seq'), may hold values from -0.00067439064 to 0.00067439064
- first_bias: float32 [1024], P('seq'), may hold values from -0.00067439064 to 0.00067439064
- second_qkv: float32 [256, 768], P('seq'), may hold values from 1.2633409e-09 to 5.0533635e-09
- second_out: float32 [256, 256], P('seq'), may hold values from 1.5791761e-10 to 6.3167044e-10
- second_expand: float32 [256, 1024], P('seq'), may hold values from 1.2633409e-09 to 5.0533635e-09
- second_shrink: float32 [1024, 256], P('seq'), may hold values from 1.2633409e-09 to 5.0533635e-09
- second_small: float32 [16, 256], P(None, 'seq'), may hold values from 1.2633409e-09 to 5.0533635e-09
- second_bias: float32 [1024], P('seq'), may hold values from 1.5791761e-10 to 6.3167044e-10
Outputs:
- block_out: float32 [32, 28, 224, 256], P('img', 'seq')
- input_grad: float32 [32, 28, 224, 256], P('img', 'seq')
- grad_norm: float32 [], replicated
- new_first_qkv: float32 [256, 768], P('seq')
- new_first_out: float32 [256, 256], P('seq')
- new_first_expand: float32 [256, 1024], P('seq')
- new_first_shrink: float32 [1024, 256], P('seq')
- new_first_small: float32 [16, 256], P(None, 'seq')
- new_first_bias: float32 [1024], P('seq')
- new_second_qkv: float32 [256, 768], P('seq')
- new_second_out: float32 [256, 256], P('seq')
- new_second_expand: float32 [256, 1024], P('seq')
- new_second_shrink: float32 [1024, 256], P('seq')
- new_second_small: float32 [16, 256], P(None, 'seq')
- new_second_bias: float32 [1024], P('seq')
- new_qkv_weight: float32 [256, 768], P('seq')
- new_out_weight: float32 [256, 256], P('seq')
- new_expand_weight: float32 [256, 1024], P('seq')
- new_shrink_weight: float32 [1024, 256], P('seq')
- new_small_params: float32 [16, 256], P(None, 'seq')
- new_expand_bias: float32 [1024], P('seq')
The draws below stay inside these ranges and needn't reach their ends.
Inputs may be any that keep to these rules, and one draw needn't show every extreme that they name: `valid_mask`: every image has exactly 168 ones, and every aligned group of 7 columns holds at least one.
All inputs are finite; a program needn't handle non-finite values.
Results may differ from the reference program's by a relative error of at most 0.012.
The reference program's roundings to bfloat16 on the way count: a program that leaves them out, or rounds other values in their place, can miss the bound.
Values may be sent and summed in bfloat16 or wider, within the bound.
No kernel may reach another device: no remote copies, remote signals or barrier semaphores. Data moves between devices by JAX's collectives and lax.ppermute only.
A program may use at most 320 MiB of HBM per device.

```python
import math
import jax
import jax.numpy as jnp
from jax import lax

C = 256
FF = 1024
HEADS = 8
HEAD_DIM = 32
STRIPE = 7
W = 224
VALID = 168
STEP = 10
IMAGES = 32
H = 28
NPARAM = 791552


def draw_valid_mask(key, part):
    key = jax.random.fold_in(key, 7)
    pick_key, rank_key = jax.random.split(key)
    stripe_count = W // STRIPE
    picked = jax.random.randint(pick_key, (IMAGES, stripe_count), 0, STRIPE)
    offsets = jnp.arange(STRIPE, dtype=jnp.int32)
    chosen = (offsets[None, None, :] == picked[:, :, None]).reshape(IMAGES, W)
    columns = jnp.arange(W, dtype=jnp.int32)
    random_part = jax.random.randint(rank_key, (IMAGES, W), 0, 65536)
    scores = jnp.where(chosen, columns[None, :] - W, random_part * W + columns[None, :])
    order_idx = jnp.argsort(scores, axis=1)
    rank_of = jnp.argsort(order_idx, axis=1)
    return (rank_of < VALID).astype(jnp.int32)


def draw_small_params(key, part):
    key = jax.random.fold_in(key, 13)
    tap_key, gain_key, shift_key = jax.random.split(key, 3)
    position = jnp.arange(C, dtype=jnp.float32) / (C - 1)
    ramp_line = 0.6 + 1.2 * position
    tap_rows = 0.03 * jax.random.truncated_normal(tap_key, -4.0, 4.0, (9, C), jnp.float32)
    gain_rows = ramp_line[None, :] * jax.random.uniform(gain_key, (2, C), jnp.float32, 0.8, 1.2)
    shift_rows = 0.2 * jax.random.truncated_normal(shift_key, -4.0, 4.0, (5, C), jnp.float32)
    return jnp.concatenate([tap_rows, gain_rows[0:1], shift_rows[0:3], gain_rows[1:2], shift_rows[3:5]], axis=0)


def block_scale(stream_key, shape, shards, least, top_value):
    gain, own = 1.0, jax.random.fold_in(stream_key, 6)
    for dim, shards_of in shards:
        steps = jnp.exp(jax.random.uniform(jax.random.fold_in(own, dim), (shards_of,), jnp.float32, least / len(shards), top_value / len(shards)))
        gain = gain * jnp.repeat(steps, shape[dim] // shards_of).reshape([-1 if axis == dim else 1 for axis in range(len(shape))])
    return gain


def centred(rng, dims, width, reach, shards=(), held_as=jnp.bfloat16):
    entries = width * jax.random.normal(rng, dims, jnp.float32)
    if shards:
        entries = entries * block_scale(rng, dims, shards, -0.22, 0.18)
    return jnp.clip(entries, -reach, reach).astype(held_as)


def setup_inputs(seed: int = 0) -> dict:
    key_of = jax.random.split(jax.random.key(seed), 22)
    return {
        "images": centred(key_of[0], (IMAGES, H, W, C), 1.0, 6.0, ((0, 8), (1, 4))),
        "cotangent": centred(key_of[1], (IMAGES, H, W, C), 1.0, 6.0, ((0, 8), (1, 4))),
        "valid_mask": draw_valid_mask(jax.random.fold_in(key_of[21], 71), 0),
        "qkv_weight": centred(key_of[3], (C, 3 * C), C ** -0.5, 0.375, ((0, 4),), jnp.float32),
        "out_weight": centred(key_of[4], (C, C), 3 ** -0.5, 3.5, ((0, 4),), jnp.float32),
        "expand_weight": centred(key_of[5], (C, FF), C ** -0.5, 0.375, ((0, 4),), jnp.float32),
        "shrink_weight": centred(key_of[6], (FF, C), FF ** -0.5, 0.1875, ((0, 4),), jnp.float32),
        "small_params": draw_small_params(jax.random.fold_in(key_of[21], 71), 0),
        "expand_bias": centred(key_of[8], (FF,), 0.2, 0.8, ((0, 4),), jnp.float32),
        "first_qkv": centred(key_of[9], (C, 3 * C), (0.111 * NPARAM ** -0.5), 0.00067439064, ((0, 4),), jnp.float32),
        "first_out": centred(key_of[10], (C, C), (0.111 * NPARAM ** -0.5), 0.00067439064, ((0, 4),), jnp.float32),
        "first_expand": centred(key_of[11], (C, FF), (0.111 * NPARAM ** -0.5), 0.00067439064, ((0, 4),), jnp.float32),
        "first_shrink": centred(key_of[12], (FF, C), (0.111 * NPARAM ** -0.5), 0.00067439064, ((0, 4),), jnp.float32),
        "first_small": centred(key_of[13], (16, C), (0.111 * NPARAM ** -0.5), 0.00067439064, ((1, 4),), jnp.float32),
        "first_bias": centred(key_of[14], (FF,), (0.111 * NPARAM ** -0.5), 0.00067439064, ((0, 4),), jnp.float32),
        "second_qkv": jnp.clip(jnp.exp(math.log(5.053363505425068e-09) - 1.3862944 * jax.random.uniform(key_of[15], (C, 3 * C), jnp.float32) ** block_scale(key_of[15], (C, 3 * C), ((0, 4),), -0.2, 0.2)), 1.263340876356267e-09, 5.053363505425068e-09),
        "second_out": jnp.clip(jnp.exp(math.log(6.316704381781335e-10) - 1.3862944 * jax.random.uniform(key_of[16], (C, C), jnp.float32) ** block_scale(key_of[16], (C, C), ((0, 4),), -0.2, 0.2)), 1.5791760954453338e-10, 6.316704381781335e-10),
        "second_expand": jnp.clip(jnp.exp(math.log(5.053363505425068e-09) - 1.3862944 * jax.random.uniform(key_of[17], (C, FF), jnp.float32) ** block_scale(key_of[17], (C, FF), ((0, 4),), -0.2, 0.2)), 1.263340876356267e-09, 5.053363505425068e-09),
        "second_shrink": jnp.clip(jnp.exp(math.log(5.053363505425068e-09) - 1.3862944 * jax.random.uniform(key_of[18], (FF, C), jnp.float32) ** block_scale(key_of[18], (FF, C), ((0, 4),), -0.2, 0.2)), 1.263340876356267e-09, 5.053363505425068e-09),
        "second_small": jnp.clip(jnp.exp(math.log(5.053363505425068e-09) - 1.3862944 * jax.random.uniform(key_of[19], (16, C), jnp.float32) ** block_scale(key_of[19], (16, C), ((1, 4),), -0.2, 0.2)), 1.263340876356267e-09, 5.053363505425068e-09),
        "second_bias": jnp.clip(jnp.exp(math.log(6.316704381781335e-10) - 1.3862944 * jax.random.uniform(key_of[20], (FF,), jnp.float32) ** block_scale(key_of[20], (FF,), ((0, 4),), -0.2, 0.2)), 1.5791760954453338e-10, 6.316704381781335e-10),
    }


@jax.custom_vjp
def low(v):
    return lax.optimization_barrier(v.astype(jnp.bfloat16)).astype(jnp.float32)

@jax.custom_vjp
def low_back(v):
    return v

def low_keep(v):
    return (low(v), None)

def low_pass(kept, grad):
    return (grad,)

def back_keep(v):
    return (v, None)

def back_low(kept, grad):
    return (low(grad),)
low.defvjp(low_keep, low_pass)
low_back.defvjp(back_keep, back_low)
EPS_NORM = 1e-05
NEG_FILL = -1000000000.0
BETA_ONE = 0.9
BETA_TWO = 0.999
ADAM_EPS = 1e-08
WEIGHT_DECAY = 0.05
CLIP_NORM = 1.0
RATE_MATRIX = 0.1
RATE_OUTPUT = 0.5
RATE_SMALL = 0.3
HIGHEST = lax.Precision.HIGHEST

def layer_norm(values, gain_row, offset_row):
    center = values - lax.optimization_barrier(jnp.mean(values, axis=-1, keepdims=True))
    spread = lax.optimization_barrier(jnp.mean(center * center, axis=-1, keepdims=True))
    return center * lax.rsqrt(spread + EPS_NORM) * gain_row + offset_row

def window_attend(window):
    queries, key_part, value_part, valid_keys = window
    raw_scores = jnp.einsum('qhd,khd->hqk', queries, key_part, precision=HIGHEST)
    scores = low_back(raw_scores * HEAD_DIM ** (-0.5))
    scores = jnp.where(valid_keys[None, None, :], scores, NEG_FILL)
    highest = lax.optimization_barrier(jnp.max(scores, axis=-1, keepdims=True))
    weights = jnp.exp(scores - highest)
    weights = weights / lax.optimization_barrier(jnp.sum(weights, axis=-1, keepdims=True))
    return jnp.einsum('hqk,khd->qhd', low(weights), value_part, precision=HIGHEST)

def position_encode(value_grid, tap_rows, offset_row):
    size_a, size_b = (value_grid.shape[1], value_grid.shape[2])
    padded = jnp.pad(value_grid, ((0, 0), (1, 1), (1, 1), (0, 0)))
    result = jnp.zeros(value_grid.shape, jnp.float32)
    for tap_row in range(3):
        for tap_col in range(3):
            result = result + padded[:, tap_row:tap_row + size_a, tap_col:tap_col + size_b, :] * tap_rows[3 * tap_row + tap_col]
    return result + offset_row

def branch(grid_part, valid_keys, tap_rows, offset_row):
    windows, size_a, size_b, triple = grid_part.shape
    half_width = triple // 3
    head_count = HEADS // 2
    flat_grid = grid_part.reshape(windows, size_a * size_b, 3, head_count, half_width // head_count)
    attended = lax.map(jax.checkpoint(window_attend), (flat_grid[:, :, 0], flat_grid[:, :, 1], flat_grid[:, :, 2], valid_keys))
    local_term = position_encode(grid_part[..., 2 * half_width:], tap_rows, offset_row)
    return attended.reshape(windows, size_a, size_b, half_width) + local_term

def block(params_in, image_in, column_valid):
    qkv_low, out_low, expand_low, shrink_low, small_low, bias_low = [low(entry) for entry in params_in]
    height, grid_width, channels = image_in.shape
    half_width = channels // 2
    normed = low(layer_norm(image_in, small_low[9], small_low[10]))
    normed_flat = normed.reshape(-1, channels)
    across_proj = jnp.dot(normed_flat, qkv_low[:, :3 * half_width], precision=HIGHEST)
    across_mixed = low(low_back(across_proj)).reshape(height, grid_width, 3 * half_width)
    down_proj = jnp.dot(low_back(normed_flat), qkv_low[:, 3 * half_width:], precision=HIGHEST)
    down_mixed = low(low_back(down_proj)).reshape(height, grid_width, 3 * half_width)
    across = across_mixed.reshape(height // STRIPE, STRIPE, grid_width, 3 * half_width)
    across_valid = jnp.broadcast_to(column_valid[None, None, :], (height // STRIPE, STRIPE, grid_width)).reshape(height // STRIPE, -1)
    across_out = branch(across, across_valid, small_low[0:9, :half_width], small_low[11, :half_width])
    across_out = across_out.reshape(height, grid_width, half_width)
    stripes = grid_width // STRIPE
    down_grid = down_mixed.reshape(height, stripes, STRIPE, 3 * half_width).transpose(1, 0, 2, 3)
    down_valid = jnp.broadcast_to(column_valid.reshape(stripes, 1, STRIPE), (stripes, height, STRIPE)).reshape(stripes, -1)
    down_out = branch(down_grid, down_valid, small_low[0:9, half_width:], small_low[11, half_width:])
    down_out = down_out.transpose(1, 0, 2, 3).reshape(height, grid_width, half_width)
    joined = low(low_back(jnp.concatenate([across_out, down_out], axis=-1)))
    attended_out = low_back(jnp.dot(joined.reshape(-1, channels), out_low, precision=HIGHEST) + small_low[12])
    middle = image_in.reshape(-1, channels) + attended_out
    normed_two = low(layer_norm(middle, small_low[13], small_low[14]))
    hidden = low_back(jnp.dot(normed_two, expand_low, precision=HIGHEST) + bias_low)
    active = low(jax.nn.gelu(hidden, approximate=False))
    mlp_out = low_back(jnp.dot(active, shrink_low, precision=HIGHEST) + small_low[15])
    return (middle + mlp_out).reshape(height, grid_width, channels)

def adam_update(weight, first_old, second_old, grad_value, rate_value, decay_value):
    new_first = BETA_ONE * first_old + (1.0 - BETA_ONE) * grad_value
    new_second = BETA_TWO * second_old + (1.0 - BETA_TWO) * grad_value * grad_value
    first_hat = new_first / (1.0 - BETA_ONE ** STEP)
    second_hat = new_second / (1.0 - BETA_TWO ** STEP)
    new_weight = weight - rate_value * (first_hat / (jnp.sqrt(second_hat) + ADAM_EPS) + decay_value * weight)
    return (new_first, new_second, new_weight)

def reference(images, cotangent, valid_mask, qkv_weight, out_weight, expand_weight, shrink_weight, small_params, expand_bias, first_qkv, first_out, first_expand, first_shrink, first_small, first_bias, second_qkv, second_out, second_expand, second_shrink, second_small, second_bias):
    params = (qkv_weight, out_weight, expand_weight, shrink_weight, small_params, expand_bias)

    def one_image(summed, item_pack):
        image_rows, back_rows, mask_row = item_pack
        column_valid = mask_row > 0
        result, pull = jax.vjp(lambda params_in, image_in: block(params_in, image_in, column_valid), params, image_rows.astype(jnp.float32))
        grads, image_grad = pull(back_rows.astype(jnp.float32))
        return (jax.tree.map(jnp.add, summed, grads), (result, image_grad))
    zeros_init = jax.tree.map(jnp.zeros_like, params)
    summed, (block_out, input_grad) = lax.scan(one_image, zeros_init, (images, cotangent, valid_mask))
    squared = jnp.float32(0.0)
    for grad_value in summed:
        squared = squared + jnp.sum(grad_value * grad_value)
    grad_norm = jnp.sqrt(squared)
    factor = CLIP_NORM / jnp.maximum(grad_norm, CLIP_NORM)
    rates = (RATE_MATRIX, RATE_OUTPUT, RATE_MATRIX, RATE_MATRIX, RATE_SMALL, RATE_MATRIX)
    decays = (WEIGHT_DECAY, WEIGHT_DECAY, WEIGHT_DECAY, WEIGHT_DECAY, 0.0, 0.0)
    firsts = (first_qkv, first_out, first_expand, first_shrink, first_small, first_bias)
    seconds = (second_qkv, second_out, second_expand, second_shrink, second_small, second_bias)
    updated = [adam_update(params[index], firsts[index], seconds[index], summed[index] * factor, rates[index], decays[index]) for index in range(6)]
    return (block_out, input_grad, grad_norm, updated[0][0], updated[1][0], updated[2][0], updated[3][0], updated[4][0], updated[5][0], updated[0][1], updated[1][1], updated[2][1], updated[3][1], updated[4][1], updated[5][1], updated[0][2], updated[1][2], updated[2][2], updated[3][2], updated[4][2], updated[5][2])
```

```python
import functools

import jax
import jax.numpy as jnp
from jax import lax
from jax.experimental import pallas as pl
from jax.experimental.pallas import tpu as pltpu
from jax.sharding import PartitionSpec as P

HEADS = 8
STRIPE = 7
STEP = 10
VALID = 168

EPS_NORM = 1e-05
BETA_ONE = 0.9
BETA_TWO = 0.999
ADAM_EPS = 1e-08
WEIGHT_DECAY = 0.05
CLIP_NORM = 1.0
RATE_MATRIX = 0.1
RATE_OUTPUT = 0.5
RATE_SMALL = 0.3
INV_ROOT_TWO = 0.7071067811865476
INV_ROOT_TAU = 0.3989422804014327
LOG2E = 1.4426950408889634

BF = jnp.bfloat16
F32 = jnp.float32
HALF = 128
BRANCH_HEADS = 4
HEAD_DIM = 32
SCALE = HEAD_DIM**-0.5
GROUP = 8
MASKED = -1e38
EXPONENT_BOUND = 60.0
VMEM_LIMIT = 60 * 2**20


def dot(left, right):
    return jnp.dot(left, right, preferred_element_type=F32)


def dot_nt(left, right):
    return lax.dot_general(left, right, (((1,), (1,)), ((), ())), preferred_element_type=F32)


def dot_tn(left, right):
    return lax.dot_general(left, right, (((0,), (0,)), ((), ())), preferred_element_type=F32)


def iota(shape, dim):
    return lax.broadcasted_iota(jnp.int32, shape, dim)


def one_hot(condition):
    return jnp.where(condition, 1.0, 0.0).astype(BF)


def expand_condition(wide, width):
    e, c = iota((wide, width), 0), iota((wide, width), 1)
    return ((e & 7) < STRIPE) & (c == STRIPE * (e >> 3) + (e & 7))


def contract_matrix(width, wide):
    c, e = iota((width, wide), 0), iota((width, wide), 1)
    return one_hot(((e & 7) < STRIPE) & (c == STRIPE * (e >> 3) + (e & 7)))


def normalize(values, gain_row, offset_row):
    center = values - jnp.mean(values, axis=-1, keepdims=True)
    spread = jnp.mean(center * center, axis=-1, keepdims=True)
    recip = lax.rsqrt(spread + EPS_NORM)
    scaled = center * recip
    return scaled * gain_row + offset_row, scaled, recip


def normalize_back(grad_out, scaled, recip, gain_row):
    grad_scaled = grad_out * gain_row
    inner_one = jnp.mean(grad_scaled, axis=-1, keepdims=True)
    inner_two = jnp.mean(grad_scaled * scaled, axis=-1, keepdims=True)
    return recip * (grad_scaled - inner_one - scaled * inner_two)


def fold_rows(values):
    rows, columns = values.shape
    return jnp.sum(values.reshape(rows // 8, 8, columns), axis=0)


def pieces_of(values):
    first = values.astype(BF).astype(F32)
    rest = values - first
    second = rest.astype(BF).astype(F32)
    return first, second, (rest - second).astype(BF).astype(F32)


def lane_place(rows, head):
    lane = iota((rows, HALF), 1)
    return ((lane >> 5) - head) & 3


def lane_sub(rows):
    return iota((rows, HALF), 1) & 31


def head_key(keys, keys_rolled, bias, head):
    rows = keys.shape[0]
    place, sub = lane_place(rows, head), lane_sub(rows)
    extra = jnp.where(sub < 3, 1.0, jnp.where(sub == 3, bias, 0.0))
    return jnp.where(
        place == 0, keys, jnp.where(place == 1, keys_rolled, jnp.where(place == 2, extra, 0.0))
    ).astype(BF)


def head_value(values, head):
    place = lane_place(values.shape[0], head)
    return jnp.where(place == 0, values, jnp.where(place == 1, 1.0, 0.0)).astype(BF)


def query_parts(queries, shift):
    rows = queries.shape[0]
    scaled = queries * (SCALE * LOG2E)
    high = scaled.astype(BF).astype(F32)
    low = pltpu.roll(scaled - high, HEAD_DIM, 1)
    one, two, three = pieces_of(-pltpu.roll(shift, 2 * HEAD_DIM, 1))
    sub = lane_sub(rows)
    extra = jnp.where(
        sub == 0,
        one,
        jnp.where(sub == 1, two, jnp.where(sub == 2, three, jnp.where(sub == 3, 1.0, 0.0))),
    )
    return high, low, extra


def head_query(parts, head):
    high, low, extra = parts
    place = lane_place(high.shape[0], head)
    return jnp.where(
        place == 0, high, jnp.where(place == 1, low, jnp.where(place == 2, extra, 0.0))
    ).astype(BF)


def grad_parts(grad, attended):
    rows = grad.shape[0]
    product = grad * attended
    block = one_hot((iota((HALF, HALF), 0) >> 5) == (iota((HALF, HALF), 1) >> 5))
    first, second, third = pieces_of(product)
    inner = dot(first.astype(BF), block) + dot(second.astype(BF), block) + dot(third.astype(BF), block)
    one, two, three = pieces_of(-pltpu.roll(inner, HEAD_DIM, 1))
    sub = lane_sub(rows)
    extra = jnp.where(sub == 0, one, jnp.where(sub == 1, two, jnp.where(sub == 2, three, 0.0)))
    return grad, extra


def head_grad(parts, head):
    grad, extra = parts
    place = lane_place(grad.shape[0], head)
    return jnp.where(place == 0, grad, jnp.where(place == 1, extra, 0.0)).astype(BF)


def head_norms(values):
    block = one_hot((iota((HALF, HALF), 0) >> 5) == (iota((HALF, HALF), 1) >> 5))
    sums = dot((values * values * 1.02).astype(BF), block)
    return jnp.max(sums, axis=0, keepdims=True)


def exceeds(query_norms, key_norms):
    bound = jnp.max(query_norms * key_norms)
    return jnp.logical_not(bound <= EXPONENT_BOUND * EXPONENT_BOUND)


def attend_heads(query_rows, shift, keys_of, values_of):
    rows = query_rows.shape[0]
    parts = query_parts(query_rows, shift)
    attended = jnp.zeros((rows, HALF), F32)
    log_total = jnp.zeros((rows, HALF), F32)
    for head in range(BRANCH_HEADS):
        scores = dot_nt(head_query(parts, head), keys_of(head))
        weights = jnp.exp2(scores).astype(BF)
        result = dot(weights, values_of(head))
        totals = pltpu.roll(result, HALF - HEAD_DIM, 1)
        mine = lane_place(rows, head) == 0
        attended = jnp.where(mine, result / totals, attended)
        log_total = jnp.where(mine, jnp.log(totals) * LOG2E + shift, log_total)
    return attended, log_total


def highest_scores(query_rows, keys_of):
    rows = query_rows.shape[0]
    parts = query_parts(query_rows, jnp.zeros((rows, HALF), F32))
    shift = jnp.zeros((rows, HALF), F32)
    for head in range(BRANCH_HEADS):
        scores = dot_nt(head_query(parts, head), keys_of(head))
        highest = jnp.max(scores, axis=-1, keepdims=True)
        shift = jnp.where(lane_place(rows, head) == 0, highest, shift)
    return shift


def attend_heads_back(query_rows, grad_rows, attended, log_total, keys_of, values_of):
    rows = query_rows.shape[0]
    eye = one_hot(iota((HALF, HALF), 0) == iota((HALF, HALF), 1))
    query_turned = dot_nt(eye, query_rows.astype(BF)).astype(BF)
    grad_turned = dot_nt(eye, grad_rows.astype(BF)).astype(BF)
    parts = query_parts(query_rows, log_total)
    back_parts = grad_parts(grad_rows, attended)
    grad_queries = jnp.zeros((rows, HALF), F32)
    grad_keys, grad_values = [], []
    for head in range(BRANCH_HEADS):
        keys, values = keys_of(head), values_of(head)
        weights = jnp.exp2(dot_nt(head_query(parts, head), keys))
        weights_low = weights.astype(BF)
        grad_weights = dot_nt(head_grad(back_parts, head), values)
        grad_scores = (weights * grad_weights).astype(BF)
        lanes = slice(head * HEAD_DIM, (head + 1) * HEAD_DIM)
        grad_values.append(dot(grad_turned[lanes], weights_low))
        grad_keys.append(dot(query_turned[lanes], grad_scores))
        mine = lane_place(rows, head) == 0
        grad_queries = jnp.where(mine, dot(grad_scores, keys), grad_queries)
    return grad_queries * SCALE, grad_keys, grad_values


def shift_down(values):
    rows = values.shape[0]
    return jnp.where(iota(values.shape, 0) == 0, 0.0, pltpu.roll(values, 1, 0))


def shift_up(values):
    rows = values.shape[0]
    return jnp.where(iota(values.shape, 0) == rows - 1, 0.0, pltpu.roll(values, rows - 1, 0))


def project_kernel(dims, ways, *refs):
    rows, width, wide, wide_part = dims
    me_ref, x_ref, small_ref, weight_ref, across_ref = refs[:5]
    down_refs = refs[5 : 5 + ways]
    down_ref = refs[5 + ways]
    gain, offset = small_ref[9:10], small_ref[10:11]
    expand = one_hot(expand_condition(wide, width))
    for row in range(rows):
        span = slice(row * width, (row + 1) * width)
        normed, _, _ = normalize(x_ref[0, span].astype(F32), gain, offset)
        normed = normed.astype(BF)
        across_ref[0, span] = dot(normed, weight_ref[:, : 3 * HALF]).astype(BF)
        spread = dot(expand, normed).astype(BF)
        down = dot(spread, weight_ref[:, 3 * HALF :]).astype(BF)
        down_ref[row] = down
        for distance in range(ways):
            start = pl.multiple_of((me_ref[0] ^ distance) * wide_part, wide_part)
            down_refs[distance][0, row] = down_ref[row, pl.ds(start, wide_part)]


def rank_row(mask_row, width):
    lower = one_hot(iota((width, width), 0) <= iota((width, width), 1))
    counted = dot(jnp.broadcast_to(mask_row, (8, width)).astype(BF), lower)[0:1]
    return jnp.where(mask_row > 0.0, counted - 1.0, -1.0)


def across_kernel(
    dims,
    across_ref,
    mask_ref,
    small_ref,
    joined_ref,
    attended_ref,
    total_ref,
    keys_ref,
    values_ref,
    shift_ref,
):
    rows, width, kept, key_rows, chunk = dims
    tokens = rows * width
    image = pl.program_id(0)
    ranks = rank_row(mask_ref[pl.ds(image, 1)].astype(F32), width)
    select = one_hot(iota((kept, width), 0).astype(F32) == ranks)
    bias = jnp.where(iota((kept, HALF), 0) >= VALID, MASKED, 0.0)
    key_norms = jnp.zeros((1, HALF), F32)
    for row in range(rows):
        picked = dot(select, across_ref[0, row * width : (row + 1) * width, HALF:])
        keys, values = picked[:, :HALF], picked[:, HALF:]
        rolled = pltpu.roll(keys, HEAD_DIM, 1)
        key_norms = jnp.maximum(key_norms, head_norms(keys))
        span = slice(row * kept, (row + 1) * kept)
        for head in range(BRANCH_HEADS):
            keys_ref[0, head, span] = head_key(keys, rolled, bias, head)
            values_ref[0, head, span] = head_value(values, head)
    spare = key_rows - rows * kept
    if spare:
        nothing = jnp.zeros((spare, HALF), F32)
        for head in range(BRANCH_HEADS):
            keys_ref[0, head, rows * kept :] = head_key(
                nothing, nothing, jnp.full((spare, HALF), MASKED, F32), head
            )
            values_ref[0, head, rows * kept :] = nothing.astype(BF)

    query_norms = head_norms(across_ref[0, :, :HALF].astype(F32) * (SCALE * LOG2E))
    large = exceeds(query_norms, key_norms)

    @pl.when(image == 0)
    def _():
        shift_ref[...] = jnp.zeros_like(shift_ref)

    def rows_of(step):
        return pl.ds(pl.multiple_of(step * chunk, 16), chunk)

    def keys_of(head):
        return keys_ref[0, head]

    def values_of(head):
        return values_ref[0, head]

    @pl.when(large)
    def _():
        def highest(step, carry):
            span = rows_of(step)
            shift_ref[span] = highest_scores(across_ref[0, span, :HALF].astype(F32), keys_of)
            return carry

        lax.fori_loop(0, tokens // chunk, highest, 0)

    def attend(step, carry):
        span = rows_of(step)
        attended, log_total = attend_heads(
            across_ref[0, span, :HALF].astype(F32), shift_ref[span], keys_of, values_of
        )
        attended_ref[0, span] = attended
        total_ref[0, span] = log_total
        return carry

    lax.fori_loop(0, tokens // chunk, attend, 0)

    @pl.when(large)
    def _():
        shift_ref[...] = jnp.zeros_like(shift_ref)

    def value_row(row):
        return across_ref[0, row * width : (row + 1) * width, 2 * HALF :].astype(F32)

    for row in range(rows):
        sums = [jnp.zeros((width, HALF), F32) for _ in range(3)]
        for tap_row in range(3):
            source = row + tap_row - 1
            if 0 <= source < rows:
                values = value_row(source)
                for tap_col in range(3):
                    tap = 3 * tap_row + tap_col
                    sums[tap_col] = sums[tap_col] + values * small_ref[tap : tap + 1, :HALF]
        local = shift_down(sums[0]) + sums[1] + shift_up(sums[2]) + small_ref[11:12, :HALF]
        span = slice(row * width, (row + 1) * width)
        joined_ref[0, span] = (attended_ref[0, span] + local).astype(BF)


def assemble(me_ref, pieces, target_ref, dim, step):
    for distance, piece in enumerate(pieces):
        place = me_ref[0] ^ distance
        if dim == 0:
            target_ref[pl.ds(place * step, step)] = piece[0].astype(target_ref.dtype)
        else:
            target_ref[:, pl.ds(pl.multiple_of(place * step, step), step)] = piece[0].astype(
                target_ref.dtype
            )


def down_setup(me_ref, mask_ref, column_ref, width, wide, wide_part):
    image = pl.program_id(0)
    mask_row = mask_ref[pl.ds(image, 1)].astype(F32)
    valid = one_hot(expand_condition(wide, width) & (mask_row > 0.0))
    column_ref[...] = dot(valid, jnp.ones((width, HALF), BF))
    return pl.multiple_of(me_ref[0] * wide_part, GROUP)


def window_bias(column_ref, start, window, height):
    valid = column_ref[pl.ds(start + pl.multiple_of(window * GROUP, GROUP), GROUP)]
    bias = jnp.where(valid > 0.5, 0.0, MASKED)
    return jnp.broadcast_to(bias[None], (height, GROUP, HALF)).reshape(height * GROUP, HALF)


def pad_keys(block, spare, fill):
    if not spare:
        return block
    return jnp.concatenate([block, jnp.full((spare, HALF), 0.0, F32) + fill], axis=0)


def window_operands(keys, values, bias, spare):
    rolled = pltpu.roll(keys, HEAD_DIM, 1)
    keys_in = pad_keys(keys, spare, 0.0)
    rolled_in = pad_keys(rolled, spare, 0.0)
    bias_in = pad_keys(bias, spare, MASKED)
    values_in = pad_keys(values, spare, 0.0)
    key_list = [head_key(keys_in, rolled_in, bias_in, head) for head in range(BRANCH_HEADS)]
    value_list = [head_value(values_in, head) for head in range(BRANCH_HEADS)]
    return key_list, value_list


def grid_shift(values, amount):
    return pltpu.roll(values, amount % GROUP, 1)


def grid_stack(values):
    edge = jnp.zeros((1,) + values.shape[1:], F32)
    return jnp.concatenate([edge, values, edge], axis=0)


def down_kernel(dims, ways, *refs):
    height, width, wide, wide_part, spare = dims
    me_ref, mask_ref, small_ref = refs[:3]
    pieces_in = refs[3 : 3 + ways]
    joined_refs = refs[3 + ways : 3 + 2 * ways]
    attended_ref, total_ref, mixed_ref, joined_ref, column_ref, shift_ref = refs[3 + 2 * ways :]
    rows = height // ways
    start = down_setup(me_ref, mask_ref, column_ref, width, wide, wide_part)
    assemble(me_ref, pieces_in, mixed_ref, 0, rows)
    tokens = height * GROUP
    windows = wide_part // GROUP

    @pl.when(pl.program_id(0) == 0)
    def _():
        shift_ref[...] = jnp.zeros_like(shift_ref)

    everything = mixed_ref[...].reshape(height * wide_part, 3 * HALF)
    large = exceeds(
        head_norms(everything[:, :HALF] * (SCALE * LOG2E)), head_norms(everything[:, HALF : 2 * HALF])
    )

    def one_window(window, carry):
        span = pl.ds(pl.multiple_of(window * GROUP, GROUP), GROUP)
        grid = mixed_ref[:, span]
        flat = grid.reshape(tokens, 3 * HALF)
        queries, keys, values = (flat[:, part * HALF : (part + 1) * HALF] for part in range(3))
        bias = window_bias(column_ref, start, window, height)
        key_list, value_list = window_operands(keys, values, bias, spare)

        @pl.when(large)
        def _():
            shift_ref[...] = highest_scores(queries, lambda head: key_list[head])

        attended, log_total = attend_heads(
            queries, shift_ref[...], lambda head: key_list[head], lambda head: value_list[head]
        )
        attended_ref[0, :, span] = attended.reshape(height, GROUP, HALF)
        total_ref[0, :, span] = log_total.reshape(height, GROUP, HALF)
        stacked = grid_stack(values.reshape(height, GROUP, HALF))
        sums = [jnp.zeros((height, GROUP, HALF), F32) for _ in range(3)]
        for tap_row in range(3):
            for tap_col in range(3):
                tap = 3 * tap_row + tap_col
                sums[tap_col] = sums[tap_col] + stacked[tap_row : tap_row + height] * small_ref[
                    tap : tap + 1, HALF:
                ].reshape(1, 1, HALF)
        local = grid_shift(sums[0], 1) + sums[1] + grid_shift(sums[2], -1)
        local = local + small_ref[11:12, HALF:].reshape(1, 1, HALF)
        joined_ref[:, span] = attended.reshape(height, GROUP, HALF) + local
        return carry

    lax.fori_loop(0, windows, one_window, 0)

    @pl.when(large)
    def _():
        shift_ref[...] = jnp.zeros_like(shift_ref)

    for distance in range(ways):
        place = me_ref[0] ^ distance
        joined_refs[distance][0] = joined_ref[pl.ds(place * rows, rows)].astype(BF)


def gelu_parts(hidden):
    size = jnp.abs(hidden) * INV_ROOT_TWO
    ratio = 1.0 / (1.0 + 0.3275911 * size)
    poly = ratio * (
        0.127414796
        + ratio * (-0.142248368 + ratio * (0.7107068705 + ratio * (-0.7265760135 + ratio * 0.5307027145)))
    )
    decay = jnp.exp2(hidden * hidden * (-0.5 * LOG2E))
    tail = poly * decay
    return jnp.where(hidden >= 0.0, 1.0 - tail, tail), decay * INV_ROOT_TAU


def middle_kernel(dims, ways, *refs):
    rows, width, wide, wide_part, chunk, hidden_part = dims
    me_ref, x_ref, cot_ref, across_ref = refs[:4]
    pieces_in = refs[4 : 4 + ways]
    out_ref, expand_ref, shrink_ref, small_ref, bias_ref = refs[4 + ways : 9 + ways]
    block_ref, middle_ref, grad_across_ref = refs[9 + ways : 12 + ways]
    grad_refs = refs[12 + ways : 12 + 2 * ways]
    dout_ref, dexpand_ref, dshrink_ref, dbias_ref, dsmall_ref = refs[12 + 2 * ways : 17 + 2 * ways]
    wide_ref, joined_ref, normed_ref, active_ref, hidden_ref, attended_ref, down_ref, gwide_ref = refs[
        17 + 2 * ways :
    ]
    tokens = rows * width
    hidden_width = expand_ref.shape[1]

    @pl.when(pl.program_id(0) == 0)
    def _():
        for ref in (dout_ref, dexpand_ref, dshrink_ref, dbias_ref, dsmall_ref):
            ref[...] = jnp.zeros_like(ref)

    assemble(me_ref, pieces_in, wide_ref, 1, wide_part)
    contract = contract_matrix(width, wide)
    for row in range(rows):
        span = slice(row * width, (row + 1) * width)
        joined_ref[span, :HALF] = across_ref[0, span]
        joined_ref[span, HALF:] = dot(contract, wide_ref[row]).astype(BF)

    def token_rows(step, carry):
        span = pl.ds(pl.multiple_of(step * chunk, 16), chunk)
        joined = joined_ref[span]
        attended_out = dot(joined, out_ref[...]) + small_ref[12:13]
        middle = x_ref[0, span].astype(F32) + attended_out
        normed, scaled, recip = normalize(middle, small_ref[13:14], small_ref[14:15])
        normed_low = normed.astype(BF)
        normed_ref[span] = normed_low
        back = cot_ref[0, span]
        result = middle + small_ref[15:16]
        grad_normed = jnp.zeros((chunk, 2 * HALF), F32)
        for part in range(0, hidden_width, hidden_part):
            lanes = slice(part, part + hidden_part)
            hidden = dot(normed_low, expand_ref[:, lanes]) + bias_ref[:, lanes]
            upper, density = gelu_parts(hidden)
            active = (hidden * upper).astype(BF)
            active_ref[span, lanes] = active
            result = result + dot(active, shrink_ref[lanes])
            grad_active = dot_nt(back, shrink_ref[lanes])
            grad_hidden = grad_active * (upper + hidden * density)
            grad_hidden = grad_hidden.astype(BF)
            hidden_ref[span, lanes] = grad_hidden
            dbias_ref[:, lanes] += fold_rows(grad_hidden.astype(F32))
            grad_normed = grad_normed + dot_nt(grad_hidden, expand_ref[:, lanes])
        block_ref[0, span] = result
        back_wide = back.astype(F32)
        grad_middle = back_wide + normalize_back(grad_normed, scaled, recip, small_ref[13:14])
        middle_ref[0, span] = grad_middle
        grad_attended = grad_middle.astype(BF)
        attended_ref[span] = grad_attended
        grad_joined = dot_nt(grad_attended, out_ref[...]).astype(BF)
        grad_across_ref[0, span] = grad_joined[:, :HALF]
        down_ref[span] = grad_joined[:, HALF:]
        dsmall_ref[0:8] += fold_rows(grad_attended.astype(F32))
        dsmall_ref[8:16] += fold_rows(grad_normed * scaled)
        dsmall_ref[16:24] += fold_rows(grad_normed)
        dsmall_ref[24:32] += fold_rows(back_wide)
        return carry

    lax.fori_loop(0, tokens // chunk, token_rows, 0)
    expand = one_hot(expand_condition(wide, width))
    for row in range(rows):
        gwide_ref[row] = dot(expand, down_ref[row * width : (row + 1) * width]).astype(BF)
    for distance in range(ways):
        place = me_ref[0] ^ distance
        grad_refs[distance][0] = gwide_ref[
            :, pl.ds(pl.multiple_of(place * wide_part, wide_part), wide_part)
        ]
    dout_ref[...] += dot_tn(joined_ref[...], attended_ref[...])
    dexpand_ref[...] += dot_tn(normed_ref[...], hidden_ref[...])
    dshrink_ref[...] += dot_tn(cot_ref[0], active_ref[...])


def across_back_kernel(
    dims,
    across_ref,
    grad_ref,
    attended_ref,
    total_ref,
    keys_ref,
    values_ref,
    mask_ref,
    small_ref,
    mixed_ref,
    taps_ref,
    dkeys_ref,
    dvalues_ref,
    local_ref,
):
    rows, width, kept, key_rows, chunk = dims
    tokens = rows * width
    image = pl.program_id(0)

    @pl.when(image == 0)
    def _():
        taps_ref[...] = jnp.zeros_like(taps_ref)

    dkeys_ref[...] = jnp.zeros_like(dkeys_ref)
    dvalues_ref[...] = jnp.zeros_like(dvalues_ref)

    def attend(step, carry):
        span = pl.ds(pl.multiple_of(step * chunk, 16), chunk)
        grad_queries, grad_keys, grad_values = attend_heads_back(
            across_ref[0, span, :HALF].astype(F32),
            grad_ref[0, span].astype(F32),
            attended_ref[0, span],
            total_ref[0, span],
            lambda head: keys_ref[0, head],
            lambda head: values_ref[0, head],
        )
        mixed_ref[0, span, :HALF] = grad_queries.astype(BF)
        for head in range(BRANCH_HEADS):
            lanes = slice(head * HEAD_DIM, (head + 1) * HEAD_DIM)
            dkeys_ref[lanes] += grad_keys[head]
            dvalues_ref[lanes] += grad_values[head]
        return carry

    lax.fori_loop(0, tokens // chunk, attend, 0)

    local_ref[...] = jnp.zeros_like(local_ref)
    for row in range(rows):
        grad = grad_ref[0, row * width : (row + 1) * width].astype(F32)
        taps_ref[72:80] += fold_rows(grad)
        for tap_col, moved in enumerate((shift_up(grad), grad, shift_down(grad))):
            for tap_row in range(3):
                target = row + tap_row - 1
                if 0 <= target < rows:
                    tap = 3 * tap_row + tap_col
                    span = slice(target * width, (target + 1) * width)
                    values = across_ref[0, span, 2 * HALF :].astype(F32)
                    taps_ref[8 * tap : 8 * tap + 8] += fold_rows(values * moved)
                    local_ref[span] += moved * small_ref[tap : tap + 1, :HALF]

    ranks = rank_row(mask_ref[pl.ds(image, 1)].astype(F32), width)
    place = jnp.transpose(jnp.broadcast_to(ranks, (HALF, width)))
    spread = one_hot(iota((width, HALF), 1).astype(F32) == place)
    spread_more = one_hot((iota((width, kept - HALF), 1) + HALF).astype(F32) == place[:, : kept - HALF])
    spread = jnp.concatenate([spread, spread_more], axis=1)
    grad_keys = jnp.transpose(dkeys_ref[...]) * SCALE
    grad_values = jnp.transpose(dvalues_ref[...])
    high = grad_values.astype(BF)
    low = (grad_values - high.astype(F32)).astype(BF)
    grad_keys = grad_keys.astype(BF)
    for row in range(rows):
        span = slice(row * kept, (row + 1) * kept)
        packed = jnp.concatenate([grad_keys[span], high[span], low[span]], axis=1)
        unpacked = dot(spread, packed)
        target = slice(row * width, (row + 1) * width)
        mixed_ref[0, target, HALF : 2 * HALF] = unpacked[:, :HALF].astype(BF)
        whole = unpacked[:, HALF : 2 * HALF] + unpacked[:, 2 * HALF :] + local_ref[target]
        mixed_ref[0, target, 2 * HALF :] = whole.astype(BF)


def down_back_kernel(dims, ways, *refs):
    height, width, wide, wide_part, spare = dims
    me_ref, mask_ref, small_ref, attended_ref, total_ref = refs[:5]
    pieces_in = refs[5 : 5 + ways]
    grads_in = refs[5 + ways : 5 + 2 * ways]
    out_refs = refs[5 + 2 * ways : 5 + 3 * ways]
    taps_ref, mixed_ref, grad_ref, out_ref, column_ref = refs[5 + 3 * ways :]
    rows = height // ways
    start = down_setup(me_ref, mask_ref, column_ref, width, wide, wide_part)
    assemble(me_ref, pieces_in, mixed_ref, 0, rows)
    assemble(me_ref, grads_in, grad_ref, 0, rows)
    tokens = height * GROUP
    windows = wide_part // GROUP

    @pl.when(pl.program_id(0) == 0)
    def _():
        taps_ref[...] = jnp.zeros_like(taps_ref)

    def one_window(window, carry):
        span = pl.ds(pl.multiple_of(window * GROUP, GROUP), GROUP)
        flat = mixed_ref[:, span].reshape(tokens, 3 * HALF)
        queries, keys, values = (flat[:, part * HALF : (part + 1) * HALF] for part in range(3))
        grad_grid = grad_ref[:, span]
        grad = grad_grid.reshape(tokens, HALF)
        bias = window_bias(column_ref, start, window, height)
        key_list, value_list = window_operands(keys, values, bias, spare)
        grad_queries, grad_keys, grad_values = attend_heads_back(
            queries,
            grad,
            attended_ref[0, :, span].reshape(tokens, HALF),
            total_ref[0, :, span].reshape(tokens, HALF),
            lambda head: key_list[head],
            lambda head: value_list[head],
        )
        grad_keys = jnp.transpose(jnp.concatenate(grad_keys, axis=0))[:tokens] * SCALE
        grad_values = jnp.transpose(jnp.concatenate(grad_values, axis=0))[:tokens]
        values_grid = values.reshape(height, GROUP, HALF)
        local = jnp.zeros((height, GROUP, HALF), F32)
        taps_ref[72:80] += jnp.sum(grad_grid, axis=0)
        shifted = (grid_shift(grad_grid, -1), grad_grid, grid_shift(grad_grid, 1))
        for tap_col, moved in enumerate(shifted):
            stacked = grid_stack(moved)
            for tap_row in range(3):
                tap = 3 * tap_row + tap_col
                source = stacked[2 - tap_row : 2 - tap_row + height]
                taps_ref[8 * tap : 8 * tap + 8] += jnp.sum(source * values_grid, axis=0)
                local = local + source * small_ref[tap : tap + 1, HALF:].reshape(1, 1, HALF)
        shape = (height, GROUP, HALF)
        out_ref[:, span, :HALF] = grad_queries.reshape(shape)
        out_ref[:, span, HALF : 2 * HALF] = grad_keys.reshape(shape)
        out_ref[:, span, 2 * HALF :] = grad_values.reshape(shape) + local
        return carry

    lax.fori_loop(0, windows, one_window, 0)
    for distance in range(ways):
        place = me_ref[0] ^ distance
        out_refs[distance][0] = out_ref[pl.ds(place * rows, rows)].astype(BF)


def final_kernel(dims, ways, *refs):
    rows, width, wide, wide_part, chunk = dims
    me_ref, x_ref, middle_ref, across_ref = refs[:4]
    pieces_in = refs[4 : 4 + ways]
    small_ref, weight_ref, grad_ref, dweight_ref, dsmall_ref, wide_ref, mixed_ref, normed_ref = refs[
        4 + ways :
    ]
    tokens = rows * width

    @pl.when(pl.program_id(0) == 0)
    def _():
        dweight_ref[...] = jnp.zeros_like(dweight_ref)
        dsmall_ref[...] = jnp.zeros_like(dsmall_ref)

    assemble(me_ref, pieces_in, wide_ref, 1, wide_part)
    contract = contract_matrix(width, wide)
    for row in range(rows):
        span = slice(row * width, (row + 1) * width)
        mixed_ref[span, : 3 * HALF] = across_ref[0, span]
        mixed_ref[span, 3 * HALF :] = dot(contract, wide_ref[row]).astype(BF)

    def token_rows(step, carry):
        span = pl.ds(pl.multiple_of(step * chunk, 16), chunk)
        normed, scaled, recip = normalize(
            x_ref[0, span].astype(F32), small_ref[9:10], small_ref[10:11]
        )
        normed_ref[span] = normed.astype(BF)
        mixed = mixed_ref[span]
        grad_normed = dot_nt(mixed[:, : 3 * HALF], weight_ref[:, : 3 * HALF])
        grad_down = dot_nt(mixed[:, 3 * HALF :], weight_ref[:, 3 * HALF :])
        grad_normed = grad_normed + grad_down.astype(BF).astype(F32)
        dsmall_ref[0:8] += fold_rows(grad_normed * scaled)
        dsmall_ref[8:16] += fold_rows(grad_normed)
        grad_ref[0, span] = middle_ref[0, span] + normalize_back(
            grad_normed, scaled, recip, small_ref[9:10]
        )
        return carry

    lax.fori_loop(0, tokens // chunk, token_rows, 0)
    dweight_ref[...] += dot_tn(normed_ref[...], mixed_ref[...])


def image_block(*shape):
    return pl.BlockSpec((1,) + shape, lambda image: (image,) + (0,) * len(shape))


def whole_block(*shape):
    return pl.BlockSpec(shape, lambda image: (0,) * len(shape))


def scalar_block():
    return pl.BlockSpec(memory_space=pltpu.SMEM)


def run_kernel(body, images, in_specs, out_specs, out_shapes, scratch, flops, operands):
    return pl.pallas_call(
        body,
        grid=(images,),
        in_specs=in_specs,
        out_specs=out_specs,
        out_shape=out_shapes,
        scratch_shapes=scratch,
        compiler_params=pltpu.CompilerParams(vmem_limit_bytes=VMEM_LIMIT),
        cost_estimate=pl.CostEstimate(
            flops=int(flops), bytes_accessed=int(flops / 300), transcendentals=0
        ),
    )(*operands)


def adam_update(weight, first_old, second_old, grad_value, rate_value, decay_value):
    new_first = BETA_ONE * first_old + (1.0 - BETA_ONE) * grad_value
    new_second = BETA_TWO * second_old + (1.0 - BETA_TWO) * grad_value * grad_value
    first_hat = new_first / (1.0 - BETA_ONE**STEP)
    second_hat = new_second / (1.0 - BETA_TWO**STEP)
    new_weight = weight - rate_value * (
        first_hat / (jnp.sqrt(second_hat) + ADAM_EPS) + decay_value * weight
    )
    return (new_first, new_second, new_weight)


def exchange(pieces, ways):
    received = [pieces[0]]
    for distance in range(1, ways):
        pairs = [(place, place ^ distance) for place in range(ways)]
        received.append(lax.ppermute(pieces[distance], "seq", pairs))
    return received


def on_device(
    images,
    cotangent,
    valid_mask,
    qkv_weight,
    out_weight,
    expand_weight,
    shrink_weight,
    small_params,
    expand_bias,
    first_qkv,
    first_out,
    first_expand,
    first_shrink,
    first_small,
    first_bias,
    second_qkv,
    second_out,
    second_expand,
    second_shrink,
    second_small,
    second_bias,
):
    ways = lax.axis_size("seq")
    owner = lax.axis_index("seq")
    me = owner.astype(jnp.int32).reshape(1)
    count, rows, width, channels = images.shape
    tokens = rows * width
    height = rows * ways
    wide = width // STRIPE * GROUP
    wide_part = wide // ways
    kept = -(-VALID // 16) * 16
    key_rows = -(-rows * kept // 256) * 256
    window_tokens = height * GROUP
    spare = -window_tokens % 128
    hidden_width = expand_weight.shape[1]
    chunk = width

    gathered = (
        lax.all_gather(qkv_weight.astype(BF), "seq", axis=0, tiled=True),
        lax.all_gather(out_weight.astype(BF), "seq", axis=0, tiled=True),
        lax.all_gather(expand_weight.astype(BF), "seq", axis=0, tiled=True),
        lax.all_gather(shrink_weight.astype(BF), "seq", axis=0, tiled=True),
        lax.all_gather(small_params.astype(BF), "seq", axis=1, tiled=True),
        lax.all_gather(expand_bias.astype(BF), "seq", axis=0, tiled=True),
    )
    qkv_low, out_low, expand_low, shrink_low, small_low, bias_low = gathered
    small_full = small_low.astype(F32)
    bias_full = bias_low.astype(F32).reshape(1, hidden_width)
    x = images.reshape(count, tokens, channels)
    cot = cotangent.reshape(count, tokens, channels)

    def shape(dims, dtype):
        return jax.ShapeDtypeStruct(dims, dtype)

    small_spec = whole_block(*small_full.shape)
    mask_spec = whole_block(*valid_mask.shape)
    piece_qkv = (rows, wide_part, 3 * HALF)
    piece_out = (rows, wide_part, HALF)

    across_mixed, *down_pieces = run_kernel(
        functools.partial(project_kernel, (rows, width, wide, wide_part), ways),
        count,
        [scalar_block(), image_block(tokens, channels), small_spec, whole_block(*qkv_low.shape)],
        [image_block(tokens, 3 * HALF)] + [image_block(*piece_qkv)] * ways,
        [shape((count, tokens, 3 * HALF), BF)] + [shape((count,) + piece_qkv, BF)] * ways,
        [pltpu.VMEM((rows, wide, 3 * HALF), BF)],
        2.2 * count * tokens * channels * 6 * HALF,
        (me, x, small_full, qkv_low),
    )
    down_mixed = exchange(down_pieces, ways)

    attention_dims = (rows, width, kept, key_rows, chunk)
    key_shape = (BRANCH_HEADS, key_rows, HALF)
    joined_across, across_attended, across_total, across_keys, across_values = run_kernel(
        functools.partial(across_kernel, attention_dims),
        count,
        [image_block(tokens, 3 * HALF), mask_spec, small_spec],
        [
            image_block(tokens, HALF),
            image_block(tokens, HALF),
            image_block(tokens, HALF),
            image_block(*key_shape),
            image_block(*key_shape),
        ],
        [
            shape((count, tokens, HALF), BF),
            shape((count, tokens, HALF), F32),
            shape((count, tokens, HALF), F32),
            shape((count,) + key_shape, BF),
            shape((count,) + key_shape, BF),
        ],
        [pltpu.VMEM((tokens, HALF), F32)],
        4.0 * count * BRANCH_HEADS * tokens * key_rows * 256,
        (across_mixed, valid_mask, small_full),
    )

    down_dims = (height, width, wide, wide_part, spare)
    grid_f32 = (height, wide_part, HALF)
    down_results = run_kernel(
        functools.partial(down_kernel, down_dims, ways),
        count,
        [scalar_block(), mask_spec, small_spec] + [image_block(*piece_qkv)] * ways,
        [image_block(*piece_out)] * ways + [image_block(*grid_f32)] * 2,
        [shape((count,) + piece_out, BF)] * ways + [shape((count,) + grid_f32, F32)] * 2,
        [
            pltpu.VMEM((height, wide_part, 3 * HALF), F32),
            pltpu.VMEM(grid_f32, F32),
            pltpu.VMEM((wide, HALF), F32),
            pltpu.VMEM((window_tokens, HALF), F32),
        ],
        4.0 * count * wide_part * BRANCH_HEADS * height * (window_tokens + spare) * 256,
        (me, valid_mask, small_full, *down_mixed),
    )
    down_attended, down_total = down_results[ways:]
    joined_down = exchange(down_results[:ways], ways)

    middle_results = run_kernel(
        functools.partial(middle_kernel, (rows, width, wide, wide_part, chunk, 2 * HALF), ways),
        count,
        [
            scalar_block(),
            image_block(tokens, channels),
            image_block(tokens, channels),
            image_block(tokens, HALF),
        ]
        + [image_block(*piece_out)] * ways
        + [
            whole_block(*out_low.shape),
            whole_block(*expand_low.shape),
            whole_block(*shrink_low.shape),
            small_spec,
            whole_block(1, hidden_width),
        ],
        [
            image_block(tokens, channels),
            image_block(tokens, channels),
            image_block(tokens, HALF),
        ]
        + [image_block(*piece_out)] * ways
        + [
            whole_block(channels, channels),
            whole_block(channels, hidden_width),
            whole_block(channels, hidden_width),
            whole_block(8, hidden_width),
            whole_block(32, channels),
        ],
        [
            shape((count, tokens, channels), F32),
            shape((count, tokens, channels), F32),
            shape((count, tokens, HALF), BF),
        ]
        + [shape((count,) + piece_out, BF)] * ways
        + [
            shape((channels, channels), F32),
            shape((channels, hidden_width), F32),
            shape((channels, hidden_width), F32),
            shape((8, hidden_width), F32),
            shape((32, channels), F32),
        ],
        [
            pltpu.VMEM((rows, wide, HALF), BF),
            pltpu.VMEM((tokens, channels), BF),
            pltpu.VMEM((tokens, channels), BF),
            pltpu.VMEM((tokens, hidden_width), BF),
            pltpu.VMEM((tokens, hidden_width), BF),
            pltpu.VMEM((tokens, channels), BF),
            pltpu.VMEM((tokens, HALF), BF),
            pltpu.VMEM((rows, wide, HALF), BF),
        ],
        6.0 * count * tokens * channels * (channels + 2 * hidden_width),
        (me, x, cot, joined_across, *joined_down, out_low, expand_low, shrink_low, small_full, bias_full),
    )
    block_out, grad_middle, grad_across = middle_results[:3]
    sum_out, sum_expand, sum_shrink, bias_part, small_part = middle_results[3 + ways :]
    grad_down = exchange(middle_results[3 : 3 + ways], ways)

    across_mixed_grad, across_taps = run_kernel(
        functools.partial(across_back_kernel, attention_dims),
        count,
        [
            image_block(tokens, 3 * HALF),
            image_block(tokens, HALF),
            image_block(tokens, HALF),
            image_block(tokens, HALF),
            image_block(*key_shape),
            image_block(*key_shape),
            mask_spec,
            small_spec,
        ],
        [image_block(tokens, 3 * HALF), whole_block(80, HALF)],
        [shape((count, tokens, 3 * HALF), BF), shape((80, HALF), F32)],
        [
            pltpu.VMEM((HALF, key_rows), F32),
            pltpu.VMEM((HALF, key_rows), F32),
            pltpu.VMEM((tokens, HALF), F32),
        ],
        10.0 * count * BRANCH_HEADS * tokens * key_rows * 256,
        (
            across_mixed,
            grad_across,
            across_attended,
            across_total,
            across_keys,
            across_values,
            valid_mask,
            small_full,
        ),
    )

    down_back_results = run_kernel(
        functools.partial(down_back_kernel, down_dims, ways),
        count,
        [scalar_block(), mask_spec, small_spec]
        + [image_block(*grid_f32)] * 2
        + [image_block(*piece_qkv)] * ways
        + [image_block(*piece_out)] * ways,
        [image_block(*piece_qkv)] * ways + [whole_block(80, HALF)],
        [shape((count,) + piece_qkv, BF)] * ways + [shape((80, HALF), F32)],
        [
            pltpu.VMEM((height, wide_part, 3 * HALF), F32),
            pltpu.VMEM(grid_f32, F32),
            pltpu.VMEM((height, wide_part, 3 * HALF), F32),
            pltpu.VMEM((wide, HALF), F32),
        ],
        10.0 * count * wide_part * BRANCH_HEADS * height * (window_tokens + spare) * 256,
        (me, valid_mask, small_full, down_attended, down_total, *down_mixed, *grad_down),
    )
    down_taps = down_back_results[ways]
    down_mixed_grad = exchange(down_back_results[:ways], ways)

    input_grad, sum_qkv, norm_part = run_kernel(
        functools.partial(final_kernel, (rows, width, wide, wide_part, chunk), ways),
        count,
        [
            scalar_block(),
            image_block(tokens, channels),
            image_block(tokens, channels),
            image_block(tokens, 3 * HALF),
        ]
        + [image_block(*piece_qkv)] * ways
        + [small_spec, whole_block(*qkv_low.shape)],
        [
            image_block(tokens, channels),
            whole_block(channels, 6 * HALF),
            whole_block(16, channels),
        ],
        [
            shape((count, tokens, channels), F32),
            shape((channels, 6 * HALF), F32),
            shape((16, channels), F32),
        ],
        [
            pltpu.VMEM((rows, wide, 3 * HALF), BF),
            pltpu.VMEM((tokens, 6 * HALF), BF),
            pltpu.VMEM((tokens, channels), BF),
        ],
        4.0 * count * tokens * channels * 6 * HALF,
        (me, x, grad_middle, across_mixed_grad, *down_mixed_grad, small_full, qkv_low),
    )

    taps = jnp.concatenate([across_taps, down_taps], axis=1).reshape(10, 8, channels).sum(axis=1)
    norm_rows = norm_part.reshape(2, 8, channels).sum(axis=1)
    mid_rows = small_part.reshape(4, 8, channels).sum(axis=1)
    sum_small = jnp.concatenate([taps[:9], norm_rows, taps[9:], mid_rows], axis=0)
    sum_bias = bias_part.sum(axis=0)

    params = (qkv_weight, out_weight, expand_weight, shrink_weight, small_params, expand_bias)
    shard_dims = (0, 0, 0, 1, 1, 0)
    full_grads = lax.psum(
        (sum_qkv, sum_out, sum_expand, sum_shrink, sum_small, sum_bias), ("img", "seq")
    )
    squared = jnp.float32(0.0)
    for full_grad in full_grads:
        squared = squared + jnp.sum(full_grad * full_grad)
    sizes = [part.shape[dim] for part, dim in zip(params, shard_dims)]
    sizes[3] = shrink_weight.shape[0]
    shares = [
        lax.dynamic_slice_in_dim(full_grad, owner * size, size, dim)
        for full_grad, size, dim in zip(full_grads, sizes, shard_dims)
    ]
    shares[3] = shares[3].T
    grad_norm = jnp.sqrt(squared)
    factor = CLIP_NORM / jnp.maximum(grad_norm, CLIP_NORM)
    rates = (RATE_MATRIX, RATE_OUTPUT, RATE_MATRIX, RATE_MATRIX, RATE_SMALL, RATE_MATRIX)
    decays = (WEIGHT_DECAY, WEIGHT_DECAY, WEIGHT_DECAY, WEIGHT_DECAY, 0.0, 0.0)
    firsts = (first_qkv, first_out, first_expand, first_shrink, first_small, first_bias)
    seconds = (second_qkv, second_out, second_expand, second_shrink, second_small, second_bias)
    updated = [
        adam_update(
            params[index],
            firsts[index],
            seconds[index],
            shares[index] * factor,
            rates[index],
            decays[index],
        )
        for index in range(6)
    ]
    return (
        block_out.reshape(images.shape),
        input_grad.reshape(images.shape),
        grad_norm,
        *(entry[0] for entry in updated),
        *(entry[1] for entry in updated),
        *(entry[2] for entry in updated),
    )


def solution(mesh):
    sharded = (
        P("seq", None),
        P("seq", None),
        P("seq", None),
        P("seq", None),
        P(None, "seq"),
        P("seq"),
    )
    grid = P("img", "seq", None, None)
    return jax.shard_map(
        on_device,
        mesh=mesh,
        in_specs=(grid, grid, P("img", None)) + sharded * 3,
        out_specs=(grid, grid, P()) + sharded * 3,
        check_vma=False,
    )
```

```python
import functools

import jax
import jax.numpy as jnp
from jax import lax
from jax.experimental import pallas as pl
from jax.experimental.pallas import tpu as pltpu
from jax.sharding import PartitionSpec as P

HEADS = 8
STRIPE = 7
STEP = 10
VALID = 168

EPS_NORM = 1e-05
BETA_ONE = 0.9
BETA_TWO = 0.999
ADAM_EPS = 1e-08
WEIGHT_DECAY = 0.05
CLIP_NORM = 1.0
RATE_MATRIX = 0.1
RATE_OUTPUT = 0.5
RATE_SMALL = 0.3
INV_ROOT_TWO = 0.7071067811865476
INV_ROOT_TAU = 0.3989422804014327
LOG2E = 1.4426950408889634

BF = jnp.bfloat16
F32 = jnp.float32
HALF = 128
BRANCH_HEADS = 4
HEAD_DIM = 32
SCALE = HEAD_DIM**-0.5
GROUP = 8
MASKED = -1e38
EXPONENT_BOUND = 60.0
VMEM_LIMIT = 60 * 2**20


def dot(left, right):
    return jnp.dot(left, right, preferred_element_type=F32)


def dot_nt(left, right):
    return lax.dot_general(left, right, (((1,), (1,)), ((), ())), preferred_element_type=F32)


def dot_tn(left, right):
    return lax.dot_general(left, right, (((0,), (0,)), ((), ())), preferred_element_type=F32)


def iota(shape, dim):
    return lax.broadcasted_iota(jnp.int32, shape, dim)


def one_hot(condition):
    return jnp.where(condition, 1.0, 0.0).astype(BF)


def expand_condition(wide, width):
    e, c = iota((wide, width), 0), iota((wide, width), 1)
    return ((e & 7) < STRIPE) & (c == STRIPE * (e >> 3) + (e & 7))


def contract_matrix(width, wide):
    c, e = iota((width, wide), 0), iota((width, wide), 1)
    return one_hot(((e & 7) < STRIPE) & (c == STRIPE * (e >> 3) + (e & 7)))


def normalize(values, gain_row, offset_row):
    center = values - jnp.mean(values, axis=-1, keepdims=True)
    spread = jnp.mean(center * center, axis=-1, keepdims=True)
    recip = lax.rsqrt(spread + EPS_NORM)
    scaled = center * recip
    return scaled * gain_row + offset_row, scaled, recip


def normalize_back(grad_out, scaled, recip, gain_row):
    grad_scaled = grad_out * gain_row
    inner_one = jnp.mean(grad_scaled, axis=-1, keepdims=True)
    inner_two = jnp.mean(grad_scaled * scaled, axis=-1, keepdims=True)
    return recip * (grad_scaled - inner_one - scaled * inner_two)


def fold_rows(values):
    rows, columns = values.shape
    return jnp.sum(values.reshape(rows // 8, 8, columns), axis=0)


def pieces_of(values):
    first = values.astype(BF).astype(F32)
    rest = values - first
    second = rest.astype(BF).astype(F32)
    return first, second, (rest - second).astype(BF).astype(F32)


def lane_place(rows, head):
    lane = iota((rows, HALF), 1)
    return ((lane >> 5) - head) & 3


def lane_sub(rows):
    return iota((rows, HALF), 1) & 31


def head_key(keys, keys_rolled, bias, head):
    rows = keys.shape[0]
    place, sub = lane_place(rows, head), lane_sub(rows)
    extra = jnp.where(sub < 3, 1.0, jnp.where(sub == 3, bias, 0.0))
    return jnp.where(
        place == 0, keys, jnp.where(place == 1, keys_rolled, jnp.where(place == 2, extra, 0.0))
    ).astype(BF)


def head_value(values, head):
    place = lane_place(values.shape[0], head)
    return jnp.where(place == 0, values, jnp.where(place == 1, 1.0, 0.0)).astype(BF)


def query_parts(queries, shift):
    rows = queries.shape[0]
    scaled = queries * (SCALE * LOG2E)
    high = scaled.astype(BF).astype(F32)
    low = pltpu.roll(scaled - high, HEAD_DIM, 1)
    one, two, three = pieces_of(-pltpu.roll(shift, 2 * HEAD_DIM, 1))
    sub = lane_sub(rows)
    extra = jnp.where(
        sub == 0,
        one,
        jnp.where(sub == 1, two, jnp.where(sub == 2, three, jnp.where(sub == 3, 1.0, 0.0))),
    )
    return high, low, extra


def head_query(parts, head):
    high, low, extra = parts
    place = lane_place(high.shape[0], head)
    return jnp.where(
        place == 0, high, jnp.where(place == 1, low, jnp.where(place == 2, extra, 0.0))
    ).astype(BF)


def grad_parts(grad, attended):
    rows = grad.shape[0]
    product = grad * attended
    block = one_hot((iota((HALF, HALF), 0) >> 5) == (iota((HALF, HALF), 1) >> 5))
    first, second, third = pieces_of(product)
    inner = dot(first.astype(BF), block) + dot(second.astype(BF), block) + dot(third.astype(BF), block)
    one, two, three = pieces_of(-pltpu.roll(inner, HEAD_DIM, 1))
    sub = lane_sub(rows)
    extra = jnp.where(sub == 0, one, jnp.where(sub == 1, two, jnp.where(sub == 2, three, 0.0)))
    return grad, extra


def head_grad(parts, head):
    grad, extra = parts
    place = lane_place(grad.shape[0], head)
    return jnp.where(place == 0, grad, jnp.where(place == 1, extra, 0.0)).astype(BF)


def head_norms(values):
    block = one_hot((iota((HALF, HALF), 0) >> 5) == (iota((HALF, HALF), 1) >> 5))
    sums = dot((values * values * 1.02).astype(BF), block)
    return jnp.max(sums, axis=0, keepdims=True)


def exceeds(query_norms, key_norms):
    bound = jnp.max(query_norms * key_norms)
    return jnp.logical_not(bound <= EXPONENT_BOUND * EXPONENT_BOUND)


def attend_heads(query_rows, shift, keys_of, values_of):
    rows = query_rows.shape[0]
    parts = query_parts(query_rows, shift)
    attended = jnp.zeros((rows, HALF), F32)
    log_total = jnp.zeros((rows, HALF), F32)
    for head in range(BRANCH_HEADS):
        scores = dot_nt(head_query(parts, head), keys_of(head))
        weights = jnp.exp2(scores).astype(BF)
        result = dot(weights, values_of(head))
        totals = pltpu.roll(result, HALF - HEAD_DIM, 1)
        mine = lane_place(rows, head) == 0
        attended = jnp.where(mine, result / totals, attended)
        log_total = jnp.where(mine, jnp.log(totals) * LOG2E + shift, log_total)
    return attended, log_total


def highest_scores(query_rows, keys_of):
    rows = query_rows.shape[0]
    parts = query_parts(query_rows, jnp.zeros((rows, HALF), F32))
    shift = jnp.zeros((rows, HALF), F32)
    for head in range(BRANCH_HEADS):
        scores = dot_nt(head_query(parts, head), keys_of(head))
        highest = jnp.max(scores, axis=-1, keepdims=True)
        shift = jnp.where(lane_place(rows, head) == 0, highest, shift)
    return shift


def attend_heads_back(query_rows, grad_rows, attended, log_total, keys_of, values_of):
    rows = query_rows.shape[0]
    eye = one_hot(iota((HALF, HALF), 0) == iota((HALF, HALF), 1))
    query_turned = dot_nt(eye, query_rows.astype(BF)).astype(BF)
    grad_turned = dot_nt(eye, grad_rows.astype(BF)).astype(BF)
    parts = query_parts(query_rows, log_total)
    back_parts = grad_parts(grad_rows, attended)
    grad_queries = jnp.zeros((rows, HALF), F32)
    grad_keys, grad_values = [], []
    for head in range(BRANCH_HEADS):
        keys, values = keys_of(head), values_of(head)
        weights = jnp.exp2(dot_nt(head_query(parts, head), keys))
        weights_low = weights.astype(BF)
        grad_weights = dot_nt(head_grad(back_parts, head), values)
        grad_scores = (weights * grad_weights).astype(BF)
        lanes = slice(head * HEAD_DIM, (head + 1) * HEAD_DIM)
        grad_values.append(dot(grad_turned[lanes], weights_low))
        grad_keys.append(dot(query_turned[lanes], grad_scores))
        mine = lane_place(rows, head) == 0
        grad_queries = jnp.where(mine, dot(grad_scores, keys), grad_queries)
    return grad_queries * SCALE, grad_keys, grad_values


def shift_down(values):
    rows = values.shape[0]
    return jnp.where(iota(values.shape, 0) == 0, 0.0, pltpu.roll(values, 1, 0))


def shift_up(values):
    rows = values.shape[0]
    return jnp.where(iota(values.shape, 0) == rows - 1, 0.0, pltpu.roll(values, rows - 1, 0))


def start_sums(sums, starts):
    @pl.when(pl.program_id(0) == 0)
    def _():
        for index, total in enumerate(sums):
            if starts:
                total[...] = starts[index][...]
            else:
                total[...] = jnp.zeros_like(total)


def at_last_step(body):
    pl.when(pl.program_id(0) == pl.num_programs(0) - 1)(body)


def project_kernel(dims, ways, *refs):
    rows, width, wide, wide_part = dims
    me_ref, x_ref = refs[:2]
    pieces = refs[2 : 2 + ways]
    across_ref, normed_ref = refs[2 + ways : 4 + ways]
    down_refs = refs[4 + ways : 4 + 2 * ways]
    weight_ref, small_ref, bias_ref, spread_ref = refs[4 + 2 * ways :]

    @pl.when(pl.program_id(0) == 0)
    def _():
        channels, hidden_width = small_ref.shape[1], bias_ref.shape[1]
        shard = channels // ways
        bias_shard = hidden_width // ways
        lanes = -(-(shard + bias_shard) // 128) * 128
        lane, column = iota((lanes, channels + hidden_width), 0), iota((lanes, channels + hidden_width), 1)
        total = jnp.zeros((16, channels + hidden_width), F32)
        for distance, piece in enumerate(pieces):
            place = me_ref[0] ^ distance
            weight_ref[pl.ds(pl.multiple_of(place * shard, shard), shard)] = piece[:shard]
            target = jnp.where(
                lane < shard,
                lane + shard * place,
                channels + lane - shard + bias_shard * place,
            )
            chosen = one_hot((column == target) & (lane < shard + bias_shard))
            total = total + dot(piece[shard : shard + 16, :lanes], chosen)
        small_ref[...] = total[:, :channels]
        bias_ref[...] = total[0:1, channels:]

    gain, offset = small_ref[9:10], small_ref[10:11]
    expand = one_hot(expand_condition(wide, width))
    for row in range(rows):
        span = slice(row * width, (row + 1) * width)
        normed, _, _ = normalize(x_ref[0, span].astype(F32), gain, offset)
        normed = normed.astype(BF)
        normed_ref[0, span] = normed
        across_ref[0, span] = dot(normed, weight_ref[:, : 3 * HALF]).astype(BF)
        spread_ref[row] = dot(expand, normed).astype(BF)
        for distance in range(ways):
            start = pl.multiple_of((me_ref[0] ^ distance) * wide_part, wide_part)
            down_refs[distance][0, row] = spread_ref[row, pl.ds(start, wide_part)]


def rank_row(mask_row, width):
    lower = one_hot(iota((width, width), 0) <= iota((width, width), 1))
    counted = dot(jnp.broadcast_to(mask_row, (8, width)).astype(BF), lower)[0:1]
    return jnp.where(mask_row > 0.0, counted - 1.0, -1.0)


def across_kernel(
    dims,
    across_ref,
    mask_ref,
    small_ref,
    joined_ref,
    attended_ref,
    total_ref,
    keys_ref,
    values_ref,
    shift_ref,
):
    rows, width, kept, key_rows, chunk = dims
    tokens = rows * width
    image = pl.program_id(0)
    ranks = rank_row(mask_ref[pl.ds(image, 1)].astype(F32), width)
    select = one_hot(iota((kept, width), 0).astype(F32) == ranks)
    bias = jnp.where(iota((kept, HALF), 0) >= VALID, MASKED, 0.0)
    key_norms = jnp.zeros((1, HALF), F32)
    for row in range(rows):
        picked = dot(select, across_ref[0, row * width : (row + 1) * width, HALF:])
        keys, values = picked[:, :HALF], picked[:, HALF:]
        rolled = pltpu.roll(keys, HEAD_DIM, 1)
        key_norms = jnp.maximum(key_norms, head_norms(keys))
        span = slice(row * kept, (row + 1) * kept)
        for head in range(BRANCH_HEADS):
            keys_ref[0, head, span] = head_key(keys, rolled, bias, head)
            values_ref[0, head, span] = head_value(values, head)
    spare = key_rows - rows * kept
    if spare:
        nothing = jnp.zeros((spare, HALF), F32)
        for head in range(BRANCH_HEADS):
            keys_ref[0, head, rows * kept :] = head_key(
                nothing, nothing, jnp.full((spare, HALF), MASKED, F32), head
            )
            values_ref[0, head, rows * kept :] = nothing.astype(BF)

    query_norms = head_norms(across_ref[0, :, :HALF].astype(F32) * (SCALE * LOG2E))
    large = exceeds(query_norms, key_norms)

    @pl.when(image == 0)
    def _():
        shift_ref[...] = jnp.zeros_like(shift_ref)

    def rows_of(step):
        return pl.ds(pl.multiple_of(step * chunk, 16), chunk)

    def keys_of(head):
        return keys_ref[0, head]

    def values_of(head):
        return values_ref[0, head]

    @pl.when(large)
    def _():
        def highest(step, carry):
            span = rows_of(step)
            shift_ref[span] = highest_scores(across_ref[0, span, :HALF].astype(F32), keys_of)
            return carry

        lax.fori_loop(0, tokens // chunk, highest, 0)

    def attend(step, carry):
        span = rows_of(step)
        attended, log_total = attend_heads(
            across_ref[0, span, :HALF].astype(F32), shift_ref[span], keys_of, values_of
        )
        attended_ref[0, span] = attended
        total_ref[0, span] = log_total
        return carry

    lax.fori_loop(0, tokens // chunk, attend, 0)

    @pl.when(large)
    def _():
        shift_ref[...] = jnp.zeros_like(shift_ref)

    def value_row(row):
        return across_ref[0, row * width : (row + 1) * width, 2 * HALF :].astype(F32)

    for row in range(rows):
        sums = [jnp.zeros((width, HALF), F32) for _ in range(3)]
        for tap_row in range(3):
            source = row + tap_row - 1
            if 0 <= source < rows:
                values = value_row(source)
                for tap_col in range(3):
                    tap = 3 * tap_row + tap_col
                    sums[tap_col] = sums[tap_col] + values * small_ref[tap : tap + 1, :HALF]
        local = shift_down(sums[0]) + sums[1] + shift_up(sums[2]) + small_ref[11:12, :HALF]
        span = slice(row * width, (row + 1) * width)
        joined_ref[0, span] = (attended_ref[0, span] + local).astype(BF)


def assemble(me_ref, pieces, target_ref, dim, step):
    for distance, piece in enumerate(pieces):
        place = me_ref[0] ^ distance
        if dim == 0:
            target_ref[pl.ds(place * step, step)] = piece[0].astype(target_ref.dtype)
        else:
            target_ref[:, pl.ds(pl.multiple_of(place * step, step), step)] = piece[0].astype(
                target_ref.dtype
            )


def down_setup(me_ref, mask_ref, column_ref, width, wide, wide_part, first):
    image = pl.program_id(0) + first
    mask_row = mask_ref[pl.ds(image, 1)].astype(F32)
    valid = one_hot(expand_condition(wide, width) & (mask_row > 0.0))
    column_ref[...] = dot(valid, jnp.ones((width, HALF), BF))
    return pl.multiple_of(me_ref[0] * wide_part, GROUP)


def window_bias(column_ref, start, window, height):
    valid = column_ref[pl.ds(start + pl.multiple_of(window * GROUP, GROUP), GROUP)]
    bias = jnp.where(valid > 0.5, 0.0, MASKED)
    return jnp.broadcast_to(bias[None], (height, GROUP, HALF)).reshape(height * GROUP, HALF)


def pad_keys(block, spare, fill):
    if not spare:
        return block
    return jnp.concatenate([block, jnp.full((spare, HALF), 0.0, F32) + fill], axis=0)


def window_operands(keys, values, bias, spare):
    rolled = pltpu.roll(keys, HEAD_DIM, 1)
    keys_in = pad_keys(keys, spare, 0.0)
    rolled_in = pad_keys(rolled, spare, 0.0)
    bias_in = pad_keys(bias, spare, MASKED)
    values_in = pad_keys(values, spare, 0.0)
    key_list = [head_key(keys_in, rolled_in, bias_in, head) for head in range(BRANCH_HEADS)]
    value_list = [head_value(values_in, head) for head in range(BRANCH_HEADS)]
    return key_list, value_list


def grid_shift(values, amount):
    return pltpu.roll(values, amount % GROUP, 1)


def grid_stack(values):
    edge = jnp.zeros((1,) + values.shape[1:], F32)
    return jnp.concatenate([edge, values, edge], axis=0)


def down_kernel(dims, ways, first, *refs):
    height, width, wide, wide_part, spare = dims
    me_ref, mask_ref, small_ref, weight_ref = refs[:4]
    pieces_in = refs[4 : 4 + ways]
    joined_refs = refs[4 + ways : 4 + 2 * ways]
    attended_ref, total_ref, saved_ref, normed_ref, mixed_ref, joined_ref, column_ref, shift_ref = refs[
        4 + 2 * ways :
    ]
    rows = height // ways
    start = down_setup(me_ref, mask_ref, column_ref, width, wide, wide_part, first)
    assemble(me_ref, pieces_in, normed_ref, 0, rows)
    tokens = height * GROUP
    windows = wide_part // GROUP
    normed = normed_ref[...].reshape(height * wide_part, 2 * HALF)
    mixed_low = dot(normed, weight_ref[:, 3 * HALF :]).astype(BF)
    mixed_low = mixed_low.reshape(height, wide_part, 3 * HALF)
    saved_ref[0] = mixed_low
    mixed_ref[...] = mixed_low.astype(F32)

    @pl.when(pl.program_id(0) == 0)
    def _():
        shift_ref[...] = jnp.zeros_like(shift_ref)

    everything = mixed_ref[...].reshape(height * wide_part, 3 * HALF)
    large = exceeds(
        head_norms(everything[:, :HALF] * (SCALE * LOG2E)), head_norms(everything[:, HALF : 2 * HALF])
    )

    def one_window(window, carry):
        span = pl.ds(pl.multiple_of(window * GROUP, GROUP), GROUP)
        grid = mixed_ref[:, span]
        flat = grid.reshape(tokens, 3 * HALF)
        queries, keys, values = (flat[:, part * HALF : (part + 1) * HALF] for part in range(3))
        bias = window_bias(column_ref, start, window, height)
        key_list, value_list = window_operands(keys, values, bias, spare)

        @pl.when(large)
        def _():
            shift_ref[...] = highest_scores(queries, lambda head: key_list[head])

        attended, log_total = attend_heads(
            queries, shift_ref[...], lambda head: key_list[head], lambda head: value_list[head]
        )
        attended_ref[0, :, span] = attended.reshape(height, GROUP, HALF)
        total_ref[0, :, span] = log_total.reshape(height, GROUP, HALF)
        stacked = grid_stack(values.reshape(height, GROUP, HALF))
        sums = [jnp.zeros((height, GROUP, HALF), F32) for _ in range(3)]
        for tap_row in range(3):
            for tap_col in range(3):
                tap = 3 * tap_row + tap_col
                sums[tap_col] = sums[tap_col] + stacked[tap_row : tap_row + height] * small_ref[
                    tap : tap + 1, HALF:
                ].reshape(1, 1, HALF)
        local = grid_shift(sums[0], 1) + sums[1] + grid_shift(sums[2], -1)
        local = local + small_ref[11:12, HALF:].reshape(1, 1, HALF)
        joined_ref[:, span] = attended.reshape(height, GROUP, HALF) + local
        return carry

    lax.fori_loop(0, windows, one_window, 0)

    @pl.when(large)
    def _():
        shift_ref[...] = jnp.zeros_like(shift_ref)

    for distance in range(ways):
        place = me_ref[0] ^ distance
        joined_refs[distance][0] = joined_ref[pl.ds(place * rows, rows)].astype(BF)


def gelu_parts(hidden):
    size = jnp.abs(hidden) * INV_ROOT_TWO
    ratio = 1.0 / (1.0 + 0.3275911 * size)
    poly = ratio * (
        0.127414796
        + ratio * (-0.142248368 + ratio * (0.7107068705 + ratio * (-0.7265760135 + ratio * 0.5307027145)))
    )
    decay = jnp.exp2(hidden * hidden * (-0.5 * LOG2E))
    tail = poly * decay
    return jnp.where(hidden >= 0.0, 1.0 - tail, tail), decay * INV_ROOT_TAU


def middle_kernel(dims, ways, last, *refs):
    rows, width, wide, wide_part, chunk, hidden_part = dims
    refs = list(refs)

    def take(number):
        taken = refs[:number]
        del refs[:number]
        return taken

    me_ref, x_ref, cot_ref, across_ref = take(4)
    pieces_in = take(ways)
    weights_in = take(ways)
    small_ref, bias_ref = take(2)
    starts = take(5) if last else None
    block_ref, middle_ref, grad_across_ref = take(3)
    grad_refs = take(ways)
    dbias_ref, dsmall_ref = take(2)
    piece_refs = take(ways) if last else None
    dout_ref, dexpand_ref, dshrink_ref = take(3)
    out_ref, expand_ref, shrink_ref = take(3)
    wide_ref, joined_ref, normed_ref, active_ref, hidden_ref, attended_ref, down_ref, gwide_ref = take(8)
    turned_ref = take(1)[0] if last else None
    tokens = rows * width
    hidden_width = expand_ref.shape[1]
    channels = 2 * HALF
    shard = channels // ways
    blocks = hidden_width // channels
    start_sums((dbias_ref, dsmall_ref, dout_ref, dexpand_ref, dshrink_ref), starts)

    @pl.when(pl.program_id(0) == 0)
    def _():
        for distance, piece in enumerate(weights_in):
            place = me_ref[0] ^ distance
            span = pl.ds(pl.multiple_of(place * shard, shard), shard)
            out_ref[span] = piece[:, :channels]
            expand_ref[span] = piece[:, channels : channels + hidden_width]
            for block in range(blocks):
                begin = pl.multiple_of((place * blocks + block) * shard, shard)
                lanes = slice(channels + hidden_width + block * channels, channels + hidden_width + (block + 1) * channels)
                shrink_ref[pl.ds(begin, shard)] = piece[:, lanes]

    assemble(me_ref, pieces_in, wide_ref, 1, wide_part)
    contract = contract_matrix(width, wide)
    for row in range(rows):
        span = slice(row * width, (row + 1) * width)
        joined_ref[span, :HALF] = across_ref[0, span]
        joined_ref[span, HALF:] = dot(contract, wide_ref[row]).astype(BF)

    def token_rows(step, carry):
        span = pl.ds(pl.multiple_of(step * chunk, 16), chunk)
        joined = joined_ref[span]
        attended_out = dot(joined, out_ref[...]) + small_ref[12:13]
        middle = x_ref[0, span].astype(F32) + attended_out
        normed, scaled, recip = normalize(middle, small_ref[13:14], small_ref[14:15])
        normed_low = normed.astype(BF)
        normed_ref[span] = normed_low
        back = cot_ref[0, span]
        result = middle + small_ref[15:16]
        grad_normed = jnp.zeros((chunk, 2 * HALF), F32)
        for part in range(0, hidden_width, hidden_part):
            lanes = slice(part, part + hidden_part)
            hidden = dot(normed_low, expand_ref[:, lanes]) + bias_ref[:, lanes]
            upper, density = gelu_parts(hidden)
            active = (hidden * upper).astype(BF)
            active_ref[span, lanes] = active
            result = result + dot(active, shrink_ref[lanes])
            grad_active = dot_nt(back, shrink_ref[lanes])
            grad_hidden = grad_active * (upper + hidden * density)
            grad_hidden = grad_hidden.astype(BF)
            hidden_ref[span, lanes] = grad_hidden
            dbias_ref[:, lanes] += fold_rows(grad_hidden.astype(F32))
            grad_normed = grad_normed + dot_nt(grad_hidden, expand_ref[:, lanes])
        block_ref[0, span] = result
        back_wide = back.astype(F32)
        grad_middle = back_wide + normalize_back(grad_normed, scaled, recip, small_ref[13:14])
        middle_ref[0, span] = grad_middle
        grad_attended = grad_middle.astype(BF)
        attended_ref[span] = grad_attended
        grad_joined = dot_nt(grad_attended, out_ref[...]).astype(BF)
        grad_across_ref[0, span] = grad_joined[:, :HALF]
        down_ref[span] = grad_joined[:, HALF:]
        dsmall_ref[0:8] += fold_rows(grad_attended.astype(F32))
        dsmall_ref[8:16] += fold_rows(grad_normed * scaled)
        dsmall_ref[16:24] += fold_rows(grad_normed)
        dsmall_ref[24:32] += fold_rows(back_wide)
        return carry

    lax.fori_loop(0, tokens // chunk, token_rows, 0)
    expand = one_hot(expand_condition(wide, width))
    for row in range(rows):
        gwide_ref[row] = dot(expand, down_ref[row * width : (row + 1) * width]).astype(BF)
    for distance in range(ways):
        place = me_ref[0] ^ distance
        grad_refs[distance][0] = gwide_ref[
            :, pl.ds(pl.multiple_of(place * wide_part, wide_part), wide_part)
        ]
    dout_ref[...] += dot_tn(joined_ref[...], attended_ref[...])
    dexpand_ref[...] += dot_tn(normed_ref[...], hidden_ref[...])
    dshrink_ref[...] += dot_tn(cot_ref[0], active_ref[...])
    if last:

        @at_last_step
        def _():
            for block in range(blocks):
                lanes = slice(block * channels, (block + 1) * channels)
                turned_ref[lanes] = jnp.transpose(dshrink_ref[:, lanes])
            for distance, piece in enumerate(piece_refs):
                place = me_ref[0] ^ distance
                span = pl.ds(pl.multiple_of(place * shard, shard), shard)
                piece[:, :channels] = dout_ref[span]
                piece[:, channels : channels + hidden_width] = dexpand_ref[span]
                for block in range(blocks):
                    begin = pl.multiple_of((place * blocks + block) * shard, shard)
                    lanes = slice(channels + hidden_width + block * channels, channels + hidden_width + (block + 1) * channels)
                    piece[:, lanes] = turned_ref[pl.ds(begin, shard)]


def shard_pieces(me_ref, piece_refs, total_ref):
    shard = piece_refs[0].shape[0]

    @at_last_step
    def _():
        for distance, piece in enumerate(piece_refs):
            begin = pl.multiple_of((me_ref[0] ^ distance) * shard, shard)
            piece[...] = total_ref[pl.ds(begin, shard)]


def across_back_kernel(dims, ways, first, last, *refs):
    rows, width, kept, key_rows, chunk = dims
    refs = list(refs)

    def take(number):
        taken = refs[:number]
        del refs[:number]
        return taken

    me_ref, across_ref, grad_ref, attended_ref, total_ref, keys_ref, values_ref, normed_ref = take(8)
    mask_ref, small_ref = take(2)
    starts = take(2) if last else None
    mixed_ref, taps_ref = take(2)
    piece_refs = take(ways) if last else None
    dweight_ref, dkeys_ref, dvalues_ref, local_ref = take(4)
    tokens = rows * width
    image = pl.program_id(0) + first
    start_sums((taps_ref, dweight_ref), starts)
    dkeys_ref[...] = jnp.zeros_like(dkeys_ref)
    dvalues_ref[...] = jnp.zeros_like(dvalues_ref)

    def attend(step, carry):
        span = pl.ds(pl.multiple_of(step * chunk, 16), chunk)
        grad_queries, grad_keys, grad_values = attend_heads_back(
            across_ref[0, span, :HALF].astype(F32),
            grad_ref[0, span].astype(F32),
            attended_ref[0, span],
            total_ref[0, span],
            lambda head: keys_ref[0, head],
            lambda head: values_ref[0, head],
        )
        mixed_ref[0, span, :HALF] = grad_queries.astype(BF)
        for head in range(BRANCH_HEADS):
            lanes = slice(head * HEAD_DIM, (head + 1) * HEAD_DIM)
            dkeys_ref[lanes] += grad_keys[head]
            dvalues_ref[lanes] += grad_values[head]
        return carry

    lax.fori_loop(0, tokens // chunk, attend, 0)

    local_ref[...] = jnp.zeros_like(local_ref)
    for row in range(rows):
        grad = grad_ref[0, row * width : (row + 1) * width].astype(F32)
        taps_ref[72:80] += fold_rows(grad)
        for tap_col, moved in enumerate((shift_up(grad), grad, shift_down(grad))):
            for tap_row in range(3):
                target = row + tap_row - 1
                if 0 <= target < rows:
                    tap = 3 * tap_row + tap_col
                    span = slice(target * width, (target + 1) * width)
                    values = across_ref[0, span, 2 * HALF :].astype(F32)
                    taps_ref[8 * tap : 8 * tap + 8] += fold_rows(values * moved)
                    local_ref[span] += moved * small_ref[tap : tap + 1, :HALF]

    ranks = rank_row(mask_ref[pl.ds(image, 1)].astype(F32), width)
    place = jnp.transpose(jnp.broadcast_to(ranks, (HALF, width)))
    spread = one_hot(iota((width, HALF), 1).astype(F32) == place)
    spread_more = one_hot((iota((width, kept - HALF), 1) + HALF).astype(F32) == place[:, : kept - HALF])
    spread = jnp.concatenate([spread, spread_more], axis=1)
    grad_keys = jnp.transpose(dkeys_ref[...]) * SCALE
    grad_values = jnp.transpose(dvalues_ref[...])
    high = grad_values.astype(BF)
    low = (grad_values - high.astype(F32)).astype(BF)
    grad_keys = grad_keys.astype(BF)
    for row in range(rows):
        span = slice(row * kept, (row + 1) * kept)
        packed = jnp.concatenate([grad_keys[span], high[span], low[span]], axis=1)
        unpacked = dot(spread, packed)
        target = slice(row * width, (row + 1) * width)
        mixed_ref[0, target, HALF : 2 * HALF] = unpacked[:, :HALF].astype(BF)
        whole = unpacked[:, HALF : 2 * HALF] + unpacked[:, 2 * HALF :] + local_ref[target]
        mixed_ref[0, target, 2 * HALF :] = whole.astype(BF)
    dweight_ref[...] += dot_tn(normed_ref[0], mixed_ref[0])
    if last:
        shard_pieces(me_ref, piece_refs, dweight_ref)


def down_back_kernel(dims, ways, first, last, *refs):
    height, width, wide, wide_part, spare = dims
    refs = list(refs)

    def take(number):
        taken = refs[:number]
        del refs[:number]
        return taken

    me_ref, mask_ref, small_ref, weight_ref, attended_ref, total_ref, saved_ref = take(7)
    normed_in = take(ways)
    grads_in = take(ways)
    starts = take(2) if last else None
    out_refs = take(ways)
    taps_ref = take(1)[0]
    piece_refs = take(ways) if last else None
    dweight_ref, normed_ref, mixed_ref, grad_ref, out_ref, turned_ref, column_ref = take(7)
    rows = height // ways
    start = down_setup(me_ref, mask_ref, column_ref, width, wide, wide_part, first)
    assemble(me_ref, normed_in, normed_ref, 0, rows)
    assemble(me_ref, grads_in, grad_ref, 0, rows)
    mixed_ref[...] = saved_ref[0].astype(F32)
    tokens = height * GROUP
    windows = wide_part // GROUP
    start_sums((taps_ref, dweight_ref), starts)

    def one_window(window, carry):
        span = pl.ds(pl.multiple_of(window * GROUP, GROUP), GROUP)
        flat = mixed_ref[:, span].reshape(tokens, 3 * HALF)
        queries, keys, values = (flat[:, part * HALF : (part + 1) * HALF] for part in range(3))
        grad_grid = grad_ref[:, span]
        grad = grad_grid.reshape(tokens, HALF)
        bias = window_bias(column_ref, start, window, height)
        key_list, value_list = window_operands(keys, values, bias, spare)
        grad_queries, grad_keys, grad_values = attend_heads_back(
            queries,
            grad,
            attended_ref[0, :, span].reshape(tokens, HALF),
            total_ref[0, :, span].reshape(tokens, HALF),
            lambda head: key_list[head],
            lambda head: value_list[head],
        )
        grad_keys = jnp.transpose(jnp.concatenate(grad_keys, axis=0))[:tokens] * SCALE
        grad_values = jnp.transpose(jnp.concatenate(grad_values, axis=0))[:tokens]
        values_grid = values.reshape(height, GROUP, HALF)
        local = jnp.zeros((height, GROUP, HALF), F32)
        taps_ref[72:80] += jnp.sum(grad_grid, axis=0)
        shifted = (grid_shift(grad_grid, -1), grad_grid, grid_shift(grad_grid, 1))
        for tap_col, moved in enumerate(shifted):
            stacked = grid_stack(moved)
            for tap_row in range(3):
                tap = 3 * tap_row + tap_col
                source = stacked[2 - tap_row : 2 - tap_row + height]
                taps_ref[8 * tap : 8 * tap + 8] += jnp.sum(source * values_grid, axis=0)
                local = local + source * small_ref[tap : tap + 1, HALF:].reshape(1, 1, HALF)
        shape = (height, GROUP, HALF)
        out_ref[:, span, :HALF] = grad_queries.reshape(shape)
        out_ref[:, span, HALF : 2 * HALF] = grad_keys.reshape(shape)
        out_ref[:, span, 2 * HALF :] = grad_values.reshape(shape) + local
        return carry

    lax.fori_loop(0, windows, one_window, 0)
    mixed_grad = out_ref[...].reshape(height * wide_part, 3 * HALF).astype(BF)
    grad_normed = dot_nt(mixed_grad, weight_ref[:, 3 * HALF :]).astype(BF)
    turned_ref[...] = grad_normed.reshape(height, wide_part, 2 * HALF)
    for distance in range(ways):
        place = me_ref[0] ^ distance
        out_refs[distance][0] = turned_ref[pl.ds(place * rows, rows)]
    normed = normed_ref[...].reshape(height * wide_part, 2 * HALF)
    dweight_ref[...] += dot_tn(normed, mixed_grad)
    if last:
        shard_pieces(me_ref, piece_refs, dweight_ref)


def final_kernel(dims, ways, last, *refs):
    rows, width, wide, wide_part, chunk = dims
    refs = list(refs)

    def take(number):
        taken = refs[:number]
        del refs[:number]
        return taken

    me_ref, x_ref, middle_ref, across_ref = take(4)
    pieces_in = take(ways)
    small_ref, weight_ref = take(2)
    starts = take(1) if last else None
    others = take(4) if last else None
    grad_ref, dsmall_ref = take(2)
    whole_ref = take(1)[0] if last else None
    wide_ref, down_ref = take(2)
    tokens = rows * width
    start_sums((dsmall_ref,), starts)
    assemble(me_ref, pieces_in, wide_ref, 1, wide_part)
    contract = contract_matrix(width, wide)
    for row in range(rows):
        down_ref[row * width : (row + 1) * width] = dot(contract, wide_ref[row])

    def token_rows(step, carry):
        span = pl.ds(pl.multiple_of(step * chunk, 16), chunk)
        _, scaled, recip = normalize(x_ref[0, span].astype(F32), small_ref[9:10], small_ref[10:11])
        grad_normed = dot_nt(across_ref[0, span], weight_ref[:, : 3 * HALF]) + down_ref[span]
        dsmall_ref[0:8] += fold_rows(grad_normed * scaled)
        dsmall_ref[8:16] += fold_rows(grad_normed)
        grad_ref[0, span] = middle_ref[0, span] + normalize_back(
            grad_normed, scaled, recip, small_ref[9:10]
        )
        return carry

    lax.fori_loop(0, tokens // chunk, token_rows, 0)
    if last:

        @at_last_step
        def _():
            across_taps, down_taps, middle_sums, bias_sums = others
            channels = 2 * HALF

            def total(ref, index):
                return jnp.sum(ref[8 * index : 8 * index + 8], axis=0, keepdims=True)

            def set_taps(row, index):
                whole_ref[row : row + 1, :HALF] = total(across_taps, index)
                whole_ref[row : row + 1, HALF:] = total(down_taps, index)

            whole_ref[...] = jnp.zeros_like(whole_ref)
            for tap in range(9):
                set_taps(tap, tap)
            whole_ref[9:10] = total(dsmall_ref, 0)
            whole_ref[10:11] = total(dsmall_ref, 1)
            set_taps(11, 9)
            for index in range(4):
                whole_ref[12 + index : 13 + index] = total(middle_sums, index)
            bias = total(bias_sums, 0)
            for block in range(bias.shape[1] // channels):
                whole_ref[16 + block : 17 + block] = bias[:, block * channels : (block + 1) * channels]


def update_kernel(blocks, factor_ref, shard_ref, across_ref, down_ref, *refs):
    old, new = refs[:12], refs[12:]
    factor = factor_ref[0]
    rows, channels = old[1].shape
    hidden_width = old[2].shape[1]

    def update(index, grads, rate, spans=(slice(None), slice(None))):
        weight, first, second = (old[part * 4 + index][spans] for part in range(3))
        results = adam_update(weight, first, second, grads * factor, rate, WEIGHT_DECAY)
        for part in range(3):
            new[part * 4 + index][spans] = results[part]

    update(0, across_ref[...], RATE_MATRIX, (slice(None), slice(0, 3 * HALF)))
    update(0, down_ref[...], RATE_MATRIX, (slice(None), slice(3 * HALF, 6 * HALF)))
    update(1, shard_ref[:, :channels], RATE_OUTPUT)
    update(2, shard_ref[:, channels : channels + hidden_width], RATE_MATRIX)
    for block in range(blocks):
        begin = channels + hidden_width + block * channels
        update(
            3,
            shard_ref[:, begin : begin + channels],
            RATE_MATRIX,
            (slice(block * rows, (block + 1) * rows), slice(None)),
        )


def image_block(*shape, first=0):
    return pl.BlockSpec((1,) + shape, lambda image: (image + first,) + (0,) * len(shape))


def whole_block(*shape):
    return pl.BlockSpec(shape, lambda image: (0,) * len(shape))


def scalar_block():
    return pl.BlockSpec(memory_space=pltpu.SMEM)


def run_kernel(body, images, inputs, outputs, scratch, micros, after=(), alias=None):
    number = len(inputs)
    hidden = list(after)
    aliases = {}
    if alias is not None:
        aliases = {number + len(hidden): alias[1]}
        hidden.append(alias[0])

    def wrapped(*refs):
        body(*refs[:number], *refs[number + len(hidden) :])

    return pl.pallas_call(
        wrapped,
        grid=(images,),
        in_specs=[spec for _, spec in inputs] + [pl.BlockSpec(memory_space=pl.ANY)] * len(hidden),
        out_specs=[spec for _, _, spec in outputs],
        out_shape=[jax.ShapeDtypeStruct(shape, dtype) for shape, dtype, _ in outputs],
        scratch_shapes=scratch,
        input_output_aliases=aliases,
        compiler_params=pltpu.CompilerParams(vmem_limit_bytes=VMEM_LIMIT),
        cost_estimate=pl.CostEstimate(
            flops=int(micros * 1e9), bytes_accessed=int(micros * 1e6), transcendentals=0
        ),
    )(*[operand for operand, _ in inputs], *hidden)


def adam_update(weight, first_old, second_old, grad_value, rate_value, decay_value):
    new_first = BETA_ONE * first_old + (1.0 - BETA_ONE) * grad_value
    new_second = BETA_TWO * second_old + (1.0 - BETA_TWO) * grad_value * grad_value
    first_hat = new_first / (1.0 - BETA_ONE**STEP)
    second_hat = new_second / (1.0 - BETA_TWO**STEP)
    new_weight = weight - rate_value * (
        first_hat / (jnp.sqrt(second_hat) + ADAM_EPS) + decay_value * weight
    )
    return (new_first, new_second, new_weight)


def swap(value, axis, distance):
    return lax.ppermute(value, axis, [(place, place ^ distance) for place in range(lax.axis_size(axis))])


def exchange(pieces):
    return [pieces[0]] + [swap(pieces[d], "seq", d) for d in range(1, len(pieces))]


def tree_sum(values):
    while len(values) > 1:
        values = [values[i] + values[i + 1] for i in range(0, len(values), 2)]
    return values[0]


def sum_chips(value):
    return tree_sum([value] + [swap(value, "img", d) for d in range(2, lax.axis_size("img"), 2)])


def sum_cores(value):
    return value + swap(value, "img", 1)


def sum_halves(value):
    core = lax.axis_index("img") % 2
    rows = value.shape[0] // 2
    mine = lax.dynamic_slice_in_dim(value, core * rows, rows, 0)
    other = lax.dynamic_slice_in_dim(value, (1 - core) * rows, rows, 0)
    stages = [mine + swap(other, "img", 1)]
    distance = 2
    while distance < lax.axis_size("img"):
        stages.append(stages[-1] + swap(stages[-1], "img", distance))
        distance *= 2
    return stages


def join_halves(mine):
    other = swap(mine, "img", 1)
    lower = lax.axis_index("img") % 2 == 0
    return jnp.concatenate([jnp.where(lower, mine, other), jnp.where(lower, other, mine)], axis=0)


def on_device(
    images,
    cotangent,
    valid_mask,
    qkv_weight,
    out_weight,
    expand_weight,
    shrink_weight,
    small_params,
    expand_bias,
    first_qkv,
    first_out,
    first_expand,
    first_shrink,
    first_small,
    first_bias,
    second_qkv,
    second_out,
    second_expand,
    second_shrink,
    second_small,
    second_bias,
):
    ways = lax.axis_size("seq")
    owner = lax.axis_index("seq")
    me = owner.astype(jnp.int32).reshape(1)
    count, rows, width, channels = images.shape
    tokens = rows * width
    height = rows * ways
    wide = width // STRIPE * GROUP
    wide_part = wide // ways
    kept = -(-VALID // 16) * 16
    key_rows = -(-rows * kept // 256) * 256
    window_tokens = height * GROUP
    spare = -window_tokens % 128
    shard = qkv_weight.shape[0]
    hidden_width = expand_weight.shape[1]
    blocks = hidden_width // channels
    chunk = width
    pair = count // 2
    halves = (0, pair)

    small_pack = jnp.concatenate(
        [small_params, jnp.pad(expand_bias[None], ((0, small_params.shape[0] - 1), (0, 0)))], axis=1
    )
    small_pack = jnp.pad(small_pack, ((0, 0), (0, qkv_weight.shape[1] - small_pack.shape[1])))
    early = jnp.concatenate([qkv_weight, small_pack], axis=0).astype(BF)
    early_pieces = exchange([early] * ways)
    shrink_blocks = [shrink_weight[block * shard : (block + 1) * shard] for block in range(blocks)]
    late = jnp.concatenate([out_weight, expand_weight, *shrink_blocks], axis=1).astype(BF)

    x = images.reshape(count, tokens, channels)
    cot = cotangent.reshape(count, tokens, channels)
    me_in = (me, scalar_block())
    mask_in = (valid_mask, whole_block(*valid_mask.shape))
    piece_in = (rows, wide_part, channels)
    piece_out = (rows, wide_part, HALF)
    qkv_shape = (channels, 6 * HALF)

    def per_image(array, first=0):
        return (array, image_block(*array.shape[1:], first=first))

    def whole(array):
        return (array, whole_block(*array.shape))

    def new_image(dims, dtype, images=pair):
        return ((images,) + dims, dtype, image_block(*dims))

    def new_whole(dims, dtype):
        return (dims, dtype, whole_block(*dims))

    results = run_kernel(
        functools.partial(project_kernel, (rows, width, wide, wide_part), ways),
        count,
        [me_in, per_image(x)] + [whole(piece) for piece in early_pieces],
        [new_image((tokens, 3 * HALF), BF, count), new_image((tokens, channels), BF, count)]
        + [new_image(piece_in, BF, count)] * ways
        + [new_whole(qkv_shape, BF), new_whole((16, channels), F32), new_whole((1, hidden_width), F32)],
        [pltpu.VMEM((rows, wide, channels), BF)],
        12,
    )
    across_mixed, normed = results[:2]
    normed_pieces = exchange(results[2 : 2 + ways])
    qkv_low, small_full, bias_full = results[2 + ways :]
    late_pieces = exchange([late] * ways)
    small_in, qkv_in = whole(small_full), whole(qkv_low)

    attention_dims = (rows, width, kept, key_rows, chunk)
    key_shape = (BRANCH_HEADS, key_rows, HALF)
    joined_across, attended, log_total, keys, values = run_kernel(
        functools.partial(across_kernel, attention_dims),
        count,
        [per_image(across_mixed), mask_in, small_in],
        [
            new_image((tokens, HALF), BF, count),
            new_image((tokens, HALF), F32, count),
            new_image((tokens, HALF), F32, count),
            new_image(key_shape, BF, count),
            new_image(key_shape, BF, count),
        ],
        [pltpu.VMEM((tokens, HALF), F32)],
        60,
    )
    last_result = attended

    down_dims = (height, width, wide, wide_part, spare)
    grid_f32 = (height, wide_part, HALF)
    mixed_grid = (height, wide_part, 3 * HALF)
    normed_grid = (height, wide_part, channels)
    down, joined_pieces = [], []
    for index, first in enumerate(halves):
        results = run_kernel(
            functools.partial(down_kernel, down_dims, ways, first),
            pair,
            [me_in, mask_in, small_in, qkv_in] + [per_image(piece, first) for piece in normed_pieces],
            [new_image(piece_out, BF)] * ways
            + [new_image(grid_f32, F32)] * 2
            + [new_image(mixed_grid, BF)],
            [
                pltpu.VMEM(normed_grid, BF),
                pltpu.VMEM(mixed_grid, F32),
                pltpu.VMEM(grid_f32, F32),
                pltpu.VMEM((wide, HALF), F32),
                pltpu.VMEM((window_tokens, HALF), F32),
            ],
            18,
            after=(last_result,),
        )
        down.append(results[ways:])
        joined_pieces.append(exchange(results[:ways]))
        last_result = results[ways]

    block_out = None
    grad_middle, grad_across, grad_pieces = [], [], []
    sums = None
    matrix_sums = [(channels, channels), (channels, hidden_width), (channels, hidden_width)]
    late_shape = late.shape
    for index, first in enumerate(halves):
        last = index == 1
        results = run_kernel(
            functools.partial(
                middle_kernel, (rows, width, wide, wide_part, chunk, channels), ways, last
            ),
            pair,
            [
                me_in,
                (x, image_block(tokens, channels, first=first)),
                (cot, image_block(tokens, channels, first=first)),
                per_image(joined_across, first),
            ]
            + [per_image(piece) for piece in joined_pieces[index]]
            + [whole(piece) for piece in late_pieces]
            + [small_in, whole(bias_full)]
            + ([whole(entry) for entry in sums] if last else []),
            [
                (x.shape, F32, image_block(tokens, channels, first=first)),
                new_image((tokens, channels), F32),
                new_image((tokens, HALF), BF),
            ]
            + [new_image(piece_out, BF)] * ways
            + [new_whole((8, hidden_width), F32), new_whole((32, channels), F32)]
            + (
                [new_whole(late_shape, F32)] * ways
                if last
                else [new_whole(dims, F32) for dims in matrix_sums]
            ),
            ([pltpu.VMEM(dims, F32) for dims in matrix_sums] if last else [])
            + [
                pltpu.VMEM((channels, channels), BF),
                pltpu.VMEM((channels, hidden_width), BF),
                pltpu.VMEM((hidden_width, channels), BF),
                pltpu.VMEM((rows, wide, HALF), BF),
                pltpu.VMEM((tokens, channels), BF),
                pltpu.VMEM((tokens, channels), BF),
                pltpu.VMEM((tokens, hidden_width), BF),
                pltpu.VMEM((tokens, hidden_width), BF),
                pltpu.VMEM((tokens, channels), BF),
                pltpu.VMEM((tokens, HALF), BF),
                pltpu.VMEM((rows, wide, HALF), BF),
            ]
            + ([pltpu.VMEM((hidden_width, channels), F32)] if last else []),
            35,
            after=(last_result,),
            alias=(block_out, 0) if last else None,
        )
        block_out = results[0]
        grad_middle.append(results[1])
        grad_across.append(results[2])
        grad_pieces.append(exchange(results[3 : 3 + ways]))
        sums = results[3 + ways :]
        last_result = results[1]
    bias_sums, middle_sums = sums[:2]
    late_seq = tree_sum(exchange(sums[2:]))
    late_stages = [late_seq] + sum_halves(late_seq)

    grad_normed_pieces = []
    sums = None
    qkv_half = (channels, 3 * HALF)
    half_shard = (shard, 3 * HALF)
    for index, first in enumerate(halves):
        last = index == 1
        results = run_kernel(
            functools.partial(down_back_kernel, down_dims, ways, first, last),
            pair,
            [me_in, mask_in, small_in, qkv_in]
            + [per_image(entry) for entry in down[index]]
            + [per_image(piece, first) for piece in normed_pieces]
            + [per_image(piece) for piece in grad_pieces[index]]
            + ([whole(entry) for entry in sums] if last else []),
            [new_image(piece_in, BF)] * ways
            + [new_whole((80, HALF), F32)]
            + ([new_whole(half_shard, F32)] * ways if last else [new_whole(qkv_half, F32)]),
            ([pltpu.VMEM(qkv_half, F32)] if last else [])
            + [
                pltpu.VMEM(normed_grid, BF),
                pltpu.VMEM(mixed_grid, F32),
                pltpu.VMEM(grid_f32, F32),
                pltpu.VMEM(mixed_grid, F32),
                pltpu.VMEM(normed_grid, BF),
                pltpu.VMEM((wide, HALF), F32),
            ],
            28,
            after=(last_result, late_stages[0]) if last else (last_result,),
        )
        grad_normed_pieces.append(exchange(results[:ways]))
        sums = results[ways:]
        last_result = sums[0]
    down_taps = sums[0]
    down_seq = tree_sum(exchange(sums[1:]))
    down_core = sum_cores(down_seq)

    across_mixed_grad = []
    sums = None
    for index, first in enumerate(halves):
        last = index == 1
        results = run_kernel(
            functools.partial(across_back_kernel, attention_dims, ways, first, last),
            pair,
            [
                me_in,
                per_image(across_mixed, first),
                per_image(grad_across[index]),
                per_image(attended, first),
                per_image(log_total, first),
                per_image(keys, first),
                per_image(values, first),
                per_image(normed, first),
                mask_in,
                small_in,
            ]
            + ([whole(entry) for entry in sums] if last else []),
            [new_image((tokens, 3 * HALF), BF), new_whole((80, HALF), F32)]
            + ([new_whole(half_shard, F32)] * ways if last else [new_whole(qkv_half, F32)]),
            ([pltpu.VMEM(qkv_half, F32)] if last else [])
            + [
                pltpu.VMEM((HALF, key_rows), F32),
                pltpu.VMEM((HALF, key_rows), F32),
                pltpu.VMEM((tokens, HALF), F32),
            ],
            45,
            after=(last_result, late_stages[2], down_seq) if last else (last_result, late_stages[1]),
        )
        across_mixed_grad.append(results[0])
        sums = results[1:]
        last_result = sums[0]
    across_taps = sums[0]
    across_seq = tree_sum(exchange(sums[1:]))
    across_core = sum_cores(across_seq)

    input_grad = None
    sums = None
    for index, first in enumerate(halves):
        last = index == 1
        results = run_kernel(
            functools.partial(final_kernel, (rows, width, wide, wide_part, chunk), ways, last),
            pair,
            [
                me_in,
                (x, image_block(tokens, channels, first=first)),
                per_image(grad_middle[index]),
                per_image(across_mixed_grad[index]),
            ]
            + [per_image(piece) for piece in grad_normed_pieces[index]]
            + [small_in, qkv_in]
            + (
                [whole(entry) for entry in (*sums, across_taps, down_taps, middle_sums, bias_sums)]
                if last
                else []
            ),
            [
                (x.shape, F32, image_block(tokens, channels, first=first)),
                new_whole((16, channels), F32),
            ]
            + ([new_whole((24, channels), F32)] if last else []),
            [pltpu.VMEM((rows, wide, channels), BF), pltpu.VMEM((tokens, channels), F32)],
            8,
            after=(last_result, across_seq) if last else (last_result, late_stages[-1], down_core),
            alias=(input_grad, 0) if last else None,
        )
        input_grad = results[0]
        sums = results[1:]
        last_result = sums[0]
    small_sum = tree_sum(exchange([results[2]] * ways))
    small_sum = sum_chips(sum_cores(small_sum))
    shard_late = join_halves(late_stages[-1])
    shard_down, shard_across = sum_chips(down_core), sum_chips(across_core)

    squared = sum(jnp.sum(entry * entry) for entry in (shard_late, shard_down, shard_across))
    squared = tree_sum(exchange([jnp.full((8, 128), squared)] * ways))[0, 0]
    grad_norm = jnp.sqrt(squared + jnp.sum(small_sum * small_sum))
    factor = CLIP_NORM / jnp.maximum(grad_norm, CLIP_NORM)
    matrices = (
        (qkv_weight, out_weight, expand_weight, shrink_weight)
        + (first_qkv, first_out, first_expand, first_shrink)
        + (second_qkv, second_out, second_expand, second_shrink)
    )
    updated = run_kernel(
        functools.partial(update_kernel, blocks),
        1,
        [(factor.reshape(1), scalar_block())]
        + [whole(entry) for entry in (shard_late, shard_across, shard_down, *matrices)],
        [new_whole(entry.shape, F32) for entry in matrices[:4]] * 3,
        [],
        4,
    )
    small_rows = small_params.shape[0]
    small_grad = lax.dynamic_slice_in_dim(
        small_sum[:small_rows], owner * small_params.shape[1], small_params.shape[1], 1
    )
    bias_grad = lax.dynamic_slice_in_dim(
        small_sum[small_rows : small_rows + blocks].reshape(-1),
        owner * expand_bias.shape[0],
        expand_bias.shape[0],
        0,
    )
    small_new = adam_update(
        small_params, first_small, second_small, small_grad * factor, RATE_SMALL, 0.0
    )
    bias_new = adam_update(expand_bias, first_bias, second_bias, bias_grad * factor, RATE_MATRIX, 0.0)
    outputs = []
    for part in range(3):
        outputs += [*updated[4 * part : 4 * part + 4], small_new[part], bias_new[part]]
    return (
        block_out.reshape(images.shape),
        input_grad.reshape(images.shape),
        grad_norm,
        *outputs,
    )


def solution(mesh):
    sharded = (
        P("seq", None),
        P("seq", None),
        P("seq", None),
        P("seq", None),
        P(None, "seq"),
        P("seq"),
    )
    grid = P("img", "seq", None, None)
    return jax.shard_map(
        on_device,
        mesh=mesh,
        in_specs=(grid, grid, P("img", None)) + sharded * 3,
        out_specs=(grid, grid, P()) + sharded * 3,
        check_vma=False,
    )
```

```python
import functools

import jax
import jax.numpy as jnp
from jax import lax
from jax.experimental import pallas as pl
from jax.experimental.pallas import tpu as pltpu
from jax.sharding import PartitionSpec as P

HEADS = 8
STRIPE = 7
STEP = 10
VALID = 168

EPS_NORM = 1e-05
BETA_ONE = 0.9
BETA_TWO = 0.999
ADAM_EPS = 1e-08
WEIGHT_DECAY = 0.05
CLIP_NORM = 1.0
RATE_MATRIX = 0.1
RATE_OUTPUT = 0.5
RATE_SMALL = 0.3
INV_ROOT_TWO = 0.7071067811865476
INV_ROOT_TAU = 0.3989422804014327
LOG2E = 1.4426950408889634

BF = jnp.bfloat16
F32 = jnp.float32
HALF = 128
BRANCH_HEADS = 4
HEAD_DIM = 32
SCALE = HEAD_DIM**-0.5
GROUP = 8
MASKED = -1e38
EXPONENT_SCALE = SCALE * LOG2E
EXPONENT_BOUND = 60.0
VMEM_LIMIT = 60 * 2**20


def dot(left, right):
    return jnp.dot(left, right, preferred_element_type=F32)


def dot_nt(left, right):
    return lax.dot_general(left, right, (((1,), (1,)), ((), ())), preferred_element_type=F32)


def dot_tn(left, right):
    return lax.dot_general(left, right, (((0,), (0,)), ((), ())), preferred_element_type=F32)


def iota(shape, dim):
    return lax.broadcasted_iota(jnp.int32, shape, dim)


def one_hot(condition):
    return jnp.where(condition, 1.0, 0.0).astype(BF)


def expand_condition(wide, width):
    e, c = iota((wide, width), 0), iota((wide, width), 1)
    return ((e & 7) < STRIPE) & (c == STRIPE * (e >> 3) + (e & 7))


def contract_matrix(width, wide):
    c, e = iota((width, wide), 0), iota((width, wide), 1)
    return one_hot(((e & 7) < STRIPE) & (c == STRIPE * (e >> 3) + (e & 7)))


def normalize(values, gain_row, offset_row):
    center = values - jnp.mean(values, axis=-1, keepdims=True)
    spread = jnp.mean(center * center, axis=-1, keepdims=True)
    recip = lax.rsqrt(spread + EPS_NORM)
    scaled = center * recip
    return scaled * gain_row + offset_row, scaled, recip


def normalize_back(grad_out, scaled, recip, gain_row):
    grad_scaled = grad_out * gain_row
    inner_one = jnp.mean(grad_scaled, axis=-1, keepdims=True)
    inner_two = jnp.mean(grad_scaled * scaled, axis=-1, keepdims=True)
    return recip * (grad_scaled - inner_one - scaled * inner_two)


def fold_rows(values):
    rows, columns = values.shape
    return jnp.sum(values.reshape(rows // 8, 8, columns), axis=0)


def pieces_of(values):
    first = values.astype(BF).astype(F32)
    rest = values - first
    second = rest.astype(BF).astype(F32)
    return first, second, (rest - second).astype(BF).astype(F32)


def lane_head(rows):
    return (iota((rows, HALF), 1) >> 5) & 3


def lane_sub(rows):
    return iota((rows, HALF), 1) & 31


def piece_lanes(values, fourth):
    one, two, three = pieces_of(values)
    sub = lane_sub(values.shape[0])
    return jnp.where(
        sub == 0, one, jnp.where(sub == 1, two, jnp.where(sub == 2, three, jnp.where(sub == 3, fourth, 0.0)))
    )


def wide_keys(keys, bias):
    sub = lane_sub(keys.shape[0])
    extra = jnp.where(sub < 3, 1.0, jnp.where(sub == 3, bias, 0.0))
    return jnp.concatenate([keys.astype(BF), extra.astype(BF)], axis=1)


def wide_values(values):
    return jnp.concatenate([values.astype(BF), jnp.ones(values.shape, BF)], axis=1)


def stack_heads(left, right):
    head_of = lane_head(left.shape[0])
    parts = []
    for head in range(BRANCH_HEADS):
        mine = head_of == head
        parts.append(
            jnp.concatenate(
                [jnp.where(mine, left, 0.0).astype(BF), jnp.where(mine, right, 0.0).astype(BF)], axis=1
            )
        )
    return jnp.concatenate(parts, axis=0)


def pick_heads(stacked, rows):
    head_of = lane_head(rows)
    picked = stacked[:rows]
    for head in range(1, BRANCH_HEADS):
        picked = jnp.where(head_of == head, stacked[head * rows : (head + 1) * rows], picked)
    return picked


def head_norms(values):
    block = one_hot((iota((HALF, HALF), 0) >> 5) == (iota((HALF, HALF), 1) >> 5))
    sums = dot((values * values * 1.02).astype(BF), block)
    return jnp.max(sums, axis=0, keepdims=True)


def exceeds(query_norms, key_norms):
    bound = jnp.max(query_norms * key_norms)
    return jnp.logical_not(bound <= EXPONENT_BOUND * EXPONENT_BOUND)


def stack_queries(queries, shift):
    return stack_heads(queries, piece_lanes(shift * (-1.0 / EXPONENT_SCALE), 1.0))


def attend_heads(queries, shift, keys, values):
    rows = queries.shape[0]
    scores = dot_nt(stack_queries(queries, shift), keys)
    weights = jnp.exp2(scores * EXPONENT_SCALE).astype(BF)
    result = dot(weights, values)
    totals = pick_heads(result[:, HALF:], rows)
    return pick_heads(result[:, :HALF], rows) / totals, jnp.log(totals) * LOG2E + shift


def highest_scores(queries, keys):
    rows = queries.shape[0]
    scores = dot_nt(stack_queries(queries, jnp.zeros((rows, HALF), F32)), keys)
    highest = jnp.max(scores, axis=-1, keepdims=True) * EXPONENT_SCALE
    return pick_heads(jnp.broadcast_to(highest, (BRANCH_HEADS * rows, HALF)), rows)


def attend_heads_back(queries, grad, attended, log_total, keys, values):
    rows = queries.shape[0]
    eye = one_hot(iota((HALF, HALF), 0) == iota((HALF, HALF), 1))
    query_turned = dot_nt(eye, queries.astype(BF)).astype(BF)
    grad_turned = dot_nt(eye, grad.astype(BF)).astype(BF)
    block = one_hot((iota((HALF, HALF), 0) >> 5) == (iota((HALF, HALF), 1) >> 5))
    inner = sum(dot(piece.astype(BF), block) for piece in pieces_of(grad * attended))
    weights = jnp.exp2(dot_nt(stack_queries(queries, log_total), keys) * EXPONENT_SCALE)
    weights_low = weights.astype(BF)
    grad_weights = dot_nt(stack_heads(grad, piece_lanes(-inner, 0.0)), values)
    grad_scores = (weights * grad_weights).astype(BF)
    grad_queries = pick_heads(dot(grad_scores, keys[:, :HALF]), rows) * SCALE
    grad_keys, grad_values = [], []
    for head in range(BRANCH_HEADS):
        lanes = slice(head * HEAD_DIM, (head + 1) * HEAD_DIM)
        span = slice(head * rows, (head + 1) * rows)
        grad_values.append(dot(grad_turned[lanes], weights_low[span]))
        grad_keys.append(dot(query_turned[lanes], grad_scores[span]))
    return grad_queries, grad_keys, grad_values


def shift_down(values):
    rows = values.shape[0]
    return jnp.where(iota(values.shape, 0) == 0, 0.0, pltpu.roll(values, 1, 0))


def shift_up(values):
    rows = values.shape[0]
    return jnp.where(iota(values.shape, 0) == rows - 1, 0.0, pltpu.roll(values, rows - 1, 0))


def start_sums(sums, starts):
    @pl.when(pl.program_id(0) == 0)
    def _():
        for index, total in enumerate(sums):
            if starts:
                total[...] = starts[index][...]
            else:
                total[...] = jnp.zeros_like(total)


def at_last_step(body):
    pl.when(pl.program_id(0) == pl.num_programs(0) - 1)(body)


def project_kernel(dims, ways, *refs):
    rows, width, wide, wide_part = dims
    me_ref, x_ref = refs[:2]
    pieces = refs[2 : 2 + ways]
    across_ref, normed_ref = refs[2 + ways : 4 + ways]
    down_refs = refs[4 + ways : 4 + 2 * ways]
    weight_ref, small_ref, bias_ref, spread_ref = refs[4 + 2 * ways :]

    @pl.when(pl.program_id(0) == 0)
    def _():
        channels, hidden_width = small_ref.shape[1], bias_ref.shape[1]
        shard = channels // ways
        bias_shard = hidden_width // ways
        lanes = -(-(shard + bias_shard) // 128) * 128
        lane, column = iota((lanes, channels + hidden_width), 0), iota((lanes, channels + hidden_width), 1)
        total = jnp.zeros((16, channels + hidden_width), F32)
        for distance, piece in enumerate(pieces):
            place = me_ref[0] ^ distance
            weight_ref[pl.ds(pl.multiple_of(place * shard, shard), shard)] = piece[:shard]
            target = jnp.where(
                lane < shard,
                lane + shard * place,
                channels + lane - shard + bias_shard * place,
            )
            chosen = one_hot((column == target) & (lane < shard + bias_shard))
            total = total + dot(piece[shard : shard + 16, :lanes], chosen)
        small_ref[...] = total[:, :channels]
        bias_ref[...] = total[0:1, channels:]

    gain, offset = small_ref[9:10], small_ref[10:11]
    expand = one_hot(expand_condition(wide, width))
    for row in range(rows):
        span = slice(row * width, (row + 1) * width)
        normed, _, _ = normalize(x_ref[0, span].astype(F32), gain, offset)
        normed = normed.astype(BF)
        normed_ref[0, span] = normed
        across_ref[0, span] = dot(normed, weight_ref[:, : 3 * HALF]).astype(BF)
        spread_ref[row] = dot(expand, normed).astype(BF)
        for distance in range(ways):
            start = pl.multiple_of((me_ref[0] ^ distance) * wide_part, wide_part)
            down_refs[distance][0, row] = spread_ref[row, pl.ds(start, wide_part)]


def rank_row(mask_row, width):
    lower = one_hot(iota((width, width), 0) <= iota((width, width), 1))
    counted = dot(jnp.broadcast_to(mask_row, (8, width)).astype(BF), lower)[0:1]
    return jnp.where(mask_row > 0.0, counted - 1.0, -1.0)


def across_kernel(
    dims,
    across_ref,
    mask_ref,
    small_ref,
    joined_ref,
    attended_ref,
    total_ref,
    keys_ref,
    values_ref,
    shift_ref,
):
    rows, width, kept, key_rows, chunk = dims
    tokens = rows * width
    image = pl.program_id(0)
    ranks = rank_row(mask_ref[pl.ds(image, 1)].astype(F32), width)
    select = one_hot(iota((kept, width), 0).astype(F32) == ranks)
    bias = jnp.where(iota((kept, HALF), 0) >= VALID, MASKED, 0.0)
    key_norms = jnp.zeros((1, HALF), F32)
    for row in range(rows):
        picked = dot(select, across_ref[0, row * width : (row + 1) * width, HALF:])
        key_norms = jnp.maximum(key_norms, head_norms(picked[:, :HALF]))
        span = slice(row * kept, (row + 1) * kept)
        keys_ref[0, span] = wide_keys(picked[:, :HALF], bias)
        values_ref[0, span] = wide_values(picked[:, HALF:])
    spare = key_rows - rows * kept
    if spare:
        nothing = jnp.zeros((spare, HALF), F32)
        keys_ref[0, rows * kept :] = wide_keys(nothing, nothing + MASKED)
        values_ref[0, rows * kept :] = wide_values(nothing)

    query_norms = head_norms(across_ref[0, :, :HALF].astype(F32) * (SCALE * LOG2E))
    large = exceeds(query_norms, key_norms)

    @pl.when(image == 0)
    def _():
        shift_ref[...] = jnp.zeros_like(shift_ref)

    def rows_of(step):
        return pl.ds(pl.multiple_of(step * chunk, 16), chunk)

    @pl.when(large)
    def _():
        def highest(step, carry):
            span = rows_of(step)
            shift_ref[span] = highest_scores(across_ref[0, span, :HALF].astype(F32), keys_ref[0])
            return carry

        lax.fori_loop(0, tokens // chunk, highest, 0)

    def attend(step, carry):
        span = rows_of(step)
        attended, log_total = attend_heads(
            across_ref[0, span, :HALF].astype(F32), shift_ref[span], keys_ref[0], values_ref[0]
        )
        attended_ref[0, span] = attended
        total_ref[0, span] = log_total
        return carry

    lax.fori_loop(0, tokens // chunk, attend, 0, unroll=True)

    @pl.when(large)
    def _():
        shift_ref[...] = jnp.zeros_like(shift_ref)

    def value_row(row):
        return across_ref[0, row * width : (row + 1) * width, 2 * HALF :].astype(F32)

    for row in range(rows):
        sums = [jnp.zeros((width, HALF), F32) for _ in range(3)]
        for tap_row in range(3):
            source = row + tap_row - 1
            if 0 <= source < rows:
                values = value_row(source)
                for tap_col in range(3):
                    tap = 3 * tap_row + tap_col
                    sums[tap_col] = sums[tap_col] + values * small_ref[tap : tap + 1, :HALF]
        local = shift_down(sums[0]) + sums[1] + shift_up(sums[2]) + small_ref[11:12, :HALF]
        span = slice(row * width, (row + 1) * width)
        joined_ref[0, span] = (attended_ref[0, span] + local).astype(BF)


def assemble(me_ref, pieces, target_ref, dim, step):
    for distance, piece in enumerate(pieces):
        place = me_ref[0] ^ distance
        if dim == 0:
            target_ref[pl.ds(place * step, step)] = piece[0].astype(target_ref.dtype)
        else:
            target_ref[:, pl.ds(pl.multiple_of(place * step, step), step)] = piece[0].astype(
                target_ref.dtype
            )


def down_setup(me_ref, mask_ref, column_ref, width, wide, wide_part, first):
    image = pl.program_id(0) + first
    mask_row = mask_ref[pl.ds(image, 1)].astype(F32)
    valid = one_hot(expand_condition(wide, width) & (mask_row > 0.0))
    column_ref[...] = dot(valid, jnp.ones((width, HALF), BF))
    return pl.multiple_of(me_ref[0] * wide_part, GROUP)


def window_bias(column_ref, start, window, height):
    valid = column_ref[pl.ds(start + pl.multiple_of(window * GROUP, GROUP), GROUP)]
    bias = jnp.where(valid > 0.5, 0.0, MASKED)
    return jnp.broadcast_to(bias[None], (height, GROUP, HALF)).reshape(height * GROUP, HALF)


def pad_keys(block, spare, fill):
    if not spare:
        return block
    return jnp.concatenate([block, jnp.full((spare, HALF), 0.0, F32) + fill], axis=0)


def window_operands(keys, values, bias, spare):
    return (
        wide_keys(pad_keys(keys, spare, 0.0), pad_keys(bias, spare, MASKED)),
        wide_values(pad_keys(values, spare, 0.0)),
    )


def grid_shift(values, amount):
    return pltpu.roll(values, amount % GROUP, 1)


def grid_stack(values):
    edge = jnp.zeros((1,) + values.shape[1:], F32)
    return jnp.concatenate([edge, values, edge], axis=0)


def down_kernel(dims, ways, first, *refs):
    height, width, wide, wide_part, spare = dims
    me_ref, mask_ref, small_ref, weight_ref = refs[:4]
    pieces_in = refs[4 : 4 + ways]
    joined_refs = refs[4 + ways : 4 + 2 * ways]
    attended_ref, total_ref, saved_ref, normed_ref, mixed_ref, joined_ref, column_ref, shift_ref = refs[
        4 + 2 * ways :
    ]
    rows = height // ways
    start = down_setup(me_ref, mask_ref, column_ref, width, wide, wide_part, first)
    assemble(me_ref, pieces_in, normed_ref, 0, rows)
    tokens = height * GROUP
    windows = wide_part // GROUP
    normed = normed_ref[...].reshape(height * wide_part, 2 * HALF)
    mixed_low = dot(normed, weight_ref[:, 3 * HALF :]).astype(BF)
    mixed_low = mixed_low.reshape(height, wide_part, 3 * HALF)
    saved_ref[0] = mixed_low
    mixed_ref[...] = mixed_low.astype(F32)

    @pl.when(pl.program_id(0) == 0)
    def _():
        shift_ref[...] = jnp.zeros_like(shift_ref)

    everything = mixed_ref[...].reshape(height * wide_part, 3 * HALF)
    large = exceeds(
        head_norms(everything[:, :HALF] * (SCALE * LOG2E)), head_norms(everything[:, HALF : 2 * HALF])
    )

    def one_window(window, carry):
        span = pl.ds(pl.multiple_of(window * GROUP, GROUP), GROUP)
        grid = mixed_ref[:, span]
        flat = grid.reshape(tokens, 3 * HALF)
        queries, keys, values = (flat[:, part * HALF : (part + 1) * HALF] for part in range(3))
        bias = window_bias(column_ref, start, window, height)
        keys_in, values_in = window_operands(keys, values, bias, spare)

        @pl.when(large)
        def _():
            shift_ref[...] = highest_scores(queries, keys_in)

        attended, log_total = attend_heads(queries, shift_ref[...], keys_in, values_in)
        attended_ref[0, :, span] = attended.reshape(height, GROUP, HALF)
        total_ref[0, :, span] = log_total.reshape(height, GROUP, HALF)
        stacked = grid_stack(values.reshape(height, GROUP, HALF))
        sums = [jnp.zeros((height, GROUP, HALF), F32) for _ in range(3)]
        for tap_row in range(3):
            for tap_col in range(3):
                tap = 3 * tap_row + tap_col
                sums[tap_col] = sums[tap_col] + stacked[tap_row : tap_row + height] * small_ref[
                    tap : tap + 1, HALF:
                ].reshape(1, 1, HALF)
        local = grid_shift(sums[0], 1) + sums[1] + grid_shift(sums[2], -1)
        local = local + small_ref[11:12, HALF:].reshape(1, 1, HALF)
        joined_ref[:, span] = attended.reshape(height, GROUP, HALF) + local
        return carry

    lax.fori_loop(0, windows, one_window, 0, unroll=min(windows, 4))

    @pl.when(large)
    def _():
        shift_ref[...] = jnp.zeros_like(shift_ref)

    for distance in range(ways):
        place = me_ref[0] ^ distance
        joined_refs[distance][0] = joined_ref[pl.ds(place * rows, rows)].astype(BF)


def gelu_parts(hidden):
    upper = 0.5 + 0.5 * lax.erf(hidden * INV_ROOT_TWO)
    return upper, jnp.exp2(hidden * hidden * (-0.5 * LOG2E)) * INV_ROOT_TAU


def middle_kernel(dims, ways, last, *refs):
    rows, width, wide, wide_part, chunk, hidden_part = dims
    refs = list(refs)

    def take(number):
        taken = refs[:number]
        del refs[:number]
        return taken

    me_ref, x_ref, cot_ref, across_ref = take(4)
    pieces_in = take(ways)
    weights_in = take(ways)
    small_ref, bias_ref = take(2)
    starts = take(5) if last else None
    block_ref, middle_ref, grad_across_ref = take(3)
    grad_refs = take(ways)
    dbias_ref, dsmall_ref = take(2)
    piece_refs = take(ways) if last else None
    dout_ref, dexpand_ref, dshrink_ref = take(3)
    out_ref, expand_ref, shrink_ref = take(3)
    wide_ref, joined_ref, normed_ref, active_ref, hidden_ref, attended_ref, down_ref, gwide_ref = take(8)
    turned_ref = take(1)[0] if last else None
    tokens = rows * width
    hidden_width = expand_ref.shape[1]
    channels = 2 * HALF
    shard = channels // ways
    blocks = hidden_width // channels
    start_sums((dbias_ref, dsmall_ref, dout_ref, dexpand_ref, dshrink_ref), starts)

    @pl.when(pl.program_id(0) == 0)
    def _():
        for distance, piece in enumerate(weights_in):
            place = me_ref[0] ^ distance
            span = pl.ds(pl.multiple_of(place * shard, shard), shard)
            out_ref[span] = piece[:, :channels]
            expand_ref[span] = piece[:, channels : channels + hidden_width]
            for block in range(blocks):
                begin = pl.multiple_of((place * blocks + block) * shard, shard)
                lanes = slice(channels + hidden_width + block * channels, channels + hidden_width + (block + 1) * channels)
                shrink_ref[pl.ds(begin, shard)] = piece[:, lanes]

    assemble(me_ref, pieces_in, wide_ref, 1, wide_part)
    contract = contract_matrix(width, wide)
    for row in range(rows):
        span = slice(row * width, (row + 1) * width)
        joined_ref[span, :HALF] = across_ref[0, span]
        joined_ref[span, HALF:] = dot(contract, wide_ref[row]).astype(BF)

    def token_rows(step, carry):
        span = pl.ds(pl.multiple_of(step * chunk, 16), chunk)
        joined = joined_ref[span]
        attended_out = dot(joined, out_ref[...]) + small_ref[12:13]
        middle = x_ref[0, span].astype(F32) + attended_out
        normed, scaled, recip = normalize(middle, small_ref[13:14], small_ref[14:15])
        normed_low = normed.astype(BF)
        normed_ref[span] = normed_low
        back = cot_ref[0, span]
        result = middle + small_ref[15:16]
        grad_normed = jnp.zeros((chunk, 2 * HALF), F32)
        for part in range(0, hidden_width, hidden_part):
            lanes = slice(part, part + hidden_part)
            hidden = dot(normed_low, expand_ref[:, lanes]) + bias_ref[:, lanes]
            upper, density = gelu_parts(hidden)
            active = (hidden * upper).astype(BF)
            active_ref[span, lanes] = active
            result = result + dot(active, shrink_ref[lanes])
            grad_active = dot_nt(back, shrink_ref[lanes])
            grad_hidden = grad_active * (upper + hidden * density)
            grad_hidden = grad_hidden.astype(BF)
            hidden_ref[span, lanes] = grad_hidden
            dbias_ref[:, lanes] += fold_rows(grad_hidden.astype(F32))
            grad_normed = grad_normed + dot_nt(grad_hidden, expand_ref[:, lanes])
        block_ref[0, span] = result
        back_wide = back.astype(F32)
        grad_middle = back_wide + normalize_back(grad_normed, scaled, recip, small_ref[13:14])
        middle_ref[0, span] = grad_middle
        grad_attended = grad_middle.astype(BF)
        attended_ref[span] = grad_attended
        grad_joined = dot_nt(grad_attended, out_ref[...]).astype(BF)
        grad_across_ref[0, span] = grad_joined[:, :HALF]
        down_ref[span] = grad_joined[:, HALF:]
        dsmall_ref[0:8] += fold_rows(grad_attended.astype(F32))
        dsmall_ref[8:16] += fold_rows(grad_normed * scaled)
        dsmall_ref[16:24] += fold_rows(grad_normed)
        dsmall_ref[24:32] += fold_rows(back_wide)
        return carry

    lax.fori_loop(0, tokens // chunk, token_rows, 0, unroll=True)
    expand = one_hot(expand_condition(wide, width))
    for row in range(rows):
        gwide_ref[row] = dot(expand, down_ref[row * width : (row + 1) * width]).astype(BF)
    for distance in range(ways):
        place = me_ref[0] ^ distance
        grad_refs[distance][0] = gwide_ref[
            :, pl.ds(pl.multiple_of(place * wide_part, wide_part), wide_part)
        ]
    dout_ref[...] += dot_tn(joined_ref[...], attended_ref[...])
    dexpand_ref[...] += dot_tn(normed_ref[...], hidden_ref[...])
    dshrink_ref[...] += dot_tn(cot_ref[0], active_ref[...])
    if last:

        @at_last_step
        def _():
            for block in range(blocks):
                lanes = slice(block * channels, (block + 1) * channels)
                turned_ref[lanes] = jnp.transpose(dshrink_ref[:, lanes])
            for distance, piece in enumerate(piece_refs):
                place = me_ref[0] ^ distance
                span = pl.ds(pl.multiple_of(place * shard, shard), shard)
                piece[:, :channels] = dout_ref[span]
                piece[:, channels : channels + hidden_width] = dexpand_ref[span]
                for block in range(blocks):
                    begin = pl.multiple_of((place * blocks + block) * shard, shard)
                    lanes = slice(channels + hidden_width + block * channels, channels + hidden_width + (block + 1) * channels)
                    piece[:, lanes] = turned_ref[pl.ds(begin, shard)]


def shard_pieces(me_ref, piece_refs, total_ref):
    shard = piece_refs[0].shape[0]

    @at_last_step
    def _():
        for distance, piece in enumerate(piece_refs):
            begin = pl.multiple_of((me_ref[0] ^ distance) * shard, shard)
            piece[...] = total_ref[pl.ds(begin, shard)]


def across_back_kernel(dims, ways, first, last, *refs):
    rows, width, kept, key_rows, chunk = dims
    refs = list(refs)

    def take(number):
        taken = refs[:number]
        del refs[:number]
        return taken

    me_ref, across_ref, grad_ref, attended_ref, total_ref, keys_ref, values_ref, normed_ref = take(8)
    mask_ref, small_ref = take(2)
    starts = take(2) if last else None
    mixed_ref, taps_ref = take(2)
    piece_refs = take(ways) if last else None
    dweight_ref, dkeys_ref, dvalues_ref, local_ref = take(4)
    tokens = rows * width
    image = pl.program_id(0) + first
    start_sums((taps_ref, dweight_ref), starts)
    dkeys_ref[...] = jnp.zeros_like(dkeys_ref)
    dvalues_ref[...] = jnp.zeros_like(dvalues_ref)

    def attend(step, carry):
        span = pl.ds(pl.multiple_of(step * chunk, 16), chunk)
        grad_queries, grad_keys, grad_values = attend_heads_back(
            across_ref[0, span, :HALF].astype(F32),
            grad_ref[0, span].astype(F32),
            attended_ref[0, span],
            total_ref[0, span],
            keys_ref[0],
            values_ref[0],
        )
        mixed_ref[0, span, :HALF] = grad_queries.astype(BF)
        for head in range(BRANCH_HEADS):
            lanes = slice(head * HEAD_DIM, (head + 1) * HEAD_DIM)
            dkeys_ref[lanes] += grad_keys[head]
            dvalues_ref[lanes] += grad_values[head]
        return carry

    lax.fori_loop(0, tokens // chunk, attend, 0, unroll=True)

    local_ref[...] = jnp.zeros_like(local_ref)
    for row in range(rows):
        grad = grad_ref[0, row * width : (row + 1) * width].astype(F32)
        taps_ref[72:80] += fold_rows(grad)
        for tap_col, moved in enumerate((shift_up(grad), grad, shift_down(grad))):
            for tap_row in range(3):
                target = row + tap_row - 1
                if 0 <= target < rows:
                    tap = 3 * tap_row + tap_col
                    span = slice(target * width, (target + 1) * width)
                    values = across_ref[0, span, 2 * HALF :].astype(F32)
                    taps_ref[8 * tap : 8 * tap + 8] += fold_rows(values * moved)
                    local_ref[span] += moved * small_ref[tap : tap + 1, :HALF]

    ranks = rank_row(mask_ref[pl.ds(image, 1)].astype(F32), width)
    place = jnp.transpose(jnp.broadcast_to(ranks, (HALF, width)))
    spread = one_hot(iota((width, HALF), 1).astype(F32) == place)
    spread_more = one_hot((iota((width, kept - HALF), 1) + HALF).astype(F32) == place[:, : kept - HALF])
    spread = jnp.concatenate([spread, spread_more], axis=1)
    grad_keys = jnp.transpose(dkeys_ref[...]) * SCALE
    grad_values = jnp.transpose(dvalues_ref[...])
    high = grad_values.astype(BF)
    low = (grad_values - high.astype(F32)).astype(BF)
    grad_keys = grad_keys.astype(BF)
    for row in range(rows):
        span = slice(row * kept, (row + 1) * kept)
        packed = jnp.concatenate([grad_keys[span], high[span], low[span]], axis=1)
        unpacked = dot(spread, packed)
        target = slice(row * width, (row + 1) * width)
        mixed_ref[0, target, HALF : 2 * HALF] = unpacked[:, :HALF].astype(BF)
        whole = unpacked[:, HALF : 2 * HALF] + unpacked[:, 2 * HALF :] + local_ref[target]
        mixed_ref[0, target, 2 * HALF :] = whole.astype(BF)
    dweight_ref[...] += dot_tn(normed_ref[0], mixed_ref[0])
    if last:
        shard_pieces(me_ref, piece_refs, dweight_ref)


def down_back_kernel(dims, ways, first, last, *refs):
    height, width, wide, wide_part, spare = dims
    refs = list(refs)

    def take(number):
        taken = refs[:number]
        del refs[:number]
        return taken

    me_ref, mask_ref, small_ref, weight_ref, attended_ref, total_ref, saved_ref = take(7)
    normed_in = take(ways)
    grads_in = take(ways)
    starts = take(2) if last else None
    out_refs = take(ways)
    taps_ref = take(1)[0]
    piece_refs = take(ways) if last else None
    dweight_ref, normed_ref, mixed_ref, grad_ref, out_ref, turned_ref, column_ref = take(7)
    rows = height // ways
    start = down_setup(me_ref, mask_ref, column_ref, width, wide, wide_part, first)
    assemble(me_ref, normed_in, normed_ref, 0, rows)
    assemble(me_ref, grads_in, grad_ref, 0, rows)
    mixed_ref[...] = saved_ref[0].astype(F32)
    tokens = height * GROUP
    windows = wide_part // GROUP
    start_sums((taps_ref, dweight_ref), starts)

    def one_window(window, carry):
        span = pl.ds(pl.multiple_of(window * GROUP, GROUP), GROUP)
        flat = mixed_ref[:, span].reshape(tokens, 3 * HALF)
        queries, keys, values = (flat[:, part * HALF : (part + 1) * HALF] for part in range(3))
        grad_grid = grad_ref[:, span]
        grad = grad_grid.reshape(tokens, HALF)
        bias = window_bias(column_ref, start, window, height)
        keys_in, values_in = window_operands(keys, values, bias, spare)
        grad_queries, grad_keys, grad_values = attend_heads_back(
            queries,
            grad,
            attended_ref[0, :, span].reshape(tokens, HALF),
            total_ref[0, :, span].reshape(tokens, HALF),
            keys_in,
            values_in,
        )
        grad_keys = jnp.transpose(jnp.concatenate(grad_keys, axis=0))[:tokens] * SCALE
        grad_values = jnp.transpose(jnp.concatenate(grad_values, axis=0))[:tokens]
        values_grid = values.reshape(height, GROUP, HALF)
        local = jnp.zeros((height, GROUP, HALF), F32)
        taps_ref[72:80] += jnp.sum(grad_grid, axis=0)
        shifted = (grid_shift(grad_grid, -1), grad_grid, grid_shift(grad_grid, 1))
        for tap_col, moved in enumerate(shifted):
            stacked = grid_stack(moved)
            for tap_row in range(3):
                tap = 3 * tap_row + tap_col
                source = stacked[2 - tap_row : 2 - tap_row + height]
                taps_ref[8 * tap : 8 * tap + 8] += jnp.sum(source * values_grid, axis=0)
                local = local + source * small_ref[tap : tap + 1, HALF:].reshape(1, 1, HALF)
        shape = (height, GROUP, HALF)
        out_ref[:, span, :HALF] = grad_queries.reshape(shape)
        out_ref[:, span, HALF : 2 * HALF] = grad_keys.reshape(shape)
        out_ref[:, span, 2 * HALF :] = grad_values.reshape(shape) + local
        return carry

    lax.fori_loop(0, windows, one_window, 0, unroll=min(windows, 4))
    mixed_grad = out_ref[...].reshape(height * wide_part, 3 * HALF).astype(BF)
    grad_normed = dot_nt(mixed_grad, weight_ref[:, 3 * HALF :]).astype(BF)
    turned_ref[...] = grad_normed.reshape(height, wide_part, 2 * HALF)
    for distance in range(ways):
        place = me_ref[0] ^ distance
        out_refs[distance][0] = turned_ref[pl.ds(place * rows, rows)]
    normed = normed_ref[...].reshape(height * wide_part, 2 * HALF)
    dweight_ref[...] += dot_tn(normed, mixed_grad)
    if last:
        shard_pieces(me_ref, piece_refs, dweight_ref)


def final_kernel(dims, ways, last, *refs):
    rows, width, wide, wide_part, chunk = dims
    refs = list(refs)

    def take(number):
        taken = refs[:number]
        del refs[:number]
        return taken

    me_ref, x_ref, middle_ref, across_ref = take(4)
    pieces_in = take(ways)
    small_ref, weight_ref = take(2)
    starts = take(1) if last else None
    others = take(4) if last else None
    grad_ref, dsmall_ref = take(2)
    whole_ref = take(1)[0] if last else None
    wide_ref, down_ref = take(2)
    tokens = rows * width
    start_sums((dsmall_ref,), starts)
    assemble(me_ref, pieces_in, wide_ref, 1, wide_part)
    contract = contract_matrix(width, wide)
    for row in range(rows):
        down_ref[row * width : (row + 1) * width] = dot(contract, wide_ref[row])

    def token_rows(step, carry):
        span = pl.ds(pl.multiple_of(step * chunk, 16), chunk)
        _, scaled, recip = normalize(x_ref[0, span].astype(F32), small_ref[9:10], small_ref[10:11])
        grad_normed = dot_nt(across_ref[0, span], weight_ref[:, : 3 * HALF]) + down_ref[span]
        dsmall_ref[0:8] += fold_rows(grad_normed * scaled)
        dsmall_ref[8:16] += fold_rows(grad_normed)
        grad_ref[0, span] = middle_ref[0, span] + normalize_back(
            grad_normed, scaled, recip, small_ref[9:10]
        )
        return carry

    lax.fori_loop(0, tokens // chunk, token_rows, 0)
    if last:

        @at_last_step
        def _():
            across_taps, down_taps, middle_sums, bias_sums = others
            channels = 2 * HALF

            def total(ref, index):
                return jnp.sum(ref[8 * index : 8 * index + 8], axis=0, keepdims=True)

            def set_taps(row, index):
                whole_ref[row : row + 1, :HALF] = total(across_taps, index)
                whole_ref[row : row + 1, HALF:] = total(down_taps, index)

            whole_ref[...] = jnp.zeros_like(whole_ref)
            for tap in range(9):
                set_taps(tap, tap)
            whole_ref[9:10] = total(dsmall_ref, 0)
            whole_ref[10:11] = total(dsmall_ref, 1)
            set_taps(11, 9)
            for index in range(4):
                whole_ref[12 + index : 13 + index] = total(middle_sums, index)
            bias = total(bias_sums, 0)
            for block in range(bias.shape[1] // channels):
                whole_ref[16 + block : 17 + block] = bias[:, block * channels : (block + 1) * channels]


def update_kernel(blocks, factor_ref, shard_ref, across_ref, down_ref, *refs):
    old, new = refs[:12], refs[12:]
    factor = factor_ref[0]
    rows, channels = old[1].shape
    hidden_width = old[2].shape[1]

    def update(index, grads, rate, spans=(slice(None), slice(None))):
        weight, first, second = (old[part * 4 + index][spans] for part in range(3))
        results = adam_update(weight, first, second, grads * factor, rate, WEIGHT_DECAY)
        for part in range(3):
            new[part * 4 + index][spans] = results[part]

    update(0, across_ref[...], RATE_MATRIX, (slice(None), slice(0, 3 * HALF)))
    update(0, down_ref[...], RATE_MATRIX, (slice(None), slice(3 * HALF, 6 * HALF)))
    update(1, shard_ref[:, :channels], RATE_OUTPUT)
    update(2, shard_ref[:, channels : channels + hidden_width], RATE_MATRIX)
    for block in range(blocks):
        begin = channels + hidden_width + block * channels
        update(
            3,
            shard_ref[:, begin : begin + channels],
            RATE_MATRIX,
            (slice(block * rows, (block + 1) * rows), slice(None)),
        )


def image_block(*shape, first=0):
    return pl.BlockSpec((1,) + shape, lambda image: (image + first,) + (0,) * len(shape))


def whole_block(*shape):
    return pl.BlockSpec(shape, lambda image: (0,) * len(shape))


def scalar_block():
    return pl.BlockSpec(memory_space=pltpu.SMEM)


def run_kernel(body, images, inputs, outputs, scratch, micros, after=(), alias=None):
    number = len(inputs)
    hidden = list(after)
    aliases = {}
    if alias is not None:
        aliases = {number + len(hidden): alias[1]}
        hidden.append(alias[0])

    def wrapped(*refs):
        body(*refs[:number], *refs[number + len(hidden) :])

    return pl.pallas_call(
        wrapped,
        grid=(images,),
        in_specs=[spec for _, spec in inputs] + [pl.BlockSpec(memory_space=pl.ANY)] * len(hidden),
        out_specs=[spec for _, _, spec in outputs],
        out_shape=[jax.ShapeDtypeStruct(shape, dtype) for shape, dtype, _ in outputs],
        scratch_shapes=scratch,
        input_output_aliases=aliases,
        compiler_params=pltpu.CompilerParams(vmem_limit_bytes=VMEM_LIMIT),
        cost_estimate=pl.CostEstimate(
            flops=int(micros * 1e9), bytes_accessed=int(micros * 1e6), transcendentals=0
        ),
    )(*[operand for operand, _ in inputs], *hidden)


def adam_update(weight, first_old, second_old, grad_value, rate_value, decay_value):
    new_first = BETA_ONE * first_old + (1.0 - BETA_ONE) * grad_value
    new_second = BETA_TWO * second_old + (1.0 - BETA_TWO) * grad_value * grad_value
    first_hat = new_first / (1.0 - BETA_ONE**STEP)
    second_hat = new_second / (1.0 - BETA_TWO**STEP)
    new_weight = weight - rate_value * (
        first_hat / (jnp.sqrt(second_hat) + ADAM_EPS) + decay_value * weight
    )
    return (new_first, new_second, new_weight)


def swap(value, axis, distance):
    return lax.ppermute(value, axis, [(place, place ^ distance) for place in range(lax.axis_size(axis))])


def exchange(pieces):
    return [pieces[0]] + [swap(pieces[d], "seq", d) for d in range(1, len(pieces))]


def tree_sum(values):
    while len(values) > 1:
        values = [values[i] + values[i + 1] for i in range(0, len(values), 2)]
    return values[0]


def sum_chips(value):
    return tree_sum([value] + [swap(value, "img", d) for d in range(2, lax.axis_size("img"), 2)])


def sum_cores(value):
    return value + swap(value, "img", 1)


def sum_halves(value):
    core = lax.axis_index("img") % 2
    rows = value.shape[0] // 2
    mine = lax.dynamic_slice_in_dim(value, core * rows, rows, 0)
    other = lax.dynamic_slice_in_dim(value, (1 - core) * rows, rows, 0)
    stages = [mine + swap(other, "img", 1)]
    distance = 2
    while distance < lax.axis_size("img"):
        stages.append(stages[-1] + swap(stages[-1], "img", distance))
        distance *= 2
    return stages


def join_halves(mine):
    other = swap(mine, "img", 1)
    lower = lax.axis_index("img") % 2 == 0
    return jnp.concatenate([jnp.where(lower, mine, other), jnp.where(lower, other, mine)], axis=0)


def on_device(
    images,
    cotangent,
    valid_mask,
    qkv_weight,
    out_weight,
    expand_weight,
    shrink_weight,
    small_params,
    expand_bias,
    first_qkv,
    first_out,
    first_expand,
    first_shrink,
    first_small,
    first_bias,
    second_qkv,
    second_out,
    second_expand,
    second_shrink,
    second_small,
    second_bias,
):
    ways = lax.axis_size("seq")
    owner = lax.axis_index("seq")
    me = owner.astype(jnp.int32).reshape(1)
    count, rows, width, channels = images.shape
    tokens = rows * width
    height = rows * ways
    wide = width // STRIPE * GROUP
    wide_part = wide // ways
    kept = -(-VALID // 16) * 16
    key_rows = -(-rows * kept // 256) * 256
    window_tokens = height * GROUP
    spare = -window_tokens % 128
    shard = qkv_weight.shape[0]
    hidden_width = expand_weight.shape[1]
    blocks = hidden_width // channels
    chunk = width
    pair = count // 2
    halves = (0, pair)

    small_pack = jnp.concatenate(
        [small_params, jnp.pad(expand_bias[None], ((0, small_params.shape[0] - 1), (0, 0)))], axis=1
    )
    small_pack = jnp.pad(small_pack, ((0, 0), (0, qkv_weight.shape[1] - small_pack.shape[1])))
    early = jnp.concatenate([qkv_weight, small_pack], axis=0).astype(BF)
    early_pieces = exchange([early] * ways)
    shrink_blocks = [shrink_weight[block * shard : (block + 1) * shard] for block in range(blocks)]
    late = jnp.concatenate([out_weight, expand_weight, *shrink_blocks], axis=1).astype(BF)

    x = images.reshape(count, tokens, channels)
    cot = cotangent.reshape(count, tokens, channels)
    me_in = (me, scalar_block())
    mask_in = (valid_mask, whole_block(*valid_mask.shape))
    piece_in = (rows, wide_part, channels)
    piece_out = (rows, wide_part, HALF)
    qkv_shape = (channels, 6 * HALF)

    def per_image(array, first=0):
        return (array, image_block(*array.shape[1:], first=first))

    def whole(array):
        return (array, whole_block(*array.shape))

    def new_image(dims, dtype, images=pair):
        return ((images,) + dims, dtype, image_block(*dims))

    def new_whole(dims, dtype):
        return (dims, dtype, whole_block(*dims))

    results = run_kernel(
        functools.partial(project_kernel, (rows, width, wide, wide_part), ways),
        count,
        [me_in, per_image(x)] + [whole(piece) for piece in early_pieces],
        [new_image((tokens, 3 * HALF), BF, count), new_image((tokens, channels), BF, count)]
        + [new_image(piece_in, BF, count)] * ways
        + [new_whole(qkv_shape, BF), new_whole((16, channels), F32), new_whole((1, hidden_width), F32)],
        [pltpu.VMEM((rows, wide, channels), BF)],
        12,
    )
    across_mixed, normed = results[:2]
    normed_pieces = exchange(results[2 : 2 + ways])
    qkv_low, small_full, bias_full = results[2 + ways :]
    late_pieces = exchange([late] * ways)
    small_in, qkv_in = whole(small_full), whole(qkv_low)

    attention_dims = (rows, width, kept, key_rows, chunk)
    key_shape = (key_rows, 2 * HALF)
    joined_across, attended, log_total, keys, values = run_kernel(
        functools.partial(across_kernel, attention_dims),
        count,
        [per_image(across_mixed), mask_in, small_in],
        [
            new_image((tokens, HALF), BF, count),
            new_image((tokens, HALF), F32, count),
            new_image((tokens, HALF), F32, count),
            new_image(key_shape, BF, count),
            new_image(key_shape, BF, count),
        ],
        [pltpu.VMEM((tokens, HALF), F32)],
        60,
    )
    last_result = attended

    down_dims = (height, width, wide, wide_part, spare)
    grid_f32 = (height, wide_part, HALF)
    mixed_grid = (height, wide_part, 3 * HALF)
    normed_grid = (height, wide_part, channels)
    down, joined_pieces = [], []
    for index, first in enumerate(halves):
        results = run_kernel(
            functools.partial(down_kernel, down_dims, ways, first),
            pair,
            [me_in, mask_in, small_in, qkv_in] + [per_image(piece, first) for piece in normed_pieces],
            [new_image(piece_out, BF)] * ways
            + [new_image(grid_f32, F32)] * 2
            + [new_image(mixed_grid, BF)],
            [
                pltpu.VMEM(normed_grid, BF),
                pltpu.VMEM(mixed_grid, F32),
                pltpu.VMEM(grid_f32, F32),
                pltpu.VMEM((wide, HALF), F32),
                pltpu.VMEM((window_tokens, HALF), F32),
            ],
            18,
            after=(last_result,),
        )
        down.append(results[ways:])
        joined_pieces.append(exchange(results[:ways]))
        last_result = results[ways]

    block_out = None
    grad_middle, grad_across, grad_pieces = [], [], []
    sums = None
    matrix_sums = [(channels, channels), (channels, hidden_width), (channels, hidden_width)]
    late_shape = late.shape
    for index, first in enumerate(halves):
        last = index == 1
        results = run_kernel(
            functools.partial(
                middle_kernel, (rows, width, wide, wide_part, tokens // 2, channels), ways, last
            ),
            pair,
            [
                me_in,
                (x, image_block(tokens, channels, first=first)),
                (cot, image_block(tokens, channels, first=first)),
                per_image(joined_across, first),
            ]
            + [per_image(piece) for piece in joined_pieces[index]]
            + [whole(piece) for piece in late_pieces]
            + [small_in, whole(bias_full)]
            + ([whole(entry) for entry in sums] if last else []),
            [
                (x.shape, F32, image_block(tokens, channels, first=first)),
                new_image((tokens, channels), F32),
                new_image((tokens, HALF), BF),
            ]
            + [new_image(piece_out, BF)] * ways
            + [new_whole((8, hidden_width), F32), new_whole((32, channels), F32)]
            + (
                [new_whole(late_shape, F32)] * ways
                if last
                else [new_whole(dims, F32) for dims in matrix_sums]
            ),
            ([pltpu.VMEM(dims, F32) for dims in matrix_sums] if last else [])
            + [
                pltpu.VMEM((channels, channels), BF),
                pltpu.VMEM((channels, hidden_width), BF),
                pltpu.VMEM((hidden_width, channels), BF),
                pltpu.VMEM((rows, wide, HALF), BF),
                pltpu.VMEM((tokens, channels), BF),
                pltpu.VMEM((tokens, channels), BF),
                pltpu.VMEM((tokens, hidden_width), BF),
                pltpu.VMEM((tokens, hidden_width), BF),
                pltpu.VMEM((tokens, channels), BF),
                pltpu.VMEM((tokens, HALF), BF),
                pltpu.VMEM((rows, wide, HALF), BF),
            ]
            + ([pltpu.VMEM((hidden_width, channels), F32)] if last else []),
            35,
            after=(last_result,),
            alias=(block_out, 0) if last else None,
        )
        block_out = results[0]
        grad_middle.append(results[1])
        grad_across.append(results[2])
        grad_pieces.append(exchange(results[3 : 3 + ways]))
        sums = results[3 + ways :]
        last_result = results[1]
    bias_sums, middle_sums = sums[:2]
    late_seq = tree_sum(exchange(sums[2:]))
    late_stages = [late_seq] + sum_halves(late_seq)

    grad_normed_pieces = []
    sums = None
    qkv_half = (channels, 3 * HALF)
    half_shard = (shard, 3 * HALF)
    for index, first in enumerate(halves):
        last = index == 1
        results = run_kernel(
            functools.partial(down_back_kernel, down_dims, ways, first, last),
            pair,
            [me_in, mask_in, small_in, qkv_in]
            + [per_image(entry) for entry in down[index]]
            + [per_image(piece, first) for piece in normed_pieces]
            + [per_image(piece) for piece in grad_pieces[index]]
            + ([whole(entry) for entry in sums] if last else []),
            [new_image(piece_in, BF)] * ways
            + [new_whole((80, HALF), F32)]
            + ([new_whole(half_shard, F32)] * ways if last else [new_whole(qkv_half, F32)]),
            ([pltpu.VMEM(qkv_half, F32)] if last else [])
            + [
                pltpu.VMEM(normed_grid, BF),
                pltpu.VMEM(mixed_grid, F32),
                pltpu.VMEM(grid_f32, F32),
                pltpu.VMEM(mixed_grid, F32),
                pltpu.VMEM(normed_grid, BF),
                pltpu.VMEM((wide, HALF), F32),
            ],
            28,
            after=(last_result, late_stages[0]) if last else (last_result,),
        )
        grad_normed_pieces.append(exchange(results[:ways]))
        sums = results[ways:]
        last_result = sums[0]
    down_taps = sums[0]
    down_seq = tree_sum(exchange(sums[1:]))
    down_core = sum_cores(down_seq)

    across_mixed_grad = []
    sums = None
    for index, first in enumerate(halves):
        last = index == 1
        results = run_kernel(
            functools.partial(across_back_kernel, attention_dims, ways, first, last),
            pair,
            [
                me_in,
                per_image(across_mixed, first),
                per_image(grad_across[index]),
                per_image(attended, first),
                per_image(log_total, first),
                per_image(keys, first),
                per_image(values, first),
                per_image(normed, first),
                mask_in,
                small_in,
            ]
            + ([whole(entry) for entry in sums] if last else []),
            [new_image((tokens, 3 * HALF), BF), new_whole((80, HALF), F32)]
            + ([new_whole(half_shard, F32)] * ways if last else [new_whole(qkv_half, F32)]),
            ([pltpu.VMEM(qkv_half, F32)] if last else [])
            + [
                pltpu.VMEM((HALF, key_rows), F32),
                pltpu.VMEM((HALF, key_rows), F32),
                pltpu.VMEM((tokens, HALF), F32),
            ],
            45,
            after=(last_result, late_stages[2], down_seq) if last else (last_result, late_stages[1]),
        )
        across_mixed_grad.append(results[0])
        sums = results[1:]
        last_result = sums[0]
    across_taps = sums[0]
    across_seq = tree_sum(exchange(sums[1:]))
    across_core = sum_cores(across_seq)

    input_grad = None
    sums = None
    for index, first in enumerate(halves):
        last = index == 1
        results = run_kernel(
            functools.partial(final_kernel, (rows, width, wide, wide_part, tokens), ways, last),
            pair,
            [
                me_in,
                (x, image_block(tokens, channels, first=first)),
                per_image(grad_middle[index]),
                per_image(across_mixed_grad[index]),
            ]
            + [per_image(piece) for piece in grad_normed_pieces[index]]
            + [small_in, qkv_in]
            + (
                [whole(entry) for entry in (*sums, across_taps, down_taps, middle_sums, bias_sums)]
                if last
                else []
            ),
            [
                (x.shape, F32, image_block(tokens, channels, first=first)),
                new_whole((16, channels), F32),
            ]
            + ([new_whole((24, channels), F32)] if last else []),
            [pltpu.VMEM((rows, wide, channels), BF), pltpu.VMEM((tokens, channels), F32)],
            8,
            after=(last_result, across_seq) if last else (last_result, late_stages[-1], down_core),
            alias=(input_grad, 0) if last else None,
        )
        input_grad = results[0]
        sums = results[1:]
        last_result = sums[0]
    small_sum = tree_sum(exchange([results[2]] * ways))
    small_sum = sum_chips(sum_cores(small_sum))
    shard_late = join_halves(late_stages[-1])
    shard_down, shard_across = sum_chips(down_core), sum_chips(across_core)

    squared = sum(jnp.sum(entry * entry) for entry in (shard_late, shard_down, shard_across))
    squared = tree_sum(exchange([jnp.full((8, 128), squared)] * ways))[0, 0]
    grad_norm = jnp.sqrt(squared + jnp.sum(small_sum * small_sum))
    factor = CLIP_NORM / jnp.maximum(grad_norm, CLIP_NORM)
    matrices = (
        (qkv_weight, out_weight, expand_weight, shrink_weight)
        + (first_qkv, first_out, first_expand, first_shrink)
        + (second_qkv, second_out, second_expand, second_shrink)
    )
    updated = run_kernel(
        functools.partial(update_kernel, blocks),
        1,
        [(factor.reshape(1), scalar_block())]
        + [whole(entry) for entry in (shard_late, shard_across, shard_down, *matrices)],
        [new_whole(entry.shape, F32) for entry in matrices[:4]] * 3,
        [],
        4,
    )
    small_rows = small_params.shape[0]
    small_grad = lax.dynamic_slice_in_dim(
        small_sum[:small_rows], owner * small_params.shape[1], small_params.shape[1], 1
    )
    bias_grad = lax.dynamic_slice_in_dim(
        small_sum[small_rows : small_rows + blocks].reshape(-1),
        owner * expand_bias.shape[0],
        expand_bias.shape[0],
        0,
    )
    small_new = adam_update(
        small_params, first_small, second_small, small_grad * factor, RATE_SMALL, 0.0
    )
    bias_new = adam_update(expand_bias, first_bias, second_bias, bias_grad * factor, RATE_MATRIX, 0.0)
    outputs = []
    for part in range(3):
        outputs += [*updated[4 * part : 4 * part + 4], small_new[part], bias_new[part]]
    return (
        block_out.reshape(images.shape),
        input_grad.reshape(images.shape),
        grad_norm,
        *outputs,
    )


def solution(mesh):
    sharded = (
        P("seq", None),
        P("seq", None),
        P("seq", None),
        P("seq", None),
        P(None, "seq"),
        P("seq"),
    )
    grid = P("img", "seq", None, None)
    return jax.shard_map(
        on_device,
        mesh=mesh,
        in_specs=(grid, grid, P("img", None)) + sharded * 3,
        out_specs=(grid, grid, P()) + sharded * 3,
        check_vma=False,
    )
```

```python
import functools

import jax
import jax.numpy as jnp
from jax import lax
from jax.experimental import pallas as pl
from jax.experimental.pallas import tpu as pltpu
from jax.sharding import PartitionSpec as P

HEADS = 8
STRIPE = 7
STEP = 10
VALID = 168

EPS_NORM = 1e-05
BETA_ONE = 0.9
BETA_TWO = 0.999
ADAM_EPS = 1e-08
WEIGHT_DECAY = 0.05
CLIP_NORM = 1.0
RATE_MATRIX = 0.1
RATE_OUTPUT = 0.5
RATE_SMALL = 0.3
INV_ROOT_TWO = 0.7071067811865476
INV_ROOT_TAU = 0.3989422804014327
LOG2E = 1.4426950408889634

BF = jnp.bfloat16
F32 = jnp.float32
HALF = 128
BRANCH_HEADS = 4
HEAD_DIM = 32
SCALE = HEAD_DIM**-0.5
GROUP = 8
MASKED = -1e38
EXPONENT_SCALE = SCALE * LOG2E
EXPONENT_BOUND = 60.0
VMEM_LIMIT = 60 * 2**20


def dot(left, right):
    return jnp.dot(left, right, preferred_element_type=F32)


def dot_nt(left, right):
    return lax.dot_general(left, right, (((1,), (1,)), ((), ())), preferred_element_type=F32)


def dot_tn(left, right):
    return lax.dot_general(left, right, (((0,), (0,)), ((), ())), preferred_element_type=F32)


def iota(shape, dim):
    return lax.broadcasted_iota(jnp.int32, shape, dim)


def one_hot(condition):
    return jnp.where(condition, 1.0, 0.0).astype(BF)


def expand_condition(wide, width):
    e, c = iota((wide, width), 0), iota((wide, width), 1)
    return ((e & 7) < STRIPE) & (c == STRIPE * (e >> 3) + (e & 7))


def contract_matrix(width, wide):
    c, e = iota((width, wide), 0), iota((width, wide), 1)
    return one_hot(((e & 7) < STRIPE) & (c == STRIPE * (e >> 3) + (e & 7)))


def normalize(values, gain_row, offset_row):
    center = values - jnp.mean(values, axis=-1, keepdims=True)
    spread = jnp.mean(center * center, axis=-1, keepdims=True)
    recip = lax.rsqrt(spread + EPS_NORM)
    scaled = center * recip
    return scaled * gain_row + offset_row, scaled, recip


def normalize_back(grad_out, scaled, recip, gain_row):
    grad_scaled = grad_out * gain_row
    inner_one = jnp.mean(grad_scaled, axis=-1, keepdims=True)
    inner_two = jnp.mean(grad_scaled * scaled, axis=-1, keepdims=True)
    return recip * (grad_scaled - inner_one - scaled * inner_two)


def fold_rows(values):
    rows, columns = values.shape
    return jnp.sum(values.reshape(rows // 8, 8, columns), axis=0)


def pieces_of(values):
    first = values.astype(BF).astype(F32)
    rest = values - first
    second = rest.astype(BF).astype(F32)
    return first, second, (rest - second).astype(BF).astype(F32)


def lane_head(rows):
    return (iota((rows, HALF), 1) >> 5) & 3


def lane_sub(rows):
    return iota((rows, HALF), 1) & 31


def piece_lanes(values, fourth):
    one, two, three = pieces_of(values)
    sub = lane_sub(values.shape[0])
    return jnp.where(
        sub == 0, one, jnp.where(sub == 1, two, jnp.where(sub == 2, three, jnp.where(sub == 3, fourth, 0.0)))
    )


def wide_keys(keys, bias):
    sub = lane_sub(keys.shape[0])
    extra = jnp.where(sub < 3, 1.0, jnp.where(sub == 3, bias, 0.0))
    return jnp.concatenate([keys.astype(BF), extra.astype(BF)], axis=1)


def wide_values(values):
    return jnp.concatenate([values.astype(BF), jnp.ones(values.shape, BF)], axis=1)


def stack_heads(left, right):
    head_of = lane_head(left.shape[0])
    parts = []
    for head in range(BRANCH_HEADS):
        mine = head_of == head
        parts.append(
            jnp.concatenate(
                [jnp.where(mine, left, 0.0).astype(BF), jnp.where(mine, right, 0.0).astype(BF)], axis=1
            )
        )
    return jnp.concatenate(parts, axis=0)


def pick_heads(stacked, rows):
    head_of = lane_head(rows)
    picked = stacked[:rows]
    for head in range(1, BRANCH_HEADS):
        picked = jnp.where(head_of == head, stacked[head * rows : (head + 1) * rows], picked)
    return picked


def head_norms(values):
    block = one_hot((iota((HALF, HALF), 0) >> 5) == (iota((HALF, HALF), 1) >> 5))
    sums = dot((values * values * 1.02).astype(BF), block)
    return jnp.max(sums, axis=0, keepdims=True)


def exceeds(query_norms, key_norms):
    bound = jnp.max(query_norms * key_norms)
    return jnp.logical_not(bound <= EXPONENT_BOUND * EXPONENT_BOUND)


def stack_queries(queries, shift):
    return stack_heads(queries, piece_lanes(shift * (-1.0 / EXPONENT_SCALE), 1.0))


def attend_heads(queries, shift, keys, values):
    rows = queries.shape[0]
    scores = dot_nt(stack_queries(queries, shift), keys)
    weights = jnp.exp2(scores * EXPONENT_SCALE).astype(BF)
    result = dot(weights, values)
    totals = pick_heads(result[:, HALF:], rows)
    return pick_heads(result[:, :HALF], rows) / totals, jnp.log(totals) * LOG2E + shift


def highest_scores(queries, keys):
    rows = queries.shape[0]
    scores = dot_nt(stack_queries(queries, jnp.zeros((rows, HALF), F32)), keys)
    highest = jnp.max(scores, axis=-1, keepdims=True) * EXPONENT_SCALE
    return pick_heads(jnp.broadcast_to(highest, (BRANCH_HEADS * rows, HALF)), rows)


def attend_heads_back(queries, grad, attended, log_total, keys, values):
    rows = queries.shape[0]
    eye = one_hot(iota((HALF, HALF), 0) == iota((HALF, HALF), 1))
    query_turned = dot_nt(eye, queries.astype(BF)).astype(BF)
    grad_turned = dot_nt(eye, grad.astype(BF)).astype(BF)
    block = one_hot((iota((HALF, HALF), 0) >> 5) == (iota((HALF, HALF), 1) >> 5))
    inner = sum(dot(piece.astype(BF), block) for piece in pieces_of(grad * attended))
    weights = jnp.exp2(dot_nt(stack_queries(queries, log_total), keys) * EXPONENT_SCALE)
    weights_low = weights.astype(BF)
    grad_weights = dot_nt(stack_heads(grad, piece_lanes(-inner, 0.0)), values)
    grad_scores = (weights * grad_weights).astype(BF)
    grad_queries = pick_heads(dot(grad_scores, keys[:, :HALF]), rows) * SCALE
    grad_keys, grad_values = [], []
    for head in range(BRANCH_HEADS):
        lanes = slice(head * HEAD_DIM, (head + 1) * HEAD_DIM)
        span = slice(head * rows, (head + 1) * rows)
        grad_values.append(dot(grad_turned[lanes], weights_low[span]))
        grad_keys.append(dot(query_turned[lanes], grad_scores[span]))
    return grad_queries, grad_keys, grad_values


def shift_down(values):
    rows = values.shape[0]
    return jnp.where(iota(values.shape, 0) == 0, 0.0, pltpu.roll(values, 1, 0))


def shift_up(values):
    rows = values.shape[0]
    return jnp.where(iota(values.shape, 0) == rows - 1, 0.0, pltpu.roll(values, rows - 1, 0))


def start_sums(sums, starts):
    @pl.when(pl.program_id(0) == 0)
    def _():
        for index, total in enumerate(sums):
            if starts:
                total[...] = starts[index][...]
            else:
                total[...] = jnp.zeros_like(total)


def at_last_step(body):
    pl.when(pl.program_id(0) == pl.num_programs(0) - 1)(body)


def pack_early_kernel(qkv_ref, small_ref, bias_ref, early_ref):
    shard, small_lanes = qkv_ref.shape[0], small_ref.shape[1]
    bias_lanes = bias_ref.shape[1]
    early_ref[:shard] = qkv_ref[...].astype(BF)
    spare = early_ref.shape[1] - small_lanes - bias_lanes
    bias = jnp.concatenate([bias_ref[...], jnp.zeros((small_ref.shape[0] - 1, bias_lanes), F32)], axis=0)
    early_ref[shard:] = jnp.concatenate(
        [small_ref[...], bias, jnp.zeros((small_ref.shape[0], spare), F32)], axis=1
    ).astype(BF)


def pack_late_kernel(out_ref, expand_ref, shrink_ref, late_ref):
    shard, channels = out_ref.shape
    begin = channels + expand_ref.shape[1]
    late_ref[:, :channels] = out_ref[...].astype(BF)
    late_ref[:, channels:begin] = expand_ref[...].astype(BF)
    for block in range(shrink_ref.shape[0] // shard):
        lanes = slice(begin + block * channels, begin + (block + 1) * channels)
        late_ref[:, lanes] = shrink_ref[block * shard : (block + 1) * shard].astype(BF)


def project_kernel(dims, ways, assembles, *refs):
    rows, width, wide, wide_part = dims
    me_ref, x_ref = refs[:2]
    if assembles:
        pieces = refs[2 : 2 + ways]
        across_ref, normed_ref = refs[2 + ways : 4 + ways]
        down_refs = refs[4 + ways : 4 + 2 * ways]
        weight_ref, small_ref, bias_ref, spread_ref = refs[4 + 2 * ways :]

        @pl.when(pl.program_id(0) == 0)
        def _():
            channels, hidden_width = small_ref.shape[1], bias_ref.shape[1]
            shard = channels // ways
            bias_shard = hidden_width // ways
            lanes = -(-(shard + bias_shard) // 128) * 128
            lane, column = iota((lanes, channels + hidden_width), 0), iota((lanes, channels + hidden_width), 1)
            total = jnp.zeros((16, channels + hidden_width), F32)
            for distance, piece in enumerate(pieces):
                place = me_ref[0] ^ distance
                weight_ref[pl.ds(pl.multiple_of(place * shard, shard), shard)] = piece[:shard]
                target = jnp.where(
                    lane < shard,
                    lane + shard * place,
                    channels + lane - shard + bias_shard * place,
                )
                chosen = one_hot((column == target) & (lane < shard + bias_shard))
                total = total + dot(piece[shard : shard + 16, :lanes], chosen)
            small_ref[...] = total[:, :channels]
            bias_ref[...] = total[0:1, channels:]

    else:
        weight_ref, small_ref, across_ref, normed_ref = refs[2:6]
        down_refs = refs[6 : 6 + ways]
        spread_ref = refs[6 + ways]
    gain, offset = small_ref[9:10], small_ref[10:11]
    expand = one_hot(expand_condition(wide, width))
    for row in range(rows):
        span = slice(row * width, (row + 1) * width)
        normed, _, _ = normalize(x_ref[0, span].astype(F32), gain, offset)
        normed = normed.astype(BF)
        normed_ref[0, span] = normed
        across_ref[0, span] = dot(normed, weight_ref[:, : 3 * HALF]).astype(BF)
        spread_ref[row] = dot(expand, normed).astype(BF)
        for distance in range(ways):
            start = pl.multiple_of((me_ref[0] ^ distance) * wide_part, wide_part)
            down_refs[distance][0, row] = spread_ref[row, pl.ds(start, wide_part)]


def rank_row(mask_row, width):
    lower = one_hot(iota((width, width), 0) <= iota((width, width), 1))
    counted = dot(jnp.broadcast_to(mask_row, (8, width)).astype(BF), lower)[0:1]
    return jnp.where(mask_row > 0.0, counted - 1.0, -1.0)


def across_kernel(
    dims,
    first,
    across_ref,
    mask_ref,
    small_ref,
    joined_ref,
    attended_ref,
    total_ref,
    keys_ref,
    values_ref,
    shift_ref,
):
    rows, width, kept, key_rows, chunk = dims
    tokens = rows * width
    image = pl.program_id(0)
    ranks = rank_row(mask_ref[pl.ds(image + first, 1)].astype(F32), width)
    select = one_hot(iota((kept, width), 0).astype(F32) == ranks)
    bias = jnp.where(iota((kept, HALF), 0) >= VALID, MASKED, 0.0)
    key_norms = jnp.zeros((1, HALF), F32)
    for row in range(rows):
        picked = dot(select, across_ref[0, row * width : (row + 1) * width, HALF:])
        key_norms = jnp.maximum(key_norms, head_norms(picked[:, :HALF]))
        span = slice(row * kept, (row + 1) * kept)
        keys_ref[0, span] = wide_keys(picked[:, :HALF], bias)
        values_ref[0, span] = wide_values(picked[:, HALF:])
    spare = key_rows - rows * kept
    if spare:
        nothing = jnp.zeros((spare, HALF), F32)
        keys_ref[0, rows * kept :] = wide_keys(nothing, nothing + MASKED)
        values_ref[0, rows * kept :] = wide_values(nothing)

    query_norms = head_norms(across_ref[0, :, :HALF].astype(F32) * (SCALE * LOG2E))
    large = exceeds(query_norms, key_norms)

    @pl.when(image == 0)
    def _():
        shift_ref[...] = jnp.zeros_like(shift_ref)

    def rows_of(step):
        return pl.ds(pl.multiple_of(step * chunk, 16), chunk)

    @pl.when(large)
    def _():
        def highest(step, carry):
            span = rows_of(step)
            shift_ref[span] = highest_scores(across_ref[0, span, :HALF].astype(F32), keys_ref[0])
            return carry

        lax.fori_loop(0, tokens // chunk, highest, 0)

    def attend(step, carry):
        span = rows_of(step)
        attended, log_total = attend_heads(
            across_ref[0, span, :HALF].astype(F32), shift_ref[span], keys_ref[0], values_ref[0]
        )
        attended_ref[0, span] = attended
        total_ref[0, span] = log_total
        return carry

    lax.fori_loop(0, tokens // chunk, attend, 0, unroll=True)

    @pl.when(large)
    def _():
        shift_ref[...] = jnp.zeros_like(shift_ref)

    def value_row(row):
        return across_ref[0, row * width : (row + 1) * width, 2 * HALF :].astype(F32)

    for row in range(rows):
        sums = [jnp.zeros((width, HALF), F32) for _ in range(3)]
        for tap_row in range(3):
            source = row + tap_row - 1
            if 0 <= source < rows:
                values = value_row(source)
                for tap_col in range(3):
                    tap = 3 * tap_row + tap_col
                    sums[tap_col] = sums[tap_col] + values * small_ref[tap : tap + 1, :HALF]
        local = shift_down(sums[0]) + sums[1] + shift_up(sums[2]) + small_ref[11:12, :HALF]
        span = slice(row * width, (row + 1) * width)
        joined_ref[0, span] = (attended_ref[0, span] + local).astype(BF)


def assemble(me_ref, pieces, target_ref, dim, step):
    for distance, piece in enumerate(pieces):
        place = me_ref[0] ^ distance
        if dim == 0:
            target_ref[pl.ds(place * step, step)] = piece[0].astype(target_ref.dtype)
        else:
            target_ref[:, pl.ds(pl.multiple_of(place * step, step), step)] = piece[0].astype(
                target_ref.dtype
            )


def down_setup(me_ref, mask_ref, column_ref, width, wide, wide_part, first):
    image = pl.program_id(0) + first
    mask_row = mask_ref[pl.ds(image, 1)].astype(F32)
    valid = one_hot(expand_condition(wide, width) & (mask_row > 0.0))
    column_ref[...] = dot(valid, jnp.ones((width, HALF), BF))
    return pl.multiple_of(me_ref[0] * wide_part, GROUP)


def window_bias(column_ref, start, window, height):
    valid = column_ref[pl.ds(start + pl.multiple_of(window * GROUP, GROUP), GROUP)]
    bias = jnp.where(valid > 0.5, 0.0, MASKED)
    return jnp.broadcast_to(bias[None], (height, GROUP, HALF)).reshape(height * GROUP, HALF)


def pad_keys(block, spare, fill):
    if not spare:
        return block
    return jnp.concatenate([block, jnp.full((spare, HALF), 0.0, F32) + fill], axis=0)


def window_operands(keys, values, bias, spare):
    return (
        wide_keys(pad_keys(keys, spare, 0.0), pad_keys(bias, spare, MASKED)),
        wide_values(pad_keys(values, spare, 0.0)),
    )


def grid_shift(values, amount):
    return pltpu.roll(values, amount % GROUP, 1)


def grid_stack(values):
    edge = jnp.zeros((1,) + values.shape[1:], F32)
    return jnp.concatenate([edge, values, edge], axis=0)


def down_kernel(dims, ways, first, *refs):
    height, width, wide, wide_part, spare = dims
    me_ref, mask_ref, small_ref, weight_ref = refs[:4]
    pieces_in = refs[4 : 4 + ways]
    joined_refs = refs[4 + ways : 4 + 2 * ways]
    attended_ref, total_ref, saved_ref, normed_out, mixed_ref, joined_ref, column_ref, shift_ref = refs[
        4 + 2 * ways :
    ]
    normed_ref = normed_out.at[0]
    rows = height // ways
    start = down_setup(me_ref, mask_ref, column_ref, width, wide, wide_part, first)
    assemble(me_ref, pieces_in, normed_ref, 0, rows)
    tokens = height * GROUP
    windows = wide_part // GROUP
    normed = normed_ref[...].reshape(height * wide_part, 2 * HALF)
    mixed_low = dot(normed, weight_ref[:, 3 * HALF :]).astype(BF)
    mixed_low = mixed_low.reshape(height, wide_part, 3 * HALF)
    saved_ref[0] = mixed_low
    mixed_ref[...] = mixed_low.astype(F32)

    @pl.when(pl.program_id(0) == 0)
    def _():
        shift_ref[...] = jnp.zeros_like(shift_ref)

    everything = mixed_ref[...].reshape(height * wide_part, 3 * HALF)
    large = exceeds(
        head_norms(everything[:, :HALF] * (SCALE * LOG2E)), head_norms(everything[:, HALF : 2 * HALF])
    )

    def one_window(window, carry):
        span = pl.ds(pl.multiple_of(window * GROUP, GROUP), GROUP)
        grid = mixed_ref[:, span]
        flat = grid.reshape(tokens, 3 * HALF)
        queries, keys, values = (flat[:, part * HALF : (part + 1) * HALF] for part in range(3))
        bias = window_bias(column_ref, start, window, height)
        keys_in, values_in = window_operands(keys, values, bias, spare)

        @pl.when(large)
        def _():
            shift_ref[...] = highest_scores(queries, keys_in)

        attended, log_total = attend_heads(queries, shift_ref[...], keys_in, values_in)
        attended_ref[0, :, span] = attended.reshape(height, GROUP, HALF)
        total_ref[0, :, span] = log_total.reshape(height, GROUP, HALF)
        stacked = grid_stack(values.reshape(height, GROUP, HALF))
        sums = [jnp.zeros((height, GROUP, HALF), F32) for _ in range(3)]
        for tap_row in range(3):
            for tap_col in range(3):
                tap = 3 * tap_row + tap_col
                sums[tap_col] = sums[tap_col] + stacked[tap_row : tap_row + height] * small_ref[
                    tap : tap + 1, HALF:
                ].reshape(1, 1, HALF)
        local = grid_shift(sums[0], 1) + sums[1] + grid_shift(sums[2], -1)
        local = local + small_ref[11:12, HALF:].reshape(1, 1, HALF)
        joined_ref[:, span] = attended.reshape(height, GROUP, HALF) + local
        return carry

    lax.fori_loop(0, windows, one_window, 0, unroll=min(windows, 4))

    @pl.when(large)
    def _():
        shift_ref[...] = jnp.zeros_like(shift_ref)

    for distance in range(ways):
        place = me_ref[0] ^ distance
        joined_refs[distance][0] = joined_ref[pl.ds(place * rows, rows)].astype(BF)


def gelu_parts(hidden):
    upper = 0.5 + 0.5 * lax.erf(hidden * INV_ROOT_TWO)
    return upper, jnp.exp2(hidden * hidden * (-0.5 * LOG2E)) * INV_ROOT_TAU


def middle_kernel(dims, ways, *refs):
    rows, width, wide, wide_part, chunk, hidden_part = dims
    refs = list(refs)

    def take(number):
        taken = refs[:number]
        del refs[:number]
        return taken

    me_ref, x_ref, cot_ref, across_ref = take(4)
    pieces_in = [take(ways), take(ways)]
    weights_in = take(ways)
    small_ref, bias_ref = take(2)
    block_ref, middle_ref, grad_across_ref = take(3)
    grad_refs = take(ways)
    dbias_ref, dsmall_ref = take(2)
    piece_refs = take(ways)
    dout_ref, dexpand_ref, dshrink_ref = take(3)
    out_ref, expand_ref, shrink_ref = take(3)
    wide_ref, joined_ref, normed_ref, active_ref, hidden_ref, attended_ref, down_ref, gwide_ref = take(8)
    turned_ref = take(1)[0]
    tokens = rows * width
    hidden_width = expand_ref.shape[1]
    channels = 2 * HALF
    shard = channels // ways
    blocks = hidden_width // channels
    start_sums((dbias_ref, dsmall_ref, dout_ref, dexpand_ref, dshrink_ref), None)

    @pl.when(pl.program_id(0) == 0)
    def _():
        for distance, piece in enumerate(weights_in):
            place = me_ref[0] ^ distance
            span = pl.ds(pl.multiple_of(place * shard, shard), shard)
            out_ref[span] = piece[:, :channels]
            expand_ref[span] = piece[:, channels : channels + hidden_width]
            for block in range(blocks):
                begin = pl.multiple_of((place * blocks + block) * shard, shard)
                lanes = slice(channels + hidden_width + block * channels, channels + hidden_width + (block + 1) * channels)
                shrink_ref[pl.ds(begin, shard)] = piece[:, lanes]

    image, pair = pl.program_id(0), pl.num_programs(0) // 2

    @pl.when(image < pair)
    def _():
        assemble(me_ref, pieces_in[0], wide_ref, 1, wide_part)

    @pl.when(image >= pair)
    def _():
        assemble(me_ref, pieces_in[1], wide_ref, 1, wide_part)

    contract = contract_matrix(width, wide)
    for row in range(rows):
        span = slice(row * width, (row + 1) * width)
        joined_ref[span, :HALF] = across_ref[0, span]
        joined_ref[span, HALF:] = dot(contract, wide_ref[row]).astype(BF)

    def token_rows(step, carry):
        span = pl.ds(pl.multiple_of(step * chunk, 16), chunk)
        joined = joined_ref[span]
        attended_out = dot(joined, out_ref[...]) + small_ref[12:13]
        middle = x_ref[0, span].astype(F32) + attended_out
        normed, scaled, recip = normalize(middle, small_ref[13:14], small_ref[14:15])
        normed_low = normed.astype(BF)
        normed_ref[span] = normed_low
        back = cot_ref[0, span]
        result = middle + small_ref[15:16]
        grad_normed = jnp.zeros((chunk, 2 * HALF), F32)
        for part in range(0, hidden_width, hidden_part):
            lanes = slice(part, part + hidden_part)
            hidden = dot(normed_low, expand_ref[:, lanes]) + bias_ref[:, lanes]
            upper, density = gelu_parts(hidden)
            active = (hidden * upper).astype(BF)
            active_ref[span, lanes] = active
            result = result + dot(active, shrink_ref[lanes])
            grad_active = dot_nt(back, shrink_ref[lanes])
            grad_hidden = grad_active * (upper + hidden * density)
            grad_hidden = grad_hidden.astype(BF)
            hidden_ref[span, lanes] = grad_hidden
            dbias_ref[:, lanes] += fold_rows(grad_hidden.astype(F32))
            grad_normed = grad_normed + dot_nt(grad_hidden, expand_ref[:, lanes])
        block_ref[0, span] = result
        back_wide = back.astype(F32)
        grad_middle = back_wide + normalize_back(grad_normed, scaled, recip, small_ref[13:14])
        middle_ref[0, span] = grad_middle
        grad_attended = grad_middle.astype(BF)
        attended_ref[span] = grad_attended
        grad_joined = dot_nt(grad_attended, out_ref[...]).astype(BF)
        grad_across_ref[0, span] = grad_joined[:, :HALF]
        down_ref[span] = grad_joined[:, HALF:]
        dsmall_ref[0:8] += fold_rows(grad_attended.astype(F32))
        dsmall_ref[8:16] += fold_rows(grad_normed * scaled)
        dsmall_ref[16:24] += fold_rows(grad_normed)
        dsmall_ref[24:32] += fold_rows(back_wide)
        return carry

    lax.fori_loop(0, tokens // chunk, token_rows, 0, unroll=True)
    expand = one_hot(expand_condition(wide, width))
    for row in range(rows):
        gwide_ref[row] = dot(expand, down_ref[row * width : (row + 1) * width]).astype(BF)
    for distance in range(ways):
        place = me_ref[0] ^ distance
        grad_refs[distance][0] = gwide_ref[
            :, pl.ds(pl.multiple_of(place * wide_part, wide_part), wide_part)
        ]
    dout_ref[...] += dot_tn(joined_ref[...], attended_ref[...])
    dexpand_ref[...] += dot_tn(normed_ref[...], hidden_ref[...])
    dshrink_ref[...] += dot_tn(cot_ref[0], active_ref[...])

    @at_last_step
    def _():
        for block in range(blocks):
            lanes = slice(block * channels, (block + 1) * channels)
            turned_ref[lanes] = jnp.transpose(dshrink_ref[:, lanes])
        for distance, piece in enumerate(piece_refs):
            place = me_ref[0] ^ distance
            span = pl.ds(pl.multiple_of(place * shard, shard), shard)
            piece[:, :channels] = dout_ref[span]
            piece[:, channels : channels + hidden_width] = dexpand_ref[span]
            for block in range(blocks):
                begin = pl.multiple_of((place * blocks + block) * shard, shard)
                lanes = slice(channels + hidden_width + block * channels, channels + hidden_width + (block + 1) * channels)
                piece[:, lanes] = turned_ref[pl.ds(begin, shard)]


def shard_pieces(me_ref, piece_refs, total_ref):
    shard = piece_refs[0].shape[0]

    @at_last_step
    def _():
        for distance, piece in enumerate(piece_refs):
            begin = pl.multiple_of((me_ref[0] ^ distance) * shard, shard)
            piece[...] = total_ref[pl.ds(begin, shard)]


def across_back_kernel(dims, first, last, *refs):
    rows, width, kept, key_rows, chunk = dims
    refs = list(refs)

    def take(number):
        taken = refs[:number]
        del refs[:number]
        return taken

    across_ref, grad_ref, attended_ref, total_ref, keys_ref, values_ref, normed_ref = take(7)
    mask_ref, small_ref = take(2)
    starts = take(2) if last else None
    mixed_ref, taps_ref, dweight_ref, dkeys_ref, dvalues_ref, local_ref = take(6)
    tokens = rows * width
    image = pl.program_id(0) + first
    start_sums((taps_ref, dweight_ref), starts)
    dkeys_ref[...] = jnp.zeros_like(dkeys_ref)
    dvalues_ref[...] = jnp.zeros_like(dvalues_ref)

    def attend(step, carry):
        span = pl.ds(pl.multiple_of(step * chunk, 16), chunk)
        grad_queries, grad_keys, grad_values = attend_heads_back(
            across_ref[0, span, :HALF].astype(F32),
            grad_ref[0, span].astype(F32),
            attended_ref[0, span],
            total_ref[0, span],
            keys_ref[0],
            values_ref[0],
        )
        mixed_ref[0, span, :HALF] = grad_queries.astype(BF)
        for head in range(BRANCH_HEADS):
            lanes = slice(head * HEAD_DIM, (head + 1) * HEAD_DIM)
            dkeys_ref[lanes] += grad_keys[head]
            dvalues_ref[lanes] += grad_values[head]
        return carry

    lax.fori_loop(0, tokens // chunk, attend, 0)

    local_ref[...] = jnp.zeros_like(local_ref)
    for row in range(rows):
        grad = grad_ref[0, row * width : (row + 1) * width].astype(F32)
        taps_ref[72:80] += fold_rows(grad)
        for tap_col, moved in enumerate((shift_up(grad), grad, shift_down(grad))):
            for tap_row in range(3):
                target = row + tap_row - 1
                if 0 <= target < rows:
                    tap = 3 * tap_row + tap_col
                    span = slice(target * width, (target + 1) * width)
                    values = across_ref[0, span, 2 * HALF :].astype(F32)
                    taps_ref[8 * tap : 8 * tap + 8] += fold_rows(values * moved)
                    local_ref[span] += moved * small_ref[tap : tap + 1, :HALF]

    ranks = rank_row(mask_ref[pl.ds(image, 1)].astype(F32), width)
    place = jnp.transpose(jnp.broadcast_to(ranks, (HALF, width)))
    spread = one_hot(iota((width, HALF), 1).astype(F32) == place)
    spread_more = one_hot((iota((width, kept - HALF), 1) + HALF).astype(F32) == place[:, : kept - HALF])
    spread = jnp.concatenate([spread, spread_more], axis=1)
    grad_keys = jnp.transpose(dkeys_ref[...]) * SCALE
    grad_values = jnp.transpose(dvalues_ref[...])
    high = grad_values.astype(BF)
    low = (grad_values - high.astype(F32)).astype(BF)
    grad_keys = grad_keys.astype(BF)
    for row in range(rows):
        span = slice(row * kept, (row + 1) * kept)
        packed = jnp.concatenate([grad_keys[span], high[span], low[span]], axis=1)
        unpacked = dot(spread, packed)
        target = slice(row * width, (row + 1) * width)
        mixed_ref[0, target, HALF : 2 * HALF] = unpacked[:, :HALF].astype(BF)
        whole = unpacked[:, HALF : 2 * HALF] + unpacked[:, 2 * HALF :] + local_ref[target]
        mixed_ref[0, target, 2 * HALF :] = whole.astype(BF)
    dweight_ref[...] += dot_tn(normed_ref[0], mixed_ref[0])


def down_back_kernel(dims, ways, *refs):
    height, width, wide, wide_part, spare = dims
    refs = list(refs)

    def take(number):
        taken = refs[:number]
        del refs[:number]
        return taken

    me_ref, mask_ref, small_ref, weight_ref, attended_ref, total_ref, saved_ref, normed_ref = take(8)
    grads_in = take(ways)
    out_refs = take(ways)
    taps_ref = take(1)[0]
    piece_refs = take(ways)
    dweight_ref, mixed_ref, grad_ref, out_ref, turned_ref, column_ref = take(6)
    rows = height // ways
    start = down_setup(me_ref, mask_ref, column_ref, width, wide, wide_part, 0)
    assemble(me_ref, grads_in, grad_ref, 0, rows)
    mixed_ref[...] = saved_ref[0].astype(F32)
    tokens = height * GROUP
    windows = wide_part // GROUP
    start_sums((taps_ref, dweight_ref), None)

    def one_window(window, carry):
        span = pl.ds(pl.multiple_of(window * GROUP, GROUP), GROUP)
        flat = mixed_ref[:, span].reshape(tokens, 3 * HALF)
        queries, keys, values = (flat[:, part * HALF : (part + 1) * HALF] for part in range(3))
        grad_grid = grad_ref[:, span]
        grad = grad_grid.reshape(tokens, HALF)
        bias = window_bias(column_ref, start, window, height)
        keys_in, values_in = window_operands(keys, values, bias, spare)
        grad_queries, grad_keys, grad_values = attend_heads_back(
            queries,
            grad,
            attended_ref[0, :, span].reshape(tokens, HALF),
            total_ref[0, :, span].reshape(tokens, HALF),
            keys_in,
            values_in,
        )
        grad_keys = jnp.transpose(jnp.concatenate(grad_keys, axis=0))[:tokens] * SCALE
        grad_values = jnp.transpose(jnp.concatenate(grad_values, axis=0))[:tokens]
        values_grid = values.reshape(height, GROUP, HALF)
        local = jnp.zeros((height, GROUP, HALF), F32)
        taps_ref[72:80] += jnp.sum(grad_grid, axis=0)
        shifted = (grid_shift(grad_grid, -1), grad_grid, grid_shift(grad_grid, 1))
        for tap_col, moved in enumerate(shifted):
            stacked = grid_stack(moved)
            for tap_row in range(3):
                tap = 3 * tap_row + tap_col
                source = stacked[2 - tap_row : 2 - tap_row + height]
                taps_ref[8 * tap : 8 * tap + 8] += jnp.sum(source * values_grid, axis=0)
                local = local + source * small_ref[tap : tap + 1, HALF:].reshape(1, 1, HALF)
        shape = (height, GROUP, HALF)
        out_ref[:, span, :HALF] = grad_queries.reshape(shape)
        out_ref[:, span, HALF : 2 * HALF] = grad_keys.reshape(shape)
        out_ref[:, span, 2 * HALF :] = grad_values.reshape(shape) + local
        return carry

    lax.fori_loop(0, windows, one_window, 0, unroll=min(windows, 4))
    mixed_grad = out_ref[...].reshape(height * wide_part, 3 * HALF).astype(BF)
    grad_normed = dot_nt(mixed_grad, weight_ref[:, 3 * HALF :]).astype(BF)
    turned_ref[...] = grad_normed.reshape(height, wide_part, 2 * HALF)
    for distance in range(ways):
        place = me_ref[0] ^ distance
        out_refs[distance][0] = turned_ref[pl.ds(place * rows, rows)]
    normed = normed_ref[0].reshape(height * wide_part, 2 * HALF)
    dweight_ref[...] += dot_tn(normed, mixed_grad)
    shard_pieces(me_ref, piece_refs, dweight_ref)


def final_kernel(dims, ways, last, *refs):
    rows, width, wide, wide_part, chunk = dims
    refs = list(refs)

    def take(number):
        taken = refs[:number]
        del refs[:number]
        return taken

    me_ref, x_ref, middle_ref, across_ref = take(4)
    pieces_in = take(ways)
    small_ref, weight_ref = take(2)
    starts = take(1) if last else None
    others = take(5) if last else None
    grad_ref, dsmall_ref = take(2)
    piece_refs = take(ways) if last else None
    wide_ref, down_ref = take(2)
    whole_ref = take(1)[0] if last else None
    tokens = rows * width
    start_sums((dsmall_ref,), starts)
    assemble(me_ref, pieces_in, wide_ref, 1, wide_part)
    contract = contract_matrix(width, wide)
    for row in range(rows):
        down_ref[row * width : (row + 1) * width] = dot(contract, wide_ref[row])

    def token_rows(step, carry):
        span = pl.ds(pl.multiple_of(step * chunk, 16), chunk)
        _, scaled, recip = normalize(x_ref[0, span].astype(F32), small_ref[9:10], small_ref[10:11])
        grad_normed = dot_nt(across_ref[0, span], weight_ref[:, : 3 * HALF]) + down_ref[span]
        dsmall_ref[0:8] += fold_rows(grad_normed * scaled)
        dsmall_ref[8:16] += fold_rows(grad_normed)
        grad_ref[0, span] = middle_ref[0, span] + normalize_back(
            grad_normed, scaled, recip, small_ref[9:10]
        )
        return carry

    lax.fori_loop(0, tokens // chunk, token_rows, 0)
    if last:

        @at_last_step
        def _():
            across_taps, down_taps, middle_sums, bias_sums, dweight = others
            channels = 2 * HALF

            def total(ref, index):
                return jnp.sum(ref[8 * index : 8 * index + 8], axis=0, keepdims=True)

            def set_taps(row, index):
                whole_ref[row : row + 1, :HALF] = total(across_taps, index)
                whole_ref[row : row + 1, HALF:] = total(down_taps, index)

            whole_ref[...] = jnp.zeros_like(whole_ref)
            for tap in range(9):
                set_taps(tap, tap)
            whole_ref[9:10] = total(dsmall_ref, 0)
            whole_ref[10:11] = total(dsmall_ref, 1)
            set_taps(11, 9)
            for index in range(4):
                whole_ref[12 + index : 13 + index] = total(middle_sums, index)
            bias = total(bias_sums, 0)
            for block in range(bias.shape[1] // channels):
                whole_ref[16 + block : 17 + block] = bias[:, block * channels : (block + 1) * channels]
            shard = dweight.shape[0] // ways
            for distance, piece in enumerate(piece_refs):
                begin = pl.multiple_of((me_ref[0] ^ distance) * shard, shard)
                piece[:shard] = dweight[pl.ds(begin, shard)].astype(BF)
                piece[shard:, :channels] = whole_ref[...].astype(BF)
                piece[shard:, channels:] = jnp.zeros(
                    (whole_ref.shape[0], dweight.shape[1] - channels), BF
                )


def update_kernel(ways, place_ref, mine_ref, other_ref, tail_ref, *refs):
    squares, old, new = refs[:ways], refs[ways : ways + 18], refs[ways + 19 : ways + 37]
    norm_ref, joined_ref = refs[ways + 18], refs[ways + 37]
    me, core = place_ref[0], place_ref[1]
    half = mine_ref.shape[0]
    joined_ref[pl.ds(pl.multiple_of(core * half, half), half)] = mine_ref[...]
    joined_ref[pl.ds(pl.multiple_of((1 - core) * half, half), half)] = other_ref[...]
    shard = 2 * half
    rows, channels = old[1].shape
    hidden_width = old[2].shape[1]
    blocks = hidden_width // channels
    small = tail_ref[shard:, :channels]
    small_rows, small_lanes = old[4].shape
    bias_lanes = old[5].shape[1]
    total = tree_sum([entry[...] for entry in squares]) + jnp.sum(small * small)
    norm = jnp.sqrt(total)
    norm_ref[0, 0] = jnp.max(norm)
    factor = (CLIP_NORM / jnp.maximum(norm, CLIP_NORM))[0:1, 0:1]

    def update(index, grads, rate, decay, spans=(slice(None), slice(None))):
        weight, first, second = (old[part * 6 + index][spans] for part in range(3))
        results = adam_update(weight, first, second, grads * factor, rate, decay)
        for part in range(3):
            new[part * 6 + index][spans] = results[part]

    update(0, tail_ref[:shard], RATE_MATRIX, WEIGHT_DECAY, (slice(None), slice(0, 3 * HALF)))
    begin = channels + 2 * hidden_width
    update(
        0,
        joined_ref[:, begin : begin + 3 * HALF],
        RATE_MATRIX,
        WEIGHT_DECAY,
        (slice(None), slice(3 * HALF, 6 * HALF)),
    )
    update(1, joined_ref[:, :channels], RATE_OUTPUT, WEIGHT_DECAY)
    update(2, joined_ref[:, channels : channels + hidden_width], RATE_MATRIX, WEIGHT_DECAY)
    for block in range(blocks):
        begin = channels + hidden_width + block * channels
        update(
            3,
            joined_ref[:, begin : begin + channels],
            RATE_MATRIX,
            WEIGHT_DECAY,
            (slice(block * rows, (block + 1) * rows), slice(None)),
        )
    small_grad = jnp.zeros((small_rows, small_lanes), F32)
    bias_grad = jnp.zeros((1, bias_lanes), F32)
    for place in range(ways):
        lanes = slice(place * small_lanes, (place + 1) * small_lanes)
        small_grad = jnp.where(me == place, small[:small_rows, lanes], small_grad)
        row, lane = divmod(place * bias_lanes, channels)
        row = small_rows + row
        bias_grad = jnp.where(me == place, small[row : row + 1, lane : lane + bias_lanes], bias_grad)
    update(4, small_grad, RATE_SMALL, 0.0)
    update(5, bias_grad, RATE_MATRIX, 0.0)


def image_block(*shape, first=0):
    return pl.BlockSpec((1,) + shape, lambda image: (image + first,) + (0,) * len(shape))


def whole_block(*shape):
    return pl.BlockSpec(shape, lambda image: (0,) * len(shape))


def scalar_block():
    return pl.BlockSpec(memory_space=pltpu.SMEM)


def run_kernel(body, images, inputs, outputs, scratch, micros, after=(), alias=()):
    number, made = len(inputs), len(outputs)
    hidden = list(after)
    aliases = {}
    for operand, output in alias:
        aliases[number + len(hidden)] = output
        hidden.append(operand)
    skipped = number + len(hidden)

    def wrapped(*refs):
        refs[skipped + made][...] = jnp.zeros((8, 128), F32)
        body(*refs[:number], *refs[skipped : skipped + made], *refs[skipped + made + 1 :])

    outputs = list(outputs) + [((8, 128), F32, whole_block(8, 128))]
    *results, token = pl.pallas_call(
        wrapped,
        grid=(images,),
        in_specs=[spec for _, spec in inputs] + [pl.BlockSpec(memory_space=pl.ANY)] * len(hidden),
        out_specs=[spec for _, _, spec in outputs],
        out_shape=[jax.ShapeDtypeStruct(shape, dtype) for shape, dtype, _ in outputs],
        scratch_shapes=scratch,
        input_output_aliases=aliases,
        compiler_params=pltpu.CompilerParams(vmem_limit_bytes=VMEM_LIMIT),
        cost_estimate=pl.CostEstimate(
            flops=int(micros * 1e9), bytes_accessed=int(micros * 1e6), transcendentals=0
        ),
    )(*[operand for operand, _ in inputs], *hidden)
    return results, token


def adam_update(weight, first_old, second_old, grad_value, rate_value, decay_value):
    new_first = BETA_ONE * first_old + (1.0 - BETA_ONE) * grad_value
    new_second = BETA_TWO * second_old + (1.0 - BETA_TWO) * grad_value * grad_value
    first_hat = new_first / (1.0 - BETA_ONE**STEP)
    second_hat = new_second / (1.0 - BETA_TWO**STEP)
    new_weight = weight - rate_value * (
        first_hat / (jnp.sqrt(second_hat) + ADAM_EPS) + decay_value * weight
    )
    return (new_first, new_second, new_weight)


def swap(value, axis, distance):
    return lax.ppermute(value, axis, [(place, place ^ distance) for place in range(lax.axis_size(axis))])


def exchange(pieces):
    return [pieces[0]] + [swap(pieces[d], "seq", d) for d in range(1, len(pieces))]


def tree_sum(values):
    while len(values) > 1:
        values = [values[i] + values[i + 1] for i in range(0, len(values), 2)]
    return values[0]


def share_low(value, distances):
    rounded = lax.reduce_precision(value, 8, 7)
    sent = rounded.astype(BF)
    return [rounded] + [swap(sent, "img", distance).astype(F32) for distance in distances]


def on_device(
    images,
    cotangent,
    valid_mask,
    qkv_weight,
    out_weight,
    expand_weight,
    shrink_weight,
    small_params,
    expand_bias,
    first_qkv,
    first_out,
    first_expand,
    first_shrink,
    first_small,
    first_bias,
    second_qkv,
    second_out,
    second_expand,
    second_shrink,
    second_small,
    second_bias,
):
    ways = lax.axis_size("seq")
    owner = lax.axis_index("seq")
    me = owner.astype(jnp.int32).reshape(1)
    count, rows, width, channels = images.shape
    tokens = rows * width
    height = rows * ways
    wide = width // STRIPE * GROUP
    wide_part = wide // ways
    kept = -(-VALID // 16) * 16
    key_rows = -(-rows * kept // 256) * 256
    window_tokens = height * GROUP
    spare = -window_tokens % 128
    shard = qkv_weight.shape[0]
    hidden_width = expand_weight.shape[1]
    blocks = hidden_width // channels
    chunk = width
    pair = count // 2
    chip_steps = [2 << bit for bit in range((lax.axis_size("img") // 2).bit_length() - 1)][::-1]

    x = images.reshape(count, tokens, channels)
    cot = cotangent.reshape(count, tokens, channels)
    me_in = (me, scalar_block())
    mask_in = (valid_mask, whole_block(*valid_mask.shape))
    piece_in = (rows, wide_part, channels)
    piece_out = (rows, wide_part, HALF)
    qkv_shape = (channels, 6 * HALF)

    def per_image(array, first=0):
        return (array, image_block(*array.shape[1:], first=first))

    def whole(array):
        return (array, whole_block(*array.shape))

    def half_images(array, first):
        last = array.shape[0] - 1
        dims = (1,) + array.shape[1:]
        return (
            array,
            pl.BlockSpec(
                dims, lambda image: (jnp.clip(image - first, 0, last),) + (0,) * (len(dims) - 1)
            ),
        )

    def new_image(dims, dtype, images):
        return ((images,) + dims, dtype, image_block(*dims))

    def part_image(dims, dtype, first):
        return ((count,) + dims, dtype, image_block(*dims, first=first))

    def new_whole(dims, dtype):
        return (dims, dtype, whole_block(*dims))

    (early,), _ = run_kernel(
        pack_early_kernel,
        1,
        [whole(qkv_weight), whole(small_params), whole(expand_bias.reshape(1, -1))],
        [new_whole((shard + 16, qkv_weight.shape[1]), BF)],
        [],
        2,
    )
    weights_in = exchange([early] * ways)

    whole_images, normed_pieces, parameters = [], [], None
    for first in (0, pair):
        assembles = first == 0
        results, token = run_kernel(
            functools.partial(project_kernel, (rows, width, wide, wide_part), ways, assembles),
            pair,
            [me_in, per_image(x, first)] + [whole(entry) for entry in weights_in],
            [part_image((tokens, 3 * HALF), BF, first), part_image((tokens, channels), BF, first)]
            + [new_image(piece_in, BF, pair)] * ways
            + (
                [new_whole(qkv_shape, BF), new_whole((16, channels), F32), new_whole((1, hidden_width), F32)]
                if assembles
                else []
            ),
            [pltpu.VMEM((rows, wide, channels), BF)],
            6,
            alias=[(entry, place) for place, entry in enumerate(whole_images)],
        )
        whole_images = results[:2]
        normed_pieces.append(exchange(results[2 : 2 + ways]))
        if assembles:
            qkv_low, small_full, bias_full = results[2 + ways :]
            weights_in = (qkv_low, small_full)
    across_mixed, normed = whole_images
    small_in, qkv_in = whole(small_full), whole(qkv_low)

    attention_dims = (rows, width, kept, key_rows, chunk)
    key_shape = (key_rows, channels)
    across = []

    def run_across(first, images_in, after):
        return run_kernel(
            functools.partial(across_kernel, attention_dims, first),
            images_in,
            [per_image(across_mixed, first), mask_in, small_in],
            [
                part_image((tokens, HALF), BF, first),
                part_image((tokens, HALF), F32, first),
                part_image((tokens, HALF), F32, first),
                part_image(key_shape, BF, first),
                part_image(key_shape, BF, first),
            ],
            [pltpu.VMEM((tokens, HALF), F32)],
            11 * images_in,
            after=after,
            alias=[(entry, place) for place, entry in enumerate(across)],
        )

    across, token = run_across(0, count - 1, (token,))
    (late,), token = run_kernel(
        pack_late_kernel,
        1,
        [whole(out_weight), whole(expand_weight), whole(shrink_weight)],
        [new_whole((shard, channels + 2 * hidden_width), BF)],
        [],
        2,
        after=(token,),
    )
    late_pieces = exchange([late] * ways)
    normed_pieces, token = lax.optimization_barrier((normed_pieces, token))

    down_dims = (height, width, wide, wide_part, spare)
    grid_f32 = (height, wide_part, HALF)
    mixed_grid = (height, wide_part, 3 * HALF)
    normed_grid = (height, wide_part, channels)
    down, joined_pieces = [], []
    for index, first in enumerate((0, pair)):
        results, token = run_kernel(
            functools.partial(down_kernel, down_dims, ways, first),
            pair,
            [me_in, mask_in, small_in, qkv_in] + [per_image(piece) for piece in normed_pieces[index]],
            [new_image(piece_out, BF, pair)] * ways
            + [part_image(grid_f32, F32, first)] * 2
            + [part_image(mixed_grid, BF, first), part_image(normed_grid, BF, first)],
            [
                pltpu.VMEM(mixed_grid, F32),
                pltpu.VMEM(grid_f32, F32),
                pltpu.VMEM((wide, HALF), F32),
                pltpu.VMEM((window_tokens, HALF), F32),
            ],
            15,
            after=(token,),
            alias=[(entry, ways + place) for place, entry in enumerate(down)],
        )
        down = results[ways:]
        joined_pieces.append(exchange(results[:ways]))
    across, token = run_across(count - 1, 1, (token,))
    joined_across, attended, log_total, keys, values = across

    matrix_sums = [(channels, channels), (channels, hidden_width), (channels, hidden_width)]
    results, token = run_kernel(
        functools.partial(middle_kernel, (rows, width, wide, wide_part, tokens // 2, channels), ways),
        count,
        [me_in, per_image(x), per_image(cot), per_image(joined_across)]
        + [half_images(piece, 0) for piece in joined_pieces[0]]
        + [half_images(piece, pair) for piece in joined_pieces[1]]
        + [whole(piece) for piece in late_pieces]
        + [small_in, whole(bias_full)],
        [
            new_image((tokens, channels), F32, count),
            new_image((tokens, channels), F32, count),
            new_image((tokens, HALF), BF, count),
        ]
        + [new_image(piece_out, BF, count)] * ways
        + [new_whole((8, hidden_width), F32), new_whole((32, channels), F32)]
        + [new_whole(late.shape, F32)] * ways,
        [pltpu.VMEM(dims, F32) for dims in matrix_sums]
        + [
            pltpu.VMEM((channels, channels), BF),
            pltpu.VMEM((channels, hidden_width), BF),
            pltpu.VMEM((hidden_width, channels), BF),
            pltpu.VMEM((rows, wide, HALF), BF),
            pltpu.VMEM((tokens, channels), BF),
            pltpu.VMEM((tokens, channels), BF),
            pltpu.VMEM((tokens, hidden_width), BF),
            pltpu.VMEM((tokens, hidden_width), BF),
            pltpu.VMEM((tokens, channels), BF),
            pltpu.VMEM((tokens, HALF), BF),
            pltpu.VMEM((rows, wide, HALF), BF),
            pltpu.VMEM((hidden_width, channels), F32),
        ],
        45,
        after=(token,),
    )
    block_out, grad_middle, grad_across = results[:3]
    grad_pieces = exchange(results[3 : 3 + ways])
    bias_sums, middle_sums, *late_sums = results[3 + ways :]

    qkv_half = (channels, 3 * HALF)
    half_shard = (shard, 3 * HALF)
    back_sums, norm_sums, input_grad = None, None, None

    def run_across_back(first, images_in, sums, after):
        results, token = run_kernel(
            functools.partial(
                across_back_kernel, (rows, width, kept, key_rows, tokens // 2), first, sums is not None
            ),
            images_in,
            [
                per_image(across_mixed, first),
                per_image(grad_across, first),
                per_image(attended, first),
                per_image(log_total, first),
                per_image(keys, first),
                per_image(values, first),
                per_image(normed, first),
                mask_in,
                small_in,
            ]
            + ([whole(entry) for entry in sums[1:]] if sums else []),
            [
                part_image((tokens, 3 * HALF), BF, first),
                new_whole((80, HALF), F32),
                new_whole(qkv_half, F32),
            ],
            [
                pltpu.VMEM((HALF, key_rows), F32),
                pltpu.VMEM((HALF, key_rows), F32),
                pltpu.VMEM((tokens, HALF), F32),
            ],
            23 * images_in,
            after=after,
            alias=[(sums[0], 0)] if sums else [],
        )
        return results, token

    def run_final(first, images_in, starts, others, after):
        last = others is not None
        return run_kernel(
            functools.partial(final_kernel, (rows, width, wide, wide_part, tokens), ways, last),
            images_in,
            [me_in, per_image(x, first), per_image(grad_middle, first), per_image(back_sums[0], first)]
            + [per_image(piece, first) for piece in grad_normed_pieces]
            + [small_in, qkv_in]
            + ([whole(entry) for entry in (starts[1], *others)] if last else []),
            [part_image((tokens, channels), F32, first), new_whole((16, channels), F32)]
            + ([new_whole((shard + 32, 3 * HALF), BF)] * ways if last else []),
            [pltpu.VMEM((rows, wide, channels), BF), pltpu.VMEM((tokens, channels), F32)]
            + ([pltpu.VMEM((32, channels), F32)] if last else []),
            4 * images_in,
            after=after,
            alias=[(starts[0], 0)] if last else [],
        )

    back_sums, token = run_across_back(0, 1, None, (token,))
    *late_sums, token = lax.optimization_barrier((*late_sums, token))
    late_parts = exchange(late_sums)
    results, token = run_kernel(
        functools.partial(down_back_kernel, down_dims, ways),
        count,
        [me_in, mask_in, small_in, qkv_in]
        + [per_image(entry) for entry in down]
        + [per_image(piece) for piece in grad_pieces],
        [new_image(piece_in, BF, count)] * ways
        + [new_whole((80, HALF), F32)]
        + [new_whole(half_shard, F32)] * ways,
        [
            pltpu.VMEM(qkv_half, F32),
            pltpu.VMEM(mixed_grid, F32),
            pltpu.VMEM(grid_f32, F32),
            pltpu.VMEM(mixed_grid, F32),
            pltpu.VMEM(normed_grid, BF),
            pltpu.VMEM((wide, HALF), F32),
        ],
        38,
        after=(token,),
    )
    grad_normed_pieces = exchange(results[:ways])
    down_taps, *down_sums = results[ways:]
    late_parts, token = lax.optimization_barrier((late_parts, token))
    late_seq = tree_sum(late_parts)
    core_place = lax.axis_index("img") % 2
    half = shard // 2
    down_parts = exchange(down_sums)
    back_sums, token = run_across_back(1, count - 2, back_sums, (token, late_seq))
    down_parts, late_seq, token = lax.optimization_barrier((down_parts, late_seq, token))
    seq_sum = jnp.concatenate([late_seq, tree_sum(down_parts)], axis=1)
    kept_half = lax.dynamic_slice_in_dim(seq_sum, core_place * half, half, 0)
    core_half = swap(lax.dynamic_slice_in_dim(seq_sum, (1 - core_place) * half, half, 0), "img", 1)
    (input_grad, norm_sums), token = run_final(0, count - 1, None, None, (token,))
    kept_half, core_half, token = lax.optimization_barrier((kept_half, core_half, token))
    halves_sum = kept_half + core_half
    chip_half = swap(halves_sum, "img", chip_steps[0])
    back_sums, token = run_across_back(count - 1, 1, back_sums, (token,))
    chip_half, halves_sum, token = lax.optimization_barrier((chip_half, halves_sum, token))
    halves_sum = halves_sum + chip_half
    chip_half = [swap(halves_sum, "img", distance) for distance in chip_steps[1:2]]
    (input_grad, _, *tail_sums), token = run_final(
        count - 1,
        1,
        (input_grad, norm_sums),
        (back_sums[1], down_taps, middle_sums, bias_sums, back_sums[2]),
        (token,),
    )
    tail_parts, halves_sum, chip_half = lax.optimization_barrier(
        (exchange(tail_sums), halves_sum, chip_half)
    )
    halves_sum = tree_sum([halves_sum, *chip_half])
    for distance in chip_steps[2:]:
        halves_sum = halves_sum + swap(halves_sum, "img", distance)
    other_half = swap(halves_sum, "img", 1)
    tail = tree_sum([part.astype(F32) for part in tail_parts])
    tail = tree_sum(share_low(tail, [1]))
    tail = tree_sum(share_low(tail, range(2, lax.axis_size("img"), 2)))

    squared = (
        jnp.sum(halves_sum * halves_sum)
        + jnp.sum(other_half * other_half)
        + jnp.sum(tail[:shard] * tail[:shard])
    )
    squares = exchange([jnp.full((8, 128), squared)] * ways)

    def as_rows(entries):
        return [entry.reshape(1, -1) if entry.ndim == 1 else entry for entry in entries]

    state = as_rows(
        (qkv_weight, out_weight, expand_weight, shrink_weight, small_params, expand_bias)
        + (first_qkv, first_out, first_expand, first_shrink, first_small, first_bias)
        + (second_qkv, second_out, second_expand, second_shrink, second_small, second_bias)
    )
    place_in = jnp.stack([owner, core_place]).astype(jnp.int32)
    (norm, *updated), _ = run_kernel(
        functools.partial(update_kernel, ways),
        1,
        [(place_in, scalar_block())]
        + [whole(entry) for entry in (halves_sum, other_half, tail, *squares, *state)],
        [((1, 1), F32, scalar_block())] + [new_whole(entry.shape, F32) for entry in state[:6]] * 3,
        [pltpu.VMEM((shard, halves_sum.shape[1]), F32)],
        4,
    )
    for index in (5, 11, 17):
        updated[index] = updated[index].reshape(-1)
    return (
        block_out.reshape(images.shape),
        input_grad.reshape(images.shape),
        norm.reshape(()),
        *updated,
    )


def solution(mesh):
    sharded = (
        P("seq", None),
        P("seq", None),
        P("seq", None),
        P("seq", None),
        P(None, "seq"),
        P("seq"),
    )
    grid = P("img", "seq", None, None)
    return jax.shard_map(
        on_device,
        mesh=mesh,
        in_specs=(grid, grid, P("img", None)) + sharded * 3,
        out_specs=(grid, grid, P()) + sharded * 3,
        check_vma=False,
    )
```

```python
import functools

import jax
import jax.numpy as jnp
from jax import lax
from jax.experimental import pallas as pl
from jax.experimental.pallas import tpu as pltpu
from jax.sharding import PartitionSpec as P

HEADS = 8
STRIPE = 7
STEP = 10
VALID = 168

EPS_NORM = 1e-05
BETA_ONE = 0.9
BETA_TWO = 0.999
ADAM_EPS = 1e-08
WEIGHT_DECAY = 0.05
CLIP_NORM = 1.0
RATE_MATRIX = 0.1
RATE_OUTPUT = 0.5
RATE_SMALL = 0.3
INV_ROOT_TWO = 0.7071067811865476
INV_ROOT_TAU = 0.3989422804014327
LOG2E = 1.4426950408889634

BF = jnp.bfloat16
F32 = jnp.float32
HALF = 128
BRANCH_HEADS = 4
HEAD_DIM = 32
SCALE = HEAD_DIM**-0.5
GROUP = 8
MASKED = -1e38
EXPONENT_SCALE = SCALE * LOG2E
EXPONENT_BOUND = 60.0
VMEM_LIMIT = 60 * 2**20


def dot(left, right):
    return jnp.dot(left, right, preferred_element_type=F32)


def dot_nt(left, right):
    return lax.dot_general(left, right, (((1,), (1,)), ((), ())), preferred_element_type=F32)


def dot_tn(left, right):
    return lax.dot_general(left, right, (((0,), (0,)), ((), ())), preferred_element_type=F32)


def iota(shape, dim):
    return lax.broadcasted_iota(jnp.int32, shape, dim)


def one_hot(condition):
    return jnp.where(condition, 1.0, 0.0).astype(BF)


def expand_condition(wide, width):
    e, c = iota((wide, width), 0), iota((wide, width), 1)
    return ((e & 7) < STRIPE) & (c == STRIPE * (e >> 3) + (e & 7))


def contract_matrix(width, wide):
    c, e = iota((width, wide), 0), iota((width, wide), 1)
    return one_hot(((e & 7) < STRIPE) & (c == STRIPE * (e >> 3) + (e & 7)))


def normalize(values, gain_row, offset_row):
    center = values - jnp.mean(values, axis=-1, keepdims=True)
    spread = jnp.mean(center * center, axis=-1, keepdims=True)
    recip = lax.rsqrt(spread + EPS_NORM)
    scaled = center * recip
    return scaled * gain_row + offset_row, scaled, recip


def normalize_back(grad_out, scaled, recip, gain_row):
    grad_scaled = grad_out * gain_row
    inner_one = jnp.mean(grad_scaled, axis=-1, keepdims=True)
    inner_two = jnp.mean(grad_scaled * scaled, axis=-1, keepdims=True)
    return recip * (grad_scaled - inner_one - scaled * inner_two)


def fold_rows(values):
    rows, columns = values.shape
    return jnp.sum(values.reshape(rows // 8, 8, columns), axis=0)


def pieces_of(values):
    first = values.astype(BF).astype(F32)
    rest = values - first
    second = rest.astype(BF).astype(F32)
    return first, second, (rest - second).astype(BF).astype(F32)


def lane_head(rows):
    return (iota((rows, HALF), 1) >> 5) & 3


def lane_sub(rows):
    return iota((rows, HALF), 1) & 31


def piece_lanes(values, fourth):
    one, two, three = pieces_of(values)
    sub = lane_sub(values.shape[0])
    return jnp.where(
        sub == 0, one, jnp.where(sub == 1, two, jnp.where(sub == 2, three, jnp.where(sub == 3, fourth, 0.0)))
    )


def wide_keys(keys, bias):
    sub = lane_sub(keys.shape[0])
    extra = jnp.where(sub < 3, 1.0, jnp.where(sub == 3, bias, 0.0))
    return jnp.concatenate([keys.astype(BF), extra.astype(BF)], axis=1)


def wide_values(values):
    return jnp.concatenate([values.astype(BF), jnp.ones(values.shape, BF)], axis=1)


def stack_heads(left, right):
    head_of = lane_head(left.shape[0])
    parts = []
    for head in range(BRANCH_HEADS):
        mine = head_of == head
        parts.append(
            jnp.concatenate(
                [jnp.where(mine, left, 0.0).astype(BF), jnp.where(mine, right, 0.0).astype(BF)], axis=1
            )
        )
    return jnp.concatenate(parts, axis=0)


def pick_heads(stacked, rows):
    head_of = lane_head(rows)
    picked = stacked[:rows]
    for head in range(1, BRANCH_HEADS):
        picked = jnp.where(head_of == head, stacked[head * rows : (head + 1) * rows], picked)
    return picked


def head_norms(values):
    block = one_hot((iota((HALF, HALF), 0) >> 5) == (iota((HALF, HALF), 1) >> 5))
    sums = dot((values * values * 1.02).astype(BF), block)
    return jnp.max(sums, axis=0, keepdims=True)


def exceeds(query_norms, key_norms):
    bound = jnp.max(query_norms * key_norms)
    return jnp.logical_not(bound <= EXPONENT_BOUND * EXPONENT_BOUND)


def stack_queries(queries, shift):
    if shift is None:
        return stack_heads(queries, jnp.where(lane_sub(queries.shape[0]) == 3, 1.0, 0.0))
    return stack_heads(queries, piece_lanes(shift * (-1.0 / EXPONENT_SCALE), 1.0))


def attend_heads(queries, shift, keys, values):
    rows = queries.shape[0]
    scores = dot_nt(stack_queries(queries, shift), keys)
    weights = jnp.exp2(scores * EXPONENT_SCALE).astype(BF)
    result = dot(weights, values)
    totals = pick_heads(result[:, HALF:], rows)
    log_total = jnp.log(totals) * LOG2E
    if shift is not None:
        log_total = log_total + shift
    return pick_heads(result[:, :HALF], rows) / totals, log_total


def highest_scores(queries, keys):
    rows = queries.shape[0]
    scores = dot_nt(stack_queries(queries, None), keys)
    highest = jnp.max(scores, axis=-1, keepdims=True) * EXPONENT_SCALE
    return pick_heads(jnp.broadcast_to(highest, (BRANCH_HEADS * rows, HALF)), rows)


def attend_heads_back(queries, grad, attended, log_total, keys, values):
    rows = queries.shape[0]
    query_turned = jnp.transpose(queries).astype(BF)
    grad_turned = jnp.transpose(grad).astype(BF)
    block = one_hot((iota((HALF, HALF), 0) >> 5) == (iota((HALF, HALF), 1) >> 5))
    inner = sum(dot(piece.astype(BF), block) for piece in pieces_of(grad * attended)[:2])
    weights = jnp.exp2(dot_nt(stack_queries(queries, log_total), keys) * EXPONENT_SCALE)
    weights_low = weights.astype(BF)
    grad_weights = dot_nt(stack_heads(grad, piece_lanes(-inner, 0.0)), values)
    grad_scores = (weights * grad_weights).astype(BF)
    grad_queries = pick_heads(dot(grad_scores, keys[:, :HALF]), rows) * SCALE
    grad_keys, grad_values = [], []
    for head in range(BRANCH_HEADS):
        lanes = slice(head * HEAD_DIM, (head + 1) * HEAD_DIM)
        span = slice(head * rows, (head + 1) * rows)
        grad_values.append(dot(grad_turned[lanes], weights_low[span]))
        grad_keys.append(dot(query_turned[lanes], grad_scores[span]))
    return grad_queries, grad_keys, grad_values


def shift_down(values):
    rows = values.shape[0]
    return jnp.where(iota(values.shape, 0) == 0, 0.0, pltpu.roll(values, 1, 0))


def shift_up(values):
    rows = values.shape[0]
    return jnp.where(iota(values.shape, 0) == rows - 1, 0.0, pltpu.roll(values, rows - 1, 0))


def start_sums(sums, starts):
    @pl.when(pl.program_id(0) == 0)
    def _():
        for index, total in enumerate(sums):
            if starts:
                total[...] = starts[index][...]
            else:
                total[...] = jnp.zeros_like(total)


def at_last_step(body):
    pl.when(pl.program_id(0) == pl.num_programs(0) - 1)(body)


def pack_early_kernel(qkv_ref, small_ref, bias_ref, early_ref):
    shard, small_lanes = qkv_ref.shape[0], small_ref.shape[1]
    bias_lanes = bias_ref.shape[1]
    early_ref[:shard] = qkv_ref[...].astype(BF)
    spare = early_ref.shape[1] - small_lanes - bias_lanes
    bias = jnp.concatenate([bias_ref[...], jnp.zeros((small_ref.shape[0] - 1, bias_lanes), F32)], axis=0)
    early_ref[shard:] = jnp.concatenate(
        [small_ref[...], bias, jnp.zeros((small_ref.shape[0], spare), F32)], axis=1
    ).astype(BF)


def pack_late_kernel(out_ref, expand_ref, shrink_ref, late_ref):
    shard, channels = out_ref.shape
    begin = channels + expand_ref.shape[1]
    late_ref[:, :channels] = out_ref[...].astype(BF)
    late_ref[:, channels:begin] = expand_ref[...].astype(BF)
    for block in range(shrink_ref.shape[0] // shard):
        lanes = slice(begin + block * channels, begin + (block + 1) * channels)
        late_ref[:, lanes] = shrink_ref[block * shard : (block + 1) * shard].astype(BF)


def project_kernel(dims, ways, assembles, *refs):
    rows, width, wide, wide_part = dims
    me_ref, x_ref = refs[:2]
    if assembles:
        pieces = refs[2 : 2 + ways]
        across_ref, normed_ref = refs[2 + ways : 4 + ways]
        down_refs = refs[4 + ways : 4 + 2 * ways]
        weight_ref, small_ref, bias_ref, spread_ref = refs[4 + 2 * ways :]

        @pl.when(pl.program_id(0) == 0)
        def _():
            channels, hidden_width = small_ref.shape[1], bias_ref.shape[1]
            shard = channels // ways
            bias_shard = hidden_width // ways
            lanes = -(-(shard + bias_shard) // 128) * 128
            lane, column = iota((lanes, channels + hidden_width), 0), iota((lanes, channels + hidden_width), 1)
            total = jnp.zeros((16, channels + hidden_width), F32)
            for distance, piece in enumerate(pieces):
                place = me_ref[0] ^ distance
                weight_ref[pl.ds(pl.multiple_of(place * shard, shard), shard)] = piece[:shard]
                target = jnp.where(
                    lane < shard,
                    lane + shard * place,
                    channels + lane - shard + bias_shard * place,
                )
                chosen = one_hot((column == target) & (lane < shard + bias_shard))
                total = total + dot(piece[shard : shard + 16, :lanes], chosen)
            small_ref[...] = total[:, :channels]
            bias_ref[...] = total[0:1, channels:]

    else:
        weight_ref, small_ref, across_ref, normed_ref = refs[2:6]
        down_refs = refs[6 : 6 + ways]
        spread_ref = refs[6 + ways]
    gain, offset = small_ref[9:10], small_ref[10:11]
    expand = one_hot(expand_condition(wide, width))
    for row in range(rows):
        span = slice(row * width, (row + 1) * width)
        normed, _, _ = normalize(x_ref[0, span].astype(F32), gain, offset)
        normed = normed.astype(BF)
        normed_ref[0, span] = normed
        across_ref[0, span] = dot(normed, weight_ref[:, : 3 * HALF]).astype(BF)
        spread_ref[row] = dot(expand, normed).astype(BF)
        for distance in range(ways):
            start = pl.multiple_of((me_ref[0] ^ distance) * wide_part, wide_part)
            down_refs[distance][0, row] = spread_ref[row, pl.ds(start, wide_part)]


def rank_row(mask_row, width):
    lower = one_hot(iota((width, width), 0) <= iota((width, width), 1))
    counted = dot(jnp.broadcast_to(mask_row, (8, width)).astype(BF), lower)[0:1]
    return jnp.where(mask_row > 0.0, counted - 1.0, -1.0)


def across_kernel(
    dims,
    first,
    across_ref,
    mask_ref,
    small_ref,
    joined_ref,
    attended_ref,
    total_ref,
    keys_ref,
    values_ref,
    shift_ref,
):
    rows, width, kept, key_rows = dims
    image = pl.program_id(0)
    ranks = rank_row(mask_ref[pl.ds(image + first, 1)].astype(F32), width)
    select = one_hot(iota((kept, width), 0).astype(F32) == ranks)
    bias = jnp.where(iota((kept, HALF), 0) >= VALID, MASKED, 0.0)
    key_norms = jnp.zeros((1, HALF), F32)
    for row in range(rows):
        picked = dot(select, across_ref[0, row * width : (row + 1) * width, HALF:])
        key_norms = jnp.maximum(key_norms, head_norms(picked[:, :HALF]))
        span = slice(row * kept, (row + 1) * kept)
        keys_ref[0, span] = wide_keys(picked[:, :HALF], bias)
        values_ref[0, span] = wide_values(picked[:, HALF:])
    spare = key_rows - rows * kept
    if spare:
        nothing = jnp.zeros((spare, HALF), F32)
        keys_ref[0, rows * kept :] = wide_keys(nothing, nothing + MASKED)
        values_ref[0, rows * kept :] = wide_values(nothing)

    query_norms = head_norms(across_ref[0, :, :HALF].astype(F32) * (SCALE * LOG2E))
    large = exceeds(query_norms, key_norms)

    @pl.when(image == 0)
    def _():
        shift_ref[...] = jnp.zeros_like(shift_ref)

    @pl.when(large)
    def _():
        def highest(row, carry):
            span = pl.ds(pl.multiple_of(row * width, 16), width)
            shift_ref[span] = highest_scores(across_ref[0, span, :HALF].astype(F32), keys_ref[0])
            return carry

        lax.fori_loop(0, rows, highest, 0)

    def value_row(row):
        return across_ref[0, row * width : (row + 1) * width, 2 * HALF :].astype(F32)

    for row in range(rows):
        span = slice(row * width, (row + 1) * width)
        sums = [jnp.zeros((width, HALF), F32) for _ in range(3)]
        for tap_row in range(3):
            source = row + tap_row - 1
            if 0 <= source < rows:
                values = value_row(source)
                for tap_col in range(3):
                    tap = 3 * tap_row + tap_col
                    sums[tap_col] = sums[tap_col] + values * small_ref[tap : tap + 1, :HALF]
        local = shift_down(sums[0]) + sums[1] + shift_up(sums[2]) + small_ref[11:12, :HALF]
        queries = across_ref[0, span, :HALF].astype(F32)
        attended, log_total = attend_heads(queries, shift_ref[span], keys_ref[0], values_ref[0])
        attended_ref[0, span] = attended
        total_ref[0, span] = log_total
        joined_ref[0, span] = (attended + local).astype(BF)

    @pl.when(large)
    def _():
        shift_ref[...] = jnp.zeros_like(shift_ref)


def assemble(me_ref, pieces, target_ref, dim, step):
    for distance, piece in enumerate(pieces):
        place = me_ref[0] ^ distance
        if dim == 0:
            target_ref[pl.ds(place * step, step)] = piece[0].astype(target_ref.dtype)
        else:
            target_ref[:, pl.ds(pl.multiple_of(place * step, step), step)] = piece[0].astype(
                target_ref.dtype
            )


def down_setup(me_ref, mask_ref, column_ref, width, wide, wide_part, first):
    image = pl.program_id(0) + first
    mask_row = mask_ref[pl.ds(image, 1)].astype(F32)
    valid = one_hot(expand_condition(wide, width) & (mask_row > 0.0))
    column_ref[...] = dot(valid, jnp.ones((width, HALF), BF))
    return pl.multiple_of(me_ref[0] * wide_part, GROUP)


def window_bias(column_ref, start, window, height):
    valid = column_ref[pl.ds(start + pl.multiple_of(window * GROUP, GROUP), GROUP)]
    bias = jnp.where(valid > 0.5, 0.0, MASKED)
    return jnp.broadcast_to(bias[None], (height, GROUP, HALF)).reshape(height * GROUP, HALF)


def pad_keys(block, spare, fill):
    if not spare:
        return block
    return jnp.concatenate([block, jnp.full((spare, HALF), 0.0, F32) + fill], axis=0)


def window_operands(keys, values, bias, spare):
    return (
        wide_keys(pad_keys(keys, spare, 0.0), pad_keys(bias, spare, MASKED)),
        wide_values(pad_keys(values, spare, 0.0)),
    )


def grid_shift(values, amount):
    return pltpu.roll(values, amount % GROUP, 1)


def grid_stack(values):
    edge = jnp.zeros((1,) + values.shape[1:], F32)
    return jnp.concatenate([edge, values, edge], axis=0)


def down_kernel(dims, ways, first, *refs):
    height, width, wide, wide_part, spare = dims
    me_ref, mask_ref, small_ref, weight_ref = refs[:4]
    pieces_in = refs[4 : 4 + ways]
    joined_refs = refs[4 + ways : 4 + 2 * ways]
    attended_ref, total_ref, saved_ref, normed_out, mixed_ref, joined_ref, column_ref = refs[
        4 + 2 * ways :
    ]
    normed_ref = normed_out.at[0]
    rows = height // ways
    start = down_setup(me_ref, mask_ref, column_ref, width, wide, wide_part, first)
    assemble(me_ref, pieces_in, normed_ref, 0, rows)
    tokens = height * GROUP
    windows = wide_part // GROUP
    normed = normed_ref[...].reshape(height * wide_part, 2 * HALF)
    mixed_low = dot(normed, weight_ref[:, 3 * HALF :]).astype(BF)
    mixed_low = mixed_low.reshape(height, wide_part, 3 * HALF)
    saved_ref[0] = mixed_low
    mixed_ref[...] = mixed_low.astype(F32)

    everything = mixed_ref[...].reshape(height * wide_part, 3 * HALF)
    large = exceeds(
        head_norms(everything[:, :HALF] * (SCALE * LOG2E)), head_norms(everything[:, HALF : 2 * HALF])
    )

    def one_window(shifted, window, carry):
        span = pl.ds(pl.multiple_of(window * GROUP, GROUP), GROUP)
        grid = mixed_ref[:, span]
        flat = grid.reshape(tokens, 3 * HALF)
        queries, keys, values = (flat[:, part * HALF : (part + 1) * HALF] for part in range(3))
        bias = window_bias(column_ref, start, window, height)
        keys_in, values_in = window_operands(keys, values, bias, spare)

        shift = highest_scores(queries, keys_in) if shifted else None
        attended, log_total = attend_heads(queries, shift, keys_in, values_in)
        attended_ref[0, :, span] = attended.reshape(height, GROUP, HALF)
        total_ref[0, :, span] = log_total.reshape(height, GROUP, HALF)
        stacked = grid_stack(values.reshape(height, GROUP, HALF))
        sums = [jnp.zeros((height, GROUP, HALF), F32) for _ in range(3)]
        for tap_row in range(3):
            for tap_col in range(3):
                tap = 3 * tap_row + tap_col
                sums[tap_col] = sums[tap_col] + stacked[tap_row : tap_row + height] * small_ref[
                    tap : tap + 1, HALF:
                ].reshape(1, 1, HALF)
        local = grid_shift(sums[0], 1) + sums[1] + grid_shift(sums[2], -1)
        local = local + small_ref[11:12, HALF:].reshape(1, 1, HALF)
        joined_ref[:, span] = attended.reshape(height, GROUP, HALF) + local
        return carry

    @pl.when(jnp.logical_not(large))
    def _():
        lax.fori_loop(0, windows, functools.partial(one_window, False), 0, unroll=min(windows, 8))

    @pl.when(large)
    def _():
        lax.fori_loop(0, windows, functools.partial(one_window, True), 0)

    for distance in range(ways):
        place = me_ref[0] ^ distance
        joined_refs[distance][0] = joined_ref[pl.ds(place * rows, rows)].astype(BF)


def gelu_parts(hidden):
    upper = 0.5 + 0.5 * lax.erf(hidden * INV_ROOT_TWO)
    return upper, jnp.exp2(hidden * hidden * (-0.5 * LOG2E)) * INV_ROOT_TAU


def middle_kernel(dims, ways, *refs):
    rows, width, wide, wide_part, chunk, hidden_part = dims
    refs = list(refs)

    def take(number):
        taken = refs[:number]
        del refs[:number]
        return taken

    me_ref, x_ref, cot_ref, across_ref = take(4)
    pieces_in = [take(ways), take(ways)]
    weights_in = take(ways)
    small_ref, bias_ref = take(2)
    block_ref, middle_ref, grad_across_ref = take(3)
    grad_refs = take(ways)
    dbias_ref, dsmall_ref = take(2)
    piece_refs = take(ways)
    dout_ref, dexpand_ref, dshrink_ref = take(3)
    out_ref, expand_ref, shrink_ref = take(3)
    wide_ref, joined_ref, normed_ref, active_ref, hidden_ref, attended_ref, down_ref, gwide_ref = take(8)
    turned_ref = take(1)[0]
    tokens = rows * width
    hidden_width = expand_ref.shape[1]
    channels = 2 * HALF
    shard = channels // ways
    blocks = hidden_width // channels
    start_sums((dbias_ref, dsmall_ref, dout_ref, dexpand_ref, dshrink_ref), None)

    @pl.when(pl.program_id(0) == 0)
    def _():
        for distance, piece in enumerate(weights_in):
            place = me_ref[0] ^ distance
            span = pl.ds(pl.multiple_of(place * shard, shard), shard)
            out_ref[span] = piece[:, :channels]
            expand_ref[span] = piece[:, channels : channels + hidden_width]
            for block in range(blocks):
                begin = pl.multiple_of((place * blocks + block) * shard, shard)
                lanes = slice(channels + hidden_width + block * channels, channels + hidden_width + (block + 1) * channels)
                shrink_ref[pl.ds(begin, shard)] = piece[:, lanes]

    image, pair = pl.program_id(0), pl.num_programs(0) // 2

    @pl.when(image < pair)
    def _():
        assemble(me_ref, pieces_in[0], wide_ref, 1, wide_part)

    @pl.when(image >= pair)
    def _():
        assemble(me_ref, pieces_in[1], wide_ref, 1, wide_part)

    contract = contract_matrix(width, wide)
    for row in range(rows):
        span = slice(row * width, (row + 1) * width)
        joined_ref[span, :HALF] = across_ref[0, span]
        joined_ref[span, HALF:] = dot(contract, wide_ref[row]).astype(BF)

    def token_rows(step, carry):
        span = pl.ds(pl.multiple_of(step * chunk, 16), chunk)
        joined = joined_ref[span]
        attended_out = dot(joined, out_ref[...]) + small_ref[12:13]
        middle = x_ref[0, span].astype(F32) + attended_out
        normed, scaled, recip = normalize(middle, small_ref[13:14], small_ref[14:15])
        normed_low = normed.astype(BF)
        normed_ref[span] = normed_low
        back = cot_ref[0, span]
        result = middle + small_ref[15:16]
        grad_normed = jnp.zeros((chunk, 2 * HALF), F32)

        def products(part):
            lanes = slice(part, part + hidden_part)
            return dot(normed_low, expand_ref[:, lanes]), dot_nt(back, shrink_ref[lanes])

        def follow(result, grad_normed, behind):
            lanes, active, grad_hidden = behind
            return (
                result + dot(active, shrink_ref[lanes]),
                grad_normed + dot_nt(grad_hidden, expand_ref[:, lanes]),
            )

        ahead, behind = products(0), None
        for part in range(0, hidden_width, hidden_part):
            lanes = slice(part, part + hidden_part)
            hidden, grad_active = ahead
            if part + hidden_part < hidden_width:
                ahead = products(part + hidden_part)
            hidden = hidden + bias_ref[:, lanes]
            upper, density = gelu_parts(hidden)
            active = (hidden * upper).astype(BF)
            active_ref[span, lanes] = active
            grad_hidden = grad_active * (upper + hidden * density)
            grad_hidden = grad_hidden.astype(BF)
            hidden_ref[span, lanes] = grad_hidden
            dbias_ref[:, lanes] += fold_rows(grad_hidden.astype(F32))
            if part:
                result, grad_normed = follow(result, grad_normed, behind)
            behind = (lanes, active, grad_hidden)
        result, grad_normed = follow(result, grad_normed, behind)
        block_ref[0, span] = result
        back_wide = back.astype(F32)
        grad_middle = back_wide + normalize_back(grad_normed, scaled, recip, small_ref[13:14])
        middle_ref[0, span] = grad_middle
        grad_attended = grad_middle.astype(BF)
        attended_ref[span] = grad_attended
        grad_joined = dot_nt(grad_attended, out_ref[...]).astype(BF)
        grad_across_ref[0, span] = grad_joined[:, :HALF]
        down_ref[span] = grad_joined[:, HALF:]
        dsmall_ref[0:8] += fold_rows(grad_attended.astype(F32))
        dsmall_ref[8:16] += fold_rows(grad_normed * scaled)
        dsmall_ref[16:24] += fold_rows(grad_normed)
        dsmall_ref[24:32] += fold_rows(back_wide)
        return carry

    lax.fori_loop(0, tokens // chunk, token_rows, 0, unroll=True)
    expand = one_hot(expand_condition(wide, width))
    for row in range(rows):
        gwide_ref[row] = dot(expand, down_ref[row * width : (row + 1) * width]).astype(BF)
    for distance in range(ways):
        place = me_ref[0] ^ distance
        grad_refs[distance][0] = gwide_ref[
            :, pl.ds(pl.multiple_of(place * wide_part, wide_part), wide_part)
        ]
    dout_ref[...] += dot_tn(joined_ref[...], attended_ref[...])
    dexpand_ref[...] += dot_tn(normed_ref[...], hidden_ref[...])
    dshrink_ref[...] += dot_tn(cot_ref[0], active_ref[...])

    @at_last_step
    def _():
        for block in range(blocks):
            lanes = slice(block * channels, (block + 1) * channels)
            turned_ref[lanes] = jnp.transpose(dshrink_ref[:, lanes])
        for distance, piece in enumerate(piece_refs):
            place = me_ref[0] ^ distance
            span = pl.ds(pl.multiple_of(place * shard, shard), shard)
            piece[:, :channels] = dout_ref[span]
            piece[:, channels : channels + hidden_width] = dexpand_ref[span]
            for block in range(blocks):
                begin = pl.multiple_of((place * blocks + block) * shard, shard)
                lanes = slice(channels + hidden_width + block * channels, channels + hidden_width + (block + 1) * channels)
                piece[:, lanes] = turned_ref[pl.ds(begin, shard)]


def shard_pieces(me_ref, piece_refs, total_ref):
    shard = piece_refs[0].shape[0]

    @at_last_step
    def _():
        for distance, piece in enumerate(piece_refs):
            begin = pl.multiple_of((me_ref[0] ^ distance) * shard, shard)
            piece[...] = total_ref[pl.ds(begin, shard)]


def across_back_kernel(dims, first, last, *refs):
    rows, width, kept, key_rows, chunk = dims
    refs = list(refs)

    def take(number):
        taken = refs[:number]
        del refs[:number]
        return taken

    across_ref, grad_ref, attended_ref, total_ref, keys_ref, values_ref, normed_ref = take(7)
    mask_ref, small_ref = take(2)
    starts = take(2) if last else None
    mixed_ref, taps_ref, dweight_ref, dkeys_ref, dvalues_ref, local_ref = take(6)
    tokens = rows * width
    image = pl.program_id(0) + first
    start_sums((taps_ref, dweight_ref), starts)
    dkeys_ref[...] = jnp.zeros_like(dkeys_ref)
    dvalues_ref[...] = jnp.zeros_like(dvalues_ref)

    def attend(step, carry):
        span = pl.ds(pl.multiple_of(step * chunk, 16), chunk)
        grad_queries, grad_keys, grad_values = attend_heads_back(
            across_ref[0, span, :HALF].astype(F32),
            grad_ref[0, span].astype(F32),
            attended_ref[0, span],
            total_ref[0, span],
            keys_ref[0],
            values_ref[0],
        )
        mixed_ref[0, span, :HALF] = grad_queries.astype(BF)
        for head in range(BRANCH_HEADS):
            lanes = slice(head * HEAD_DIM, (head + 1) * HEAD_DIM)
            dkeys_ref[lanes] += grad_keys[head]
            dvalues_ref[lanes] += grad_values[head]
        return carry

    lax.fori_loop(0, tokens // chunk, attend, 0)

    local_ref[...] = jnp.zeros_like(local_ref)
    for row in range(rows):
        grad = grad_ref[0, row * width : (row + 1) * width].astype(F32)
        taps_ref[72:80] += fold_rows(grad)
        for tap_col, moved in enumerate((shift_up(grad), grad, shift_down(grad))):
            for tap_row in range(3):
                target = row + tap_row - 1
                if 0 <= target < rows:
                    tap = 3 * tap_row + tap_col
                    span = slice(target * width, (target + 1) * width)
                    values = across_ref[0, span, 2 * HALF :].astype(F32)
                    taps_ref[8 * tap : 8 * tap + 8] += fold_rows(values * moved)
                    local_ref[span] += moved * small_ref[tap : tap + 1, :HALF]

    ranks = rank_row(mask_ref[pl.ds(image, 1)].astype(F32), width)
    place = jnp.transpose(jnp.broadcast_to(ranks, (HALF, width)))
    spread = one_hot(iota((width, HALF), 1).astype(F32) == place)
    spread_more = one_hot((iota((width, kept - HALF), 1) + HALF).astype(F32) == place[:, : kept - HALF])
    spread = jnp.concatenate([spread, spread_more], axis=1)
    grad_keys = jnp.transpose(dkeys_ref[...]) * SCALE
    grad_values = jnp.transpose(dvalues_ref[...])
    high = grad_values.astype(BF)
    low = (grad_values - high.astype(F32)).astype(BF)
    grad_keys = grad_keys.astype(BF)
    for row in range(rows):
        span = slice(row * kept, (row + 1) * kept)
        packed = jnp.concatenate([grad_keys[span], high[span], low[span]], axis=1)
        unpacked = dot(spread, packed)
        target = slice(row * width, (row + 1) * width)
        mixed_ref[0, target, HALF : 2 * HALF] = unpacked[:, :HALF].astype(BF)
        whole = unpacked[:, HALF : 2 * HALF] + unpacked[:, 2 * HALF :] + local_ref[target]
        mixed_ref[0, target, 2 * HALF :] = whole.astype(BF)
    dweight_ref[...] += dot_tn(normed_ref[0], mixed_ref[0])


def down_back_kernel(dims, ways, *refs):
    height, width, wide, wide_part, spare = dims
    refs = list(refs)

    def take(number):
        taken = refs[:number]
        del refs[:number]
        return taken

    me_ref, mask_ref, small_ref, weight_ref, attended_ref, total_ref, saved_ref, normed_ref = take(8)
    grads_in = take(ways)
    out_refs = take(ways)
    taps_ref = take(1)[0]
    piece_refs = take(ways)
    dweight_ref, mixed_ref, grad_ref, out_ref, turned_ref, column_ref = take(6)
    rows = height // ways
    start = down_setup(me_ref, mask_ref, column_ref, width, wide, wide_part, 0)
    assemble(me_ref, grads_in, grad_ref, 0, rows)
    mixed_ref[...] = saved_ref[0].astype(F32)
    tokens = height * GROUP
    windows = wide_part // GROUP
    start_sums((taps_ref, dweight_ref), None)

    def one_window(window, carry):
        span = pl.ds(pl.multiple_of(window * GROUP, GROUP), GROUP)
        flat = mixed_ref[:, span].reshape(tokens, 3 * HALF)
        queries, keys, values = (flat[:, part * HALF : (part + 1) * HALF] for part in range(3))
        grad_grid = grad_ref[:, span]
        grad = grad_grid.reshape(tokens, HALF)
        bias = window_bias(column_ref, start, window, height)
        keys_in, values_in = window_operands(keys, values, bias, spare)
        grad_queries, grad_keys, grad_values = attend_heads_back(
            queries,
            grad,
            attended_ref[0, :, span].reshape(tokens, HALF),
            total_ref[0, :, span].reshape(tokens, HALF),
            keys_in,
            values_in,
        )
        grad_keys = jnp.transpose(jnp.concatenate(grad_keys, axis=0))[:tokens] * SCALE
        grad_values = jnp.transpose(jnp.concatenate(grad_values, axis=0))[:tokens]
        values_grid = values.reshape(height, GROUP, HALF)
        local = jnp.zeros((height, GROUP, HALF), F32)
        taps_ref[72:80] += jnp.sum(grad_grid, axis=0)
        shifted = (grid_shift(grad_grid, -1), grad_grid, grid_shift(grad_grid, 1))
        for tap_col, moved in enumerate(shifted):
            stacked = grid_stack(moved)
            for tap_row in range(3):
                tap = 3 * tap_row + tap_col
                source = stacked[2 - tap_row : 2 - tap_row + height]
                taps_ref[8 * tap : 8 * tap + 8] += jnp.sum(source * values_grid, axis=0)
                local = local + source * small_ref[tap : tap + 1, HALF:].reshape(1, 1, HALF)
        shape = (height, GROUP, HALF)
        out_ref[:, span, :HALF] = grad_queries.reshape(shape)
        out_ref[:, span, HALF : 2 * HALF] = grad_keys.reshape(shape)
        out_ref[:, span, 2 * HALF :] = grad_values.reshape(shape) + local
        return carry

    lax.fori_loop(0, windows, one_window, 0, unroll=min(windows, 8))
    mixed_grad = out_ref[...].reshape(height * wide_part, 3 * HALF).astype(BF)
    grad_normed = dot_nt(mixed_grad, weight_ref[:, 3 * HALF :]).astype(BF)
    turned_ref[...] = grad_normed.reshape(height, wide_part, 2 * HALF)
    for distance in range(ways):
        place = me_ref[0] ^ distance
        out_refs[distance][0] = turned_ref[pl.ds(place * rows, rows)]
    normed = normed_ref[0].reshape(height * wide_part, 2 * HALF)
    dweight_ref[...] += dot_tn(normed, mixed_grad)
    shard_pieces(me_ref, piece_refs, dweight_ref)


def final_kernel(dims, ways, last, *refs):
    rows, width, wide, wide_part, chunk = dims
    refs = list(refs)

    def take(number):
        taken = refs[:number]
        del refs[:number]
        return taken

    me_ref, x_ref, middle_ref, across_ref = take(4)
    pieces_in = take(ways)
    small_ref, weight_ref = take(2)
    starts = take(1) if last else None
    others = take(5) if last else None
    grad_ref, dsmall_ref = take(2)
    piece_refs = take(ways) if last else None
    wide_ref, down_ref = take(2)
    whole_ref = take(1)[0] if last else None
    tokens = rows * width
    start_sums((dsmall_ref,), starts)
    assemble(me_ref, pieces_in, wide_ref, 1, wide_part)
    contract = contract_matrix(width, wide)
    for row in range(rows):
        down_ref[row * width : (row + 1) * width] = dot(contract, wide_ref[row])

    def token_rows(step, carry):
        span = pl.ds(pl.multiple_of(step * chunk, 16), chunk)
        _, scaled, recip = normalize(x_ref[0, span].astype(F32), small_ref[9:10], small_ref[10:11])
        grad_normed = dot_nt(across_ref[0, span], weight_ref[:, : 3 * HALF]) + down_ref[span]
        dsmall_ref[0:8] += fold_rows(grad_normed * scaled)
        dsmall_ref[8:16] += fold_rows(grad_normed)
        grad_ref[0, span] = middle_ref[0, span] + normalize_back(
            grad_normed, scaled, recip, small_ref[9:10]
        )
        return carry

    lax.fori_loop(0, tokens // chunk, token_rows, 0)
    if last:

        @at_last_step
        def _():
            across_taps, down_taps, middle_sums, bias_sums, dweight = others
            channels = 2 * HALF

            def total(ref, index):
                return jnp.sum(ref[8 * index : 8 * index + 8], axis=0, keepdims=True)

            def set_taps(row, index):
                whole_ref[row : row + 1, :HALF] = total(across_taps, index)
                whole_ref[row : row + 1, HALF:] = total(down_taps, index)

            whole_ref[...] = jnp.zeros_like(whole_ref)
            for tap in range(9):
                set_taps(tap, tap)
            whole_ref[9:10] = total(dsmall_ref, 0)
            whole_ref[10:11] = total(dsmall_ref, 1)
            set_taps(11, 9)
            for index in range(4):
                whole_ref[12 + index : 13 + index] = total(middle_sums, index)
            bias = total(bias_sums, 0)
            for block in range(bias.shape[1] // channels):
                whole_ref[16 + block : 17 + block] = bias[:, block * channels : (block + 1) * channels]
            shard = dweight.shape[0] // ways
            for distance, piece in enumerate(piece_refs):
                begin = pl.multiple_of((me_ref[0] ^ distance) * shard, shard)
                piece[:shard] = dweight[pl.ds(begin, shard)].astype(BF)
                piece[shard:, :channels] = whole_ref[...].astype(BF)
                piece[shard:, channels:] = jnp.zeros(
                    (whole_ref.shape[0], dweight.shape[1] - channels), BF
                )


def update_kernel(ways, place_ref, mine_ref, other_ref, tail_ref, *refs):
    squares, old, new = refs[:ways], refs[ways : ways + 18], refs[ways + 19 : ways + 37]
    norm_ref, joined_ref = refs[ways + 18], refs[ways + 37]
    me, core = place_ref[0], place_ref[1]
    half = mine_ref.shape[0]
    joined_ref[pl.ds(pl.multiple_of(core * half, half), half)] = mine_ref[...]
    joined_ref[pl.ds(pl.multiple_of((1 - core) * half, half), half)] = other_ref[...]
    shard = 2 * half
    rows, channels = old[1].shape
    hidden_width = old[2].shape[1]
    blocks = hidden_width // channels
    small = tail_ref[shard:, :channels]
    small_rows, small_lanes = old[4].shape
    bias_lanes = old[5].shape[1]
    total = tree_sum([entry[...] for entry in squares]) + jnp.sum(small * small)
    norm = jnp.sqrt(total)
    norm_ref[0, 0] = jnp.max(norm)
    factor = (CLIP_NORM / jnp.maximum(norm, CLIP_NORM))[0:1, 0:1]

    def update(index, grads, rate, decay, spans=(slice(None), slice(None))):
        weight, first, second = (old[part * 6 + index][spans] for part in range(3))
        results = adam_update(weight, first, second, grads * factor, rate, decay)
        for part in range(3):
            new[part * 6 + index][spans] = results[part]

    update(0, tail_ref[:shard], RATE_MATRIX, WEIGHT_DECAY, (slice(None), slice(0, 3 * HALF)))
    begin = channels + 2 * hidden_width
    update(
        0,
        joined_ref[:, begin : begin + 3 * HALF],
        RATE_MATRIX,
        WEIGHT_DECAY,
        (slice(None), slice(3 * HALF, 6 * HALF)),
    )
    update(1, joined_ref[:, :channels], RATE_OUTPUT, WEIGHT_DECAY)
    update(2, joined_ref[:, channels : channels + hidden_width], RATE_MATRIX, WEIGHT_DECAY)
    for block in range(blocks):
        begin = channels + hidden_width + block * channels
        update(
            3,
            joined_ref[:, begin : begin + channels],
            RATE_MATRIX,
            WEIGHT_DECAY,
            (slice(block * rows, (block + 1) * rows), slice(None)),
        )
    small_grad = jnp.zeros((small_rows, small_lanes), F32)
    bias_grad = jnp.zeros((1, bias_lanes), F32)
    for place in range(ways):
        lanes = slice(place * small_lanes, (place + 1) * small_lanes)
        small_grad = jnp.where(me == place, small[:small_rows, lanes], small_grad)
        row, lane = divmod(place * bias_lanes, channels)
        row = small_rows + row
        bias_grad = jnp.where(me == place, small[row : row + 1, lane : lane + bias_lanes], bias_grad)
    update(4, small_grad, RATE_SMALL, 0.0)
    update(5, bias_grad, RATE_MATRIX, 0.0)


def image_block(*shape, first=0):
    return pl.BlockSpec((1,) + shape, lambda image: (image + first,) + (0,) * len(shape))


def whole_block(*shape):
    return pl.BlockSpec(shape, lambda image: (0,) * len(shape))


def scalar_block():
    return pl.BlockSpec(memory_space=pltpu.SMEM)


def run_kernel(body, images, inputs, outputs, scratch, micros, after=(), alias=()):
    number, made = len(inputs), len(outputs)
    hidden = list(after)
    aliases = {}
    for operand, output in alias:
        aliases[number + len(hidden)] = output
        hidden.append(operand)
    skipped = number + len(hidden)

    def wrapped(*refs):
        refs[skipped + made][...] = jnp.zeros((8, 128), F32)
        body(*refs[:number], *refs[skipped : skipped + made], *refs[skipped + made + 1 :])

    outputs = list(outputs) + [((8, 128), F32, whole_block(8, 128))]
    *results, token = pl.pallas_call(
        wrapped,
        grid=(images,),
        in_specs=[spec for _, spec in inputs] + [pl.BlockSpec(memory_space=pl.ANY)] * len(hidden),
        out_specs=[spec for _, _, spec in outputs],
        out_shape=[jax.ShapeDtypeStruct(shape, dtype) for shape, dtype, _ in outputs],
        scratch_shapes=scratch,
        input_output_aliases=aliases,
        compiler_params=pltpu.CompilerParams(vmem_limit_bytes=VMEM_LIMIT),
        cost_estimate=pl.CostEstimate(
            flops=int(micros * 1e9), bytes_accessed=int(micros * 1e6), transcendentals=0
        ),
    )(*[operand for operand, _ in inputs], *hidden)
    return results, token


def adam_update(weight, first_old, second_old, grad_value, rate_value, decay_value):
    new_first = BETA_ONE * first_old + (1.0 - BETA_ONE) * grad_value
    new_second = BETA_TWO * second_old + (1.0 - BETA_TWO) * grad_value * grad_value
    first_hat = new_first / (1.0 - BETA_ONE**STEP)
    second_hat = new_second / (1.0 - BETA_TWO**STEP)
    new_weight = weight - rate_value * (
        first_hat / (jnp.sqrt(second_hat) + ADAM_EPS) + decay_value * weight
    )
    return (new_first, new_second, new_weight)


def swap(value, axis, distance):
    return lax.ppermute(value, axis, [(place, place ^ distance) for place in range(lax.axis_size(axis))])


def exchange(pieces):
    return [pieces[0]] + [swap(pieces[d], "seq", d) for d in range(1, len(pieces))]


def tree_sum(values):
    while len(values) > 1:
        values = [values[i] + values[i + 1] for i in range(0, len(values), 2)]
    return values[0]


def share_low(value, distances):
    rounded = lax.reduce_precision(value, 8, 7)
    sent = rounded.astype(BF)
    return [rounded] + [swap(sent, "img", distance).astype(F32) for distance in distances]


def on_device(
    images,
    cotangent,
    valid_mask,
    qkv_weight,
    out_weight,
    expand_weight,
    shrink_weight,
    small_params,
    expand_bias,
    first_qkv,
    first_out,
    first_expand,
    first_shrink,
    first_small,
    first_bias,
    second_qkv,
    second_out,
    second_expand,
    second_shrink,
    second_small,
    second_bias,
):
    ways = lax.axis_size("seq")
    owner = lax.axis_index("seq")
    me = owner.astype(jnp.int32).reshape(1)
    count, rows, width, channels = images.shape
    tokens = rows * width
    height = rows * ways
    wide = width // STRIPE * GROUP
    wide_part = wide // ways
    kept = -(-VALID // 16) * 16
    key_rows = -(-rows * kept // 256) * 256
    window_tokens = height * GROUP
    spare = -window_tokens % 128
    shard = qkv_weight.shape[0]
    hidden_width = expand_weight.shape[1]
    blocks = hidden_width // channels
    pair = count // 2
    chip_steps = [2 << bit for bit in range((lax.axis_size("img") // 2).bit_length() - 1)][::-1]

    x = images.reshape(count, tokens, channels)
    cot = cotangent.reshape(count, tokens, channels)
    me_in = (me, scalar_block())
    mask_in = (valid_mask, whole_block(*valid_mask.shape))
    piece_in = (rows, wide_part, channels)
    piece_out = (rows, wide_part, HALF)
    qkv_shape = (channels, 6 * HALF)

    def per_image(array, first=0):
        return (array, image_block(*array.shape[1:], first=first))

    def whole(array):
        return (array, whole_block(*array.shape))

    def half_images(array, first):
        last = array.shape[0] - 1
        dims = (1,) + array.shape[1:]
        return (
            array,
            pl.BlockSpec(
                dims, lambda image: (jnp.clip(image - first, 0, last),) + (0,) * (len(dims) - 1)
            ),
        )

    def new_image(dims, dtype, images):
        return ((images,) + dims, dtype, image_block(*dims))

    def part_image(dims, dtype, first):
        return ((count,) + dims, dtype, image_block(*dims, first=first))

    def new_whole(dims, dtype):
        return (dims, dtype, whole_block(*dims))

    (early,), _ = run_kernel(
        pack_early_kernel,
        1,
        [whole(qkv_weight), whole(small_params), whole(expand_bias.reshape(1, -1))],
        [new_whole((shard + 16, qkv_weight.shape[1]), BF)],
        [],
        2,
    )
    weights_in = exchange([early] * ways)

    whole_images, normed_pieces, parameters = [], [], None
    for first in (0, pair):
        assembles = first == 0
        results, token = run_kernel(
            functools.partial(project_kernel, (rows, width, wide, wide_part), ways, assembles),
            pair,
            [me_in, per_image(x, first)] + [whole(entry) for entry in weights_in],
            [part_image((tokens, 3 * HALF), BF, first), part_image((tokens, channels), BF, first)]
            + [new_image(piece_in, BF, pair)] * ways
            + (
                [new_whole(qkv_shape, BF), new_whole((16, channels), F32), new_whole((1, hidden_width), F32)]
                if assembles
                else []
            ),
            [pltpu.VMEM((rows, wide, channels), BF)],
            6,
            alias=[(entry, place) for place, entry in enumerate(whole_images)],
        )
        whole_images = results[:2]
        normed_pieces.append(exchange(results[2 : 2 + ways]))
        if assembles:
            qkv_low, small_full, bias_full = results[2 + ways :]
            weights_in = (qkv_low, small_full)
    across_mixed, normed = whole_images
    small_in, qkv_in = whole(small_full), whole(qkv_low)

    attention_dims = (rows, width, kept, key_rows)
    key_shape = (key_rows, channels)
    across = []

    def run_across(first, images_in, after):
        return run_kernel(
            functools.partial(across_kernel, attention_dims, first),
            images_in,
            [per_image(across_mixed, first), mask_in, small_in],
            [
                part_image((tokens, HALF), BF, first),
                part_image((tokens, HALF), F32, first),
                part_image((tokens, HALF), F32, first),
                part_image(key_shape, BF, first),
                part_image(key_shape, BF, first),
            ],
            [pltpu.VMEM((tokens, HALF), F32)],
            11 * images_in,
            after=after,
            alias=[(entry, place) for place, entry in enumerate(across)],
        )

    across, token = run_across(0, count - 1, (token,))
    (late,), token = run_kernel(
        pack_late_kernel,
        1,
        [whole(out_weight), whole(expand_weight), whole(shrink_weight)],
        [new_whole((shard, channels + 2 * hidden_width), BF)],
        [],
        2,
        after=(token,),
    )
    late_pieces = exchange([late] * ways)
    normed_pieces, token = lax.optimization_barrier((normed_pieces, token))

    down_dims = (height, width, wide, wide_part, spare)
    grid_f32 = (height, wide_part, HALF)
    mixed_grid = (height, wide_part, 3 * HALF)
    normed_grid = (height, wide_part, channels)
    down, joined_pieces = [], []
    for index, first in enumerate((0, pair)):
        results, token = run_kernel(
            functools.partial(down_kernel, down_dims, ways, first),
            pair,
            [me_in, mask_in, small_in, qkv_in] + [per_image(piece) for piece in normed_pieces[index]],
            [new_image(piece_out, BF, pair)] * ways
            + [part_image(grid_f32, F32, first)] * 2
            + [part_image(mixed_grid, BF, first), part_image(normed_grid, BF, first)],
            [
                pltpu.VMEM(mixed_grid, F32),
                pltpu.VMEM(grid_f32, F32),
                pltpu.VMEM((wide, HALF), F32),
            ],
            15,
            after=(token,),
            alias=[(entry, ways + place) for place, entry in enumerate(down)],
        )
        down = results[ways:]
        joined_pieces.append(exchange(results[:ways]))
    across, token = run_across(count - 1, 1, (token,))
    joined_across, attended, log_total, keys, values = across

    matrix_sums = [(channels, channels), (channels, hidden_width), (channels, hidden_width)]
    results, token = run_kernel(
        functools.partial(middle_kernel, (rows, width, wide, wide_part, tokens // 2, channels), ways),
        count,
        [me_in, per_image(x), per_image(cot), per_image(joined_across)]
        + [half_images(piece, 0) for piece in joined_pieces[0]]
        + [half_images(piece, pair) for piece in joined_pieces[1]]
        + [whole(piece) for piece in late_pieces]
        + [small_in, whole(bias_full)],
        [
            new_image((tokens, channels), F32, count),
            new_image((tokens, channels), F32, count),
            new_image((tokens, HALF), BF, count),
        ]
        + [new_image(piece_out, BF, count)] * ways
        + [new_whole((8, hidden_width), F32), new_whole((32, channels), F32)]
        + [new_whole(late.shape, F32)] * ways,
        [pltpu.VMEM(dims, F32) for dims in matrix_sums]
        + [
            pltpu.VMEM((channels, channels), BF),
            pltpu.VMEM((channels, hidden_width), BF),
            pltpu.VMEM((hidden_width, channels), BF),
            pltpu.VMEM((rows, wide, HALF), BF),
            pltpu.VMEM((tokens, channels), BF),
            pltpu.VMEM((tokens, channels), BF),
            pltpu.VMEM((tokens, hidden_width), BF),
            pltpu.VMEM((tokens, hidden_width), BF),
            pltpu.VMEM((tokens, channels), BF),
            pltpu.VMEM((tokens, HALF), BF),
            pltpu.VMEM((rows, wide, HALF), BF),
            pltpu.VMEM((hidden_width, channels), F32),
        ],
        45,
        after=(token,),
    )
    block_out, grad_middle, grad_across = results[:3]
    grad_pieces = exchange(results[3 : 3 + ways])
    bias_sums, middle_sums, *late_sums = results[3 + ways :]

    qkv_half = (channels, 3 * HALF)
    half_shard = (shard, 3 * HALF)
    back_sums, norm_sums, input_grad = None, None, None

    def run_across_back(first, images_in, sums, after):
        results, token = run_kernel(
            functools.partial(
                across_back_kernel, (*attention_dims, tokens // 2), first, sums is not None
            ),
            images_in,
            [
                per_image(across_mixed, first),
                per_image(grad_across, first),
                per_image(attended, first),
                per_image(log_total, first),
                per_image(keys, first),
                per_image(values, first),
                per_image(normed, first),
                mask_in,
                small_in,
            ]
            + ([whole(entry) for entry in sums[1:]] if sums else []),
            [
                part_image((tokens, 3 * HALF), BF, first),
                new_whole((80, HALF), F32),
                new_whole(qkv_half, F32),
            ],
            [
                pltpu.VMEM((HALF, key_rows), F32),
                pltpu.VMEM((HALF, key_rows), F32),
                pltpu.VMEM((tokens, HALF), F32),
            ],
            23 * images_in,
            after=after,
            alias=[(sums[0], 0)] if sums else [],
        )
        return results, token

    def run_final(first, images_in, starts, others, after):
        last = others is not None
        return run_kernel(
            functools.partial(final_kernel, (rows, width, wide, wide_part, tokens), ways, last),
            images_in,
            [me_in, per_image(x, first), per_image(grad_middle, first), per_image(back_sums[0], first)]
            + [per_image(piece, first) for piece in grad_normed_pieces]
            + [small_in, qkv_in]
            + ([whole(entry) for entry in (starts[1], *others)] if last else []),
            [part_image((tokens, channels), F32, first), new_whole((16, channels), F32)]
            + ([new_whole((shard + 32, 3 * HALF), BF)] * ways if last else []),
            [pltpu.VMEM((rows, wide, channels), BF), pltpu.VMEM((tokens, channels), F32)]
            + ([pltpu.VMEM((32, channels), F32)] if last else []),
            4 * images_in,
            after=after,
            alias=[(starts[0], 0)] if last else [],
        )

    back_sums, token = run_across_back(0, 1, None, (token,))
    *late_sums, token = lax.optimization_barrier((*late_sums, token))
    late_parts = exchange(late_sums)
    results, token = run_kernel(
        functools.partial(down_back_kernel, down_dims, ways),
        count,
        [me_in, mask_in, small_in, qkv_in]
        + [per_image(entry) for entry in down]
        + [per_image(piece) for piece in grad_pieces],
        [new_image(piece_in, BF, count)] * ways
        + [new_whole((80, HALF), F32)]
        + [new_whole(half_shard, F32)] * ways,
        [
            pltpu.VMEM(qkv_half, F32),
            pltpu.VMEM(mixed_grid, F32),
            pltpu.VMEM(grid_f32, F32),
            pltpu.VMEM(mixed_grid, F32),
            pltpu.VMEM(normed_grid, BF),
            pltpu.VMEM((wide, HALF), F32),
        ],
        38,
        after=(token,),
    )
    grad_normed_pieces = exchange(results[:ways])
    down_taps, *down_sums = results[ways:]
    late_parts, token = lax.optimization_barrier((late_parts, token))
    late_seq = tree_sum(late_parts)
    core_place = lax.axis_index("img") % 2
    half = shard // 2
    down_parts = exchange(down_sums)
    back_sums, token = run_across_back(1, count - 2, back_sums, (token, late_seq))
    down_parts, late_seq, token = lax.optimization_barrier((down_parts, late_seq, token))
    seq_sum = jnp.concatenate([late_seq, tree_sum(down_parts)], axis=1)
    kept_half = lax.dynamic_slice_in_dim(seq_sum, core_place * half, half, 0)
    core_half = swap(lax.dynamic_slice_in_dim(seq_sum, (1 - core_place) * half, half, 0), "img", 1)
    (input_grad, norm_sums), token = run_final(0, count - 1, None, None, (token,))
    kept_half, core_half, token = lax.optimization_barrier((kept_half, core_half, token))
    halves_sum = kept_half + core_half
    chip_half = swap(halves_sum, "img", chip_steps[0])
    back_sums, token = run_across_back(count - 1, 1, back_sums, (token,))
    chip_half, halves_sum, token = lax.optimization_barrier((chip_half, halves_sum, token))
    halves_sum = halves_sum + chip_half
    chip_half = [swap(halves_sum, "img", distance) for distance in chip_steps[1:2]]
    (input_grad, _, *tail_sums), token = run_final(
        count - 1,
        1,
        (input_grad, norm_sums),
        (back_sums[1], down_taps, middle_sums, bias_sums, back_sums[2]),
        (token,),
    )
    tail_parts, halves_sum, chip_half = lax.optimization_barrier(
        (exchange(tail_sums), halves_sum, chip_half)
    )
    halves_sum = tree_sum([halves_sum, *chip_half])
    for distance in chip_steps[2:]:
        halves_sum = halves_sum + swap(halves_sum, "img", distance)
    other_half = swap(halves_sum, "img", 1)
    tail = tree_sum([part.astype(F32) for part in tail_parts])
    tail = tree_sum(share_low(tail, [1]))
    tail = tree_sum(share_low(tail, range(2, lax.axis_size("img"), 2)))

    squared = (
        jnp.sum(halves_sum * halves_sum)
        + jnp.sum(other_half * other_half)
        + jnp.sum(tail[:shard] * tail[:shard])
    )
    squares = exchange([jnp.full((8, 128), squared)] * ways)

    def as_rows(entries):
        return [entry.reshape(1, -1) if entry.ndim == 1 else entry for entry in entries]

    state = as_rows(
        (qkv_weight, out_weight, expand_weight, shrink_weight, small_params, expand_bias)
        + (first_qkv, first_out, first_expand, first_shrink, first_small, first_bias)
        + (second_qkv, second_out, second_expand, second_shrink, second_small, second_bias)
    )
    place_in = jnp.stack([owner, core_place]).astype(jnp.int32)
    (norm, *updated), _ = run_kernel(
        functools.partial(update_kernel, ways),
        1,
        [(place_in, scalar_block())]
        + [whole(entry) for entry in (halves_sum, other_half, tail, *squares, *state)],
        [((1, 1), F32, scalar_block())] + [new_whole(entry.shape, F32) for entry in state[:6]] * 3,
        [pltpu.VMEM((shard, halves_sum.shape[1]), F32)],
        4,
    )
    for index in (5, 11, 17):
        updated[index] = updated[index].reshape(-1)
    return (
        block_out.reshape(images.shape),
        input_grad.reshape(images.shape),
        norm.reshape(()),
        *updated,
    )


def solution(mesh):
    sharded = (
        P("seq", None),
        P("seq", None),
        P("seq", None),
        P("seq", None),
        P(None, "seq"),
        P("seq"),
    )
    grid = P("img", "seq", None, None)
    return jax.shard_map(
        on_device,
        mesh=mesh,
        in_specs=(grid, grid, P("img", None)) + sharded * 3,
        out_specs=(grid, grid, P()) + sharded * 3,
        check_vma=False,
    )
```

```python
import functools

import jax
import jax.numpy as jnp
from jax import lax
from jax.experimental import pallas as pl
from jax.experimental.pallas import tpu as pltpu
from jax.sharding import PartitionSpec as P

HEADS = 8
STRIPE = 7
STEP = 10
VALID = 168

EPS_NORM = 1e-05
BETA_ONE = 0.9
BETA_TWO = 0.999
ADAM_EPS = 1e-08
WEIGHT_DECAY = 0.05
CLIP_NORM = 1.0
RATE_MATRIX = 0.1
RATE_OUTPUT = 0.5
RATE_SMALL = 0.3
INV_ROOT_TWO = 0.7071067811865476
INV_ROOT_TAU = 0.3989422804014327
LOG2E = 1.4426950408889634

BF = jnp.bfloat16
F32 = jnp.float32
HALF = 128
BRANCH_HEADS = 4
HEAD_DIM = 32
SCALE = HEAD_DIM**-0.5
GROUP = 8
MASKED = -1e38
EXPONENT_SCALE = SCALE * LOG2E
EXPONENT_BOUND = 60.0
VMEM_LIMIT = 60 * 2**20


def dot(left, right):
    return jnp.dot(left, right, preferred_element_type=F32)


def dot_nt(left, right):
    return lax.dot_general(left, right, (((1,), (1,)), ((), ())), preferred_element_type=F32)


def dot_tn(left, right):
    return lax.dot_general(left, right, (((0,), (0,)), ((), ())), preferred_element_type=F32)


def iota(shape, dim):
    return lax.broadcasted_iota(jnp.int32, shape, dim)


def one_hot(condition):
    return jnp.where(condition, 1.0, 0.0).astype(BF)


def expand_condition(wide, width):
    e, c = iota((wide, width), 0), iota((wide, width), 1)
    return ((e & 7) < STRIPE) & (c == STRIPE * (e >> 3) + (e & 7))


def contract_matrix(width, wide):
    c, e = iota((width, wide), 0), iota((width, wide), 1)
    return one_hot(((e & 7) < STRIPE) & (c == STRIPE * (e >> 3) + (e & 7)))


def normalize(values, gain_row, offset_row):
    center = values - jnp.mean(values, axis=-1, keepdims=True)
    spread = jnp.mean(center * center, axis=-1, keepdims=True)
    recip = lax.rsqrt(spread + EPS_NORM)
    scaled = center * recip
    return scaled * gain_row + offset_row, scaled, recip


def normalize_back(grad_out, scaled, recip, gain_row):
    grad_scaled = grad_out * gain_row
    inner_one = jnp.mean(grad_scaled, axis=-1, keepdims=True)
    inner_two = jnp.mean(grad_scaled * scaled, axis=-1, keepdims=True)
    return recip * (grad_scaled - inner_one - scaled * inner_two)


def fold_rows(values):
    rows, columns = values.shape
    return jnp.sum(values.reshape(rows // 8, 8, columns), axis=0)


def pieces_of(values):
    first = values.astype(BF).astype(F32)
    rest = values - first
    second = rest.astype(BF).astype(F32)
    return first, second, (rest - second).astype(BF).astype(F32)


def lane_head(rows):
    return (iota((rows, HALF), 1) >> 5) & 3


def lane_sub(rows):
    return iota((rows, HALF), 1) & 31


def piece_lanes(values, fourth):
    one, two, three = pieces_of(values)
    sub = lane_sub(values.shape[0])
    return jnp.where(
        sub == 0, one, jnp.where(sub == 1, two, jnp.where(sub == 2, three, jnp.where(sub == 3, fourth, 0.0)))
    )


def wide_keys(keys, bias):
    sub = lane_sub(keys.shape[0])
    extra = jnp.where(sub < 3, 1.0, jnp.where(sub == 3, bias, 0.0))
    return jnp.concatenate([keys.astype(BF), extra.astype(BF)], axis=1)


def wide_values(values):
    return jnp.concatenate([values.astype(BF), jnp.ones(values.shape, BF)], axis=1)


def stack_heads(left, right):
    head_of = lane_head(left.shape[0])
    parts = []
    for head in range(BRANCH_HEADS):
        mine = head_of == head
        parts.append(
            jnp.concatenate(
                [jnp.where(mine, left, 0.0).astype(BF), jnp.where(mine, right, 0.0).astype(BF)], axis=1
            )
        )
    return jnp.concatenate(parts, axis=0)


def pick_heads(stacked, rows):
    head_of = lane_head(rows)
    picked = stacked[:rows]
    for head in range(1, BRANCH_HEADS):
        picked = jnp.where(head_of == head, stacked[head * rows : (head + 1) * rows], picked)
    return picked


def head_norms(values):
    block = one_hot((iota((HALF, HALF), 0) >> 5) == (iota((HALF, HALF), 1) >> 5))
    sums = dot((values * values * 1.02).astype(BF), block)
    return jnp.max(sums, axis=0, keepdims=True)


def exceeds(query_norms, key_norms):
    bound = jnp.max(query_norms * key_norms)
    return jnp.logical_not(bound <= EXPONENT_BOUND * EXPONENT_BOUND)


def stack_queries(queries, shift):
    if shift is None:
        return stack_heads(queries, jnp.where(lane_sub(queries.shape[0]) == 3, 1.0, 0.0))
    return stack_heads(queries, piece_lanes(shift * (-1.0 / EXPONENT_SCALE), 1.0))


def attend_heads(queries, shift, keys, values):
    rows = queries.shape[0]
    scores = dot_nt(stack_queries(queries, shift), keys)
    weights = jnp.exp2(scores * EXPONENT_SCALE).astype(BF)
    result = dot(weights, values)
    totals = pick_heads(result[:, HALF:], rows)
    log_total = jnp.log(totals) * LOG2E
    if shift is not None:
        log_total = log_total + shift
    return pick_heads(result[:, :HALF], rows) / totals, log_total


def highest_scores(queries, keys):
    rows = queries.shape[0]
    scores = dot_nt(stack_queries(queries, None), keys)
    highest = jnp.max(scores, axis=-1, keepdims=True) * EXPONENT_SCALE
    return pick_heads(jnp.broadcast_to(highest, (BRANCH_HEADS * rows, HALF)), rows)


def attend_heads_back(queries, grad, attended, log_total, keys, values):
    rows = queries.shape[0]
    query_turned = jnp.transpose(queries).astype(BF)
    grad_turned = jnp.transpose(grad).astype(BF)
    block = one_hot((iota((HALF, HALF), 0) >> 5) == (iota((HALF, HALF), 1) >> 5))
    inner = sum(dot(piece.astype(BF), block) for piece in pieces_of(grad * attended)[:2])
    weights = jnp.exp2(dot_nt(stack_queries(queries, log_total), keys) * EXPONENT_SCALE)
    weights_low = weights.astype(BF)
    grad_weights = dot_nt(stack_heads(grad, piece_lanes(-inner, 0.0)), values)
    grad_scores = (weights * grad_weights).astype(BF)
    grad_queries = pick_heads(dot(grad_scores, keys[:, :HALF]), rows) * SCALE
    grad_keys, grad_values = [], []
    for head in range(BRANCH_HEADS):
        lanes = slice(head * HEAD_DIM, (head + 1) * HEAD_DIM)
        span = slice(head * rows, (head + 1) * rows)
        grad_values.append(dot(grad_turned[lanes], weights_low[span]))
        grad_keys.append(dot(query_turned[lanes], grad_scores[span]))
    return grad_queries, grad_keys, grad_values


def shift_down(values):
    rows = values.shape[0]
    return jnp.where(iota(values.shape, 0) == 0, 0.0, pltpu.roll(values, 1, 0))


def shift_up(values):
    rows = values.shape[0]
    return jnp.where(iota(values.shape, 0) == rows - 1, 0.0, pltpu.roll(values, rows - 1, 0))


def start_sums(sums, starts):
    @pl.when(pl.program_id(0) == 0)
    def _():
        for index, total in enumerate(sums):
            if starts:
                total[...] = starts[index][...]
            else:
                total[...] = jnp.zeros_like(total)


def at_last_step(body):
    pl.when(pl.program_id(0) == pl.num_programs(0) - 1)(body)


def pack_early_kernel(qkv_ref, small_ref, bias_ref, early_ref):
    shard, small_lanes = qkv_ref.shape[0], small_ref.shape[1]
    bias_lanes = bias_ref.shape[1]
    early_ref[:shard] = qkv_ref[...].astype(BF)
    spare = early_ref.shape[1] - small_lanes - bias_lanes
    bias = jnp.concatenate([bias_ref[...], jnp.zeros((small_ref.shape[0] - 1, bias_lanes), F32)], axis=0)
    early_ref[shard:] = jnp.concatenate(
        [small_ref[...], bias, jnp.zeros((small_ref.shape[0], spare), F32)], axis=1
    ).astype(BF)


def pack_late_kernel(out_ref, expand_ref, shrink_ref, late_ref):
    shard, channels = out_ref.shape
    begin = channels + expand_ref.shape[1]
    late_ref[:, :channels] = out_ref[...].astype(BF)
    late_ref[:, channels:begin] = expand_ref[...].astype(BF)
    for block in range(shrink_ref.shape[0] // shard):
        lanes = slice(begin + block * channels, begin + (block + 1) * channels)
        late_ref[:, lanes] = shrink_ref[block * shard : (block + 1) * shard].astype(BF)


def project_kernel(dims, ways, assembles, *refs):
    rows, width, wide, wide_part = dims
    me_ref, x_ref = refs[:2]
    if assembles:
        pieces = refs[2 : 2 + ways]
        across_ref, normed_ref = refs[2 + ways : 4 + ways]
        down_refs = refs[4 + ways : 4 + 2 * ways]
        weight_ref, small_ref, bias_ref, spread_ref = refs[4 + 2 * ways :]

        @pl.when(pl.program_id(0) == 0)
        def _():
            channels, hidden_width = small_ref.shape[1], bias_ref.shape[1]
            shard = channels // ways
            bias_shard = hidden_width // ways
            lanes = -(-(shard + bias_shard) // 128) * 128
            lane, column = iota((lanes, channels + hidden_width), 0), iota((lanes, channels + hidden_width), 1)
            total = jnp.zeros((16, channels + hidden_width), F32)
            for distance, piece in enumerate(pieces):
                place = me_ref[0] ^ distance
                weight_ref[pl.ds(pl.multiple_of(place * shard, shard), shard)] = piece[:shard]
                target = jnp.where(
                    lane < shard,
                    lane + shard * place,
                    channels + lane - shard + bias_shard * place,
                )
                chosen = one_hot((column == target) & (lane < shard + bias_shard))
                total = total + dot(piece[shard : shard + 16, :lanes], chosen)
            small_ref[...] = total[:, :channels]
            bias_ref[...] = total[0:1, channels:]

    else:
        weight_ref, small_ref, across_ref, normed_ref = refs[2:6]
        down_refs = refs[6 : 6 + ways]
        spread_ref = refs[6 + ways]
    gain, offset = small_ref[9:10], small_ref[10:11]
    expand = one_hot(expand_condition(wide, width))
    for row in range(rows):
        span = slice(row * width, (row + 1) * width)
        normed, _, _ = normalize(x_ref[0, span].astype(F32), gain, offset)
        normed = normed.astype(BF)
        normed_ref[0, span] = normed
        across_ref[0, span] = dot(normed, weight_ref[:, : 3 * HALF]).astype(BF)
        spread_ref[row] = dot(expand, normed).astype(BF)
        for distance in range(ways):
            start = pl.multiple_of((me_ref[0] ^ distance) * wide_part, wide_part)
            down_refs[distance][0, row] = spread_ref[row, pl.ds(start, wide_part)]


def rank_row(mask_row, width):
    lower = one_hot(iota((width, width), 0) <= iota((width, width), 1))
    counted = dot(jnp.broadcast_to(mask_row, (8, width)).astype(BF), lower)[0:1]
    return jnp.where(mask_row > 0.0, counted - 1.0, -1.0)


def across_kernel(
    dims,
    first,
    across_ref,
    mask_ref,
    small_ref,
    joined_ref,
    attended_ref,
    total_ref,
    keys_ref,
    values_ref,
    shift_ref,
):
    rows, width, kept, key_rows = dims
    image = pl.program_id(0)
    ranks = rank_row(mask_ref[pl.ds(image + first, 1)].astype(F32), width)
    select = one_hot(iota((kept, width), 0).astype(F32) == ranks)
    bias = jnp.where(iota((kept, HALF), 0) >= VALID, MASKED, 0.0)
    key_norms = jnp.zeros((1, HALF), F32)
    for row in range(rows):
        picked = dot(select, across_ref[0, row * width : (row + 1) * width, HALF:])
        key_norms = jnp.maximum(key_norms, head_norms(picked[:, :HALF]))
        span = slice(row * kept, (row + 1) * kept)
        keys_ref[0, span] = wide_keys(picked[:, :HALF], bias)
        values_ref[0, span] = wide_values(picked[:, HALF:])
    spare = key_rows - rows * kept
    if spare:
        nothing = jnp.zeros((spare, HALF), F32)
        keys_ref[0, rows * kept :] = wide_keys(nothing, nothing + MASKED)
        values_ref[0, rows * kept :] = wide_values(nothing)

    query_norms = head_norms(across_ref[0, :, :HALF].astype(F32) * (SCALE * LOG2E))
    large = exceeds(query_norms, key_norms)

    @pl.when(image == 0)
    def _():
        shift_ref[...] = jnp.zeros_like(shift_ref)

    @pl.when(large)
    def _():
        def highest(row, carry):
            span = pl.ds(pl.multiple_of(row * width, 16), width)
            shift_ref[span] = highest_scores(across_ref[0, span, :HALF].astype(F32), keys_ref[0])
            return carry

        lax.fori_loop(0, rows, highest, 0)

    def value_row(row):
        return across_ref[0, row * width : (row + 1) * width, 2 * HALF :].astype(F32)

    for row in range(rows):
        span = slice(row * width, (row + 1) * width)
        sums = [jnp.zeros((width, HALF), F32) for _ in range(3)]
        for tap_row in range(3):
            source = row + tap_row - 1
            if 0 <= source < rows:
                values = value_row(source)
                for tap_col in range(3):
                    tap = 3 * tap_row + tap_col
                    sums[tap_col] = sums[tap_col] + values * small_ref[tap : tap + 1, :HALF]
        local = shift_down(sums[0]) + sums[1] + shift_up(sums[2]) + small_ref[11:12, :HALF]
        queries = across_ref[0, span, :HALF].astype(F32)
        attended, log_total = attend_heads(queries, shift_ref[span], keys_ref[0], values_ref[0])
        attended_ref[0, span] = attended
        total_ref[0, span] = log_total
        joined_ref[0, span] = (attended + local).astype(BF)

    @pl.when(large)
    def _():
        shift_ref[...] = jnp.zeros_like(shift_ref)


def assemble(me_ref, pieces, target_ref, dim, step):
    for distance, piece in enumerate(pieces):
        place = me_ref[0] ^ distance
        if dim == 0:
            target_ref[pl.ds(place * step, step)] = piece[0].astype(target_ref.dtype)
        else:
            target_ref[:, pl.ds(pl.multiple_of(place * step, step), step)] = piece[0].astype(
                target_ref.dtype
            )


def down_setup(me_ref, mask_ref, column_ref, width, wide, wide_part, first):
    image = pl.program_id(0) + first
    mask_row = mask_ref[pl.ds(image, 1)].astype(F32)
    valid = one_hot(expand_condition(wide, width) & (mask_row > 0.0))
    column_ref[...] = dot(valid, jnp.ones((width, HALF), BF))
    return pl.multiple_of(me_ref[0] * wide_part, GROUP)


def window_bias(column_ref, start, window, height):
    valid = column_ref[pl.ds(start + pl.multiple_of(window * GROUP, GROUP), GROUP)]
    bias = jnp.where(valid > 0.5, 0.0, MASKED)
    return jnp.broadcast_to(bias[None], (height, GROUP, HALF)).reshape(height * GROUP, HALF)


def pad_keys(block, spare, fill):
    if not spare:
        return block
    return jnp.concatenate([block, jnp.full((spare, HALF), 0.0, F32) + fill], axis=0)


def window_operands(keys, values, bias, spare):
    return (
        wide_keys(pad_keys(keys, spare, 0.0), pad_keys(bias, spare, MASKED)),
        wide_values(pad_keys(values, spare, 0.0)),
    )


def grid_shift(values, amount):
    return pltpu.roll(values, amount % GROUP, 1)


def grid_stack(values):
    edge = jnp.zeros((1,) + values.shape[1:], F32)
    return jnp.concatenate([edge, values, edge], axis=0)


def down_kernel(dims, ways, first, *refs):
    height, width, wide, wide_part, spare = dims
    me_ref, mask_ref, small_ref, weight_ref = refs[:4]
    pieces_in = refs[4 : 4 + ways]
    joined_refs = refs[4 + ways : 4 + 2 * ways]
    attended_ref, total_ref, saved_ref, normed_out, mixed_ref, joined_ref, column_ref = refs[
        4 + 2 * ways :
    ]
    normed_ref = normed_out.at[0]
    rows = height // ways
    start = down_setup(me_ref, mask_ref, column_ref, width, wide, wide_part, first)
    assemble(me_ref, pieces_in, normed_ref, 0, rows)
    tokens = height * GROUP
    windows = wide_part // GROUP
    normed = normed_ref[...].reshape(height * wide_part, 2 * HALF)
    mixed_low = dot(normed, weight_ref[:, 3 * HALF :]).astype(BF)
    mixed_low = mixed_low.reshape(height, wide_part, 3 * HALF)
    saved_ref[0] = mixed_low
    mixed_ref[...] = mixed_low.astype(F32)

    everything = mixed_ref[...].reshape(height * wide_part, 3 * HALF)
    large = exceeds(
        head_norms(everything[:, :HALF] * (SCALE * LOG2E)), head_norms(everything[:, HALF : 2 * HALF])
    )

    def one_window(shifted, window, carry):
        span = pl.ds(pl.multiple_of(window * GROUP, GROUP), GROUP)
        grid = mixed_ref[:, span]
        flat = grid.reshape(tokens, 3 * HALF)
        queries, keys, values = (flat[:, part * HALF : (part + 1) * HALF] for part in range(3))
        bias = window_bias(column_ref, start, window, height)
        keys_in, values_in = window_operands(keys, values, bias, spare)

        shift = highest_scores(queries, keys_in) if shifted else None
        attended, log_total = attend_heads(queries, shift, keys_in, values_in)
        attended_ref[0, :, span] = attended.reshape(height, GROUP, HALF)
        total_ref[0, :, span] = log_total.reshape(height, GROUP, HALF)
        stacked = grid_stack(values.reshape(height, GROUP, HALF))
        sums = [jnp.zeros((height, GROUP, HALF), F32) for _ in range(3)]
        for tap_row in range(3):
            for tap_col in range(3):
                tap = 3 * tap_row + tap_col
                sums[tap_col] = sums[tap_col] + stacked[tap_row : tap_row + height] * small_ref[
                    tap : tap + 1, HALF:
                ].reshape(1, 1, HALF)
        local = grid_shift(sums[0], 1) + sums[1] + grid_shift(sums[2], -1)
        local = local + small_ref[11:12, HALF:].reshape(1, 1, HALF)
        joined_ref[:, span] = attended.reshape(height, GROUP, HALF) + local
        return carry

    @pl.when(jnp.logical_not(large))
    def _():
        lax.fori_loop(0, windows, functools.partial(one_window, False), 0, unroll=min(windows, 8))

    @pl.when(large)
    def _():
        lax.fori_loop(0, windows, functools.partial(one_window, True), 0)

    for distance in range(ways):
        place = me_ref[0] ^ distance
        joined_refs[distance][0] = joined_ref[pl.ds(place * rows, rows)].astype(BF)


def gelu_parts(hidden):
    upper = 0.5 + 0.5 * lax.erf(hidden * INV_ROOT_TWO)
    return upper, jnp.exp2(hidden * hidden * (-0.5 * LOG2E)) * INV_ROOT_TAU


def middle_kernel(dims, ways, *refs):
    rows, width, wide, wide_part, chunk, hidden_part = dims
    refs = list(refs)

    def take(number):
        taken = refs[:number]
        del refs[:number]
        return taken

    me_ref, x_ref, cot_ref, across_ref = take(4)
    pieces_in = [take(ways), take(ways)]
    weights_in = take(ways)
    small_ref, bias_ref = take(2)
    block_ref, middle_ref, grad_across_ref = take(3)
    grad_refs = take(ways)
    dbias_ref, dsmall_ref = take(2)
    piece_refs = take(ways)
    dout_ref, dexpand_ref, dshrink_ref = take(3)
    out_ref, expand_ref, shrink_ref = take(3)
    wide_ref, joined_ref, normed_ref, active_ref, hidden_ref, attended_ref, down_ref, gwide_ref = take(8)
    turned_ref = take(1)[0]
    tokens = rows * width
    hidden_width = expand_ref.shape[1]
    channels = 2 * HALF
    shard = channels // ways
    blocks = hidden_width // channels
    start_sums((dbias_ref, dsmall_ref, dout_ref, dexpand_ref, dshrink_ref), None)

    @pl.when(pl.program_id(0) == 0)
    def _():
        for distance, piece in enumerate(weights_in):
            place = me_ref[0] ^ distance
            span = pl.ds(pl.multiple_of(place * shard, shard), shard)
            out_ref[span] = piece[:, :channels]
            expand_ref[span] = piece[:, channels : channels + hidden_width]
            for block in range(blocks):
                begin = pl.multiple_of((place * blocks + block) * shard, shard)
                lanes = slice(channels + hidden_width + block * channels, channels + hidden_width + (block + 1) * channels)
                shrink_ref[pl.ds(begin, shard)] = piece[:, lanes]

    image, pair = pl.program_id(0), pl.num_programs(0) // 2

    @pl.when(image < pair)
    def _():
        assemble(me_ref, pieces_in[0], wide_ref, 1, wide_part)

    @pl.when(image >= pair)
    def _():
        assemble(me_ref, pieces_in[1], wide_ref, 1, wide_part)

    contract = contract_matrix(width, wide)
    for row in range(rows):
        span = slice(row * width, (row + 1) * width)
        joined_ref[span, :HALF] = across_ref[0, span]
        joined_ref[span, HALF:] = dot(contract, wide_ref[row]).astype(BF)

    def token_rows(step, carry):
        span = pl.ds(pl.multiple_of(step * chunk, 16), chunk)
        joined = joined_ref[span]
        attended_out = dot(joined, out_ref[...]) + small_ref[12:13]
        middle = x_ref[0, span].astype(F32) + attended_out
        normed, scaled, recip = normalize(middle, small_ref[13:14], small_ref[14:15])
        normed_low = normed.astype(BF)
        normed_ref[span] = normed_low
        back = cot_ref[0, span]
        result = middle + small_ref[15:16]
        grad_normed = jnp.zeros((chunk, 2 * HALF), F32)

        def products(part):
            lanes = slice(part, part + hidden_part)
            return dot(normed_low, expand_ref[:, lanes]), dot_nt(back, shrink_ref[lanes])

        def follow(result, grad_normed, behind):
            lanes, active, grad_hidden = behind
            return (
                result + dot(active, shrink_ref[lanes]),
                grad_normed + dot_nt(grad_hidden, expand_ref[:, lanes]),
            )

        ahead, behind = products(0), None
        for part in range(0, hidden_width, hidden_part):
            lanes = slice(part, part + hidden_part)
            hidden, grad_active = ahead
            if part + hidden_part < hidden_width:
                ahead = products(part + hidden_part)
            hidden = hidden + bias_ref[:, lanes]
            upper, density = gelu_parts(hidden)
            active = (hidden * upper).astype(BF)
            active_ref[span, lanes] = active
            grad_hidden = grad_active * (upper + hidden * density)
            grad_hidden = grad_hidden.astype(BF)
            hidden_ref[span, lanes] = grad_hidden
            dbias_ref[:, lanes] += fold_rows(grad_hidden.astype(F32))
            if part:
                result, grad_normed = follow(result, grad_normed, behind)
            behind = (lanes, active, grad_hidden)
        result, grad_normed = follow(result, grad_normed, behind)
        block_ref[0, span] = result
        back_wide = back.astype(F32)
        grad_middle = back_wide + normalize_back(grad_normed, scaled, recip, small_ref[13:14])
        middle_ref[0, span] = grad_middle
        grad_attended = grad_middle.astype(BF)
        attended_ref[span] = grad_attended
        grad_joined = dot_nt(grad_attended, out_ref[...]).astype(BF)
        grad_across_ref[0, span] = grad_joined[:, :HALF]
        down_ref[span] = grad_joined[:, HALF:]
        dsmall_ref[0:8] += fold_rows(grad_attended.astype(F32))
        dsmall_ref[8:16] += fold_rows(grad_normed * scaled)
        dsmall_ref[16:24] += fold_rows(grad_normed)
        dsmall_ref[24:32] += fold_rows(back_wide)
        return carry

    lax.fori_loop(0, tokens // chunk, token_rows, 0, unroll=True)
    expand = one_hot(expand_condition(wide, width))
    for row in range(rows):
        gwide_ref[row] = dot(expand, down_ref[row * width : (row + 1) * width]).astype(BF)
    for distance in range(ways):
        place = me_ref[0] ^ distance
        grad_refs[distance][0] = gwide_ref[
            :, pl.ds(pl.multiple_of(place * wide_part, wide_part), wide_part)
        ]
    dout_ref[...] += dot_tn(joined_ref[...], attended_ref[...])
    dexpand_ref[...] += dot_tn(normed_ref[...], hidden_ref[...])
    dshrink_ref[...] += dot_tn(cot_ref[0], active_ref[...])

    @at_last_step
    def _():
        for block in range(blocks):
            lanes = slice(block * channels, (block + 1) * channels)
            turned_ref[lanes] = jnp.transpose(dshrink_ref[:, lanes])
        for distance, piece in enumerate(piece_refs):
            place = me_ref[0] ^ distance
            span = pl.ds(pl.multiple_of(place * shard, shard), shard)
            piece[:, :channels] = dout_ref[span]
            piece[:, channels : channels + hidden_width] = dexpand_ref[span]
            for block in range(blocks):
                begin = pl.multiple_of((place * blocks + block) * shard, shard)
                lanes = slice(channels + hidden_width + block * channels, channels + hidden_width + (block + 1) * channels)
                piece[:, lanes] = turned_ref[pl.ds(begin, shard)]


def shard_pieces(me_ref, piece_refs, total_ref):
    shard = piece_refs[0].shape[0]

    @at_last_step
    def _():
        for distance, piece in enumerate(piece_refs):
            begin = pl.multiple_of((me_ref[0] ^ distance) * shard, shard)
            piece[...] = total_ref[pl.ds(begin, shard)]


def across_back_kernel(dims, first, last, *refs):
    rows, width, kept, key_rows, chunk = dims
    refs = list(refs)

    def take(number):
        taken = refs[:number]
        del refs[:number]
        return taken

    across_ref, grad_ref, attended_ref, total_ref, keys_ref, values_ref, normed_ref = take(7)
    mask_ref, small_ref = take(2)
    starts = take(2) if last else None
    mixed_ref, taps_ref, dweight_ref, dkeys_ref, dvalues_ref, local_ref = take(6)
    tokens = rows * width
    image = pl.program_id(0) + first
    start_sums((taps_ref, dweight_ref), starts)
    dkeys_ref[...] = jnp.zeros_like(dkeys_ref)
    dvalues_ref[...] = jnp.zeros_like(dvalues_ref)

    def attend(step, carry):
        span = pl.ds(pl.multiple_of(step * chunk, 16), chunk)
        grad_queries, grad_keys, grad_values = attend_heads_back(
            across_ref[0, span, :HALF].astype(F32),
            grad_ref[0, span].astype(F32),
            attended_ref[0, span],
            total_ref[0, span],
            keys_ref[0],
            values_ref[0],
        )
        mixed_ref[0, span, :HALF] = grad_queries.astype(BF)
        for head in range(BRANCH_HEADS):
            lanes = slice(head * HEAD_DIM, (head + 1) * HEAD_DIM)
            dkeys_ref[lanes] += grad_keys[head]
            dvalues_ref[lanes] += grad_values[head]
        return carry

    lax.fori_loop(0, tokens // chunk, attend, 0)

    local_ref[...] = jnp.zeros_like(local_ref)
    for row in range(rows):
        grad = grad_ref[0, row * width : (row + 1) * width].astype(F32)
        taps_ref[72:80] += fold_rows(grad)
        for tap_col, moved in enumerate((shift_up(grad), grad, shift_down(grad))):
            for tap_row in range(3):
                target = row + tap_row - 1
                if 0 <= target < rows:
                    tap = 3 * tap_row + tap_col
                    span = slice(target * width, (target + 1) * width)
                    values = across_ref[0, span, 2 * HALF :].astype(F32)
                    taps_ref[8 * tap : 8 * tap + 8] += fold_rows(values * moved)
                    local_ref[span] += moved * small_ref[tap : tap + 1, :HALF]

    ranks = rank_row(mask_ref[pl.ds(image, 1)].astype(F32), width)
    place = jnp.transpose(jnp.broadcast_to(ranks, (HALF, width)))
    spread = one_hot(iota((width, HALF), 1).astype(F32) == place)
    spread_more = one_hot((iota((width, kept - HALF), 1) + HALF).astype(F32) == place[:, : kept - HALF])
    spread = jnp.concatenate([spread, spread_more], axis=1)
    grad_keys = jnp.transpose(dkeys_ref[...]) * SCALE
    grad_values = jnp.transpose(dvalues_ref[...])
    high = grad_values.astype(BF)
    low = (grad_values - high.astype(F32)).astype(BF)
    grad_keys = grad_keys.astype(BF)
    for row in range(rows):
        span = slice(row * kept, (row + 1) * kept)
        packed = jnp.concatenate([grad_keys[span], high[span], low[span]], axis=1)
        unpacked = dot(spread, packed)
        target = slice(row * width, (row + 1) * width)
        mixed_ref[0, target, HALF : 2 * HALF] = unpacked[:, :HALF].astype(BF)
        whole = unpacked[:, HALF : 2 * HALF] + unpacked[:, 2 * HALF :] + local_ref[target]
        mixed_ref[0, target, 2 * HALF :] = whole.astype(BF)
    dweight_ref[...] += dot_tn(normed_ref[0], mixed_ref[0])


def down_back_kernel(dims, ways, *refs):
    height, width, wide, wide_part, spare = dims
    refs = list(refs)

    def take(number):
        taken = refs[:number]
        del refs[:number]
        return taken

    me_ref, mask_ref, small_ref, weight_ref, attended_ref, total_ref, saved_ref, normed_ref = take(8)
    grads_in = take(ways)
    out_refs = take(ways)
    taps_ref = take(1)[0]
    piece_refs = take(ways)
    dweight_ref, mixed_ref, grad_ref, out_ref, turned_ref, column_ref = take(6)
    rows = height // ways
    start = down_setup(me_ref, mask_ref, column_ref, width, wide, wide_part, 0)
    assemble(me_ref, grads_in, grad_ref, 0, rows)
    mixed_ref[...] = saved_ref[0].astype(F32)
    tokens = height * GROUP
    windows = wide_part // GROUP
    start_sums((taps_ref, dweight_ref), None)

    def one_window(window, carry):
        span = pl.ds(pl.multiple_of(window * GROUP, GROUP), GROUP)
        flat = mixed_ref[:, span].reshape(tokens, 3 * HALF)
        queries, keys, values = (flat[:, part * HALF : (part + 1) * HALF] for part in range(3))
        grad_grid = grad_ref[:, span]
        grad = grad_grid.reshape(tokens, HALF)
        bias = window_bias(column_ref, start, window, height)
        keys_in, values_in = window_operands(keys, values, bias, spare)
        grad_queries, grad_keys, grad_values = attend_heads_back(
            queries,
            grad,
            attended_ref[0, :, span].reshape(tokens, HALF),
            total_ref[0, :, span].reshape(tokens, HALF),
            keys_in,
            values_in,
        )
        grad_keys = jnp.transpose(jnp.concatenate(grad_keys, axis=0))[:tokens] * SCALE
        grad_values = jnp.transpose(jnp.concatenate(grad_values, axis=0))[:tokens]
        values_grid = values.reshape(height, GROUP, HALF)
        local = jnp.zeros((height, GROUP, HALF), F32)
        taps_ref[72:80] += jnp.sum(grad_grid, axis=0)
        shifted = (grid_shift(grad_grid, -1), grad_grid, grid_shift(grad_grid, 1))
        for tap_col, moved in enumerate(shifted):
            stacked = grid_stack(moved)
            for tap_row in range(3):
                tap = 3 * tap_row + tap_col
                source = stacked[2 - tap_row : 2 - tap_row + height]
                taps_ref[8 * tap : 8 * tap + 8] += jnp.sum(source * values_grid, axis=0)
                local = local + source * small_ref[tap : tap + 1, HALF:].reshape(1, 1, HALF)
        shape = (height, GROUP, HALF)
        out_ref[:, span, :HALF] = grad_queries.reshape(shape)
        out_ref[:, span, HALF : 2 * HALF] = grad_keys.reshape(shape)
        out_ref[:, span, 2 * HALF :] = grad_values.reshape(shape) + local
        return carry

    lax.fori_loop(0, windows, one_window, 0, unroll=min(windows, 8))
    mixed_grad = out_ref[...].reshape(height * wide_part, 3 * HALF).astype(BF)
    grad_normed = dot_nt(mixed_grad, weight_ref[:, 3 * HALF :]).astype(BF)
    turned_ref[...] = grad_normed.reshape(height, wide_part, 2 * HALF)
    for distance in range(ways):
        place = me_ref[0] ^ distance
        out_refs[distance][0] = turned_ref[pl.ds(place * rows, rows)]
    normed = normed_ref[0].reshape(height * wide_part, 2 * HALF)
    dweight_ref[...] += dot_tn(normed, mixed_grad)
    shard_pieces(me_ref, piece_refs, dweight_ref)


def final_kernel(dims, ways, last, *refs):
    rows, width, wide, wide_part, chunk = dims
    refs = list(refs)

    def take(number):
        taken = refs[:number]
        del refs[:number]
        return taken

    me_ref, x_ref, middle_ref, across_ref = take(4)
    pieces_in = take(ways)
    small_ref, weight_ref = take(2)
    starts = take(1) if last else None
    others = take(5) if last else None
    grad_ref, dsmall_ref = take(2)
    piece_refs = take(ways) if last else None
    wide_ref, down_ref = take(2)
    whole_ref = take(1)[0] if last else None
    tokens = rows * width
    start_sums((dsmall_ref,), starts)
    assemble(me_ref, pieces_in, wide_ref, 1, wide_part)
    contract = contract_matrix(width, wide)
    for row in range(rows):
        down_ref[row * width : (row + 1) * width] = dot(contract, wide_ref[row])

    def token_rows(step, carry):
        span = pl.ds(pl.multiple_of(step * chunk, 16), chunk)
        _, scaled, recip = normalize(x_ref[0, span].astype(F32), small_ref[9:10], small_ref[10:11])
        grad_normed = dot_nt(across_ref[0, span], weight_ref[:, : 3 * HALF]) + down_ref[span]
        dsmall_ref[0:8] += fold_rows(grad_normed * scaled)
        dsmall_ref[8:16] += fold_rows(grad_normed)
        grad_ref[0, span] = middle_ref[0, span] + normalize_back(
            grad_normed, scaled, recip, small_ref[9:10]
        )
        return carry

    lax.fori_loop(0, tokens // chunk, token_rows, 0)
    if last:

        @at_last_step
        def _():
            across_taps, down_taps, middle_sums, bias_sums, dweight = others
            channels = 2 * HALF

            def total(ref, index):
                return jnp.sum(ref[8 * index : 8 * index + 8], axis=0, keepdims=True)

            def set_taps(row, index):
                whole_ref[row : row + 1, :HALF] = total(across_taps, index)
                whole_ref[row : row + 1, HALF:] = total(down_taps, index)

            whole_ref[...] = jnp.zeros_like(whole_ref)
            for tap in range(9):
                set_taps(tap, tap)
            whole_ref[9:10] = total(dsmall_ref, 0)
            whole_ref[10:11] = total(dsmall_ref, 1)
            set_taps(11, 9)
            for index in range(4):
                whole_ref[12 + index : 13 + index] = total(middle_sums, index)
            bias = total(bias_sums, 0)
            for block in range(bias.shape[1] // channels):
                whole_ref[16 + block : 17 + block] = bias[:, block * channels : (block + 1) * channels]
            shard = dweight.shape[0] // ways
            for distance, piece in enumerate(piece_refs):
                begin = pl.multiple_of((me_ref[0] ^ distance) * shard, shard)
                piece[:shard] = dweight[pl.ds(begin, shard)].astype(BF)
                piece[shard:, :channels] = whole_ref[...].astype(BF)
                piece[shard:, channels:] = jnp.zeros(
                    (whole_ref.shape[0], dweight.shape[1] - channels), BF
                )


def last_back_kernel(dims, final_dims, ways, first, *refs):
    refs = list(refs)

    def take(number):
        taken = refs[:number]
        del refs[:number]
        return taken

    attention_in = take(9)
    attention_starts = take(2)
    me_ref, x_ref, middle_ref = take(3)
    pieces_in = take(ways)
    small_ref, weight_ref, norm_start, down_taps, middle_sums, bias_sums = take(6)
    grad_ref = take(1)[0]
    piece_refs = take(ways)
    mixed_ref, taps_ref, dweight_ref, dkeys_ref, dvalues_ref, local_ref = take(6)
    dsmall_ref, wide_ref, down_ref, whole_ref = take(4)
    across_back_kernel(
        dims,
        first,
        True,
        *attention_in,
        *attention_starts,
        mixed_ref,
        taps_ref,
        dweight_ref,
        dkeys_ref,
        dvalues_ref,
        local_ref,
    )
    final_kernel(
        final_dims,
        ways,
        True,
        me_ref,
        x_ref,
        middle_ref,
        mixed_ref,
        *pieces_in,
        small_ref,
        weight_ref,
        norm_start,
        taps_ref,
        down_taps,
        middle_sums,
        bias_sums,
        dweight_ref,
        grad_ref,
        dsmall_ref,
        *piece_refs,
        wide_ref,
        down_ref,
        whole_ref,
    )


def update_kernel(ways, place_ref, mine_ref, other_ref, tail_ref, *refs):
    squares, old, new = refs[:ways], refs[ways : ways + 18], refs[ways + 19 : ways + 37]
    norm_ref, joined_ref = refs[ways + 18], refs[ways + 37]
    me, core = place_ref[0], place_ref[1]
    half = mine_ref.shape[0]
    joined_ref[pl.ds(pl.multiple_of(core * half, half), half)] = mine_ref[...]
    joined_ref[pl.ds(pl.multiple_of((1 - core) * half, half), half)] = other_ref[...]
    shard = 2 * half
    rows, channels = old[1].shape
    hidden_width = old[2].shape[1]
    blocks = hidden_width // channels
    small = tail_ref[shard:, :channels]
    small_rows, small_lanes = old[4].shape
    bias_lanes = old[5].shape[1]
    total = tree_sum([entry[...] for entry in squares]) + jnp.sum(small * small)
    norm = jnp.sqrt(total)
    norm_ref[0, 0] = jnp.max(norm)
    factor = (CLIP_NORM / jnp.maximum(norm, CLIP_NORM))[0:1, 0:1]

    def update(index, grads, rate, decay, spans=(slice(None), slice(None))):
        weight, first, second = (old[part * 6 + index][spans] for part in range(3))
        results = adam_update(weight, first, second, grads * factor, rate, decay)
        for part in range(3):
            new[part * 6 + index][spans] = results[part]

    update(0, tail_ref[:shard], RATE_MATRIX, WEIGHT_DECAY, (slice(None), slice(0, 3 * HALF)))
    begin = channels + 2 * hidden_width
    update(
        0,
        joined_ref[:, begin : begin + 3 * HALF],
        RATE_MATRIX,
        WEIGHT_DECAY,
        (slice(None), slice(3 * HALF, 6 * HALF)),
    )
    update(1, joined_ref[:, :channels], RATE_OUTPUT, WEIGHT_DECAY)
    update(2, joined_ref[:, channels : channels + hidden_width], RATE_MATRIX, WEIGHT_DECAY)
    for block in range(blocks):
        begin = channels + hidden_width + block * channels
        update(
            3,
            joined_ref[:, begin : begin + channels],
            RATE_MATRIX,
            WEIGHT_DECAY,
            (slice(block * rows, (block + 1) * rows), slice(None)),
        )
    small_grad = jnp.zeros((small_rows, small_lanes), F32)
    bias_grad = jnp.zeros((1, bias_lanes), F32)
    for place in range(ways):
        lanes = slice(place * small_lanes, (place + 1) * small_lanes)
        small_grad = jnp.where(me == place, small[:small_rows, lanes], small_grad)
        row, lane = divmod(place * bias_lanes, channels)
        row = small_rows + row
        bias_grad = jnp.where(me == place, small[row : row + 1, lane : lane + bias_lanes], bias_grad)
    update(4, small_grad, RATE_SMALL, 0.0)
    update(5, bias_grad, RATE_MATRIX, 0.0)


def image_block(*shape, first=0):
    return pl.BlockSpec((1,) + shape, lambda image: (image + first,) + (0,) * len(shape))


def whole_block(*shape):
    return pl.BlockSpec(shape, lambda image: (0,) * len(shape))


def scalar_block():
    return pl.BlockSpec(memory_space=pltpu.SMEM)


def run_kernel(body, images, inputs, outputs, scratch, micros, after=(), alias=()):
    number, made = len(inputs), len(outputs)
    hidden = list(after)
    aliases = {}
    for operand, output in alias:
        aliases[number + len(hidden)] = output
        hidden.append(operand)
    skipped = number + len(hidden)

    def wrapped(*refs):
        refs[skipped + made][...] = jnp.zeros((8, 128), F32)
        body(*refs[:number], *refs[skipped : skipped + made], *refs[skipped + made + 1 :])

    outputs = list(outputs) + [((8, 128), F32, whole_block(8, 128))]
    *results, token = pl.pallas_call(
        wrapped,
        grid=(images,),
        in_specs=[spec for _, spec in inputs] + [pl.BlockSpec(memory_space=pl.ANY)] * len(hidden),
        out_specs=[spec for _, _, spec in outputs],
        out_shape=[jax.ShapeDtypeStruct(shape, dtype) for shape, dtype, _ in outputs],
        scratch_shapes=scratch,
        input_output_aliases=aliases,
        compiler_params=pltpu.CompilerParams(vmem_limit_bytes=VMEM_LIMIT),
        cost_estimate=pl.CostEstimate(
            flops=int(micros * 1e9), bytes_accessed=int(micros * 1e6), transcendentals=0
        ),
    )(*[operand for operand, _ in inputs], *hidden)
    return results, token


def adam_update(weight, first_old, second_old, grad_value, rate_value, decay_value):
    new_first = BETA_ONE * first_old + (1.0 - BETA_ONE) * grad_value
    new_second = BETA_TWO * second_old + (1.0 - BETA_TWO) * grad_value * grad_value
    first_hat = new_first / (1.0 - BETA_ONE**STEP)
    second_hat = new_second / (1.0 - BETA_TWO**STEP)
    new_weight = weight - rate_value * (
        first_hat / (jnp.sqrt(second_hat) + ADAM_EPS) + decay_value * weight
    )
    return (new_first, new_second, new_weight)


def swap(value, axis, distance):
    return lax.ppermute(value, axis, [(place, place ^ distance) for place in range(lax.axis_size(axis))])


def exchange(pieces):
    return [pieces[0]] + [swap(pieces[d], "seq", d) for d in range(1, len(pieces))]


def tree_sum(values):
    while len(values) > 1:
        values = [values[i] + values[i + 1] for i in range(0, len(values), 2)]
    return values[0]


def share_low(value, distances):
    rounded = lax.reduce_precision(value, 8, 7)
    sent = rounded.astype(BF)
    return [rounded] + [swap(sent, "img", distance).astype(F32) for distance in distances]


def on_device(
    images,
    cotangent,
    valid_mask,
    qkv_weight,
    out_weight,
    expand_weight,
    shrink_weight,
    small_params,
    expand_bias,
    first_qkv,
    first_out,
    first_expand,
    first_shrink,
    first_small,
    first_bias,
    second_qkv,
    second_out,
    second_expand,
    second_shrink,
    second_small,
    second_bias,
):
    ways = lax.axis_size("seq")
    owner = lax.axis_index("seq")
    me = owner.astype(jnp.int32).reshape(1)
    count, rows, width, channels = images.shape
    tokens = rows * width
    height = rows * ways
    wide = width // STRIPE * GROUP
    wide_part = wide // ways
    kept = -(-VALID // 16) * 16
    key_rows = -(-rows * kept // 256) * 256
    window_tokens = height * GROUP
    spare = -window_tokens % 128
    shard = qkv_weight.shape[0]
    hidden_width = expand_weight.shape[1]
    blocks = hidden_width // channels
    pair = count // 2
    chip_steps = [2 << bit for bit in range((lax.axis_size("img") // 2).bit_length() - 1)][::-1]

    x = images.reshape(count, tokens, channels)
    cot = cotangent.reshape(count, tokens, channels)
    me_in = (me, scalar_block())
    mask_in = (valid_mask, whole_block(*valid_mask.shape))
    piece_in = (rows, wide_part, channels)
    piece_out = (rows, wide_part, HALF)
    qkv_shape = (channels, 6 * HALF)

    def per_image(array, first=0):
        return (array, image_block(*array.shape[1:], first=first))

    def whole(array):
        return (array, whole_block(*array.shape))

    def half_images(array, first):
        last = array.shape[0] - 1
        dims = (1,) + array.shape[1:]
        return (
            array,
            pl.BlockSpec(
                dims, lambda image: (jnp.clip(image - first, 0, last),) + (0,) * (len(dims) - 1)
            ),
        )

    def new_image(dims, dtype, images):
        return ((images,) + dims, dtype, image_block(*dims))

    def part_image(dims, dtype, first):
        return ((count,) + dims, dtype, image_block(*dims, first=first))

    def new_whole(dims, dtype):
        return (dims, dtype, whole_block(*dims))

    (early,), _ = run_kernel(
        pack_early_kernel,
        1,
        [whole(qkv_weight), whole(small_params), whole(expand_bias.reshape(1, -1))],
        [new_whole((shard + 16, qkv_weight.shape[1]), BF)],
        [],
        2,
    )
    weights_in = exchange([early] * ways)
    (late,), _ = run_kernel(
        pack_late_kernel,
        1,
        [whole(out_weight), whole(expand_weight), whole(shrink_weight)],
        [new_whole((shard, channels + 2 * hidden_width), BF)],
        [],
        2,
        after=(early,),
    )

    whole_images, normed_pieces, parameters = [], [], None
    for first in (0, pair):
        assembles = first == 0
        results, token = run_kernel(
            functools.partial(project_kernel, (rows, width, wide, wide_part), ways, assembles),
            pair,
            [me_in, per_image(x, first)] + [whole(entry) for entry in weights_in],
            [part_image((tokens, 3 * HALF), BF, first), part_image((tokens, channels), BF, first)]
            + [new_image(piece_in, BF, pair)] * ways
            + (
                [new_whole(qkv_shape, BF), new_whole((16, channels), F32), new_whole((1, hidden_width), F32)]
                if assembles
                else []
            ),
            [pltpu.VMEM((rows, wide, channels), BF)],
            6,
            alias=[(entry, place) for place, entry in enumerate(whole_images)],
        )
        whole_images = results[:2]
        normed_pieces.append(exchange(results[2 : 2 + ways]))
        if assembles:
            qkv_low, small_full, bias_full = results[2 + ways :]
            weights_in = (qkv_low, small_full)
    across_mixed, normed = whole_images
    small_in, qkv_in = whole(small_full), whole(qkv_low)

    attention_dims = (rows, width, kept, key_rows)
    key_shape = (key_rows, channels)
    across = []

    def run_across(first, images_in, after):
        return run_kernel(
            functools.partial(across_kernel, attention_dims, first),
            images_in,
            [per_image(across_mixed, first), mask_in, small_in],
            [
                part_image((tokens, HALF), BF, first),
                part_image((tokens, HALF), F32, first),
                part_image((tokens, HALF), F32, first),
                part_image(key_shape, BF, first),
                part_image(key_shape, BF, first),
            ],
            [pltpu.VMEM((tokens, HALF), F32)],
            11 * images_in,
            after=after,
            alias=[(entry, place) for place, entry in enumerate(across)],
        )

    across, token = run_across(0, count - 1, (token,))
    late, token = lax.optimization_barrier((late, token))
    late_pieces = exchange([late] * ways)
    normed_pieces, token = lax.optimization_barrier((normed_pieces, token))

    down_dims = (height, width, wide, wide_part, spare)
    grid_f32 = (height, wide_part, HALF)
    mixed_grid = (height, wide_part, 3 * HALF)
    normed_grid = (height, wide_part, channels)
    down, joined_pieces = [], []
    for index, first in enumerate((0, pair)):
        results, token = run_kernel(
            functools.partial(down_kernel, down_dims, ways, first),
            pair,
            [me_in, mask_in, small_in, qkv_in] + [per_image(piece) for piece in normed_pieces[index]],
            [new_image(piece_out, BF, pair)] * ways
            + [part_image(grid_f32, F32, first)] * 2
            + [part_image(mixed_grid, BF, first), part_image(normed_grid, BF, first)],
            [
                pltpu.VMEM(mixed_grid, F32),
                pltpu.VMEM(grid_f32, F32),
                pltpu.VMEM((wide, HALF), F32),
            ],
            15,
            after=(token,),
            alias=[(entry, ways + place) for place, entry in enumerate(down)],
        )
        down = results[ways:]
        joined_pieces.append(exchange(results[:ways]))
    across, token = run_across(count - 1, 1, (token,))
    joined_across, attended, log_total, keys, values = across

    matrix_sums = [(channels, channels), (channels, hidden_width), (channels, hidden_width)]
    results, token = run_kernel(
        functools.partial(middle_kernel, (rows, width, wide, wide_part, tokens // 2, channels), ways),
        count,
        [me_in, per_image(x), per_image(cot), per_image(joined_across)]
        + [half_images(piece, 0) for piece in joined_pieces[0]]
        + [half_images(piece, pair) for piece in joined_pieces[1]]
        + [whole(piece) for piece in late_pieces]
        + [small_in, whole(bias_full)],
        [
            new_image((tokens, channels), F32, count),
            new_image((tokens, channels), F32, count),
            new_image((tokens, HALF), BF, count),
        ]
        + [new_image(piece_out, BF, count)] * ways
        + [new_whole((8, hidden_width), F32), new_whole((32, channels), F32)]
        + [new_whole(late.shape, F32)] * ways,
        [pltpu.VMEM(dims, F32) for dims in matrix_sums]
        + [
            pltpu.VMEM((channels, channels), BF),
            pltpu.VMEM((channels, hidden_width), BF),
            pltpu.VMEM((hidden_width, channels), BF),
            pltpu.VMEM((rows, wide, HALF), BF),
            pltpu.VMEM((tokens, channels), BF),
            pltpu.VMEM((tokens, channels), BF),
            pltpu.VMEM((tokens, hidden_width), BF),
            pltpu.VMEM((tokens, hidden_width), BF),
            pltpu.VMEM((tokens, channels), BF),
            pltpu.VMEM((tokens, HALF), BF),
            pltpu.VMEM((rows, wide, HALF), BF),
            pltpu.VMEM((hidden_width, channels), F32),
        ],
        45,
        after=(token,),
    )
    block_out, grad_middle, grad_across = results[:3]
    grad_pieces = exchange(results[3 : 3 + ways])
    bias_sums, middle_sums, *late_sums = results[3 + ways :]

    qkv_half = (channels, 3 * HALF)
    half_shard = (shard, 3 * HALF)
    back_sums, norm_sums, input_grad = None, None, None

    def run_across_back(first, images_in, sums, after):
        results, token = run_kernel(
            functools.partial(
                across_back_kernel, (*attention_dims, tokens // 2), first, sums is not None
            ),
            images_in,
            [
                per_image(across_mixed, first),
                per_image(grad_across, first),
                per_image(attended, first),
                per_image(log_total, first),
                per_image(keys, first),
                per_image(values, first),
                per_image(normed, first),
                mask_in,
                small_in,
            ]
            + ([whole(entry) for entry in sums[1:]] if sums else []),
            [
                part_image((tokens, 3 * HALF), BF, first),
                new_whole((80, HALF), F32),
                new_whole(qkv_half, F32),
            ],
            [
                pltpu.VMEM((HALF, key_rows), F32),
                pltpu.VMEM((HALF, key_rows), F32),
                pltpu.VMEM((tokens, HALF), F32),
            ],
            23 * images_in,
            after=after,
            alias=[(sums[0], 0)] if sums else [],
        )
        return results, token

    def run_final(first, images_in, after):
        return run_kernel(
            functools.partial(final_kernel, (rows, width, wide, wide_part, tokens), ways, False),
            images_in,
            [me_in, per_image(x, first), per_image(grad_middle, first), per_image(back_sums[0], first)]
            + [per_image(piece, first) for piece in grad_normed_pieces]
            + [small_in, qkv_in],
            [part_image((tokens, channels), F32, first), new_whole((16, channels), F32)],
            [pltpu.VMEM((rows, wide, channels), BF), pltpu.VMEM((tokens, channels), F32)],
            4 * images_in,
            after=after,
        )

    back_sums, token = run_across_back(0, 1, None, (token,))
    *late_sums, token = lax.optimization_barrier((*late_sums, token))
    late_parts = exchange(late_sums)
    results, token = run_kernel(
        functools.partial(down_back_kernel, down_dims, ways),
        count,
        [me_in, mask_in, small_in, qkv_in]
        + [per_image(entry) for entry in down]
        + [per_image(piece) for piece in grad_pieces],
        [new_image(piece_in, BF, count)] * ways
        + [new_whole((80, HALF), F32)]
        + [new_whole(half_shard, F32)] * ways,
        [
            pltpu.VMEM(qkv_half, F32),
            pltpu.VMEM(mixed_grid, F32),
            pltpu.VMEM(grid_f32, F32),
            pltpu.VMEM(mixed_grid, F32),
            pltpu.VMEM(normed_grid, BF),
            pltpu.VMEM((wide, HALF), F32),
        ],
        38,
        after=(token,),
    )
    down_taps, *down_sums = results[ways:]
    late_parts, token = lax.optimization_barrier((late_parts, token))
    late_seq = tree_sum(late_parts)
    core_place = lax.axis_index("img") % 2
    half = shard // 2
    down_parts = exchange(down_sums)
    grad_sent, late_seq = lax.optimization_barrier((results[:ways], late_seq))
    grad_normed_pieces = exchange(grad_sent)
    back_sums, token = run_across_back(1, count - 2, back_sums, (token, late_seq))
    down_parts, late_seq, token = lax.optimization_barrier((down_parts, late_seq, token))
    seq_sum = jnp.concatenate([late_seq, tree_sum(down_parts)], axis=1)
    kept_half = lax.dynamic_slice_in_dim(seq_sum, core_place * half, half, 0)
    core_half = swap(lax.dynamic_slice_in_dim(seq_sum, (1 - core_place) * half, half, 0), "img", 1)
    (input_grad, norm_sums), token = run_final(0, count - 1, (token,))
    kept_half, core_half, token = lax.optimization_barrier((kept_half, core_half, token))
    halves_sum = kept_half + core_half
    chip_half = swap(halves_sum, "img", chip_steps[0])
    final = count - 1
    (input_grad, *tail_sums), token = run_kernel(
        functools.partial(
            last_back_kernel,
            (*attention_dims, tokens // 2),
            (rows, width, wide, wide_part, tokens),
            ways,
            final,
        ),
        1,
        [
            per_image(across_mixed, final),
            per_image(grad_across, final),
            per_image(attended, final),
            per_image(log_total, final),
            per_image(keys, final),
            per_image(values, final),
            per_image(normed, final),
            mask_in,
            small_in,
            whole(back_sums[1]),
            whole(back_sums[2]),
            me_in,
            per_image(x, final),
            per_image(grad_middle, final),
        ]
        + [per_image(piece, final) for piece in grad_normed_pieces]
        + [small_in, qkv_in]
        + [whole(entry) for entry in (norm_sums, down_taps, middle_sums, bias_sums)],
        [part_image((tokens, channels), F32, final)]
        + [new_whole((shard + 32, 3 * HALF), BF)] * ways,
        [
            pltpu.VMEM((1, tokens, 3 * HALF), BF),
            pltpu.VMEM((80, HALF), F32),
            pltpu.VMEM(qkv_half, F32),
            pltpu.VMEM((HALF, key_rows), F32),
            pltpu.VMEM((HALF, key_rows), F32),
            pltpu.VMEM((tokens, HALF), F32),
            pltpu.VMEM((16, channels), F32),
            pltpu.VMEM((rows, wide, channels), BF),
            pltpu.VMEM((tokens, channels), F32),
            pltpu.VMEM((32, channels), F32),
        ],
        26,
        after=(token,),
        alias=[(input_grad, 0)],
    )
    halves_sum = halves_sum + chip_half
    halves_sum, *tail_sums = lax.optimization_barrier((halves_sum, *tail_sums))
    chip_half = [swap(halves_sum, "img", distance) for distance in chip_steps[1:2]]
    tail_parts, halves_sum, chip_half = lax.optimization_barrier(
        (exchange(tail_sums), halves_sum, chip_half)
    )
    halves_sum = tree_sum([halves_sum, *chip_half])
    for distance in chip_steps[2:]:
        halves_sum = halves_sum + swap(halves_sum, "img", distance)
    other_half = swap(halves_sum, "img", 1)
    tail = tree_sum([part.astype(F32) for part in tail_parts])
    tail = tree_sum(share_low(tail, [1]))
    tail = tree_sum(share_low(tail, range(2, lax.axis_size("img"), 2)))

    squared = (
        jnp.sum(halves_sum * halves_sum)
        + jnp.sum(other_half * other_half)
        + jnp.sum(tail[:shard] * tail[:shard])
    )
    squares = exchange([jnp.full((8, 128), squared)] * ways)

    def as_rows(entries):
        return [entry.reshape(1, -1) if entry.ndim == 1 else entry for entry in entries]

    state = as_rows(
        (qkv_weight, out_weight, expand_weight, shrink_weight, small_params, expand_bias)
        + (first_qkv, first_out, first_expand, first_shrink, first_small, first_bias)
        + (second_qkv, second_out, second_expand, second_shrink, second_small, second_bias)
    )
    place_in = jnp.stack([owner, core_place]).astype(jnp.int32)
    (norm, *updated), _ = run_kernel(
        functools.partial(update_kernel, ways),
        1,
        [(place_in, scalar_block())]
        + [whole(entry) for entry in (halves_sum, other_half, tail, *squares, *state)],
        [((1, 1), F32, scalar_block())] + [new_whole(entry.shape, F32) for entry in state[:6]] * 3,
        [pltpu.VMEM((shard, halves_sum.shape[1]), F32)],
        4,
    )
    for index in (5, 11, 17):
        updated[index] = updated[index].reshape(-1)
    return (
        block_out.reshape(images.shape),
        input_grad.reshape(images.shape),
        norm.reshape(()),
        *updated,
    )


def solution(mesh):
    sharded = (
        P("seq", None),
        P("seq", None),
        P("seq", None),
        P("seq", None),
        P(None, "seq"),
        P("seq"),
    )
    grid = P("img", "seq", None, None)
    return jax.shard_map(
        on_device,
        mesh=mesh,
        in_specs=(grid, grid, P("img", None)) + sharded * 3,
        out_specs=(grid, grid, P()) + sharded * 3,
        check_vma=False,
    )
```

```python
import functools

import jax
import jax.numpy as jnp
from jax import lax
from jax.experimental import pallas as pl
from jax.experimental.pallas import tpu as pltpu
from jax.sharding import PartitionSpec as P

HEADS = 8
STRIPE = 7
STEP = 10
VALID = 168

EPS_NORM = 1e-05
BETA_ONE = 0.9
BETA_TWO = 0.999
ADAM_EPS = 1e-08
WEIGHT_DECAY = 0.05
CLIP_NORM = 1.0
RATE_MATRIX = 0.1
RATE_OUTPUT = 0.5
RATE_SMALL = 0.3
INV_ROOT_TWO = 0.7071067811865476
INV_ROOT_TAU = 0.3989422804014327
LOG2E = 1.4426950408889634

BF = jnp.bfloat16
F32 = jnp.float32
HALF = 128
BRANCH_HEADS = 4
HEAD_DIM = 32
SCALE = HEAD_DIM**-0.5
GROUP = 8
MASKED = -1e38
EXPONENT_SCALE = SCALE * LOG2E
EXPONENT_BOUND = 60.0
VMEM_LIMIT = 60 * 2**20


def dot(left, right):
    return jnp.dot(left, right, preferred_element_type=F32)


def dot_nt(left, right):
    return lax.dot_general(left, right, (((1,), (1,)), ((), ())), preferred_element_type=F32)


def dot_tn(left, right):
    return lax.dot_general(left, right, (((0,), (0,)), ((), ())), preferred_element_type=F32)


def iota(shape, dim):
    return lax.broadcasted_iota(jnp.int32, shape, dim)


def one_hot(condition):
    return jnp.where(condition, 1.0, 0.0).astype(BF)


def expand_condition(wide, width):
    e, c = iota((wide, width), 0), iota((wide, width), 1)
    return ((e & 7) < STRIPE) & (c == STRIPE * (e >> 3) + (e & 7))


def contract_matrix(width, wide):
    c, e = iota((width, wide), 0), iota((width, wide), 1)
    return one_hot(((e & 7) < STRIPE) & (c == STRIPE * (e >> 3) + (e & 7)))


def normalize(values, gain_row, offset_row):
    center = values - jnp.mean(values, axis=-1, keepdims=True)
    spread = jnp.mean(center * center, axis=-1, keepdims=True)
    recip = lax.rsqrt(spread + EPS_NORM)
    scaled = center * recip
    return scaled * gain_row + offset_row, scaled, recip


def normalize_back(grad_out, scaled, recip, gain_row):
    grad_scaled = grad_out * gain_row
    inner_one = jnp.mean(grad_scaled, axis=-1, keepdims=True)
    inner_two = jnp.mean(grad_scaled * scaled, axis=-1, keepdims=True)
    return recip * (grad_scaled - inner_one - scaled * inner_two)


def fold_rows(values):
    rows, columns = values.shape
    return jnp.sum(values.reshape(rows // 8, 8, columns), axis=0)


def pieces_of(values):
    first = values.astype(BF).astype(F32)
    rest = values - first
    second = rest.astype(BF).astype(F32)
    return first, second, (rest - second).astype(BF).astype(F32)


def lane_head(rows):
    return (iota((rows, HALF), 1) >> 5) & 3


def lane_sub(rows):
    return iota((rows, HALF), 1) & 31


def piece_lanes(values, fourth):
    one, two, three = pieces_of(values)
    sub = lane_sub(values.shape[0])
    return jnp.where(
        sub == 0, one, jnp.where(sub == 1, two, jnp.where(sub == 2, three, jnp.where(sub == 3, fourth, 0.0)))
    )


def wide_keys(keys, bias):
    sub = lane_sub(keys.shape[0])
    extra = jnp.where(sub < 3, 1.0, jnp.where(sub == 3, bias, 0.0))
    return jnp.concatenate([keys.astype(BF), extra.astype(BF)], axis=1)


def wide_values(values):
    return jnp.concatenate([values.astype(BF), jnp.ones(values.shape, BF)], axis=1)


def stack_heads(left, right):
    head_of = lane_head(left.shape[0])
    parts = []
    for head in range(BRANCH_HEADS):
        mine = head_of == head
        parts.append(
            jnp.concatenate(
                [jnp.where(mine, left, 0.0).astype(BF), jnp.where(mine, right, 0.0).astype(BF)], axis=1
            )
        )
    return jnp.concatenate(parts, axis=0)


def pick_heads(stacked, rows):
    head_of = lane_head(rows)
    picked = stacked[:rows]
    for head in range(1, BRANCH_HEADS):
        picked = jnp.where(head_of == head, stacked[head * rows : (head + 1) * rows], picked)
    return picked


def head_norms(values):
    block = one_hot((iota((HALF, HALF), 0) >> 5) == (iota((HALF, HALF), 1) >> 5))
    sums = dot((values * values * 1.02).astype(BF), block)
    return jnp.max(sums, axis=0, keepdims=True)


def exceeds(query_norms, key_norms):
    bound = jnp.max(query_norms * key_norms)
    return jnp.logical_not(bound <= EXPONENT_BOUND * EXPONENT_BOUND)


def stack_queries(queries, shift):
    if shift is None:
        return stack_heads(queries, jnp.where(lane_sub(queries.shape[0]) == 3, 1.0, 0.0))
    return stack_heads(queries, piece_lanes(shift * (-1.0 / EXPONENT_SCALE), 1.0))


def attend_heads(queries, shift, keys, values):
    rows = queries.shape[0]
    scores = dot_nt(stack_queries(queries, shift), keys)
    weights = jnp.exp2(scores * EXPONENT_SCALE).astype(BF)
    result = dot(weights, values)
    totals = pick_heads(result[:, HALF:], rows)
    log_total = jnp.log(totals) * LOG2E
    if shift is not None:
        log_total = log_total + shift
    return pick_heads(result[:, :HALF], rows) / totals, log_total


def highest_scores(queries, keys):
    rows = queries.shape[0]
    scores = dot_nt(stack_queries(queries, None), keys)
    highest = jnp.max(scores, axis=-1, keepdims=True) * EXPONENT_SCALE
    return pick_heads(jnp.broadcast_to(highest, (BRANCH_HEADS * rows, HALF)), rows)


def attend_heads_back(queries, grad, attended, log_total, keys, values):
    rows = queries.shape[0]
    query_turned = jnp.transpose(queries).astype(BF)
    grad_turned = jnp.transpose(grad).astype(BF)
    block = one_hot((iota((HALF, HALF), 0) >> 5) == (iota((HALF, HALF), 1) >> 5))
    inner = sum(dot(piece.astype(BF), block) for piece in pieces_of(grad * attended)[:2])
    weights = jnp.exp2(dot_nt(stack_queries(queries, log_total), keys) * EXPONENT_SCALE)
    weights_low = weights.astype(BF)
    grad_weights = dot_nt(stack_heads(grad, piece_lanes(-inner, 0.0)), values)
    grad_scores = (weights * grad_weights).astype(BF)
    grad_queries = pick_heads(dot(grad_scores, keys[:, :HALF]), rows) * SCALE
    grad_keys, grad_values = [], []
    for head in range(BRANCH_HEADS):
        lanes = slice(head * HEAD_DIM, (head + 1) * HEAD_DIM)
        span = slice(head * rows, (head + 1) * rows)
        grad_values.append(dot(grad_turned[lanes], weights_low[span]))
        grad_keys.append(dot(query_turned[lanes], grad_scores[span]))
    return grad_queries, grad_keys, grad_values


def shift_down(values):
    rows = values.shape[0]
    return jnp.where(iota(values.shape, 0) == 0, 0.0, pltpu.roll(values, 1, 0))


def shift_up(values):
    rows = values.shape[0]
    return jnp.where(iota(values.shape, 0) == rows - 1, 0.0, pltpu.roll(values, rows - 1, 0))


def start_sums(sums, starts):
    @pl.when(pl.program_id(0) == 0)
    def _():
        for index, total in enumerate(sums):
            if starts:
                total[...] = starts[index][...]
            else:
                total[...] = jnp.zeros_like(total)


def at_last_step(body):
    pl.when(pl.program_id(0) == pl.num_programs(0) - 1)(body)


def pack_early_kernel(qkv_ref, small_ref, bias_ref, early_ref):
    shard, small_lanes = qkv_ref.shape[0], small_ref.shape[1]
    bias_lanes = bias_ref.shape[1]
    early_ref[:shard] = qkv_ref[...].astype(BF)
    spare = early_ref.shape[1] - small_lanes - bias_lanes
    bias = jnp.concatenate([bias_ref[...], jnp.zeros((small_ref.shape[0] - 1, bias_lanes), F32)], axis=0)
    early_ref[shard:] = jnp.concatenate(
        [small_ref[...], bias, jnp.zeros((small_ref.shape[0], spare), F32)], axis=1
    ).astype(BF)


def pack_late_kernel(out_ref, expand_ref, shrink_ref, late_ref):
    shard, channels = out_ref.shape
    begin = channels + expand_ref.shape[1]
    late_ref[:, :channels] = out_ref[...].astype(BF)
    late_ref[:, channels:begin] = expand_ref[...].astype(BF)
    for block in range(shrink_ref.shape[0] // shard):
        lanes = slice(begin + block * channels, begin + (block + 1) * channels)
        late_ref[:, lanes] = shrink_ref[block * shard : (block + 1) * shard].astype(BF)


def project_kernel(dims, ways, assembles, *refs):
    rows, width, wide, wide_part = dims
    me_ref, x_ref = refs[:2]
    if assembles:
        pieces = refs[2 : 2 + ways]
        across_ref, normed_ref = refs[2 + ways : 4 + ways]
        down_refs = refs[4 + ways : 4 + 2 * ways]
        weight_ref, small_ref, bias_ref, spread_ref = refs[4 + 2 * ways :]

        @pl.when(pl.program_id(0) == 0)
        def _():
            channels, hidden_width = small_ref.shape[1], bias_ref.shape[1]
            shard = channels // ways
            bias_shard = hidden_width // ways
            lanes = -(-(shard + bias_shard) // 128) * 128
            lane, column = iota((lanes, channels + hidden_width), 0), iota((lanes, channels + hidden_width), 1)
            total = jnp.zeros((16, channels + hidden_width), F32)
            for distance, piece in enumerate(pieces):
                place = me_ref[0] ^ distance
                weight_ref[pl.ds(pl.multiple_of(place * shard, shard), shard)] = piece[:shard]
                target = jnp.where(
                    lane < shard,
                    lane + shard * place,
                    channels + lane - shard + bias_shard * place,
                )
                chosen = one_hot((column == target) & (lane < shard + bias_shard))
                total = total + dot(piece[shard : shard + 16, :lanes], chosen)
            small_ref[...] = total[:, :channels]
            bias_ref[...] = total[0:1, channels:]

    else:
        weight_ref, small_ref, across_ref, normed_ref = refs[2:6]
        down_refs = refs[6 : 6 + ways]
        spread_ref = refs[6 + ways]
    gain, offset = small_ref[9:10], small_ref[10:11]
    expand = one_hot(expand_condition(wide, width))
    for row in range(rows):
        span = slice(row * width, (row + 1) * width)
        normed, _, _ = normalize(x_ref[0, span].astype(F32), gain, offset)
        normed = normed.astype(BF)
        normed_ref[0, span] = normed
        across_ref[0, span] = dot(normed, weight_ref[:, : 3 * HALF]).astype(BF)
        spread_ref[row] = dot(expand, normed).astype(BF)
        for distance in range(ways):
            start = pl.multiple_of((me_ref[0] ^ distance) * wide_part, wide_part)
            down_refs[distance][0, row] = spread_ref[row, pl.ds(start, wide_part)]


def rank_row(mask_row, width):
    lower = one_hot(iota((width, width), 0) <= iota((width, width), 1))
    counted = dot(jnp.broadcast_to(mask_row, (8, width)).astype(BF), lower)[0:1]
    return jnp.where(mask_row > 0.0, counted - 1.0, -1.0)


def across_kernel(
    dims,
    first,
    across_ref,
    mask_ref,
    small_ref,
    joined_ref,
    attended_ref,
    total_ref,
    keys_ref,
    values_ref,
    shift_ref,
):
    rows, width, kept, key_rows = dims
    image = pl.program_id(0)
    ranks = rank_row(mask_ref[pl.ds(image + first, 1)].astype(F32), width)
    select = one_hot(iota((kept, width), 0).astype(F32) == ranks)
    bias = jnp.where(iota((kept, HALF), 0) >= VALID, MASKED, 0.0)
    key_norms = jnp.zeros((1, HALF), F32)
    for row in range(rows):
        picked = dot(select, across_ref[0, row * width : (row + 1) * width, HALF:])
        key_norms = jnp.maximum(key_norms, head_norms(picked[:, :HALF]))
        span = slice(row * kept, (row + 1) * kept)
        keys_ref[0, span] = wide_keys(picked[:, :HALF], bias)
        values_ref[0, span] = wide_values(picked[:, HALF:])
    spare = key_rows - rows * kept
    if spare:
        nothing = jnp.zeros((spare, HALF), F32)
        keys_ref[0, rows * kept :] = wide_keys(nothing, nothing + MASKED)
        values_ref[0, rows * kept :] = wide_values(nothing)

    query_norms = head_norms(across_ref[0, :, :HALF].astype(F32) * (SCALE * LOG2E))
    large = exceeds(query_norms, key_norms)

    @pl.when(image == 0)
    def _():
        shift_ref[...] = jnp.zeros_like(shift_ref)

    @pl.when(large)
    def _():
        def highest(row, carry):
            span = pl.ds(pl.multiple_of(row * width, 16), width)
            shift_ref[span] = highest_scores(across_ref[0, span, :HALF].astype(F32), keys_ref[0])
            return carry

        lax.fori_loop(0, rows, highest, 0)

    def value_row(row):
        return across_ref[0, row * width : (row + 1) * width, 2 * HALF :].astype(F32)

    for row in range(rows):
        span = slice(row * width, (row + 1) * width)
        sums = [jnp.zeros((width, HALF), F32) for _ in range(3)]
        for tap_row in range(3):
            source = row + tap_row - 1
            if 0 <= source < rows:
                values = value_row(source)
                for tap_col in range(3):
                    tap = 3 * tap_row + tap_col
                    sums[tap_col] = sums[tap_col] + values * small_ref[tap : tap + 1, :HALF]
        local = shift_down(sums[0]) + sums[1] + shift_up(sums[2]) + small_ref[11:12, :HALF]
        queries = across_ref[0, span, :HALF].astype(F32)
        attended, log_total = attend_heads(queries, shift_ref[span], keys_ref[0], values_ref[0])
        attended_ref[0, span] = attended
        total_ref[0, span] = log_total
        joined_ref[0, span] = (attended + local).astype(BF)

    @pl.when(large)
    def _():
        shift_ref[...] = jnp.zeros_like(shift_ref)


def assemble(me_ref, pieces, target_ref, dim, step):
    for distance, piece in enumerate(pieces):
        place = me_ref[0] ^ distance
        if dim == 0:
            target_ref[pl.ds(place * step, step)] = piece[0].astype(target_ref.dtype)
        else:
            target_ref[:, pl.ds(pl.multiple_of(place * step, step), step)] = piece[0].astype(
                target_ref.dtype
            )


def down_setup(me_ref, mask_ref, column_ref, width, wide, wide_part, first):
    image = pl.program_id(0) + first
    mask_row = mask_ref[pl.ds(image, 1)].astype(F32)
    valid = one_hot(expand_condition(wide, width) & (mask_row > 0.0))
    column_ref[...] = dot(valid, jnp.ones((width, HALF), BF))
    return pl.multiple_of(me_ref[0] * wide_part, GROUP)


def window_bias(column_ref, start, window, height):
    valid = column_ref[pl.ds(start + pl.multiple_of(window * GROUP, GROUP), GROUP)]
    bias = jnp.where(valid > 0.5, 0.0, MASKED)
    return jnp.broadcast_to(bias[None], (height, GROUP, HALF)).reshape(height * GROUP, HALF)


def pad_keys(block, spare, fill):
    if not spare:
        return block
    return jnp.concatenate([block, jnp.full((spare, HALF), 0.0, F32) + fill], axis=0)


def window_operands(keys, values, bias, spare):
    return (
        wide_keys(pad_keys(keys, spare, 0.0), pad_keys(bias, spare, MASKED)),
        wide_values(pad_keys(values, spare, 0.0)),
    )


def grid_shift(values, amount):
    return pltpu.roll(values, amount % GROUP, 1)


def grid_stack(values):
    edge = jnp.zeros((1,) + values.shape[1:], F32)
    return jnp.concatenate([edge, values, edge], axis=0)


def down_kernel(dims, ways, first, *refs):
    height, width, wide, wide_part, spare = dims
    me_ref, mask_ref, small_ref, weight_ref = refs[:4]
    pieces_in = refs[4 : 4 + ways]
    joined_refs = refs[4 + ways : 4 + 2 * ways]
    attended_ref, total_ref, saved_ref, normed_out, mixed_ref, joined_ref, column_ref = refs[
        4 + 2 * ways :
    ]
    normed_ref = normed_out.at[0]
    rows = height // ways
    start = down_setup(me_ref, mask_ref, column_ref, width, wide, wide_part, first)
    assemble(me_ref, pieces_in, normed_ref, 0, rows)
    tokens = height * GROUP
    windows = wide_part // GROUP
    normed = normed_ref[...].reshape(height * wide_part, 2 * HALF)
    mixed_low = dot(normed, weight_ref[:, 3 * HALF :]).astype(BF)
    mixed_low = mixed_low.reshape(height, wide_part, 3 * HALF)
    saved_ref[0] = mixed_low
    mixed_ref[...] = mixed_low.astype(F32)

    everything = mixed_ref[...].reshape(height * wide_part, 3 * HALF)
    large = exceeds(
        head_norms(everything[:, :HALF] * (SCALE * LOG2E)), head_norms(everything[:, HALF : 2 * HALF])
    )

    def one_window(shifted, window, carry):
        span = pl.ds(pl.multiple_of(window * GROUP, GROUP), GROUP)
        grid = mixed_ref[:, span]
        flat = grid.reshape(tokens, 3 * HALF)
        queries, keys, values = (flat[:, part * HALF : (part + 1) * HALF] for part in range(3))
        bias = window_bias(column_ref, start, window, height)
        keys_in, values_in = window_operands(keys, values, bias, spare)

        shift = highest_scores(queries, keys_in) if shifted else None
        attended, log_total = attend_heads(queries, shift, keys_in, values_in)
        attended_ref[0, :, span] = attended.reshape(height, GROUP, HALF)
        total_ref[0, :, span] = log_total.reshape(height, GROUP, HALF)
        stacked = grid_stack(values.reshape(height, GROUP, HALF))
        sums = [jnp.zeros((height, GROUP, HALF), F32) for _ in range(3)]
        for tap_row in range(3):
            for tap_col in range(3):
                tap = 3 * tap_row + tap_col
                sums[tap_col] = sums[tap_col] + stacked[tap_row : tap_row + height] * small_ref[
                    tap : tap + 1, HALF:
                ].reshape(1, 1, HALF)
        local = grid_shift(sums[0], 1) + sums[1] + grid_shift(sums[2], -1)
        local = local + small_ref[11:12, HALF:].reshape(1, 1, HALF)
        joined_ref[:, span] = attended.reshape(height, GROUP, HALF) + local
        return carry

    @pl.when(jnp.logical_not(large))
    def _():
        lax.fori_loop(0, windows, functools.partial(one_window, False), 0, unroll=min(windows, 8))

    @pl.when(large)
    def _():
        lax.fori_loop(0, windows, functools.partial(one_window, True), 0)

    for distance in range(ways):
        place = me_ref[0] ^ distance
        joined_refs[distance][0] = joined_ref[pl.ds(place * rows, rows)].astype(BF)


def gelu_parts(hidden):
    upper = 0.5 + 0.5 * lax.erf(hidden * INV_ROOT_TWO)
    return upper, jnp.exp2(hidden * hidden * (-0.5 * LOG2E)) * INV_ROOT_TAU


def middle_kernel(dims, ways, *refs):
    rows, width, wide, wide_part, chunk, hidden_part = dims
    refs = list(refs)

    def take(number):
        taken = refs[:number]
        del refs[:number]
        return taken

    me_ref, x_ref, cot_ref, across_ref = take(4)
    pieces_in = [take(ways), take(ways)]
    weights_in = take(ways)
    small_ref, bias_ref = take(2)
    block_ref, middle_ref, grad_across_ref = take(3)
    grad_refs = take(ways)
    dbias_ref, dsmall_ref = take(2)
    piece_refs = take(ways)
    dout_ref, dexpand_ref, dshrink_ref = take(3)
    out_ref, expand_ref, shrink_ref = take(3)
    wide_ref, joined_ref, normed_ref, active_ref, hidden_ref, attended_ref, down_ref, gwide_ref = take(8)
    turned_ref = take(1)[0]
    tokens = rows * width
    hidden_width = expand_ref.shape[1]
    channels = 2 * HALF
    shard = channels // ways
    blocks = hidden_width // channels
    start_sums((dbias_ref, dsmall_ref, dout_ref, dexpand_ref, dshrink_ref), None)

    @pl.when(pl.program_id(0) == 0)
    def _():
        for distance, piece in enumerate(weights_in):
            place = me_ref[0] ^ distance
            span = pl.ds(pl.multiple_of(place * shard, shard), shard)
            out_ref[span] = piece[:, :channels]
            expand_ref[span] = piece[:, channels : channels + hidden_width]
            for block in range(blocks):
                begin = pl.multiple_of((place * blocks + block) * shard, shard)
                lanes = slice(channels + hidden_width + block * channels, channels + hidden_width + (block + 1) * channels)
                shrink_ref[pl.ds(begin, shard)] = piece[:, lanes]

    image, pair = pl.program_id(0), pl.num_programs(0) // 2

    @pl.when(image < pair)
    def _():
        assemble(me_ref, pieces_in[0], wide_ref, 1, wide_part)

    @pl.when(image >= pair)
    def _():
        assemble(me_ref, pieces_in[1], wide_ref, 1, wide_part)

    contract = contract_matrix(width, wide)
    for row in range(rows):
        span = slice(row * width, (row + 1) * width)
        joined_ref[span, :HALF] = across_ref[0, span]
        joined_ref[span, HALF:] = dot(contract, wide_ref[row]).astype(BF)

    def token_rows(step, carry):
        span = pl.ds(pl.multiple_of(step * chunk, 16), chunk)
        joined = joined_ref[span]
        attended_out = dot(joined, out_ref[...]) + small_ref[12:13]
        middle = x_ref[0, span].astype(F32) + attended_out
        normed, scaled, recip = normalize(middle, small_ref[13:14], small_ref[14:15])
        normed_low = normed.astype(BF)
        normed_ref[span] = normed_low
        back = cot_ref[0, span]
        result = middle + small_ref[15:16]
        grad_normed = jnp.zeros((chunk, 2 * HALF), F32)

        def products(part):
            lanes = slice(part, part + hidden_part)
            return dot(normed_low, expand_ref[:, lanes]), dot_nt(back, shrink_ref[lanes])

        def follow(result, grad_normed, behind):
            lanes, active, grad_hidden = behind
            return (
                result + dot(active, shrink_ref[lanes]),
                grad_normed + dot_nt(grad_hidden, expand_ref[:, lanes]),
            )

        ahead, behind = products(0), None
        for part in range(0, hidden_width, hidden_part):
            lanes = slice(part, part + hidden_part)
            hidden, grad_active = ahead
            if part + hidden_part < hidden_width:
                ahead = products(part + hidden_part)
            hidden = hidden + bias_ref[:, lanes]
            upper, density = gelu_parts(hidden)
            active = (hidden * upper).astype(BF)
            active_ref[span, lanes] = active
            grad_hidden = grad_active * (upper + hidden * density)
            grad_hidden = grad_hidden.astype(BF)
            hidden_ref[span, lanes] = grad_hidden
            dbias_ref[:, lanes] += fold_rows(grad_hidden.astype(F32))
            if part:
                result, grad_normed = follow(result, grad_normed, behind)
            behind = (lanes, active, grad_hidden)
        result, grad_normed = follow(result, grad_normed, behind)
        block_ref[0, span] = result
        back_wide = back.astype(F32)
        grad_middle = back_wide + normalize_back(grad_normed, scaled, recip, small_ref[13:14])
        middle_ref[0, span] = grad_middle
        grad_attended = grad_middle.astype(BF)
        attended_ref[span] = grad_attended
        grad_joined = dot_nt(grad_attended, out_ref[...]).astype(BF)
        grad_across_ref[0, span] = grad_joined[:, :HALF]
        down_ref[span] = grad_joined[:, HALF:]
        dsmall_ref[0:8] += fold_rows(grad_attended.astype(F32))
        dsmall_ref[8:16] += fold_rows(grad_normed * scaled)
        dsmall_ref[16:24] += fold_rows(grad_normed)
        dsmall_ref[24:32] += fold_rows(back_wide)
        return carry

    lax.fori_loop(0, tokens // chunk, token_rows, 0, unroll=True)
    expand = one_hot(expand_condition(wide, width))
    for row in range(rows):
        gwide_ref[row] = dot(expand, down_ref[row * width : (row + 1) * width]).astype(BF)
    for distance in range(ways):
        place = me_ref[0] ^ distance
        grad_refs[distance][0] = gwide_ref[
            :, pl.ds(pl.multiple_of(place * wide_part, wide_part), wide_part)
        ]
    dout_ref[...] += dot_tn(joined_ref[...], attended_ref[...])
    dexpand_ref[...] += dot_tn(normed_ref[...], hidden_ref[...])
    dshrink_ref[...] += dot_tn(cot_ref[0], active_ref[...])

    @at_last_step
    def _():
        for block in range(blocks):
            lanes = slice(block * channels, (block + 1) * channels)
            turned_ref[lanes] = jnp.transpose(dshrink_ref[:, lanes])
        for distance, piece in enumerate(piece_refs):
            place = me_ref[0] ^ distance
            span = pl.ds(pl.multiple_of(place * shard, shard), shard)
            piece[:, :channels] = dout_ref[span]
            piece[:, channels : channels + hidden_width] = dexpand_ref[span]
            for block in range(blocks):
                begin = pl.multiple_of((place * blocks + block) * shard, shard)
                lanes = slice(channels + hidden_width + block * channels, channels + hidden_width + (block + 1) * channels)
                piece[:, lanes] = turned_ref[pl.ds(begin, shard)]


def shard_pieces(me_ref, piece_refs, total_ref):
    shard = piece_refs[0].shape[0]

    @at_last_step
    def _():
        for distance, piece in enumerate(piece_refs):
            begin = pl.multiple_of((me_ref[0] ^ distance) * shard, shard)
            piece[...] = total_ref[pl.ds(begin, shard)]


def across_back_kernel(dims, first, last, *refs):
    rows, width, kept, key_rows, chunk = dims
    refs = list(refs)

    def take(number):
        taken = refs[:number]
        del refs[:number]
        return taken

    across_ref, grad_ref, attended_ref, total_ref, keys_ref, values_ref, normed_ref = take(7)
    mask_ref, small_ref = take(2)
    starts = take(2) if last else None
    mixed_ref, taps_ref, dweight_ref, dkeys_ref, dvalues_ref, local_ref = take(6)
    tokens = rows * width
    image = pl.program_id(0) + first
    start_sums((taps_ref, dweight_ref), starts)
    dkeys_ref[...] = jnp.zeros_like(dkeys_ref)
    dvalues_ref[...] = jnp.zeros_like(dvalues_ref)

    def attend(step, carry):
        span = pl.ds(pl.multiple_of(step * chunk, 16), chunk)
        grad_queries, grad_keys, grad_values = attend_heads_back(
            across_ref[0, span, :HALF].astype(F32),
            grad_ref[0, span].astype(F32),
            attended_ref[0, span],
            total_ref[0, span],
            keys_ref[0],
            values_ref[0],
        )
        mixed_ref[0, span, :HALF] = grad_queries.astype(BF)
        for head in range(BRANCH_HEADS):
            lanes = slice(head * HEAD_DIM, (head + 1) * HEAD_DIM)
            dkeys_ref[lanes] += grad_keys[head]
            dvalues_ref[lanes] += grad_values[head]
        return carry

    lax.fori_loop(0, tokens // chunk, attend, 0)

    local_ref[...] = jnp.zeros_like(local_ref)
    for row in range(rows):
        grad = grad_ref[0, row * width : (row + 1) * width].astype(F32)
        taps_ref[72:80] += fold_rows(grad)
        for tap_col, moved in enumerate((shift_up(grad), grad, shift_down(grad))):
            for tap_row in range(3):
                target = row + tap_row - 1
                if 0 <= target < rows:
                    tap = 3 * tap_row + tap_col
                    span = slice(target * width, (target + 1) * width)
                    values = across_ref[0, span, 2 * HALF :].astype(F32)
                    taps_ref[8 * tap : 8 * tap + 8] += fold_rows(values * moved)
                    local_ref[span] += moved * small_ref[tap : tap + 1, :HALF]

    ranks = rank_row(mask_ref[pl.ds(image, 1)].astype(F32), width)
    place = jnp.transpose(jnp.broadcast_to(ranks, (HALF, width)))
    spread = one_hot(iota((width, HALF), 1).astype(F32) == place)
    spread_more = one_hot((iota((width, kept - HALF), 1) + HALF).astype(F32) == place[:, : kept - HALF])
    spread = jnp.concatenate([spread, spread_more], axis=1)
    grad_keys = jnp.transpose(dkeys_ref[...]) * SCALE
    grad_values = jnp.transpose(dvalues_ref[...])
    high = grad_values.astype(BF)
    low = (grad_values - high.astype(F32)).astype(BF)
    grad_keys = grad_keys.astype(BF)
    for row in range(rows):
        span = slice(row * kept, (row + 1) * kept)
        packed = jnp.concatenate([grad_keys[span], high[span], low[span]], axis=1)
        unpacked = dot(spread, packed)
        target = slice(row * width, (row + 1) * width)
        mixed_ref[0, target, HALF : 2 * HALF] = unpacked[:, :HALF].astype(BF)
        whole = unpacked[:, HALF : 2 * HALF] + unpacked[:, 2 * HALF :] + local_ref[target]
        mixed_ref[0, target, 2 * HALF :] = whole.astype(BF)
    dweight_ref[...] += dot_tn(normed_ref[0], mixed_ref[0])


def down_back_kernel(dims, ways, *refs):
    height, width, wide, wide_part, spare = dims
    refs = list(refs)

    def take(number):
        taken = refs[:number]
        del refs[:number]
        return taken

    me_ref, mask_ref, small_ref, weight_ref, attended_ref, total_ref, saved_ref, normed_ref = take(8)
    grads_in = take(ways)
    out_refs = take(ways)
    taps_ref = take(1)[0]
    piece_refs = take(ways)
    dweight_ref, mixed_ref, grad_ref, out_ref, turned_ref, column_ref = take(6)
    rows = height // ways
    start = down_setup(me_ref, mask_ref, column_ref, width, wide, wide_part, 0)
    assemble(me_ref, grads_in, grad_ref, 0, rows)
    mixed_ref[...] = saved_ref[0].astype(F32)
    tokens = height * GROUP
    windows = wide_part // GROUP
    start_sums((taps_ref, dweight_ref), None)

    def one_window(window, carry):
        span = pl.ds(pl.multiple_of(window * GROUP, GROUP), GROUP)
        flat = mixed_ref[:, span].reshape(tokens, 3 * HALF)
        queries, keys, values = (flat[:, part * HALF : (part + 1) * HALF] for part in range(3))
        grad_grid = grad_ref[:, span]
        grad = grad_grid.reshape(tokens, HALF)
        bias = window_bias(column_ref, start, window, height)
        keys_in, values_in = window_operands(keys, values, bias, spare)
        grad_queries, grad_keys, grad_values = attend_heads_back(
            queries,
            grad,
            attended_ref[0, :, span].reshape(tokens, HALF),
            total_ref[0, :, span].reshape(tokens, HALF),
            keys_in,
            values_in,
        )
        grad_keys = jnp.transpose(jnp.concatenate(grad_keys, axis=0))[:tokens] * SCALE
        grad_values = jnp.transpose(jnp.concatenate(grad_values, axis=0))[:tokens]
        values_grid = values.reshape(height, GROUP, HALF)
        local = jnp.zeros((height, GROUP, HALF), F32)
        taps_ref[72:80] += jnp.sum(grad_grid, axis=0)
        shifted = (grid_shift(grad_grid, -1), grad_grid, grid_shift(grad_grid, 1))
        for tap_col, moved in enumerate(shifted):
            stacked = grid_stack(moved)
            for tap_row in range(3):
                tap = 3 * tap_row + tap_col
                source = stacked[2 - tap_row : 2 - tap_row + height]
                taps_ref[8 * tap : 8 * tap + 8] += jnp.sum(source * values_grid, axis=0)
                local = local + source * small_ref[tap : tap + 1, HALF:].reshape(1, 1, HALF)
        shape = (height, GROUP, HALF)
        out_ref[:, span, :HALF] = grad_queries.reshape(shape)
        out_ref[:, span, HALF : 2 * HALF] = grad_keys.reshape(shape)
        out_ref[:, span, 2 * HALF :] = grad_values.reshape(shape) + local
        return carry

    lax.fori_loop(0, windows, one_window, 0, unroll=min(windows, 8))
    mixed_grad = out_ref[...].reshape(height * wide_part, 3 * HALF).astype(BF)
    grad_normed = dot_nt(mixed_grad, weight_ref[:, 3 * HALF :]).astype(BF)
    turned_ref[...] = grad_normed.reshape(height, wide_part, 2 * HALF)
    for distance in range(ways):
        place = me_ref[0] ^ distance
        out_refs[distance][0] = turned_ref[pl.ds(place * rows, rows)]
    normed = normed_ref[0].reshape(height * wide_part, 2 * HALF)
    dweight_ref[...] += dot_tn(normed, mixed_grad)
    shard_pieces(me_ref, piece_refs, dweight_ref)


def final_kernel(dims, ways, last, *refs):
    rows, width, wide, wide_part, chunk = dims
    refs = list(refs)

    def take(number):
        taken = refs[:number]
        del refs[:number]
        return taken

    me_ref, x_ref, middle_ref, across_ref = take(4)
    pieces_in = take(ways)
    small_ref, weight_ref = take(2)
    starts = take(1) if last else None
    others = take(5) if last else None
    grad_ref, dsmall_ref = take(2)
    piece_refs = take(ways) if last else None
    wide_ref, down_ref = take(2)
    whole_ref = take(1)[0] if last else None
    tokens = rows * width
    start_sums((dsmall_ref,), starts)
    assemble(me_ref, pieces_in, wide_ref, 1, wide_part)
    contract = contract_matrix(width, wide)
    for row in range(rows):
        down_ref[row * width : (row + 1) * width] = dot(contract, wide_ref[row])

    def token_rows(step, carry):
        span = pl.ds(pl.multiple_of(step * chunk, 16), chunk)
        _, scaled, recip = normalize(x_ref[0, span].astype(F32), small_ref[9:10], small_ref[10:11])
        grad_normed = dot_nt(across_ref[0, span], weight_ref[:, : 3 * HALF]) + down_ref[span]
        dsmall_ref[0:8] += fold_rows(grad_normed * scaled)
        dsmall_ref[8:16] += fold_rows(grad_normed)
        grad_ref[0, span] = middle_ref[0, span] + normalize_back(
            grad_normed, scaled, recip, small_ref[9:10]
        )
        return carry

    lax.fori_loop(0, tokens // chunk, token_rows, 0)
    if last:

        @at_last_step
        def _():
            across_taps, down_taps, middle_sums, bias_sums, dweight = others
            channels = 2 * HALF

            def total(ref, index):
                return jnp.sum(ref[8 * index : 8 * index + 8], axis=0, keepdims=True)

            def set_taps(row, index):
                whole_ref[row : row + 1, :HALF] = total(across_taps, index)
                whole_ref[row : row + 1, HALF:] = total(down_taps, index)

            whole_ref[...] = jnp.zeros_like(whole_ref)
            for tap in range(9):
                set_taps(tap, tap)
            whole_ref[9:10] = total(dsmall_ref, 0)
            whole_ref[10:11] = total(dsmall_ref, 1)
            set_taps(11, 9)
            for index in range(4):
                whole_ref[12 + index : 13 + index] = total(middle_sums, index)
            bias = total(bias_sums, 0)
            for block in range(bias.shape[1] // channels):
                whole_ref[16 + block : 17 + block] = bias[:, block * channels : (block + 1) * channels]
            shard = dweight.shape[0] // ways
            for distance, piece in enumerate(piece_refs):
                begin = pl.multiple_of((me_ref[0] ^ distance) * shard, shard)
                piece[:shard] = dweight[pl.ds(begin, shard)].astype(BF)
                piece[shard:, :channels] = whole_ref[...].astype(BF)
                piece[shard:, channels:] = jnp.zeros(
                    (whole_ref.shape[0], dweight.shape[1] - channels), BF
                )


def last_back_kernel(dims, final_dims, ways, first, *refs):
    refs = list(refs)

    def take(number):
        taken = refs[:number]
        del refs[:number]
        return taken

    attention_in = take(9)
    attention_starts = take(2)
    me_ref, x_ref, middle_ref = take(3)
    pieces_in = take(ways)
    small_ref, weight_ref, norm_start, down_taps, middle_sums, bias_sums = take(6)
    grad_ref = take(1)[0]
    piece_refs = take(ways)
    mixed_ref, taps_ref, dweight_ref, dkeys_ref, dvalues_ref, local_ref = take(6)
    dsmall_ref, wide_ref, down_ref, whole_ref = take(4)
    across_back_kernel(
        dims,
        first,
        True,
        *attention_in,
        *attention_starts,
        mixed_ref,
        taps_ref,
        dweight_ref,
        dkeys_ref,
        dvalues_ref,
        local_ref,
    )
    final_kernel(
        final_dims,
        ways,
        True,
        me_ref,
        x_ref,
        middle_ref,
        mixed_ref,
        *pieces_in,
        small_ref,
        weight_ref,
        norm_start,
        taps_ref,
        down_taps,
        middle_sums,
        bias_sums,
        dweight_ref,
        grad_ref,
        dsmall_ref,
        *piece_refs,
        wide_ref,
        down_ref,
        whole_ref,
    )


def tail_kernel(known_ref, *refs):
    *parts, tail_ref, squares_ref = refs
    tail = tree_sum([part[...].astype(F32) for part in parts])
    tail_ref[...] = tail
    mine = tail[: tail.shape[0] - 32]
    squares_ref[...] = jnp.zeros(squares_ref.shape, F32) + (known_ref[0] + jnp.sum(mine * mine))


def update_kernel(ways, place_ref, mine_ref, other_ref, tail_ref, *refs):
    squares, old, new = refs[:ways], refs[ways : ways + 18], refs[ways + 19 : ways + 37]
    norm_ref, joined_ref = refs[ways + 18], refs[ways + 37]
    me, core = place_ref[0], place_ref[1]
    half = mine_ref.shape[0]
    joined_ref[pl.ds(pl.multiple_of(core * half, half), half)] = mine_ref[...]
    joined_ref[pl.ds(pl.multiple_of((1 - core) * half, half), half)] = other_ref[...]
    shard = 2 * half
    rows, channels = old[1].shape
    hidden_width = old[2].shape[1]
    blocks = hidden_width // channels
    small = tail_ref[shard:, :channels]
    small_rows, small_lanes = old[4].shape
    bias_lanes = old[5].shape[1]
    total = tree_sum([entry[...] for entry in squares]) + jnp.sum(small * small)
    norm = jnp.sqrt(total)
    norm_ref[0, 0] = jnp.max(norm)
    factor = (CLIP_NORM / jnp.maximum(norm, CLIP_NORM))[0:1, 0:1]

    def update(index, grads, rate, decay, spans=(slice(None), slice(None))):
        weight, first, second = (old[part * 6 + index][spans] for part in range(3))
        results = adam_update(weight, first, second, grads * factor, rate, decay)
        for part in range(3):
            new[part * 6 + index][spans] = results[part]

    update(0, tail_ref[:shard], RATE_MATRIX, WEIGHT_DECAY, (slice(None), slice(0, 3 * HALF)))
    begin = channels + 2 * hidden_width
    update(
        0,
        joined_ref[:, begin : begin + 3 * HALF],
        RATE_MATRIX,
        WEIGHT_DECAY,
        (slice(None), slice(3 * HALF, 6 * HALF)),
    )
    update(1, joined_ref[:, :channels], RATE_OUTPUT, WEIGHT_DECAY)
    update(2, joined_ref[:, channels : channels + hidden_width], RATE_MATRIX, WEIGHT_DECAY)
    for block in range(blocks):
        begin = channels + hidden_width + block * channels
        update(
            3,
            joined_ref[:, begin : begin + channels],
            RATE_MATRIX,
            WEIGHT_DECAY,
            (slice(block * rows, (block + 1) * rows), slice(None)),
        )
    small_grad = jnp.zeros((small_rows, small_lanes), F32)
    bias_grad = jnp.zeros((1, bias_lanes), F32)
    for place in range(ways):
        lanes = slice(place * small_lanes, (place + 1) * small_lanes)
        small_grad = jnp.where(me == place, small[:small_rows, lanes], small_grad)
        row, lane = divmod(place * bias_lanes, channels)
        row = small_rows + row
        bias_grad = jnp.where(me == place, small[row : row + 1, lane : lane + bias_lanes], bias_grad)
    update(4, small_grad, RATE_SMALL, 0.0)
    update(5, bias_grad, RATE_MATRIX, 0.0)


def image_block(*shape, first=0):
    return pl.BlockSpec((1,) + shape, lambda image: (image + first,) + (0,) * len(shape))


def whole_block(*shape):
    return pl.BlockSpec(shape, lambda image: (0,) * len(shape))


def scalar_block():
    return pl.BlockSpec(memory_space=pltpu.SMEM)


def run_kernel(body, images, inputs, outputs, scratch, micros, after=(), alias=()):
    number, made = len(inputs), len(outputs)
    hidden = list(after)
    aliases = {}
    for operand, output in alias:
        aliases[number + len(hidden)] = output
        hidden.append(operand)
    skipped = number + len(hidden)

    def wrapped(*refs):
        refs[skipped + made][...] = jnp.zeros((8, 128), F32)
        body(*refs[:number], *refs[skipped : skipped + made], *refs[skipped + made + 1 :])

    outputs = list(outputs) + [((8, 128), F32, whole_block(8, 128))]
    *results, token = pl.pallas_call(
        wrapped,
        grid=(images,),
        in_specs=[spec for _, spec in inputs] + [pl.BlockSpec(memory_space=pl.ANY)] * len(hidden),
        out_specs=[spec for _, _, spec in outputs],
        out_shape=[jax.ShapeDtypeStruct(shape, dtype) for shape, dtype, _ in outputs],
        scratch_shapes=scratch,
        input_output_aliases=aliases,
        compiler_params=pltpu.CompilerParams(vmem_limit_bytes=VMEM_LIMIT),
        cost_estimate=pl.CostEstimate(
            flops=int(micros * 1e9), bytes_accessed=int(micros * 1e6), transcendentals=0
        ),
    )(*[operand for operand, _ in inputs], *hidden)
    return results, token


def adam_update(weight, first_old, second_old, grad_value, rate_value, decay_value):
    new_first = BETA_ONE * first_old + (1.0 - BETA_ONE) * grad_value
    new_second = BETA_TWO * second_old + (1.0 - BETA_TWO) * grad_value * grad_value
    first_hat = new_first / (1.0 - BETA_ONE**STEP)
    second_hat = new_second / (1.0 - BETA_TWO**STEP)
    new_weight = weight - rate_value * (
        first_hat / (jnp.sqrt(second_hat) + ADAM_EPS) + decay_value * weight
    )
    return (new_first, new_second, new_weight)


def swap(value, axis, distance):
    return lax.ppermute(value, axis, [(place, place ^ distance) for place in range(lax.axis_size(axis))])


def exchange(pieces):
    return [pieces[0]] + [swap(pieces[d], "seq", d) for d in range(1, len(pieces))]


def tree_sum(values):
    while len(values) > 1:
        values = [values[i] + values[i + 1] for i in range(0, len(values), 2)]
    return values[0]


def share_low(value, distances):
    rounded = lax.reduce_precision(value, 8, 7)
    sent = rounded.astype(BF)
    return [rounded] + [swap(sent, "img", distance) for distance in distances]


def on_device(
    images,
    cotangent,
    valid_mask,
    qkv_weight,
    out_weight,
    expand_weight,
    shrink_weight,
    small_params,
    expand_bias,
    first_qkv,
    first_out,
    first_expand,
    first_shrink,
    first_small,
    first_bias,
    second_qkv,
    second_out,
    second_expand,
    second_shrink,
    second_small,
    second_bias,
):
    ways = lax.axis_size("seq")
    owner = lax.axis_index("seq")
    me = owner.astype(jnp.int32).reshape(1)
    count, rows, width, channels = images.shape
    tokens = rows * width
    height = rows * ways
    wide = width // STRIPE * GROUP
    wide_part = wide // ways
    kept = -(-VALID // 16) * 16
    key_rows = -(-rows * kept // 256) * 256
    window_tokens = height * GROUP
    spare = -window_tokens % 128
    shard = qkv_weight.shape[0]
    hidden_width = expand_weight.shape[1]
    blocks = hidden_width // channels
    pair = count // 2
    chip_steps = [2 << bit for bit in range((lax.axis_size("img") // 2).bit_length() - 1)][::-1]

    x = images.reshape(count, tokens, channels)
    cot = cotangent.reshape(count, tokens, channels)
    me_in = (me, scalar_block())
    mask_in = (valid_mask, whole_block(*valid_mask.shape))
    piece_in = (rows, wide_part, channels)
    piece_out = (rows, wide_part, HALF)
    qkv_shape = (channels, 6 * HALF)

    def per_image(array, first=0):
        return (array, image_block(*array.shape[1:], first=first))

    def whole(array):
        return (array, whole_block(*array.shape))

    def half_images(array, first):
        last = array.shape[0] - 1
        dims = (1,) + array.shape[1:]
        return (
            array,
            pl.BlockSpec(
                dims, lambda image: (jnp.clip(image - first, 0, last),) + (0,) * (len(dims) - 1)
            ),
        )

    def new_image(dims, dtype, images):
        return ((images,) + dims, dtype, image_block(*dims))

    def part_image(dims, dtype, first):
        return ((count,) + dims, dtype, image_block(*dims, first=first))

    def new_whole(dims, dtype):
        return (dims, dtype, whole_block(*dims))

    (early,), _ = run_kernel(
        pack_early_kernel,
        1,
        [whole(qkv_weight), whole(small_params), whole(expand_bias.reshape(1, -1))],
        [new_whole((shard + 16, qkv_weight.shape[1]), BF)],
        [],
        2,
    )
    weights_in = exchange([early] * ways)
    (late,), _ = run_kernel(
        pack_late_kernel,
        1,
        [whole(out_weight), whole(expand_weight), whole(shrink_weight)],
        [new_whole((shard, channels + 2 * hidden_width), BF)],
        [],
        2,
        after=(early,),
    )

    whole_images, normed_pieces, parameters = [], [], None
    for first in (0, pair):
        assembles = first == 0
        results, token = run_kernel(
            functools.partial(project_kernel, (rows, width, wide, wide_part), ways, assembles),
            pair,
            [me_in, per_image(x, first)] + [whole(entry) for entry in weights_in],
            [part_image((tokens, 3 * HALF), BF, first), part_image((tokens, channels), BF, first)]
            + [new_image(piece_in, BF, pair)] * ways
            + (
                [new_whole(qkv_shape, BF), new_whole((16, channels), F32), new_whole((1, hidden_width), F32)]
                if assembles
                else []
            ),
            [pltpu.VMEM((rows, wide, channels), BF)],
            6,
            alias=[(entry, place) for place, entry in enumerate(whole_images)],
        )
        whole_images = results[:2]
        normed_pieces.append(exchange(results[2 : 2 + ways]))
        if assembles:
            qkv_low, small_full, bias_full = results[2 + ways :]
            weights_in = (qkv_low, small_full)
    across_mixed, normed = whole_images
    small_in, qkv_in = whole(small_full), whole(qkv_low)

    attention_dims = (rows, width, kept, key_rows)
    key_shape = (key_rows, channels)
    across = []

    def run_across(first, images_in, after):
        return run_kernel(
            functools.partial(across_kernel, attention_dims, first),
            images_in,
            [per_image(across_mixed, first), mask_in, small_in],
            [
                part_image((tokens, HALF), BF, first),
                part_image((tokens, HALF), F32, first),
                part_image((tokens, HALF), F32, first),
                part_image(key_shape, BF, first),
                part_image(key_shape, BF, first),
            ],
            [pltpu.VMEM((tokens, HALF), F32)],
            11 * images_in,
            after=after,
            alias=[(entry, place) for place, entry in enumerate(across)],
        )

    across, token = run_across(0, count - 1, (token,))
    late, token = lax.optimization_barrier((late, token))
    late_pieces = exchange([late] * ways)
    normed_pieces, token = lax.optimization_barrier((normed_pieces, token))

    down_dims = (height, width, wide, wide_part, spare)
    grid_f32 = (height, wide_part, HALF)
    mixed_grid = (height, wide_part, 3 * HALF)
    normed_grid = (height, wide_part, channels)
    down, joined_pieces = [], []
    for index, first in enumerate((0, pair)):
        results, token = run_kernel(
            functools.partial(down_kernel, down_dims, ways, first),
            pair,
            [me_in, mask_in, small_in, qkv_in] + [per_image(piece) for piece in normed_pieces[index]],
            [new_image(piece_out, BF, pair)] * ways
            + [part_image(grid_f32, F32, first)] * 2
            + [part_image(mixed_grid, BF, first), part_image(normed_grid, BF, first)],
            [
                pltpu.VMEM(mixed_grid, F32),
                pltpu.VMEM(grid_f32, F32),
                pltpu.VMEM((wide, HALF), F32),
            ],
            15,
            after=(token,),
            alias=[(entry, ways + place) for place, entry in enumerate(down)],
        )
        down = results[ways:]
        joined_pieces.append(exchange(results[:ways]))
    across, token = run_across(count - 1, 1, (token,))
    joined_across, attended, log_total, keys, values = across

    matrix_sums = [(channels, channels), (channels, hidden_width), (channels, hidden_width)]
    results, token = run_kernel(
        functools.partial(middle_kernel, (rows, width, wide, wide_part, tokens // 2, channels), ways),
        count,
        [me_in, per_image(x), per_image(cot), per_image(joined_across)]
        + [half_images(piece, 0) for piece in joined_pieces[0]]
        + [half_images(piece, pair) for piece in joined_pieces[1]]
        + [whole(piece) for piece in late_pieces]
        + [small_in, whole(bias_full)],
        [
            new_image((tokens, channels), F32, count),
            new_image((tokens, channels), F32, count),
            new_image((tokens, HALF), BF, count),
        ]
        + [new_image(piece_out, BF, count)] * ways
        + [new_whole((8, hidden_width), F32), new_whole((32, channels), F32)]
        + [new_whole(late.shape, F32)] * ways,
        [pltpu.VMEM(dims, F32) for dims in matrix_sums]
        + [
            pltpu.VMEM((channels, channels), BF),
            pltpu.VMEM((channels, hidden_width), BF),
            pltpu.VMEM((hidden_width, channels), BF),
            pltpu.VMEM((rows, wide, HALF), BF),
            pltpu.VMEM((tokens, channels), BF),
            pltpu.VMEM((tokens, channels), BF),
            pltpu.VMEM((tokens, hidden_width), BF),
            pltpu.VMEM((tokens, hidden_width), BF),
            pltpu.VMEM((tokens, channels), BF),
            pltpu.VMEM((tokens, HALF), BF),
            pltpu.VMEM((rows, wide, HALF), BF),
            pltpu.VMEM((hidden_width, channels), F32),
        ],
        45,
        after=(token,),
    )
    block_out, grad_middle, grad_across = results[:3]
    grad_pieces = exchange(results[3 : 3 + ways])
    bias_sums, middle_sums, *late_sums = results[3 + ways :]

    qkv_half = (channels, 3 * HALF)
    half_shard = (shard, 3 * HALF)
    back_sums, norm_sums, input_grad = None, None, None

    def run_across_back(first, images_in, sums, after):
        results, token = run_kernel(
            functools.partial(
                across_back_kernel, (*attention_dims, tokens // 2), first, sums is not None
            ),
            images_in,
            [
                per_image(across_mixed, first),
                per_image(grad_across, first),
                per_image(attended, first),
                per_image(log_total, first),
                per_image(keys, first),
                per_image(values, first),
                per_image(normed, first),
                mask_in,
                small_in,
            ]
            + ([whole(entry) for entry in sums[1:]] if sums else []),
            [
                part_image((tokens, 3 * HALF), BF, first),
                new_whole((80, HALF), F32),
                new_whole(qkv_half, F32),
            ],
            [
                pltpu.VMEM((HALF, key_rows), F32),
                pltpu.VMEM((HALF, key_rows), F32),
                pltpu.VMEM((tokens, HALF), F32),
            ],
            23 * images_in,
            after=after,
            alias=[(sums[0], 0)] if sums else [],
        )
        return results, token

    def run_final(first, images_in, after):
        return run_kernel(
            functools.partial(final_kernel, (rows, width, wide, wide_part, tokens), ways, False),
            images_in,
            [me_in, per_image(x, first), per_image(grad_middle, first), per_image(back_sums[0], first)]
            + [per_image(piece, first) for piece in grad_normed_pieces]
            + [small_in, qkv_in],
            [part_image((tokens, channels), F32, first), new_whole((16, channels), F32)],
            [pltpu.VMEM((rows, wide, channels), BF), pltpu.VMEM((tokens, channels), F32)],
            4 * images_in,
            after=after,
        )

    back_sums, token = run_across_back(0, 1, None, (token,))
    *late_sums, token = lax.optimization_barrier((*late_sums, token))
    late_parts = exchange(late_sums)
    results, token = run_kernel(
        functools.partial(down_back_kernel, down_dims, ways),
        count,
        [me_in, mask_in, small_in, qkv_in]
        + [per_image(entry) for entry in down]
        + [per_image(piece) for piece in grad_pieces],
        [new_image(piece_in, BF, count)] * ways
        + [new_whole((80, HALF), F32)]
        + [new_whole(half_shard, F32)] * ways,
        [
            pltpu.VMEM(qkv_half, F32),
            pltpu.VMEM(mixed_grid, F32),
            pltpu.VMEM(grid_f32, F32),
            pltpu.VMEM(mixed_grid, F32),
            pltpu.VMEM(normed_grid, BF),
            pltpu.VMEM((wide, HALF), F32),
        ],
        38,
        after=(token,),
    )
    down_taps, *down_sums = results[ways:]
    late_parts, token = lax.optimization_barrier((late_parts, token))
    late_seq = tree_sum(late_parts)
    core_place = lax.axis_index("img") % 2
    half = shard // 2
    down_parts = exchange(down_sums)
    grad_sent, late_seq = lax.optimization_barrier((results[:ways], late_seq))
    grad_normed_pieces = exchange(grad_sent)
    back_sums, token = run_across_back(1, count - 2, back_sums, (token, late_seq))
    down_parts, late_seq, token = lax.optimization_barrier((down_parts, late_seq, token))
    seq_sum = jnp.concatenate([late_seq, tree_sum(down_parts)], axis=1)
    kept_half = lax.dynamic_slice_in_dim(seq_sum, core_place * half, half, 0)
    core_half = swap(lax.dynamic_slice_in_dim(seq_sum, (1 - core_place) * half, half, 0), "img", 1)
    (input_grad, norm_sums), token = run_final(0, count - 1, (token,))
    kept_half, core_half, token = lax.optimization_barrier((kept_half, core_half, token))
    halves_sum = kept_half + core_half
    chip_half = swap(halves_sum, "img", chip_steps[0])
    final = count - 1
    (input_grad, *tail_sums), token = run_kernel(
        functools.partial(
            last_back_kernel,
            (*attention_dims, tokens // 2),
            (rows, width, wide, wide_part, tokens),
            ways,
            final,
        ),
        1,
        [
            per_image(across_mixed, final),
            per_image(grad_across, final),
            per_image(attended, final),
            per_image(log_total, final),
            per_image(keys, final),
            per_image(values, final),
            per_image(normed, final),
            mask_in,
            small_in,
            whole(back_sums[1]),
            whole(back_sums[2]),
            me_in,
            per_image(x, final),
            per_image(grad_middle, final),
        ]
        + [per_image(piece, final) for piece in grad_normed_pieces]
        + [small_in, qkv_in]
        + [whole(entry) for entry in (norm_sums, down_taps, middle_sums, bias_sums)],
        [part_image((tokens, channels), F32, final)]
        + [new_whole((shard + 32, 3 * HALF), BF)] * ways,
        [
            pltpu.VMEM((1, tokens, 3 * HALF), BF),
            pltpu.VMEM((80, HALF), F32),
            pltpu.VMEM(qkv_half, F32),
            pltpu.VMEM((HALF, key_rows), F32),
            pltpu.VMEM((HALF, key_rows), F32),
            pltpu.VMEM((tokens, HALF), F32),
            pltpu.VMEM((16, channels), F32),
            pltpu.VMEM((rows, wide, channels), BF),
            pltpu.VMEM((tokens, channels), F32),
            pltpu.VMEM((32, channels), F32),
        ],
        26,
        after=(token,),
        alias=[(input_grad, 0)],
    )
    halves_sum = halves_sum + chip_half
    halves_sum, *tail_sums = lax.optimization_barrier((halves_sum, *tail_sums))
    chip_half = [swap(halves_sum, "img", distance) for distance in chip_steps[1:2]]
    tail_parts, halves_sum, chip_half = lax.optimization_barrier(
        (exchange(tail_sums), halves_sum, chip_half)
    )
    halves_sum = tree_sum([halves_sum, *chip_half])
    for distance in chip_steps[2:]:
        halves_sum = halves_sum + swap(halves_sum, "img", distance)
    other_half = swap(halves_sum, "img", 1)
    tail = tree_sum([part.astype(F32) for part in tail_parts])
    tail = tree_sum([part.astype(F32) for part in share_low(tail, [1])])
    tail_parts = share_low(tail, range(2, lax.axis_size("img"), 2))

    known = jnp.sum(halves_sum * halves_sum) + jnp.sum(other_half * other_half)
    (tail, squared), _ = run_kernel(
        tail_kernel,
        1,
        [(known.reshape(1), scalar_block())] + [whole(part) for part in tail_parts],
        [new_whole(tail_parts[0].shape, F32), new_whole((8, 128), F32)],
        [],
        1,
    )
    squares = exchange([squared] * ways)

    def as_rows(entries):
        return [entry.reshape(1, -1) if entry.ndim == 1 else entry for entry in entries]

    state = as_rows(
        (qkv_weight, out_weight, expand_weight, shrink_weight, small_params, expand_bias)
        + (first_qkv, first_out, first_expand, first_shrink, first_small, first_bias)
        + (second_qkv, second_out, second_expand, second_shrink, second_small, second_bias)
    )
    place_in = jnp.stack([owner, core_place]).astype(jnp.int32)
    (norm, *updated), _ = run_kernel(
        functools.partial(update_kernel, ways),
        1,
        [(place_in, scalar_block())]
        + [whole(entry) for entry in (halves_sum, other_half, tail, *squares, *state)],
        [((1, 1), F32, scalar_block())] + [new_whole(entry.shape, F32) for entry in state[:6]] * 3,
        [pltpu.VMEM((shard, halves_sum.shape[1]), F32)],
        4,
    )
    for index in (5, 11, 17):
        updated[index] = updated[index].reshape(-1)
    return (
        block_out.reshape(images.shape),
        input_grad.reshape(images.shape),
        norm.reshape(()),
        *updated,
    )


def solution(mesh):
    sharded = (
        P("seq", None),
        P("seq", None),
        P("seq", None),
        P("seq", None),
        P(None, "seq"),
        P("seq"),
    )
    grid = P("img", "seq", None, None)
    return jax.shard_map(
        on_device,
        mesh=mesh,
        in_specs=(grid, grid, P("img", None)) + sharded * 3,
        out_specs=(grid, grid, P()) + sharded * 3,
        check_vma=False,
    )
```
